128 devices in a mesh: dp: 16 (over y, z_hi, core), tensor: 8 (over z_lo, x).
Axes of the slice: x: 4, y: 4, z: 4 (z_hi: 2, z_lo: 2; z = z_hi * 2 + z_lo), core: 2. Of those that a mesh axis runs over, the one named last changes fastest.
Arguments:
- tokens: bfloat16 [2, 64, 16, 2304], P(None, None, 'dp'), may hold values from -6 to 6
- cotangent: bfloat16 [3, 2, 64, 16, 2304], P(None, None, None, 'dp'), may hold values from -6 to 6
- segments: int32 [2, 1024], replicated, may hold values from 0 to 4, never falling along the last dimension, each value on 1 to 512 neighbouring positions
- codes_query: int32 [2304, 2048], P('dp', 'tensor'), may hold values from -128 to 127
- codes_key: int32 [2304, 1024], P('dp', 'tensor'), may hold values from -128 to 127
- codes_value: int32 [2304, 1024], P('dp', 'tensor'), may hold values from -128 to 127
- codes_out: int32 [2048, 2304], P('tensor', 'dp'), may hold values from -128 to 127
- codes_gate: int32 [2304, 9216], P('dp', 'tensor'), may hold values from -128 to 127
- codes_up: int32 [2304, 9216], P('dp', 'tensor'), may hold values from -128 to 127
- codes_down: int32 [9216, 2304], P('tensor', 'dp'), may hold values from -128 to 127
- query_column_scale: float32 [2048], P('tensor'), may hold values from 0.00014583333 to 0.0005833333
- key_column_scale: float32 [1024], P('tensor'), may hold values from 0.00014583333 to 0.0005833333
- value_column_scale: float32 [1024], P('tensor'), may hold values from 0.00014583333 to 0.0005833333
- output_column_scale: float32 [2304], replicated, may hold values from 0.00015467961 to 0.00061871845
- gate_column_scale: float32 [9216], P('tensor'), may hold values from 0.00014583333 to 0.0005833333
- up_column_scale: float32 [9216], P('tensor'), may hold values from 0.00014583333 to 0.0005833333
- down_column_scale: float32 [2304], replicated, may hold values from 7.2916664e-05 to 0.00029166666
- gain_first: float32 [2304], replicated, may hold values from -0.5 to 0.5
- gain_second: float32 [2304], replicated, may hold values from -0.5 to 0.5
- gain_third: float32 [2304], replicated, may hold values from -0.5 to 0.5
- gain_fourth: float32 [2304], replicated, may hold values from -0.5 to 0.5
Outputs:
- results: bfloat16 [3, 2, 64, 16, 2304], P(None, None, None, 'dp')
- input_token_gradient: float32 [2, 64, 16, 2304], P(None, None, 'dp')
- query_grad: float32 [2304, 2048], P('dp', 'tensor')
- key_grad: float32 [2304, 1024], P('dp', 'tensor')
- value_grad: float32 [2304, 1024], P('dp', 'tensor')
- out_grad: float32 [2048, 2304], P('tensor', 'dp')
- gate_grad: float32 [2304, 9216], P('dp', 'tensor')
- up_grad: float32 [2304, 9216], P('dp', 'tensor')
- down_grad: float32 [9216, 2304], P('tensor', 'dp')
- query_scale_grad: float32 [2048], P('tensor')
- key_scale_grad: float32 [1024], P('tensor')
- value_scale_grad: float32 [1024], P('tensor')
- out_scale_grad: float32 [2304], P('dp')
- gate_scale_grad: float32 [9216], P('tensor')
- up_scale_grad: float32 [9216], P('tensor')
- down_scale_grad: float32 [2304], P('dp')
- gain_first_grad: float32 [2304], P('dp')
- gain_second_grad: float32 [2304], P('dp')
- gain_third_grad: float32 [2304], P('dp')
- gain_fourth_grad: float32 [2304], P('dp')
The draws below stay inside these ranges and needn't reach their ends.
Inputs may be any that keep to these rules, and one draw needn't show every extreme that they name: `segments`: in each micro-batch the document number starts at 0, never falls, and each of the 5 documents covers 1 to min(512, 1020) positions; one covers exactly that many.
All inputs are finite; a program needn't handle non-finite values.
Results may differ from the reference program's by a relative error of at most 0.025.
Values may be sent and summed in bfloat16 or wider, within the bound.
A program may use at most 640 MiB of HBM per device.

```python
import math
import jax
import jax.numpy as jnp
import numpy as np
from jax import lax

MODEL_WIDTH = 2304
HQ = 8
KVH = 4
HD = 256
FF = 9216
TOK_MB = 64
MICRO_BATCHES = 2
DOCS = 5
DOC_LEN = 512
BATCH_TOKENS = 1024
N_DP = 16


def with_ends(values, own_key, smallest, high):
    index_at = [jax.random.randint(jax.random.fold_in(own_key, axis), (), 0, length) for axis, length in enumerate(values.shape)]
    main_axis = values.shape.index(max(values.shape))
    neighbour = index_at[:main_axis] + [(index_at[main_axis] + 1) % values.shape[main_axis]] + index_at[main_axis + 1:]
    return values.at[tuple(index_at)].set(smallest).at[tuple(neighbour)].set(high)


def steps_of(rng, extent, pieces, smallest, largest):
    factor_of, own = 1.0, jax.random.fold_in(rng, 6)
    for position, shards_of in pieces:
        steps = jnp.exp(jax.random.uniform(jax.random.fold_in(own, position), (shards_of,), jnp.float32, smallest / len(pieces), largest / len(pieces)))
        factor_of = factor_of * jnp.repeat(steps, extent[position] // shards_of).reshape([-1 if axis == position else 1 for axis in range(len(extent))])
    return factor_of


def length_profile(count, total, reach, skew):
    weights = [(1 << 20) // math.isqrt(standing ** skew) + 1 for standing in range(2, count + 1)]
    surplus, counts = total - reach - (count - 1), [1] * (count - 1)
    while surplus > 0:
        candidates = [i for i in range(count - 1) if counts[i] < reach]
        pool, budget = sum([weights[i] for i in candidates]), surplus
        for i in candidates:
            more = min(reach - counts[i], max(1, budget * weights[i] // pool), surplus)
            counts[i] = counts[i] + more
            surplus = surplus - more
    return np.array([reach] + counts)


def ragged(rng, amount, total, limit, skew):
    if amount == 2:
        one = jax.random.randint(rng, (), max(1, total - limit), min(limit, total - 1) + 1)
        return jnp.stack([one, total - one])
    lengths = jnp.asarray(length_profile(amount, total, limit, skew), jnp.int32)
    twos = (amount - 1) // 2
    donor, sink = lengths[1:1 + 2 * twos:2], lengths[2:2 + 2 * twos:2]
    slack = jnp.minimum(donor - 1, limit - sink)
    passed = jax.random.randint(jax.random.fold_in(rng, 1), (twos,), 0, 1 << 20) % (slack + 1)
    lengths = lengths.at[1:1 + 2 * twos:2].set(donor - passed).at[2:2 + 2 * twos:2].set(sink + passed)
    return lengths[jax.random.permutation(jax.random.fold_in(rng, 2), amount)]


def centred(key, extent, deviation, most, pieces=(), held_as=jnp.bfloat16):
    array = deviation * jax.random.normal(key, extent, jnp.float32)
    if pieces:
        array = array * steps_of(key, extent, pieces, -0.22, 0.18)
    return jnp.clip(array, -most, most).astype(held_as)


def setup_inputs(seed: int = 0) -> dict:
    splits = jax.random.split(jax.random.key(seed), 22)
    tokens = centred(splits[0], (MICRO_BATCHES, TOK_MB, N_DP, MODEL_WIDTH), 1.0, 6.0, ((2, 16),))
    cotangent = centred(splits[1], (3, MICRO_BATCHES, TOK_MB, N_DP, MODEL_WIDTH), 1.0, 6.0, ((3, 16),))
    segments = jax.vmap(lambda own: jnp.searchsorted(jnp.cumsum(ragged(own, DOCS, BATCH_TOKENS, min(DOC_LEN, BATCH_TOKENS - DOCS + 1), 2)), jnp.arange(BATCH_TOKENS), side="right"))(jax.random.split(splits[2], MICRO_BATCHES)).reshape((MICRO_BATCHES, BATCH_TOKENS)).astype(jnp.int32)
    codes_query = with_ends(jax.random.randint(splits[3], (MODEL_WIDTH, HQ * HD), -128, 128), jax.random.fold_in(splits[3], 1), -128, 127).astype(jnp.int32)
    codes_key = with_ends(jax.random.randint(splits[4], (MODEL_WIDTH, KVH * HD), -128, 128), jax.random.fold_in(splits[4], 1), -128, 127).astype(jnp.int32)
    codes_value = with_ends(jax.random.randint(splits[5], (MODEL_WIDTH, KVH * HD), -128, 128), jax.random.fold_in(splits[5], 1), -128, 127).astype(jnp.int32)
    codes_out = with_ends(jax.random.randint(splits[6], (HQ * HD, MODEL_WIDTH), -128, 128), jax.random.fold_in(splits[6], 1), -128, 127).astype(jnp.int32)
    codes_gate = with_ends(jax.random.randint(splits[7], (MODEL_WIDTH, FF), -128, 128), jax.random.fold_in(splits[7], 1), -128, 127).astype(jnp.int32)
    codes_up = with_ends(jax.random.randint(splits[8], (MODEL_WIDTH, FF), -128, 128), jax.random.fold_in(splits[8], 1), -128, 127).astype(jnp.int32)
    codes_down = with_ends(jax.random.randint(splits[9], (FF, MODEL_WIDTH), -128, 128), jax.random.fold_in(splits[9], 1), -128, 127).astype(jnp.int32)
    query_column_scale = jnp.clip(jnp.exp(math.log(0.0005833333) - 1.3862944 * jax.random.uniform(splits[10], (HQ * HD,), jnp.float32) ** steps_of(splits[10], (HQ * HD,), ((0, 8),), -0.2, 0.2)), 0.00014583333, 0.0005833333)
    key_column_scale = jnp.clip(jnp.exp(math.log(0.0005833333) - 1.3862944 * jax.random.uniform(splits[11], (KVH * HD,), jnp.float32) ** steps_of(splits[11], (KVH * HD,), ((0, 8),), -0.2, 0.2)), 0.00014583333, 0.0005833333)
    value_column_scale = jnp.clip(jnp.exp(math.log(0.0005833333) - 1.3862944 * jax.random.uniform(splits[12], (KVH * HD,), jnp.float32) ** steps_of(splits[12], (KVH * HD,), ((0, 8),), -0.2, 0.2)), 0.00014583333, 0.0005833333)
    output_column_scale = jnp.clip(jnp.exp(jax.random.uniform(splits[13], (MODEL_WIDTH,), jnp.float32, math.log(0.00015467961), math.log(0.00061871845))), 0.00015467961, 0.00061871845)
    gate_column_scale = jnp.clip(jnp.exp(math.log(0.0005833333) - 1.3862944 * jax.random.uniform(splits[14], (FF,), jnp.float32) ** steps_of(splits[14], (FF,), ((0, 8),), -0.2, 0.2)), 0.00014583333, 0.0005833333)
    up_column_scale = jnp.clip(jnp.exp(math.log(0.0005833333) - 1.3862944 * jax.random.uniform(splits[15], (FF,), jnp.float32) ** steps_of(splits[15], (FF,), ((0, 8),), -0.2, 0.2)), 0.00014583333, 0.0005833333)
    down_column_scale = jnp.clip(jnp.exp(jax.random.uniform(splits[16], (MODEL_WIDTH,), jnp.float32, math.log(7.291666406672448e-05), math.log(0.00029166666))), 7.291666406672448e-05, 0.00029166666)
    gain_first = jnp.clip(jax.random.uniform(splits[17], (MODEL_WIDTH,), jnp.float32, -0.5, 0.5), -0.5, 0.5)
    gain_second = jnp.clip(jax.random.uniform(splits[18], (MODEL_WIDTH,), jnp.float32, -0.5, 0.5), -0.5, 0.5)
    gain_third = jnp.clip(jax.random.uniform(splits[19], (MODEL_WIDTH,), jnp.float32, -0.5, 0.5), -0.5, 0.5)
    gain_fourth = jnp.clip(jax.random.uniform(splits[20], (MODEL_WIDTH,), jnp.float32, -0.5, 0.5), -0.5, 0.5)
    return dict(tokens=tokens, cotangent=cotangent, segments=segments, codes_query=codes_query, codes_key=codes_key, codes_value=codes_value, codes_out=codes_out, codes_gate=codes_gate, codes_up=codes_up, codes_down=codes_down, query_column_scale=query_column_scale, key_column_scale=key_column_scale, value_column_scale=value_column_scale, output_column_scale=output_column_scale, gate_column_scale=gate_column_scale, up_column_scale=up_column_scale, down_column_scale=down_column_scale, gain_first=gain_first, gain_second=gain_second, gain_third=gain_third, gain_fourth=gain_fourth)


@jax.custom_vjp
def lower_codes(v):
    return lax.optimization_barrier(v.astype(jnp.bfloat16)).astype(jnp.float32)

@jax.custom_vjp
def low_back(v):
    return v

def low_keep(v):
    return (lower_codes(v), None)

def low_pass(kept, grad):
    return (grad,)

def back_keep(v):
    return (v, None)

def back_low(kept, grad):
    return (lower_codes(grad),)
lower_codes.defvjp(low_keep, low_pass)
low_back.defvjp(back_keep, back_low)
EPSILON = 1e-06
SOFTCAP = 50.0
ROPE_BASE = 10000.0
SHIFTS = (0, 4, 6)
HIGHEST = lax.Precision.HIGHEST

def matmul(left_op, right_op):
    return jnp.dot(left_op, right_op, precision=HIGHEST, preferred_element_type=jnp.float32)

def rms_gain(signal, gain):
    inverse = lax.rsqrt(lax.optimization_barrier(jnp.mean(signal * signal, axis=-1, keepdims=True)) + EPSILON)
    return signal * inverse * (1.0 + gain)

def level_widths(code_array, shift_bits):
    if shift_bits == 0:
        return code_array.astype(jnp.float32)
    stride = 2 ** shift_bits
    return (jnp.floor_divide(code_array, stride) * stride + stride // 2).astype(jnp.float32)

def angles(places, head_size):
    halfway = head_size // 2
    expo = jnp.arange(halfway, dtype=jnp.float32) * (2.0 / head_size)
    freqs = places.astype(jnp.float32)[:, None] * jnp.power(ROPE_BASE, -expo)[None, :]
    return (jnp.cos(freqs), jnp.sin(freqs))

def rotate(signal, cosine, sine):
    halfway = signal.shape[-1] // 2
    former = signal[..., :halfway]
    latter = signal[..., halfway:]
    return jnp.concatenate([former * cosine - latter * sine, latter * cosine + former * sine], axis=-1)

def reference(tokens, cotangent, segments, codes_query, codes_key, codes_value, codes_out, codes_gate, codes_up, codes_down, query_column_scale, key_column_scale, value_column_scale, output_column_scale, gate_column_scale, up_column_scale, down_column_scale, gain_first, gain_second, gain_third, gain_fourth):
    every_code = (codes_query, codes_key, codes_value, codes_out, codes_gate, codes_up, codes_down)
    group = HQ // KVH

    def micro_batch(layer_inputs, document_index, latent_weights, scaling_factors, gain_collection):
        length = layer_inputs.shape[0]
        places = jnp.arange(length, dtype=jnp.int32)
        starts = lax.optimization_barrier(jnp.sum((document_index[None, :] < document_index[:, None]).astype(jnp.int32), axis=1))
        cosine, sine = angles(places - starts, HD)
        cosine = cosine[:, None, :]
        sine = sine[:, None, :]
        allowed = (document_index[None, :] == document_index[:, None]) & (places[None, :] <= places[:, None])
        normed_input = lower_codes(rms_gain(layer_inputs, gain_collection[0]))
        stacked = []
        for shift_bits in SHIFTS:
            weight_matrices = [lower_codes(scaling_factors[level_choice] * level_widths(every_code[level_choice], shift_bits) + latent_weights[level_choice]) for level_choice in range(7)]
            w_query, w_key, w_value, w_out, w_gate, w_up, w_down = weight_matrices
            query_pre = low_back(matmul(normed_input, w_query)).reshape(length, HQ, HD)
            key_pre = low_back(matmul(normed_input, w_key)).reshape(length, KVH, HD)
            value_pre = low_back(matmul(normed_input, w_value)).reshape(length, KVH, HD)
            query = lower_codes(rotate(query_pre, cosine, sine))
            keys = jnp.repeat(lower_codes(rotate(key_pre, cosine, sine)), group, axis=1)
            values = jnp.repeat(lower_codes(value_pre), group, axis=1)
            scores = low_back(jnp.einsum('qhd,khd->hqk', query, keys, precision=HIGHEST) * 0.0625)
            capped = SOFTCAP * jnp.tanh(scores / SOFTCAP)
            probs = jax.nn.softmax(jnp.where(allowed[None], capped, -1e+30), axis=-1)
            attended = jnp.einsum('hqk,khd->qhd', lower_codes(probs), values, precision=HIGHEST)
            attended = lower_codes(low_back(attended)).reshape(length, HQ * HD)
            branch = low_back(matmul(attended, w_out))
            middle = layer_inputs + rms_gain(branch, gain_collection[1])
            normed_middle = lower_codes(rms_gain(middle, gain_collection[2]))
            gate_pre = low_back(matmul(normed_middle, w_gate))
            up_pre = low_back(matmul(normed_middle, w_up))
            hidden = lower_codes(jax.nn.gelu(gate_pre, approximate=True) * up_pre)
            feedforward = low_back(matmul(hidden, w_down))
            stacked.append(middle + rms_gain(feedforward, gain_collection[3]))
        return jnp.stack(stacked)
    batch_loop = jax.checkpoint(micro_batch)

    def forward_pass(flattened, latent_weights, scaling_factors, gain_collection):
        return jnp.stack([batch_loop(flattened[micro_batch_index], segments[micro_batch_index], latent_weights, scaling_factors, gain_collection) for micro_batch_index in range(MICRO_BATCHES)], axis=1)
    flattened = tokens.astype(jnp.float32).reshape(MICRO_BATCHES, BATCH_TOKENS, MODEL_WIDTH)
    latent_weights = tuple((jnp.zeros(code_array.shape, jnp.float32) for code_array in every_code))
    scaling_factors = (query_column_scale, key_column_scale, value_column_scale, output_column_scale, gate_column_scale, up_column_scale, down_column_scale)
    gain_collection = (gain_first, gain_second, gain_third, gain_fourth)
    layer_outputs, backward_step = jax.vjp(forward_pass, flattened, latent_weights, scaling_factors, gain_collection)
    flattened_gradient, latent_gradients, scaling_gradients, gain_gradients = backward_step(cotangent.astype(jnp.float32).reshape(3, MICRO_BATCHES, BATCH_TOKENS, MODEL_WIDTH))
    results = layer_outputs.reshape(3, MICRO_BATCHES, TOK_MB, N_DP, MODEL_WIDTH).astype(jnp.bfloat16)
    input_token_gradient = flattened_gradient.reshape(MICRO_BATCHES, TOK_MB, N_DP, MODEL_WIDTH)
    return (results, input_token_gradient, latent_gradients[0], latent_gradients[1], latent_gradients[2], latent_gradients[3], latent_gradients[4], latent_gradients[5], latent_gradients[6], scaling_gradients[0], scaling_gradients[1], scaling_gradients[2], scaling_gradients[3], scaling_gradients[4], scaling_gradients[5], scaling_gradients[6], gain_gradients[0], gain_gradients[1], gain_gradients[2], gain_gradients[3])
```

```python
import functools

import jax
import jax.numpy as jnp
from jax import lax
from jax.experimental import pallas as pl
from jax.experimental.pallas import tpu as pltpu
from jax.sharding import PartitionSpec as P

MESH = pl.DeviceIdType.MESH
F32 = jnp.float32
B16 = jnp.bfloat16
EPSILON = 1e-06
SOFTCAP = 50.0
ROPE_BASE = 10000.0
MASKED = -1e30
HD = 256
WIDE = 2304
SHARD = 144
LOW = 64
HIGH = SHARD - LOW
TENSOR = 8
ROWS = 128
SLICE = ROWS // TENSOR
VMEM_BYTES = 56 * 2**20


def here():
    dp = lax.axis_index("dp")
    return lax.div(dp, 4), lax.rem(lax.div(dp, 2), 2), lax.rem(dp, 2), lax.axis_index("tensor")


def rank(y, z_hi, core):
    return (y * 2 + z_hi) * 2 + core


def remote(src, dst, send, recv, dp, tensor):
    return pltpu.make_async_remote_copy(
        src, dst, send, recv, device_id=(dp, tensor), device_id_type=MESH
    )


def greet(devices):
    barrier = pltpu.get_barrier_semaphore()
    for device in devices:
        pl.semaphore_signal(barrier, inc=1, device_id=device, device_id_type=MESH)
    pl.semaphore_wait(barrier, len(devices))


def any_space(count):
    return [pl.BlockSpec(memory_space=pl.ANY)] * count


def vmem_space(count):
    return [pl.BlockSpec(memory_space=pltpu.VMEM)] * count


def params(collective_id):
    return pltpu.CompilerParams(
        collective_id=collective_id, has_side_effects=True, vmem_limit_bytes=VMEM_BYTES
    )


def gather_kernel(count, *refs):
    srcs, outs = refs[:count], refs[count : 2 * count]
    send, recv, local = refs[2 * count :]
    y, zh, core, t = here()
    me, sib, zz = rank(y, zh, core), rank(y, zh, 1 - core), rank(y, 1 - zh, core)
    fore = [rank(lax.rem(y + dy, 4), zh, core) for dy in (1, 2, 3)]
    behind = [lax.rem(y + 4 - dy, 4) for dy in (1, 2, 3)]
    low, high = pl.ds(0, LOW), pl.ds(LOW, HIGH)
    greet([(sib, t), (zz, t)] + [(dp, t) for dp in fore])
    started = []

    def push(k, slot, src, dst, dp):
        copy = remote(src, dst, send.at[k, slot], recv.at[k, slot], dp, t)
        copy.start()
        started.append(copy)

    def arrive(k, slot, ref):
        remote(ref, ref, send.at[k, slot], recv.at[k, slot], sib, t).wait_recv()

    mine = []
    for k in range(count):
        src, out = srcs[k], outs[k]
        copy = pltpu.make_async_copy(src, out.at[me], local.at[k])
        copy.start()
        mine.append(copy)
        push(k, 0, src.at[low], out.at[me, low], zz)
        for i in range(3):
            push(k, 4 + i, src.at[high], out.at[me, high], fore[i])
        for i in range(3):
            push(k, 1 + i, src.at[low], out.at[me, low], fore[i])
        push(k, 7, src.at[high], out.at[me, high], zz)
        push(k, 14, src, out.at[me], sib)
    for k in range(count):
        out = outs[k]
        block = out.at[zz, low]
        arrive(k, 0, block)
        for i in range(3):
            push(k, 8 + i, block, block, fore[i])
        push(k, 15, block, block, sib)
        for i in range(3):
            block = out.at[rank(behind[i], zh, core), high]
            arrive(k, 4 + i, block)
            push(k, 11 + i, block, block, zz)
            push(k, 16 + i, block, block, sib)
        for i in range(3):
            block = out.at[rank(behind[i], zh, core), low]
            arrive(k, 1 + i, block)
            push(k, 19 + i, block, block, sib)
        block = out.at[zz, high]
        arrive(k, 7, block)
        push(k, 22, block, block, sib)
        for i in range(3):
            block = out.at[rank(behind[i], 1 - zh, core), low]
            arrive(k, 8 + i, block)
            push(k, 23 + i, block, block, sib)
            block = out.at[rank(behind[i], 1 - zh, core), high]
            arrive(k, 11 + i, block)
            push(k, 26 + i, block, block, sib)
    for k in range(count):
        out = outs[k]
        zz_sib = rank(y, 1 - zh, 1 - core)
        arrive(k, 14, out.at[sib])
        arrive(k, 15, out.at[zz_sib, low])
        arrive(k, 22, out.at[zz_sib, high])
        for i in range(3):
            near, far = rank(behind[i], zh, 1 - core), rank(behind[i], 1 - zh, 1 - core)
            arrive(k, 16 + i, out.at[near, high])
            arrive(k, 19 + i, out.at[near, low])
            arrive(k, 23 + i, out.at[far, low])
            arrive(k, 26 + i, out.at[far, high])
    for copy in mine:
        copy.wait()
    for copy in started:
        copy.wait_send()


def gather_weights(shards):
    count = len(shards)
    return pl.pallas_call(
        functools.partial(gather_kernel, count),
        name="gather_weights",
        out_shape=[jax.ShapeDtypeStruct((16,) + s.shape, s.dtype) for s in shards],
        in_specs=any_space(count),
        out_specs=any_space(count),
        scratch_shapes=[
            pltpu.SemaphoreType.DMA((count, 29)),
            pltpu.SemaphoreType.DMA((count, 29)),
            pltpu.SemaphoreType.DMA((count,)),
        ],
        compiler_params=params(1),
    )(*shards)


def scatter_kernel(count, *refs):
    parts, outs = refs[:count], refs[count : 2 * count]
    own, sibs, yrecv, zrecv, ylast, zlast = (
        refs[(2 + i) * count : (3 + i) * count] for i in range(6)
    )
    send, recv, local = refs[8 * count :]
    y, zh, core, t = here()
    sib, zz = rank(y, zh, 1 - core), rank(y, 1 - zh, core)
    ahead = [lax.rem(y + dy, 4) for dy in (1, 2, 3)]
    fore = [rank(place, zh, core) for place in ahead]
    greet([(sib, t), (zz, t)] + [(dp, t) for dp in fore])
    started = []

    def push(k, slot, src, dst, dp):
        copy = remote(src, dst, send.at[k, slot], recv.at[k, slot], dp, t)
        copy.start()
        started.append(copy)

    def arrive(k, slot, ref):
        remote(ref, ref, send.at[k, slot], recv.at[k, slot], sib, t).wait_recv()

    order = ahead + [y]
    for k in range(count):
        for i, place in enumerate(order):
            pair = pl.ds(place * 2, 2)
            back = lax.rem(y + 4 - (i + 1), 4)
            push(k, i, parts[k].at[pair, 1 - core], sibs[k].at[pair], sib)
            pltpu.make_async_copy(
                parts[k].at[pair, core], own[k].at[pair], local.at[k, i]
            ).start()
    for k in range(count):
        for i, place in enumerate(order):
            pair = pl.ds(place * 2, 2)
            pltpu.make_async_copy(
                parts[k].at[pair, core], own[k].at[pair], local.at[k, i]
            ).wait()
            arrive(k, i, sibs[k].at[pair])

            def add(step, _, k=k, place=place):
                chip = place * 2 + lax.div(step, SHARD // 16)
                rows = pl.ds(pl.multiple_of(lax.rem(step, SHARD // 16) * 16, 16), 16)
                own[k][chip, rows] = (
                    own[k][chip, rows].astype(F32) + sibs[k][chip, rows].astype(F32)
                ).astype(B16)
                return 0

            lax.fori_loop(0, 2 * SHARD // 16, add, 0)
            if i < 3:
                push(k, 4 + i, own[k].at[pair, pl.ds(0, LOW)], yrecv[k].at[i], fore[i])
            push(
                k, 7 + i, own[k].at[place * 2 + 1 - zh, pl.ds(LOW, HIGH)], zrecv[k].at[place], zz
            )
    for k in range(count):
        for i, place in enumerate(order):
            arrive(k, 7 + i, zrecv[k].at[place])

            def merge(step, _, k=k, place=place):
                rows = pl.ds(pl.multiple_of(step * 16, 16), 16)
                mine = pl.ds(pl.multiple_of(step * 16 + LOW, 16), 16)
                zrecv[k][place, rows] = (
                    zrecv[k][place, rows].astype(F32) + own[k][place * 2 + zh, mine].astype(F32)
                ).astype(B16)
                return 0

            lax.fori_loop(0, HIGH // 16, merge, 0)
            if i < 3:
                push(k, 11 + i, zrecv[k].at[place], ylast[k].at[i], fore[i])
        for i in range(3):
            arrive(k, 4 + i, yrecv[k].at[i])

        def pool(step, _, k=k):
            chip = lax.div(step, LOW // 16)
            rows = pl.ds(pl.multiple_of(lax.rem(step, LOW // 16) * 16, 16), 16)
            total = own[k][y * 2 + chip, rows].astype(F32)
            for i in range(3):
                total = total + yrecv[k][i, chip, rows].astype(F32)
            own[k][y * 2 + chip, rows] = total.astype(B16)
            return 0

        lax.fori_loop(0, 2 * LOW // 16, pool, 0)
        push(k, 14, own[k].at[y * 2 + 1 - zh, pl.ds(0, LOW)], zlast[k], zz)
    for k in range(count):
        arrive(k, 14, zlast[k])

        def end_low(step, _, k=k):
            rows = pl.ds(pl.multiple_of(step * 16, 16), 16)
            outs[k][rows] = own[k][y * 2 + zh, rows].astype(F32) + zlast[k][rows].astype(F32)
            return 0

        lax.fori_loop(0, LOW // 16, end_low, 0)
        for i in range(3):
            arrive(k, 11 + i, ylast[k].at[i])

        def end_high(step, _, k=k):
            rows = pl.ds(pl.multiple_of(step * 16, 16), 16)
            total = zrecv[k][y, rows].astype(F32)
            for i in range(3):
                total = total + ylast[k][i, rows].astype(F32)
            outs[k][pl.ds(pl.multiple_of(step * 16 + LOW, 16), 16)] = total
            return 0

        lax.fori_loop(0, HIGH // 16, end_high, 0)
    for copy in started:
        copy.wait_send()


def scatter_gradients(parts):
    count = len(parts)
    columns = [part.shape[-1] for part in parts]
    scratch = [pltpu.VMEM((8, SHARD, c), B16) for c in columns]
    scratch += [pltpu.VMEM((8, SHARD, c), B16) for c in columns]
    scratch += [pltpu.VMEM((3, 2, LOW, c), B16) for c in columns]
    scratch += [pltpu.VMEM((4, HIGH, c), B16) for c in columns]
    scratch += [pltpu.VMEM((3, HIGH, c), B16) for c in columns]
    scratch += [pltpu.VMEM((LOW, c), B16) for c in columns]
    return pl.pallas_call(
        functools.partial(scatter_kernel, count),
        name="scatter_gradients",
        out_shape=[jax.ShapeDtypeStruct((SHARD, c), F32) for c in columns],
        in_specs=any_space(count),
        out_specs=vmem_space(count),
        scratch_shapes=scratch
        + [
            pltpu.SemaphoreType.DMA((count, 15)),
            pltpu.SemaphoreType.DMA((count, 15)),
            pltpu.SemaphoreType.DMA((count, 4)),
        ],
        compiler_params=params(2),
    )(*[part.reshape(8, 2, SHARD, part.shape[-1]) for part in parts])


def row_block(index):
    return pl.ds(pl.multiple_of(index * SLICE, SLICE), SLICE)


def tensor_peers():
    t = lax.axis_index("tensor")
    return [lax.rem(t + k, TENSOR) for k in range(TENSOR)]


def greet_tensor():
    dp = lax.axis_index("dp")
    greet([(dp, peer) for peer in tensor_peers()[1:]])


def scatter_rows(part, held, send, recv, local):
    dp = lax.axis_index("dp")
    peers = tensor_peers()
    copies = []
    for k in range(1, TENSOR):
        copy = remote(
            part.at[:, row_block(peers[k])], held.at[k], send.at[k], recv.at[k], dp, peers[k]
        )
        copy.start()
        copies.append(copy)
    mine = pltpu.make_async_copy(part.at[:, row_block(peers[0])], held.at[0], local)
    mine.start()
    mine.wait()
    return copies


def summed(held, copies):
    total = held[0].astype(F32)
    for k in range(1, TENSOR):
        copies[k - 1].wait_recv()
        total = total + held[k].astype(F32)
    return total


def spread_rows(block, whole, send, recv, local):
    dp = lax.axis_index("dp")
    peers = tensor_peers()
    here_rows = whole.at[:, row_block(peers[0])]
    copies = []
    for k in range(1, TENSOR):
        copy = remote(block, here_rows, send.at[k], recv.at[k], dp, peers[k])
        copy.start()
        copies.append(copy)
    mine = pltpu.make_async_copy(block, here_rows, local)
    mine.start()

    def finish():
        mine.wait()
        for k in range(1, TENSOR):
            source = whole.at[:, row_block(peers[TENSOR - k])]
            remote(source, source, send.at[k], recv.at[k], dp, peers[k]).wait_recv()
        for copy in copies:
            copy.wait_send()

    return finish


def inverse_rms(signal):
    return lax.rsqrt(jnp.mean(signal * signal, axis=-1, keepdims=True) + EPSILON)


def norm_back(normed, inverse, gain, upstream):
    inner = upstream * (1.0 + gain)
    return inverse * (inner - normed * jnp.mean(inner * normed, axis=-1, keepdims=True))


def over_rows(term):
    return jnp.sum(term, axis=(0, 1))[None]


def load_rows(whole, block, local):
    copy = pltpu.make_async_copy(
        whole.at[:, row_block(lax.axis_index("tensor"))], block, local
    )
    copy.start()
    return copy


def middle_kernel(
    part, tokens, gains, normed, branch, middle, held, mine, block, send, recv, local
):
    greet_tensor()
    copies = scatter_rows(part, held, send.at[0], recv.at[0], local.at[0])
    load = load_rows(tokens, mine, local.at[1])
    load.wait()
    signal = summed(held, copies)
    branch[...] = signal
    total = mine[...].astype(F32) + signal * inverse_rms(signal) * (1.0 + gains[1:2])
    middle[...] = total
    block[...] = (total * inverse_rms(total) * (1.0 + gains[2:3])).astype(B16)
    finish = spread_rows(block, normed, send.at[1], recv.at[1], local.at[2])
    for copy in copies:
        copy.wait_send()
    finish()


def feed_kernel(
    part, cotangent, middle, gains, d_feed, results, sums, held, mine, block, final, send, recv, local
):
    greet_tensor()
    copies = scatter_rows(part, held, send.at[0], recv.at[0], local.at[0])
    load = load_rows(cotangent, mine, local.at[1])
    load.wait()
    signal = summed(held, copies)
    inverse = inverse_rms(signal)
    normed = signal * inverse
    upstream = mine[...].astype(F32)
    lowered = norm_back(normed, inverse, gains[3:4], upstream).astype(B16)
    block[...] = lowered
    finish = spread_rows(block, d_feed, send.at[1], recv.at[1], local.at[2])
    final[...] = (middle[...] + normed * (1.0 + gains[3:4])).astype(B16)
    finish_results = spread_rows(final, results, send.at[2], recv.at[2], local.at[3])
    sums[0:1] = over_rows(upstream * normed)
    sums[1:2] = over_rows(lowered.astype(F32) * signal)
    for copy in copies:
        copy.wait_send()
    finish()
    finish_results()


def branch_kernel(
    part, cotangent, middle, branch, gains, d_branch, d_middle, sums, held, mine, block, send, recv, local
):
    greet_tensor()
    copies = scatter_rows(part, held, send.at[0], recv.at[0], local.at[0])
    load = load_rows(cotangent, mine, local.at[1])
    load.wait()
    upstream = summed(held, copies)
    signal = middle[...]
    inverse = inverse_rms(signal)
    normed = signal * inverse
    gradient = mine[...].astype(F32) + norm_back(normed, inverse, gains[2:3], upstream)
    lower = branch[...]
    inverse_lower = inverse_rms(lower)
    normed_lower = lower * inverse_lower
    lowered = norm_back(normed_lower, inverse_lower, gains[1:2], gradient).astype(B16)
    block[...] = lowered
    finish = spread_rows(block, d_branch, send.at[1], recv.at[1], local.at[2])
    d_middle[...] = jnp.sum(gradient, axis=0, keepdims=True)
    sums[0:1] = over_rows(upstream * normed)
    sums[1:2] = over_rows(gradient * normed_lower)
    sums[2:3] = over_rows(lowered.astype(F32) * lower)
    for copy in copies:
        copy.wait_send()
    finish()


def input_kernel(
    part, tokens, d_middle, gains, gradient, sums, held, mine, block, send, recv, local
):
    greet_tensor()
    copies = scatter_rows(part, held, send.at[0], recv.at[0], local.at[0])
    load = load_rows(tokens, mine, local.at[1])
    load.wait()
    upstream = summed(held, copies)
    signal = mine[...].astype(F32)
    inverse = inverse_rms(signal)
    normed = signal * inverse
    block[...] = d_middle[...] + norm_back(normed, inverse, gains[0:1], upstream)
    finish = spread_rows(block, gradient, send.at[1], recv.at[1], local.at[2])
    sums[0:1] = over_rows(upstream * normed)
    for copy in copies:
        copy.wait_send()
    finish()


def tensor_call(
    kernel, name, collective_id, depth, loaded, operands, in_specs, outs, out_specs, blocks
):
    return pl.pallas_call(
        kernel,
        name=name,
        out_shape=outs,
        in_specs=in_specs,
        out_specs=out_specs,
        scratch_shapes=[
            pltpu.VMEM((TENSOR, depth, SLICE, WIDE), B16),
            pltpu.VMEM((loaded, SLICE, WIDE), B16),
        ]
        + blocks
        + [
            pltpu.SemaphoreType.DMA((3, TENSOR)),
            pltpu.SemaphoreType.DMA((3, TENSOR)),
            pltpu.SemaphoreType.DMA((4,)),
        ],
        compiler_params=params(collective_id),
    )(*operands)


def struct(shape, dtype):
    return jax.ShapeDtypeStruct(shape, dtype)


def unit_owner(micro, width):
    return rank(width, micro, 0)


def rotate(signal, cosine, sine):
    former, latter = signal[:, : HD // 2], signal[:, HD // 2 :]
    return jnp.concatenate([former * cosine - latter * sine, latter * cosine + former * sine], -1)


def unrotate(signal, cosine, sine):
    former, latter = signal[:, : HD // 2], signal[:, HD // 2 :]
    return jnp.concatenate([former * cosine + latter * sine, latter * cosine - former * sine], -1)


def block_scores(queries, keys, first, b, kb):
    scores = lax.dot_general(queries, keys, (((1,), (1,)), ((), ())), preferred_element_type=F32)
    bent = jnp.tanh(scores * (0.0625 / SOFTCAP))
    lane = lax.broadcasted_iota(jnp.int32, (256, 256), 1)
    row = lax.broadcasted_iota(jnp.int32, (256, 256), 0)
    key_place = (16 * kb + (lane & 15)) * 16 + (lane >> 4)
    query_place = (16 * b + (row & 15)) * 16 + (row >> 4)
    allowed = (key_place >= first) & (key_place <= query_place)
    return bent, jnp.where(allowed, SOFTCAP * bent, MASKED)


def block_probs(queries, keys, first, b):
    pieces = [
        block_scores(queries, keys[kb], first, b, kb) for kb in range(max(0, b - 2), b + 1)
    ]
    peak = functools.reduce(
        jnp.maximum, [jnp.max(capped, axis=-1, keepdims=True) for _, capped in pieces]
    )
    exps = [jnp.exp(capped - peak) for _, capped in pieces]
    total = functools.reduce(jnp.add, [jnp.sum(e, axis=-1, keepdims=True) for e in exps])
    return [bent for bent, _ in pieces], [e / total for e in exps]


def dot(left, right, left_dim, right_dim):
    return lax.dot_general(
        left, right, (((left_dim,), (right_dim,)), ((), ())), preferred_element_type=F32
    )


def attend_kernel(
    qkv, first, cosine, sine, attended, q_rot, k_rot, v_all,
    rq, rkv, held, send, recv_q, recv_kv, send_back, recv_back, local,
):
    y, zh, core, t = here()
    me = rank(y, zh, core)
    half = lax.rem(t, 2)
    other = t + 1 - 2 * half
    owner = (y < 3) & (core == 0)
    units = [(m, w) for m in range(2) for w in range(3)]
    barrier = pltpu.get_barrier_semaphore()

    def signal(dp, tensor):
        pl.semaphore_signal(barrier, inc=1, device_id=(dp, tensor), device_id_type=MESH)

    @pl.when(owner)
    def _():
        def each(d, _):
            pl.when(d != me)(lambda: signal(d, t))
            signal(d, other)
            return 0

        lax.fori_loop(0, 16, each, 0)

    for m, w in units:
        pl.when(unit_owner(m, w) != me)(functools.partial(signal, unit_owner(m, w), t))

    @pl.when(owner)
    def _():
        pl.semaphore_wait(barrier, 26)

    @pl.when(jnp.logical_not(owner))
    def _():
        pl.semaphore_wait(barrier, 12)

    def to_owner(u, m, w, start):
        o = unit_owner(m, w)
        q_src, kv_src = qkv.at[w, m, :, pl.ds(0, HD)], qkv.at[w, m, :, pl.ds(HD, HD)]
        across = remote(kv_src, rkv.at[half, me], send.at[u, 2], recv_kv.at[half, me], o, other)
        away = [
            remote(q_src, rq.at[me], send.at[u, 0], recv_q.at[me], o, t),
            remote(kv_src, rkv.at[half, me], send.at[u, 1], recv_kv.at[half, me], o, t),
        ]
        near = [
            pltpu.make_async_copy(q_src, rq.at[me], local.at[0]),
            pltpu.make_async_copy(kv_src, rkv.at[half, me], local.at[1]),
        ]

        @pl.when(o != me)
        def _():
            for copy in away:
                copy.start() if start else copy.wait_send()

        @pl.when(o == me)
        def _():
            for copy in near:
                copy.start() if start else copy.wait()

        across.start() if start else across.wait_send()

    for u, (m, w) in enumerate(units):
        to_owner(u, m, w, True)
    for u, (m, w) in enumerate(units):
        to_owner(u, m, w, False)

    @pl.when(owner)
    def _():
        def each(d, _):
            @pl.when(d != me)
            def _():
                remote(rq.at[d], rq.at[d], send.at[0, 0], recv_q.at[d], me, other).wait_recv()
                remote(
                    rkv.at[half, d], rkv.at[half, d], send.at[0, 0], recv_kv.at[half, d], me, other
                ).wait_recv()

            remote(
                rkv.at[1 - half, d], rkv.at[1 - half, d], send.at[0, 0], recv_kv.at[1 - half, d], me, other
            ).wait_recv()
            return 0

        lax.fori_loop(0, 16, each, 0)
        for b in range(4):
            rows = slice(16 * b, 16 * b + 16)
            c, s = cosine[b], sine[b]
            q = rq[:, rows, :].reshape(256, HD).astype(F32)
            q_rot[b] = rotate(q, c, s).astype(B16)
            k = jnp.concatenate(
                [rkv[i, :, rows, : HD // 2].reshape(256, HD // 2) for i in range(2)], -1
            )
            k_rot[b] = rotate(k.astype(F32), c, s).astype(B16)
            v_all[b] = jnp.concatenate(
                [rkv[i, :, rows, HD // 2 :].reshape(256, HD // 2) for i in range(2)], -1
            )
        for b in range(4):
            keys = {kb: k_rot[kb] for kb in range(max(0, b - 2), b + 1)}
            _, probs = block_probs(q_rot[b], keys, first[b], b)
            out = sum(
                dot(p.astype(B16), v_all[kb], 1, 0) for p, kb in zip(probs, sorted(keys))
            )
            held[:, 16 * b : 16 * b + 16, :] = out.astype(B16).reshape(16, 16, HD)

        def hand_back(d, start):
            @pl.when(d != me)
            def _():
                copy = remote(
                    held.at[d], attended.at[y, zh], send_back.at[d], recv_back.at[zh * 3 + y], d, t
                )
                copy.start() if start else copy.wait_send()

            @pl.when(d == me)
            def _():
                copy = pltpu.make_async_copy(held.at[d], attended.at[y, zh], local.at[0])
                copy.start() if start else copy.wait()

        lax.fori_loop(0, 16, lambda d, _: (hand_back(d, True), 0)[1], 0)
        lax.fori_loop(0, 16, lambda d, _: (hand_back(d, False), 0)[1], 0)

    for u, (m, w) in enumerate(units):

        @pl.when(unit_owner(m, w) != me)
        def _():
            ref = attended.at[w, m]
            remote(ref, ref, send.at[0, 0], recv_back.at[u], me, other).wait_recv()


def attend(qkv, first, cosine, sine):
    return pl.pallas_call(
        attend_kernel,
        name="attend",
        out_shape=[struct((3, 2, 64, HD), B16)] + [struct((4, 256, HD), B16)] * 3,
        in_specs=any_space(1) + vmem_space(3),
        out_specs=any_space(1) + vmem_space(3),
        scratch_shapes=[
            pltpu.VMEM((16, 64, HD), B16),
            pltpu.VMEM((2, 16, 64, HD), B16),
            pltpu.VMEM((16, 64, HD), B16),
            pltpu.SemaphoreType.DMA((6, 3)),
            pltpu.SemaphoreType.DMA((16,)),
            pltpu.SemaphoreType.DMA((2, 16)),
            pltpu.SemaphoreType.DMA((16,)),
            pltpu.SemaphoreType.DMA((6,)),
            pltpu.SemaphoreType.DMA((2,)),
        ],
        compiler_params=params(3),
    )(qkv, first, cosine, sine)


def attend_back_kernel(
    d_attended, first, cosine, sine, q_rot, k_rot, v_all, d_query, d_kv,
    rdo, held_q, held_kv, acc_k, acc_v, send, recv, send_q, send_kv, recv_q, recv_kv, local,
):
    y, zh, core, t = here()
    me = rank(y, zh, core)
    half = lax.rem(t, 2)
    other = t + 1 - 2 * half
    owner = (y < 3) & (core == 0)
    units = [(m, w) for m in range(2) for w in range(3)]
    barrier = pltpu.get_barrier_semaphore()

    def signal(dp, tensor):
        pl.semaphore_signal(barrier, inc=1, device_id=(dp, tensor), device_id_type=MESH)

    @pl.when(owner)
    def _():
        def each(d, _):
            pl.when(d != me)(lambda: signal(d, t))
            return 0

        lax.fori_loop(0, 16, each, 0)

    for m, w in units:
        pl.when(unit_owner(m, w) != me)(functools.partial(signal, unit_owner(m, w), t))
        signal(unit_owner(m, w), other)

    @pl.when(owner)
    def _():
        pl.semaphore_wait(barrier, 36)

    @pl.when(jnp.logical_not(owner))
    def _():
        pl.semaphore_wait(barrier, 6)

    def to_owner(u, m, w, start):
        o = unit_owner(m, w)
        src = d_attended.at[w, m]

        @pl.when(o != me)
        def _():
            copy = remote(src, rdo.at[me], send.at[u], recv.at[me], o, t)
            copy.start() if start else copy.wait_send()

        @pl.when(o == me)
        def _():
            copy = pltpu.make_async_copy(src, rdo.at[me], local.at[0])
            copy.start() if start else copy.wait()

    for u, (m, w) in enumerate(units):
        to_owner(u, m, w, True)
    for u, (m, w) in enumerate(units):
        to_owner(u, m, w, False)

    @pl.when(owner)
    def _():
        def each(d, _):
            @pl.when(d != me)
            def _():
                remote(rdo.at[d], rdo.at[d], send.at[0], recv.at[d], me, other).wait_recv()

            return 0

        lax.fori_loop(0, 16, each, 0)
        acc_k[...] = jnp.zeros_like(acc_k)
        acc_v[...] = jnp.zeros_like(acc_v)
        for b in range(4):
            rows = slice(16 * b, 16 * b + 16)
            blocks = list(range(max(0, b - 2), b + 1))
            queries = q_rot[b]
            keys = {kb: k_rot[kb] for kb in blocks}
            upstream = rdo[:, rows, :].reshape(256, HD)
            bents, probs = block_probs(queries, keys, first[b], b)
            d_probs = [dot(upstream, v_all[kb], 1, 1) for kb in blocks]
            centre = sum(
                jnp.sum(p * dp, axis=-1, keepdims=True) for p, dp in zip(probs, d_probs)
            )
            d_q = jnp.zeros((256, HD), F32)
            for kb, bent, p, dp in zip(blocks, bents, probs, d_probs):
                d_scores = (p * (dp - centre) * (1.0 - bent * bent)).astype(B16)
                d_q = d_q + dot(d_scores, keys[kb], 1, 0)
                acc_k[kb] += dot(d_scores, queries, 0, 0)
                acc_v[kb] += dot(p.astype(B16), upstream, 0, 0)
            d_q = unrotate(d_q * 0.0625, cosine[b], sine[b])
            held_q[:, rows, :] = d_q.astype(B16).reshape(16, 16, HD)
        for b in range(4):
            rows = slice(16 * b, 16 * b + 16)
            d_k = unrotate(acc_k[b] * 0.0625, cosine[b], sine[b]).astype(B16)
            d_v = acc_v[b].astype(B16)
            for i in range(2):
                cols = slice(128 * i, 128 * i + 128)
                held_kv[i, :, rows, :128] = d_k[:, cols].reshape(16, 16, 128)
                held_kv[i, :, rows, 128:] = d_v[:, cols].reshape(16, 16, 128)

        def hand_back(d, start):
            u = zh * 3 + y
            across = remote(
                held_kv.at[1 - half, d], d_kv.at[half, y, zh], send_kv.at[1, d], recv_kv.at[half, u], d, other
            )
            across.start() if start else across.wait_send()

            @pl.when(d != me)
            def _():
                for copy in (
                    remote(held_q.at[d], d_query.at[y, zh], send_q.at[d], recv_q.at[u], d, t),
                    remote(
                        held_kv.at[half, d], d_kv.at[half, y, zh], send_kv.at[0, d], recv_kv.at[half, u], d, t
                    ),
                ):
                    copy.start() if start else copy.wait_send()

            @pl.when(d == me)
            def _():
                for copy in (
                    pltpu.make_async_copy(held_q.at[d], d_query.at[y, zh], local.at[0]),
                    pltpu.make_async_copy(held_kv.at[half, d], d_kv.at[half, y, zh], local.at[1]),
                ):
                    copy.start() if start else copy.wait()

        lax.fori_loop(0, 16, lambda d, _: (hand_back(d, True), 0)[1], 0)
        lax.fori_loop(0, 16, lambda d, _: (hand_back(d, False), 0)[1], 0)

    for u, (m, w) in enumerate(units):

        @pl.when(unit_owner(m, w) != me)
        def _():
            ref = d_query.at[w, m]
            remote(ref, ref, send.at[0], recv_q.at[u], me, other).wait_recv()
            ref = d_kv.at[half, w, m]
            remote(ref, ref, send.at[0], recv_kv.at[half, u], me, other).wait_recv()

        ref = d_kv.at[1 - half, w, m]
        remote(ref, ref, send.at[0], recv_kv.at[1 - half, u], me, other).wait_recv()


def attend_back(d_attended, first, cosine, sine, q_rot, k_rot, v_all):
    return pl.pallas_call(
        attend_back_kernel,
        name="attend_back",
        out_shape=[struct((3, 2, 64, HD), B16), struct((2, 3, 2, 64, HD), B16)],
        in_specs=any_space(1) + vmem_space(6),
        out_specs=any_space(2),
        scratch_shapes=[
            pltpu.VMEM((16, 64, HD), B16),
            pltpu.VMEM((16, 64, HD), B16),
            pltpu.VMEM((2, 16, 64, HD), B16),
            pltpu.VMEM((4, 256, HD), F32),
            pltpu.VMEM((4, 256, HD), F32),
            pltpu.SemaphoreType.DMA((6,)),
            pltpu.SemaphoreType.DMA((16,)),
            pltpu.SemaphoreType.DMA((16,)),
            pltpu.SemaphoreType.DMA((2, 16)),
            pltpu.SemaphoreType.DMA((6,)),
            pltpu.SemaphoreType.DMA((2, 6)),
            pltpu.SemaphoreType.DMA((2,)),
        ],
        compiler_params=params(4),
    )(d_attended, first, cosine, sine, q_rot, k_rot, v_all)


def level(codes, width):
    if width == 0:
        return codes
    stride = (1, 16, 64)[width]
    return jnp.floor(codes * B16(1.0 / stride)) * B16(stride) + B16(stride // 2)


def gelu_parts(value):
    slope = 0.7978845608028654
    inner = jnp.tanh(slope * (value + 0.044715 * value * value * value))
    grown = 0.5 * value * (1.0 + inner)
    rate = 0.5 * (1.0 + inner) + 0.5 * value * (1.0 - inner * inner) * slope * (
        1.0 + 3 * 0.044715 * value * value
    )
    return grown, rate


def body(
    tokens,
    cotangent,
    segments,
    codes_query,
    codes_key,
    codes_value,
    codes_out,
    codes_gate,
    codes_up,
    codes_down,
    query_column_scale,
    key_column_scale,
    value_column_scale,
    output_column_scale,
    gate_column_scale,
    up_column_scale,
    down_column_scale,
    gain_first,
    gain_second,
    gain_third,
    gain_fourth,
):
    widths = range(3)
    z_hi = lax.rem(lax.div(lax.axis_index("dp"), 2), 2)
    tokens = tokens.reshape(ROWS, WIDE)
    cotangent = cotangent.reshape(3, ROWS, WIDE)
    gains = jnp.stack([gain_first, gain_second, gain_third, gain_fourth])
    w_qkv, w_out, w_gu, w_down = (
        gathered.reshape(WIDE, -1)
        for gathered in gather_weights(
            [
                jnp.concatenate([codes_query, codes_key, codes_value], 1).astype(B16),
                codes_out.astype(B16).T,
                jnp.concatenate([codes_gate, codes_up], 1).astype(B16),
                codes_down.astype(B16).T,
            ]
        )
    )
    scale_qkv = jnp.concatenate([query_column_scale, key_column_scale, value_column_scale])
    scale_gu = jnp.concatenate([gate_column_scale, up_column_scale])

    documents = lax.dynamic_index_in_dim(segments, z_hi, 0, False)
    starts = jnp.sum((documents[None, :] < documents[:, None]).astype(jnp.int32), axis=1)
    place = jnp.arange(1024, dtype=jnp.int32)

    def blocked(rows):
        return rows.reshape(4, 16, 16).transpose(0, 2, 1).reshape(4, 256)

    first = blocked(starts)[:, :, None]
    expo = jnp.arange(HD // 2, dtype=F32) * (2.0 / HD)
    angle = blocked(place - starts).astype(F32)[:, :, None] * jnp.power(ROPE_BASE, -expo)
    cosine, sine = jnp.cos(angle), jnp.sin(angle)

    inputs = tokens.astype(F32)
    normed_input = (inputs * inverse_rms(inputs) * (1.0 + gain_first)).astype(B16)
    qkv_pre = jnp.stack([dot(normed_input, level(w_qkv, w), 1, 0) * scale_qkv for w in widths])
    attended, q_rot, k_rot, v_all = attend(
        qkv_pre.astype(B16).reshape(3, 2, 64, 2 * HD), first, cosine, sine
    )
    attended = attended.reshape(3, ROWS, HD)
    branch_part = jnp.stack(
        [dot(attended[w], level(w_out, w), 1, 1) * output_column_scale for w in widths]
    ).astype(B16)
    normed_middle, branch, middle = tensor_call(
        middle_kernel,
        "middle",
        5,
        3,
        1,
        (branch_part, tokens[None], gains),
        any_space(2) + vmem_space(1),
        [struct((3, ROWS, WIDE), B16)] + [struct((3, SLICE, WIDE), F32)] * 2,
        any_space(1) + vmem_space(2),
        [pltpu.VMEM((3, SLICE, WIDE), B16)],
    )
    gu_pre = jnp.stack([dot(normed_middle[w], level(w_gu, w), 1, 0) * scale_gu for w in widths])
    half = gu_pre.shape[-1] // 2
    gate_pre, up_pre = gu_pre[..., :half], gu_pre[..., half:]
    grown, rate = gelu_parts(gate_pre)
    hidden = (grown * up_pre).astype(B16)
    feed_part = jnp.stack(
        [dot(hidden[w], level(w_down, w), 1, 1) * down_column_scale for w in widths]
    ).astype(B16)
    d_feed, results, feed_sums = tensor_call(
        feed_kernel,
        "feed",
        6,
        3,
        3,
        (feed_part, cotangent, middle, gains),
        any_space(2) + vmem_space(2),
        [struct((3, ROWS, WIDE), B16)] * 2 + [struct((8, WIDE), F32)],
        any_space(2) + vmem_space(1),
        [pltpu.VMEM((3, SLICE, WIDE), B16)] * 2,
    )

    d_feed_scaled = (d_feed.astype(F32) * down_column_scale).astype(B16)
    d_hidden = jnp.stack([dot(d_feed_scaled[w], level(w_down, w), 1, 0) for w in widths])
    d_gu = jnp.concatenate([d_hidden * up_pre * rate, d_hidden * grown], -1)
    d_gu_low = d_gu.astype(B16)
    gu_sums = jnp.sum(d_gu_low.astype(F32) * gu_pre, axis=(0, 1)) / scale_gu
    d_gu_scaled = (d_gu * scale_gu).astype(B16)
    d_middle_part = jnp.stack([dot(d_gu_scaled[w], level(w_gu, w), 1, 1) for w in widths]).astype(
        B16
    )
    d_branch, d_middle, branch_sums = tensor_call(
        branch_kernel,
        "branch",
        7,
        3,
        3,
        (d_middle_part, cotangent, middle, branch, gains),
        any_space(2) + vmem_space(3),
        [struct((3, ROWS, WIDE), B16), struct((1, SLICE, WIDE), F32), struct((8, WIDE), F32)],
        any_space(1) + vmem_space(2),
        [pltpu.VMEM((3, SLICE, WIDE), B16)],
    )
    d_branch_scaled = (d_branch.astype(F32) * output_column_scale).astype(B16)
    d_attended = jnp.stack([dot(d_branch_scaled[w], level(w_out, w), 1, 0) for w in widths]).astype(
        B16
    )
    d_query, d_kv = attend_back(
        d_attended.reshape(3, 2, 64, HD), first, cosine, sine, q_rot, k_rot, v_all
    )
    d_kv = (d_kv[0].astype(F32) + d_kv[1].astype(F32)).astype(B16)
    d_qkv = jnp.concatenate([d_query, d_kv], -1).reshape(3, ROWS, 2 * HD).astype(F32)
    qkv_sums = jnp.sum(d_qkv * qkv_pre, axis=(0, 1)) / scale_qkv
    d_qkv_scaled = (d_qkv * scale_qkv).astype(B16)
    d_input_part = sum(dot(d_qkv_scaled[w], level(w_qkv, w), 1, 1) for w in widths).astype(B16)
    input_gradient, input_sums = tensor_call(
        input_kernel,
        "input",
        8,
        1,
        1,
        (d_input_part[None], tokens[None], d_middle, gains),
        any_space(2) + vmem_space(2),
        [struct((1, ROWS, WIDE), F32), struct((8, WIDE), F32)],
        any_space(1) + vmem_space(1),
        [pltpu.VMEM((1, SLICE, WIDE), F32)],
    )
    flat = (3 * ROWS, -1)
    parts = (
        dot(normed_input, jnp.sum(d_qkv, axis=0).astype(B16), 0, 0).astype(B16),
        dot(d_branch.reshape(flat), attended.reshape(flat), 0, 0).astype(B16),
        dot(normed_middle.reshape(flat), d_gu_low.reshape(flat), 0, 0).astype(B16),
        dot(d_feed.reshape(flat), hidden.reshape(flat), 0, 0).astype(B16),
    )
    g_qkv, g_out, g_gu, g_down = scatter_gradients(parts)

    rows = jnp.stack(
        [
            input_sums[0],
            branch_sums[1],
            branch_sums[0],
            feed_sums[0],
            branch_sums[2] / output_column_scale,
            feed_sums[1] / down_column_scale,
        ]
    )
    rows = lax.psum(rows, ("dp", "tensor"))
    rows = lax.dynamic_slice_in_dim(rows, lax.axis_index("dp") * SHARD, SHARD, 1)
    columns = lax.psum(jnp.concatenate([qkv_sums, gu_sums]), "dp")
    return (
        results.reshape(3, 2, 64, 1, WIDE),
        input_gradient.reshape(2, 64, 1, WIDE),
        g_qkv[:, :256],
        g_qkv[:, 256:384],
        g_qkv[:, 384:],
        g_out.T,
        g_gu[:, :half],
        g_gu[:, half:],
        g_down.T,
        columns[:256],
        columns[256:384],
        columns[384:512],
        rows[4],
        columns[512 : 512 + half],
        columns[512 + half :],
        rows[5],
        rows[0],
        rows[1],
        rows[2],
        rows[3],
    )


def solution(mesh):
    matrix, turned = P("dp", "tensor"), P("tensor", "dp")
    columns, whole, shard = P("tensor"), P(), P("dp")
    in_specs = (
        P(None, None, "dp", None),
        P(None, None, None, "dp", None),
        whole,
        *(matrix, matrix, matrix, turned, matrix, matrix, turned),
        *(columns, columns, columns, whole, columns, columns, whole),
        *(whole, whole, whole, whole),
    )
    out_specs = (
        P(None, None, None, "dp", None),
        P(None, None, "dp", None),
        *(matrix, matrix, matrix, turned, matrix, matrix, turned),
        *(columns, columns, columns, shard, columns, columns, shard),
        *(shard, shard, shard, shard),
    )
    return jax.shard_map(body, mesh=mesh, in_specs=in_specs, out_specs=out_specs, check_vma=False)
```

```python
import functools

import jax
import jax.numpy as jnp
from jax import lax
from jax.experimental import pallas as pl
from jax.experimental.pallas import tpu as pltpu
from jax.sharding import PartitionSpec as P

MESH = pl.DeviceIdType.MESH
F32 = jnp.float32
B16 = jnp.bfloat16
EPSILON = 1e-06
SOFTCAP = 50.0
ROPE_BASE = 10000.0
MASKED = -1e30
HD = 256
WIDE = 2304
SHARD = 144
LOW = 64
HIGH = SHARD - LOW
TENSOR = 8
ROWS = 128
SLICE = ROWS // TENSOR
EXTRA = 384
VMEM_BYTES = 56 * 2**20


def here():
    dp = lax.axis_index("dp")
    return lax.div(dp, 4), lax.rem(lax.div(dp, 2), 2), lax.rem(dp, 2), lax.axis_index("tensor")


def rank(y, z_hi, core):
    return (y * 2 + z_hi) * 2 + core


def remote(src, dst, send, recv, dp, tensor):
    return pltpu.make_async_remote_copy(
        src, dst, send, recv, device_id=(dp, tensor), device_id_type=MESH
    )


def greet(devices):
    barrier = pltpu.get_barrier_semaphore()
    for device in devices:
        pl.semaphore_signal(barrier, inc=1, device_id=device, device_id_type=MESH)
    pl.semaphore_wait(barrier, len(devices))


def struct(shape, dtype):
    return jax.ShapeDtypeStruct(shape, dtype)


def any_space(count):
    return [pl.BlockSpec(memory_space=pl.ANY)] * count


def vmem_space(count):
    return [pl.BlockSpec(memory_space=pltpu.VMEM)] * count


def params(collective_id):
    return pltpu.CompilerParams(
        collective_id=collective_id, has_side_effects=True, vmem_limit_bytes=VMEM_BYTES
    )


def gather_kernel(count, *refs):
    srcs, outs = refs[:count], refs[count : 2 * count]
    send, recv, local = refs[2 * count :]
    y, zh, core, t = here()
    me, sib, zz = rank(y, zh, core), rank(y, zh, 1 - core), rank(y, 1 - zh, core)
    fore = [rank(lax.rem(y + dy, 4), zh, core) for dy in (1, 2, 3)]
    behind = [lax.rem(y + 4 - dy, 4) for dy in (1, 2, 3)]
    low, high = pl.ds(0, LOW), pl.ds(LOW, HIGH)
    greet([(sib, t), (zz, t)] + [(dp, t) for dp in fore])
    started = []

    def push(k, slot, src, dst, dp):
        copy = remote(src, dst, send.at[k, slot], recv.at[k, slot], dp, t)
        copy.start()
        started.append(copy)

    def arrive(k, slot, ref):
        remote(ref, ref, send.at[k, slot], recv.at[k, slot], sib, t).wait_recv()

    mine = []
    for k in range(count):
        src, out = srcs[k], outs[k]
        copy = pltpu.make_async_copy(src, out.at[me], local.at[k])
        copy.start()
        mine.append(copy)
        push(k, 0, src.at[low], out.at[me, low], zz)
        for i in range(3):
            push(k, 4 + i, src.at[high], out.at[me, high], fore[i])
        for i in range(3):
            push(k, 1 + i, src.at[low], out.at[me, low], fore[i])
        push(k, 7, src.at[high], out.at[me, high], zz)
        push(k, 14, src, out.at[me], sib)
    for k in range(count):
        out = outs[k]
        block = out.at[zz, low]
        arrive(k, 0, block)
        for i in range(3):
            push(k, 8 + i, block, block, fore[i])
        push(k, 15, block, block, sib)
        for i in range(3):
            block = out.at[rank(behind[i], zh, core), high]
            arrive(k, 4 + i, block)
            push(k, 11 + i, block, block, zz)
            push(k, 16 + i, block, block, sib)
        for i in range(3):
            block = out.at[rank(behind[i], zh, core), low]
            arrive(k, 1 + i, block)
            push(k, 19 + i, block, block, sib)
        block = out.at[zz, high]
        arrive(k, 7, block)
        push(k, 22, block, block, sib)
        for i in range(3):
            block = out.at[rank(behind[i], 1 - zh, core), low]
            arrive(k, 8 + i, block)
            push(k, 23 + i, block, block, sib)
            block = out.at[rank(behind[i], 1 - zh, core), high]
            arrive(k, 11 + i, block)
            push(k, 26 + i, block, block, sib)
    for k in range(count):
        out = outs[k]
        zz_sib = rank(y, 1 - zh, 1 - core)
        arrive(k, 14, out.at[sib])
        arrive(k, 15, out.at[zz_sib, low])
        arrive(k, 22, out.at[zz_sib, high])
        for i in range(3):
            near, far = rank(behind[i], zh, 1 - core), rank(behind[i], 1 - zh, 1 - core)
            arrive(k, 16 + i, out.at[near, high])
            arrive(k, 19 + i, out.at[near, low])
            arrive(k, 23 + i, out.at[far, low])
            arrive(k, 26 + i, out.at[far, high])
    for copy in mine:
        copy.wait()
    for copy in started:
        copy.wait_send()


def gather_weights(shards):
    count = len(shards)
    return pl.pallas_call(
        functools.partial(gather_kernel, count),
        name="gather_weights",
        out_shape=[jax.ShapeDtypeStruct((16,) + s.shape, s.dtype) for s in shards],
        in_specs=any_space(count),
        out_specs=any_space(count),
        scratch_shapes=[
            pltpu.SemaphoreType.DMA((count, 29)),
            pltpu.SemaphoreType.DMA((count, 29)),
            pltpu.SemaphoreType.DMA((count,)),
        ],
        compiler_params=params(1),
    )(*shards)


def finish_kernel(count, *refs):
    parts, refs = refs[:count], refs[count:]
    (part, tokens, d_middle, gains, final, sums, columns), refs = refs[:7], refs[7:]
    outs, refs = refs[:count], refs[count:]
    (results, gradient, totals), refs = refs[:3], refs[3:]
    own, sibs, yrecv, zrecv, ylast, zlast = (
        refs[i * count : (i + 1) * count] for i in range(6)
    )
    refs = refs[6 * count :]
    held, mine, block, vectors, from_t, from_sib, from_y, from_z = refs[:8]
    send, recv, local, send_t, recv_t, local_t, send_v, recv_v = refs[8:]
    y, zh, core, t = here()
    me, sib, zz = rank(y, zh, core), rank(y, zh, 1 - core), rank(y, 1 - zh, core)
    ahead = [lax.rem(y + dy, 4) for dy in (1, 2, 3)]
    fore = [rank(place, zh, core) for place in ahead]
    peers = tensor_peers()
    greet([(sib, t), (zz, t)] + [(dp, t) for dp in fore] + [(me, peer) for peer in peers[1:]])
    started = scatter_rows(part, held, send_t.at[0], recv_t.at[0], local_t.at[0])
    input_copies = list(started)
    finish_results = spread_rows(final, results, send_t.at[1], recv_t.at[1], local_t.at[1])

    def push(k, slot, src, dst, dp):
        copy = remote(src, dst, send.at[k, slot], recv.at[k, slot], dp, t)
        copy.start()
        started.append(copy)

    def arrive(k, slot, ref):
        remote(ref, ref, send.at[k, slot], recv.at[k, slot], sib, t).wait_recv()

    order = ahead + [y]
    for k in range(count):
        for i, place in enumerate(order):
            pair = pl.ds(place * 2, 2)
            push(k, i, parts[k].at[pair, 1 - core], sibs[k].at[pair], sib)
            pltpu.make_async_copy(
                parts[k].at[pair, core], own[k].at[pair], local.at[k, i]
            ).start()

    load = load_rows(tokens, mine, local_t.at[2])
    load.wait()
    upstream = summed(held, input_copies)
    signal = mine[...].astype(F32)
    inverse = inverse_rms(signal)
    normed = signal * inverse
    block[...] = d_middle[...] + norm_back(normed, inverse, gains[0:1], upstream)
    finish_input = spread_rows(block, gradient, send_t.at[2], recv_t.at[2], local_t.at[3])
    from_t[t] = jnp.concatenate(
        [over_rows(upstream * normed), sums[...], jnp.zeros((2, WIDE), F32)], 0
    )
    vector_copies = []
    for k in range(1, TENSOR):
        copy = remote(from_t.at[t], from_t.at[t], send_t.at[3, k], recv_t.at[3, k], me, peers[k])
        copy.start()
        vector_copies.append(copy)

    for k in range(count):
        for i, place in enumerate(order):
            pair = pl.ds(place * 2, 2)
            pltpu.make_async_copy(
                parts[k].at[pair, core], own[k].at[pair], local.at[k, i]
            ).wait()
            arrive(k, i, sibs[k].at[pair])

            def add(step, _, k=k, place=place):
                chip = place * 2 + lax.div(step, SHARD // 16)
                rows = pl.ds(pl.multiple_of(lax.rem(step, SHARD // 16) * 16, 16), 16)
                own[k][chip, rows] = (
                    own[k][chip, rows].astype(F32) + sibs[k][chip, rows].astype(F32)
                ).astype(B16)
                return 0

            lax.fori_loop(0, 2 * SHARD // 16, add, 0)
            if i < 3:
                push(k, 4 + i, own[k].at[pair, pl.ds(0, LOW)], yrecv[k].at[i], fore[i])
            push(
                k, 7 + i, own[k].at[place * 2 + 1 - zh, pl.ds(LOW, HIGH)], zrecv[k].at[place], zz
            )
    for k in range(1, TENSOR):
        source = from_t.at[peers[TENSOR - k]]
        remote(source, source, send_t.at[3, k], recv_t.at[3, k], me, peers[k]).wait_recv()
    vectors[:, :WIDE] = functools.reduce(jnp.add, [from_t[i] for i in range(TENSOR)])
    vectors[:, WIDE:] = columns[...]
    copy = remote(vectors, from_sib, send_v.at[0], recv_v.at[0], sib, t)
    copy.start()
    copy.wait()
    from_y[y] = vectors[...] + from_sib[...]
    for i in range(3):
        copy = remote(from_y.at[y], from_y.at[y], send_v.at[1 + i], recv_v.at[1 + i], fore[i], t)
        copy.start()
        vector_copies.append(copy)

    for k in range(count):
        for i, place in enumerate(order):
            arrive(k, 7 + i, zrecv[k].at[place])

            def merge(step, _, k=k, place=place):
                rows = pl.ds(pl.multiple_of(step * 16, 16), 16)
                mine = pl.ds(pl.multiple_of(step * 16 + LOW, 16), 16)
                zrecv[k][place, rows] = (
                    zrecv[k][place, rows].astype(F32) + own[k][place * 2 + zh, mine].astype(F32)
                ).astype(B16)
                return 0

            lax.fori_loop(0, HIGH // 16, merge, 0)
            if i < 3:
                push(k, 11 + i, zrecv[k].at[place], ylast[k].at[i], fore[i])
        for i in range(3):
            arrive(k, 4 + i, yrecv[k].at[i])

        def pool(step, _, k=k):
            chip = lax.div(step, LOW // 16)
            rows = pl.ds(pl.multiple_of(lax.rem(step, LOW // 16) * 16, 16), 16)
            total = own[k][y * 2 + chip, rows].astype(F32)
            for i in range(3):
                total = total + yrecv[k][i, chip, rows].astype(F32)
            own[k][y * 2 + chip, rows] = total.astype(B16)
            return 0

        lax.fori_loop(0, 2 * LOW // 16, pool, 0)
        push(k, 14, own[k].at[y * 2 + 1 - zh, pl.ds(0, LOW)], zlast[k], zz)
    for i in range(3):
        source = from_y.at[lax.rem(y + 3 - i, 4)]
        remote(source, source, send_v.at[1 + i], recv_v.at[1 + i], fore[i], t).wait_recv()
    totals[...] = functools.reduce(jnp.add, [from_y[i] for i in range(4)])
    vectors_z = remote(totals, from_z, send_v.at[4], recv_v.at[4], zz, t)
    vectors_z.start()
    for k in range(count):
        arrive(k, 14, zlast[k])

        def end_low(step, _, k=k):
            rows = pl.ds(pl.multiple_of(step * 16, 16), 16)
            outs[k][rows] = own[k][y * 2 + zh, rows].astype(F32) + zlast[k][rows].astype(F32)
            return 0

        lax.fori_loop(0, LOW // 16, end_low, 0)
        for i in range(3):
            arrive(k, 11 + i, ylast[k].at[i])

        def end_high(step, _, k=k):
            rows = pl.ds(pl.multiple_of(step * 16, 16), 16)
            total = zrecv[k][y, rows].astype(F32)
            for i in range(3):
                total = total + ylast[k][i, rows].astype(F32)
            outs[k][pl.ds(pl.multiple_of(step * 16 + LOW, 16), 16)] = total
            return 0

        lax.fori_loop(0, HIGH // 16, end_high, 0)
    vectors_z.wait()
    totals[...] = totals[...] + from_z[...]
    finish_results()
    finish_input()
    for copy in started + vector_copies:
        copy.wait_send()


def finish_layer(parts, *others):
    count = len(parts)
    columns = [part.shape[-1] for part in parts]
    scratch = [pltpu.VMEM((8, SHARD, c), B16) for c in columns]
    scratch += [pltpu.VMEM((8, SHARD, c), B16) for c in columns]
    scratch += [pltpu.VMEM((3, 2, LOW, c), B16) for c in columns]
    scratch += [pltpu.VMEM((4, HIGH, c), B16) for c in columns]
    scratch += [pltpu.VMEM((3, HIGH, c), B16) for c in columns]
    scratch += [pltpu.VMEM((LOW, c), B16) for c in columns]
    return pl.pallas_call(
        functools.partial(finish_kernel, count),
        name="finish_layer",
        out_shape=[struct((SHARD, c), F32) for c in columns]
        + [
            struct((3, ROWS, WIDE), B16),
            struct((1, ROWS, WIDE), F32),
            struct((8, WIDE + EXTRA), F32),
        ],
        in_specs=any_space(count + 2) + vmem_space(5),
        out_specs=vmem_space(count) + any_space(2) + vmem_space(1),
        scratch_shapes=scratch
        + [
            pltpu.VMEM((TENSOR, 1, SLICE, WIDE), B16),
            pltpu.VMEM((1, SLICE, WIDE), B16),
            pltpu.VMEM((1, SLICE, WIDE), F32),
            pltpu.VMEM((8, WIDE + EXTRA), F32),
            pltpu.VMEM((TENSOR, 8, WIDE), F32),
            pltpu.VMEM((8, WIDE + EXTRA), F32),
            pltpu.VMEM((4, 8, WIDE + EXTRA), F32),
            pltpu.VMEM((8, WIDE + EXTRA), F32),
            pltpu.SemaphoreType.DMA((count, 15)),
            pltpu.SemaphoreType.DMA((count, 15)),
            pltpu.SemaphoreType.DMA((count, 4)),
            pltpu.SemaphoreType.DMA((4, TENSOR)),
            pltpu.SemaphoreType.DMA((4, TENSOR)),
            pltpu.SemaphoreType.DMA((4,)),
            pltpu.SemaphoreType.DMA((5,)),
            pltpu.SemaphoreType.DMA((5,)),
        ],
        compiler_params=params(2),
    )(*[part.reshape(8, 2, SHARD, part.shape[-1]) for part in parts], *others)


def row_block(index):
    return pl.ds(pl.multiple_of(index * SLICE, SLICE), SLICE)


def tensor_peers():
    t = lax.axis_index("tensor")
    return [lax.rem(t + k, TENSOR) for k in range(TENSOR)]


def greet_tensor():
    dp = lax.axis_index("dp")
    greet([(dp, peer) for peer in tensor_peers()[1:]])


def scatter_rows(part, held, send, recv, local):
    dp = lax.axis_index("dp")
    peers = tensor_peers()
    copies = []
    for k in range(1, TENSOR):
        copy = remote(
            part.at[:, row_block(peers[k])], held.at[k], send.at[k], recv.at[k], dp, peers[k]
        )
        copy.start()
        copies.append(copy)
    mine = pltpu.make_async_copy(part.at[:, row_block(peers[0])], held.at[0], local)
    mine.start()
    mine.wait()
    return copies


def summed(held, copies):
    total = held[0].astype(F32)
    for k in range(1, TENSOR):
        copies[k - 1].wait_recv()
        total = total + held[k].astype(F32)
    return total


def spread_rows(block, whole, send, recv, local):
    dp = lax.axis_index("dp")
    peers = tensor_peers()
    here_rows = whole.at[:, row_block(peers[0])]
    copies = []
    for k in range(1, TENSOR):
        copy = remote(block, here_rows, send.at[k], recv.at[k], dp, peers[k])
        copy.start()
        copies.append(copy)
    mine = pltpu.make_async_copy(block, here_rows, local)
    mine.start()

    def finish():
        mine.wait()
        for k in range(1, TENSOR):
            source = whole.at[:, row_block(peers[TENSOR - k])]
            remote(source, source, send.at[k], recv.at[k], dp, peers[k]).wait_recv()
        for copy in copies:
            copy.wait_send()

    return finish


def inverse_rms(signal):
    return lax.rsqrt(jnp.mean(signal * signal, axis=-1, keepdims=True) + EPSILON)


def norm_back(normed, inverse, gain, upstream):
    inner = upstream * (1.0 + gain)
    return inverse * (inner - normed * jnp.mean(inner * normed, axis=-1, keepdims=True))


def over_rows(term):
    return jnp.sum(term, axis=(0, 1))[None]


def load_rows(whole, block, local):
    copy = pltpu.make_async_copy(
        whole.at[:, row_block(lax.axis_index("tensor"))], block, local
    )
    copy.start()
    return copy


def middle_kernel(
    part, tokens, gains, normed, branch, middle, held, mine, block, send, recv, local
):
    greet_tensor()
    copies = scatter_rows(part, held, send.at[0], recv.at[0], local.at[0])
    load = load_rows(tokens, mine, local.at[1])
    load.wait()
    signal = summed(held, copies)
    branch[...] = signal
    total = mine[...].astype(F32) + signal * inverse_rms(signal) * (1.0 + gains[1:2])
    middle[...] = total
    block[...] = (total * inverse_rms(total) * (1.0 + gains[2:3])).astype(B16)
    finish = spread_rows(block, normed, send.at[1], recv.at[1], local.at[2])
    for copy in copies:
        copy.wait_send()
    finish()


def feed_kernel(
    part, cotangent, middle, gains, d_feed, final, sums, held, mine, block, send, recv, local
):
    greet_tensor()
    copies = scatter_rows(part, held, send.at[0], recv.at[0], local.at[0])
    load = load_rows(cotangent, mine, local.at[1])
    load.wait()
    signal = summed(held, copies)
    inverse = inverse_rms(signal)
    normed = signal * inverse
    upstream = mine[...].astype(F32)
    lowered = norm_back(normed, inverse, gains[3:4], upstream).astype(B16)
    block[...] = lowered
    finish = spread_rows(block, d_feed, send.at[1], recv.at[1], local.at[2])
    final[...] = (middle[...] + normed * (1.0 + gains[3:4])).astype(B16)
    sums[0:1] = over_rows(upstream * normed)
    sums[1:2] = over_rows(lowered.astype(F32) * signal)
    for copy in copies:
        copy.wait_send()
    finish()


def branch_kernel(
    part, cotangent, middle, branch, gains, d_branch, d_middle, sums, held, mine, block, send, recv, local
):
    greet_tensor()
    copies = scatter_rows(part, held, send.at[0], recv.at[0], local.at[0])
    load = load_rows(cotangent, mine, local.at[1])
    load.wait()
    upstream = summed(held, copies)
    signal = middle[...]
    inverse = inverse_rms(signal)
    normed = signal * inverse
    gradient = mine[...].astype(F32) + norm_back(normed, inverse, gains[2:3], upstream)
    lower = branch[...]
    inverse_lower = inverse_rms(lower)
    normed_lower = lower * inverse_lower
    lowered = norm_back(normed_lower, inverse_lower, gains[1:2], gradient).astype(B16)
    block[...] = lowered
    finish = spread_rows(block, d_branch, send.at[1], recv.at[1], local.at[2])
    d_middle[...] = jnp.sum(gradient, axis=0, keepdims=True)
    sums[0:1] = over_rows(upstream * normed)
    sums[1:2] = over_rows(gradient * normed_lower)
    sums[2:3] = over_rows(lowered.astype(F32) * lower)
    for copy in copies:
        copy.wait_send()
    finish()


def tensor_call(
    kernel, name, collective_id, depth, loaded, operands, in_specs, outs, out_specs, blocks
):
    return pl.pallas_call(
        kernel,
        name=name,
        out_shape=outs,
        in_specs=in_specs,
        out_specs=out_specs,
        scratch_shapes=[
            pltpu.VMEM((TENSOR, depth, SLICE, WIDE), B16),
            pltpu.VMEM((loaded, SLICE, WIDE), B16),
        ]
        + blocks
        + [
            pltpu.SemaphoreType.DMA((3, TENSOR)),
            pltpu.SemaphoreType.DMA((3, TENSOR)),
            pltpu.SemaphoreType.DMA((4,)),
        ],
        compiler_params=params(collective_id),
    )(*operands)


def unit_owner(micro, width):
    return rank(width, micro, 0)


def rotate(signal, cosine, sine):
    former, latter = signal[:, : HD // 2], signal[:, HD // 2 :]
    return jnp.concatenate([former * cosine - latter * sine, latter * cosine + former * sine], -1)


def unrotate(signal, cosine, sine):
    former, latter = signal[:, : HD // 2], signal[:, HD // 2 :]
    return jnp.concatenate([former * cosine + latter * sine, latter * cosine - former * sine], -1)


def block_scores(queries, keys, first, b, kb):
    scores = lax.dot_general(queries, keys, (((1,), (1,)), ((), ())), preferred_element_type=F32)
    bent = jnp.tanh(scores * (0.0625 / SOFTCAP))
    lane = lax.broadcasted_iota(jnp.int32, (256, 256), 1)
    row = lax.broadcasted_iota(jnp.int32, (256, 256), 0)
    key_place = (16 * kb + (lane & 15)) * 16 + (lane >> 4)
    query_place = (16 * b + (row & 15)) * 16 + (row >> 4)
    allowed = (key_place >= first) & (key_place <= query_place)
    return bent, jnp.where(allowed, SOFTCAP * bent, MASKED)


def block_probs(queries, keys, first, b):
    pieces = [
        block_scores(queries, keys[kb], first, b, kb) for kb in range(max(0, b - 2), b + 1)
    ]
    peak = functools.reduce(
        jnp.maximum, [jnp.max(capped, axis=-1, keepdims=True) for _, capped in pieces]
    )
    exps = [jnp.exp(capped - peak) for _, capped in pieces]
    total = functools.reduce(jnp.add, [jnp.sum(e, axis=-1, keepdims=True) for e in exps])
    return [bent for bent, _ in pieces], [e / total for e in exps]


def dot(left, right, left_dim, right_dim):
    return lax.dot_general(
        left, right, (((left_dim,), (right_dim,)), ((), ())), preferred_element_type=F32
    )


def attend_kernel(
    qkv, first, cosine, sine, attended, q_rot, k_rot, v_all,
    rq, rkv, held, send, recv_q, recv_kv, send_back, recv_back, local,
):
    y, zh, core, t = here()
    me = rank(y, zh, core)
    half = lax.rem(t, 2)
    other = t + 1 - 2 * half
    owner = (y < 3) & (core == 0)
    units = [(m, w) for m in range(2) for w in range(3)]
    barrier = pltpu.get_barrier_semaphore()

    def signal(dp, tensor):
        pl.semaphore_signal(barrier, inc=1, device_id=(dp, tensor), device_id_type=MESH)

    @pl.when(owner)
    def _():
        def each(d, _):
            pl.when(d != me)(lambda: signal(d, t))
            signal(d, other)
            return 0

        lax.fori_loop(0, 16, each, 0)

    for m, w in units:
        pl.when(unit_owner(m, w) != me)(functools.partial(signal, unit_owner(m, w), t))

    @pl.when(owner)
    def _():
        pl.semaphore_wait(barrier, 26)

    @pl.when(jnp.logical_not(owner))
    def _():
        pl.semaphore_wait(barrier, 12)

    def to_owner(u, m, w, start):
        o = unit_owner(m, w)
        q_src, kv_src = qkv.at[w, m, :, pl.ds(0, HD)], qkv.at[w, m, :, pl.ds(HD, HD)]
        across = remote(kv_src, rkv.at[half, me], send.at[u, 2], recv_kv.at[half, me], o, other)
        away = [
            remote(q_src, rq.at[me], send.at[u, 0], recv_q.at[me], o, t),
            remote(kv_src, rkv.at[half, me], send.at[u, 1], recv_kv.at[half, me], o, t),
        ]
        near = [
            pltpu.make_async_copy(q_src, rq.at[me], local.at[0]),
            pltpu.make_async_copy(kv_src, rkv.at[half, me], local.at[1]),
        ]

        @pl.when(o != me)
        def _():
            for copy in away:
                copy.start() if start else copy.wait_send()

        @pl.when(o == me)
        def _():
            for copy in near:
                copy.start() if start else copy.wait()

        across.start() if start else across.wait_send()

    for u, (m, w) in enumerate(units):
        to_owner(u, m, w, True)
    for u, (m, w) in enumerate(units):
        to_owner(u, m, w, False)

    @pl.when(owner)
    def _():
        def each(d, _):
            @pl.when(d != me)
            def _():
                remote(rq.at[d], rq.at[d], send.at[0, 0], recv_q.at[d], me, other).wait_recv()
                remote(
                    rkv.at[half, d], rkv.at[half, d], send.at[0, 0], recv_kv.at[half, d], me, other
                ).wait_recv()

            remote(
                rkv.at[1 - half, d], rkv.at[1 - half, d], send.at[0, 0], recv_kv.at[1 - half, d], me, other
            ).wait_recv()
            return 0

        lax.fori_loop(0, 16, each, 0)
        for b in range(4):
            rows = slice(16 * b, 16 * b + 16)
            c, s = cosine[b], sine[b]
            q = rq[:, rows, :].reshape(256, HD).astype(F32)
            q_rot[b] = rotate(q, c, s).astype(B16)
            k = jnp.concatenate(
                [rkv[i, :, rows, : HD // 2].reshape(256, HD // 2) for i in range(2)], -1
            )
            k_rot[b] = rotate(k.astype(F32), c, s).astype(B16)
            v_all[b] = jnp.concatenate(
                [rkv[i, :, rows, HD // 2 :].reshape(256, HD // 2) for i in range(2)], -1
            )
        for b in range(4):
            keys = {kb: k_rot[kb] for kb in range(max(0, b - 2), b + 1)}
            _, probs = block_probs(q_rot[b], keys, first[b], b)
            out = sum(
                dot(p.astype(B16), v_all[kb], 1, 0) for p, kb in zip(probs, sorted(keys))
            )
            held[:, 16 * b : 16 * b + 16, :] = out.astype(B16).reshape(16, 16, HD)

        def hand_back(d, start):
            @pl.when(d != me)
            def _():
                copy = remote(
                    held.at[d], attended.at[y, zh], send_back.at[d], recv_back.at[zh * 3 + y], d, t
                )
                copy.start() if start else copy.wait_send()

            @pl.when(d == me)
            def _():
                copy = pltpu.make_async_copy(held.at[d], attended.at[y, zh], local.at[0])
                copy.start() if start else copy.wait()

        lax.fori_loop(0, 16, lambda d, _: (hand_back(d, True), 0)[1], 0)
        lax.fori_loop(0, 16, lambda d, _: (hand_back(d, False), 0)[1], 0)

    for u, (m, w) in enumerate(units):

        @pl.when(unit_owner(m, w) != me)
        def _():
            ref = attended.at[w, m]
            remote(ref, ref, send.at[0, 0], recv_back.at[u], me, other).wait_recv()


def attend(qkv, first, cosine, sine):
    return pl.pallas_call(
        attend_kernel,
        name="attend",
        out_shape=[struct((3, 2, 64, HD), B16)] + [struct((4, 256, HD), B16)] * 3,
        in_specs=any_space(1) + vmem_space(3),
        out_specs=any_space(1) + vmem_space(3),
        scratch_shapes=[
            pltpu.VMEM((16, 64, HD), B16),
            pltpu.VMEM((2, 16, 64, HD), B16),
            pltpu.VMEM((16, 64, HD), B16),
            pltpu.SemaphoreType.DMA((6, 3)),
            pltpu.SemaphoreType.DMA((16,)),
            pltpu.SemaphoreType.DMA((2, 16)),
            pltpu.SemaphoreType.DMA((16,)),
            pltpu.SemaphoreType.DMA((6,)),
            pltpu.SemaphoreType.DMA((2,)),
        ],
        compiler_params=params(3),
    )(qkv, first, cosine, sine)


def attend_back_kernel(
    d_attended, first, cosine, sine, q_rot, k_rot, v_all, d_query, d_kv,
    rdo, held_q, held_kv, acc_k, acc_v, send, recv, send_q, send_kv, recv_q, recv_kv, local,
):
    y, zh, core, t = here()
    me = rank(y, zh, core)
    half = lax.rem(t, 2)
    other = t + 1 - 2 * half
    owner = (y < 3) & (core == 0)
    units = [(m, w) for m in range(2) for w in range(3)]
    barrier = pltpu.get_barrier_semaphore()

    def signal(dp, tensor):
        pl.semaphore_signal(barrier, inc=1, device_id=(dp, tensor), device_id_type=MESH)

    @pl.when(owner)
    def _():
        def each(d, _):
            pl.when(d != me)(lambda: signal(d, t))
            return 0

        lax.fori_loop(0, 16, each, 0)

    for m, w in units:
        pl.when(unit_owner(m, w) != me)(functools.partial(signal, unit_owner(m, w), t))
        signal(unit_owner(m, w), other)

    @pl.when(owner)
    def _():
        pl.semaphore_wait(barrier, 36)

    @pl.when(jnp.logical_not(owner))
    def _():
        pl.semaphore_wait(barrier, 6)

    def to_owner(u, m, w, start):
        o = unit_owner(m, w)
        src = d_attended.at[w, m]

        @pl.when(o != me)
        def _():
            copy = remote(src, rdo.at[me], send.at[u], recv.at[me], o, t)
            copy.start() if start else copy.wait_send()

        @pl.when(o == me)
        def _():
            copy = pltpu.make_async_copy(src, rdo.at[me], local.at[0])
            copy.start() if start else copy.wait()

    for u, (m, w) in enumerate(units):
        to_owner(u, m, w, True)
    for u, (m, w) in enumerate(units):
        to_owner(u, m, w, False)

    @pl.when(owner)
    def _():
        def each(d, _):
            @pl.when(d != me)
            def _():
                remote(rdo.at[d], rdo.at[d], send.at[0], recv.at[d], me, other).wait_recv()

            return 0

        lax.fori_loop(0, 16, each, 0)
        acc_k[...] = jnp.zeros_like(acc_k)
        acc_v[...] = jnp.zeros_like(acc_v)
        for b in range(4):
            rows = slice(16 * b, 16 * b + 16)
            blocks = list(range(max(0, b - 2), b + 1))
            queries = q_rot[b]
            keys = {kb: k_rot[kb] for kb in blocks}
            upstream = rdo[:, rows, :].reshape(256, HD)
            bents, probs = block_probs(queries, keys, first[b], b)
            d_probs = [dot(upstream, v_all[kb], 1, 1) for kb in blocks]
            centre = sum(
                jnp.sum(p * dp, axis=-1, keepdims=True) for p, dp in zip(probs, d_probs)
            )
            d_q = jnp.zeros((256, HD), F32)
            for kb, bent, p, dp in zip(blocks, bents, probs, d_probs):
                d_scores = (p * (dp - centre) * (1.0 - bent * bent)).astype(B16)
                d_q = d_q + dot(d_scores, keys[kb], 1, 0)
                acc_k[kb] += dot(d_scores, queries, 0, 0)
                acc_v[kb] += dot(p.astype(B16), upstream, 0, 0)
            d_q = unrotate(d_q * 0.0625, cosine[b], sine[b])
            held_q[:, rows, :] = d_q.astype(B16).reshape(16, 16, HD)
        for b in range(4):
            rows = slice(16 * b, 16 * b + 16)
            d_k = unrotate(acc_k[b] * 0.0625, cosine[b], sine[b]).astype(B16)
            d_v = acc_v[b].astype(B16)
            for i in range(2):
                cols = slice(128 * i, 128 * i + 128)
                held_kv[i, :, rows, :128] = d_k[:, cols].reshape(16, 16, 128)
                held_kv[i, :, rows, 128:] = d_v[:, cols].reshape(16, 16, 128)

        def hand_back(d, start):
            u = zh * 3 + y
            across = remote(
                held_kv.at[1 - half, d], d_kv.at[half, y, zh], send_kv.at[1, d], recv_kv.at[half, u], d, other
            )
            across.start() if start else across.wait_send()

            @pl.when(d != me)
            def _():
                for copy in (
                    remote(held_q.at[d], d_query.at[y, zh], send_q.at[d], recv_q.at[u], d, t),
                    remote(
                        held_kv.at[half, d], d_kv.at[half, y, zh], send_kv.at[0, d], recv_kv.at[half, u], d, t
                    ),
                ):
                    copy.start() if start else copy.wait_send()

            @pl.when(d == me)
            def _():
                for copy in (
                    pltpu.make_async_copy(held_q.at[d], d_query.at[y, zh], local.at[0]),
                    pltpu.make_async_copy(held_kv.at[half, d], d_kv.at[half, y, zh], local.at[1]),
                ):
                    copy.start() if start else copy.wait()

        lax.fori_loop(0, 16, lambda d, _: (hand_back(d, True), 0)[1], 0)
        lax.fori_loop(0, 16, lambda d, _: (hand_back(d, False), 0)[1], 0)

    for u, (m, w) in enumerate(units):

        @pl.when(unit_owner(m, w) != me)
        def _():
            ref = d_query.at[w, m]
            remote(ref, ref, send.at[0], recv_q.at[u], me, other).wait_recv()
            ref = d_kv.at[half, w, m]
            remote(ref, ref, send.at[0], recv_kv.at[half, u], me, other).wait_recv()

        ref = d_kv.at[1 - half, w, m]
        remote(ref, ref, send.at[0], recv_kv.at[1 - half, u], me, other).wait_recv()


def attend_back(d_attended, first, cosine, sine, q_rot, k_rot, v_all):
    return pl.pallas_call(
        attend_back_kernel,
        name="attend_back",
        out_shape=[struct((3, 2, 64, HD), B16), struct((2, 3, 2, 64, HD), B16)],
        in_specs=any_space(1) + vmem_space(6),
        out_specs=any_space(2),
        scratch_shapes=[
            pltpu.VMEM((16, 64, HD), B16),
            pltpu.VMEM((16, 64, HD), B16),
            pltpu.VMEM((2, 16, 64, HD), B16),
            pltpu.VMEM((4, 256, HD), F32),
            pltpu.VMEM((4, 256, HD), F32),
            pltpu.SemaphoreType.DMA((6,)),
            pltpu.SemaphoreType.DMA((16,)),
            pltpu.SemaphoreType.DMA((16,)),
            pltpu.SemaphoreType.DMA((2, 16)),
            pltpu.SemaphoreType.DMA((6,)),
            pltpu.SemaphoreType.DMA((2, 6)),
            pltpu.SemaphoreType.DMA((2,)),
        ],
        compiler_params=params(4),
    )(d_attended, first, cosine, sine, q_rot, k_rot, v_all)


def level(codes, width):
    if width == 0:
        return codes
    stride = (1, 16, 64)[width]
    return jnp.floor(codes * B16(1.0 / stride)) * B16(stride) + B16(stride // 2)


def gelu_parts(value):
    slope = 0.7978845608028654
    inner = jnp.tanh(slope * (value + 0.044715 * value * value * value))
    grown = 0.5 * value * (1.0 + inner)
    rate = 0.5 * (1.0 + inner) + 0.5 * value * (1.0 - inner * inner) * slope * (
        1.0 + 3 * 0.044715 * value * value
    )
    return grown, rate


def body(
    tokens,
    cotangent,
    segments,
    codes_query,
    codes_key,
    codes_value,
    codes_out,
    codes_gate,
    codes_up,
    codes_down,
    query_column_scale,
    key_column_scale,
    value_column_scale,
    output_column_scale,
    gate_column_scale,
    up_column_scale,
    down_column_scale,
    gain_first,
    gain_second,
    gain_third,
    gain_fourth,
):
    widths = range(3)
    z_hi = lax.rem(lax.div(lax.axis_index("dp"), 2), 2)
    tokens = tokens.reshape(ROWS, WIDE)
    cotangent = cotangent.reshape(3, ROWS, WIDE)
    gains = jnp.stack([gain_first, gain_second, gain_third, gain_fourth])
    w_qkv, w_out, w_gu, w_down = (
        gathered.reshape(WIDE, -1)
        for gathered in gather_weights(
            [
                jnp.concatenate([codes_query, codes_key, codes_value], 1).astype(B16),
                codes_out.astype(B16).T,
                jnp.concatenate([codes_gate, codes_up], 1).astype(B16),
                codes_down.astype(B16).T,
            ]
        )
    )
    scale_qkv = jnp.concatenate([query_column_scale, key_column_scale, value_column_scale])
    scale_gu = jnp.concatenate([gate_column_scale, up_column_scale])

    documents = lax.dynamic_index_in_dim(segments, z_hi, 0, False)
    starts = jnp.sum((documents[None, :] < documents[:, None]).astype(jnp.int32), axis=1)
    place = jnp.arange(1024, dtype=jnp.int32)

    def blocked(rows):
        return rows.reshape(4, 16, 16).transpose(0, 2, 1).reshape(4, 256)

    first = blocked(starts)[:, :, None]
    expo = jnp.arange(HD // 2, dtype=F32) * (2.0 / HD)
    angle = blocked(place - starts).astype(F32)[:, :, None] * jnp.power(ROPE_BASE, -expo)
    cosine, sine = jnp.cos(angle), jnp.sin(angle)

    inputs = tokens.astype(F32)
    normed_input = (inputs * inverse_rms(inputs) * (1.0 + gain_first)).astype(B16)
    qkv_pre = jnp.stack([dot(normed_input, level(w_qkv, w), 1, 0) * scale_qkv for w in widths])
    attended, q_rot, k_rot, v_all = attend(
        qkv_pre.astype(B16).reshape(3, 2, 64, 2 * HD), first, cosine, sine
    )
    attended = attended.reshape(3, ROWS, HD)
    branch_part = jnp.stack(
        [dot(attended[w], level(w_out, w), 1, 1) * output_column_scale for w in widths]
    ).astype(B16)
    normed_middle, branch, middle = tensor_call(
        middle_kernel,
        "middle",
        5,
        3,
        1,
        (branch_part, tokens[None], gains),
        any_space(2) + vmem_space(1),
        [struct((3, ROWS, WIDE), B16)] + [struct((3, SLICE, WIDE), F32)] * 2,
        any_space(1) + vmem_space(2),
        [pltpu.VMEM((3, SLICE, WIDE), B16)],
    )
    gu_pre = jnp.stack([dot(normed_middle[w], level(w_gu, w), 1, 0) * scale_gu for w in widths])
    half = gu_pre.shape[-1] // 2
    gate_pre, up_pre = gu_pre[..., :half], gu_pre[..., half:]
    grown, rate = gelu_parts(gate_pre)
    hidden = (grown * up_pre).astype(B16)
    feed_part = jnp.stack(
        [dot(hidden[w], level(w_down, w), 1, 1) * down_column_scale for w in widths]
    ).astype(B16)
    d_feed, final, feed_sums = tensor_call(
        feed_kernel,
        "feed",
        6,
        3,
        3,
        (feed_part, cotangent, middle, gains),
        any_space(2) + vmem_space(2),
        [struct((3, ROWS, WIDE), B16), struct((3, SLICE, WIDE), B16), struct((8, WIDE), F32)],
        any_space(1) + vmem_space(2),
        [pltpu.VMEM((3, SLICE, WIDE), B16)],
    )

    d_feed_scaled = (d_feed.astype(F32) * down_column_scale).astype(B16)
    d_hidden = jnp.stack([dot(d_feed_scaled[w], level(w_down, w), 1, 0) for w in widths])
    d_gu = jnp.concatenate([d_hidden * up_pre * rate, d_hidden * grown], -1)
    d_gu_low = d_gu.astype(B16)
    gu_sums = jnp.sum(d_gu_low.astype(F32) * gu_pre, axis=(0, 1)) / scale_gu
    d_gu_scaled = (d_gu * scale_gu).astype(B16)
    d_middle_part = jnp.stack([dot(d_gu_scaled[w], level(w_gu, w), 1, 1) for w in widths]).astype(
        B16
    )
    d_branch, d_middle, branch_sums = tensor_call(
        branch_kernel,
        "branch",
        7,
        3,
        3,
        (d_middle_part, cotangent, middle, branch, gains),
        any_space(2) + vmem_space(3),
        [struct((3, ROWS, WIDE), B16), struct((1, SLICE, WIDE), F32), struct((8, WIDE), F32)],
        any_space(1) + vmem_space(2),
        [pltpu.VMEM((3, SLICE, WIDE), B16)],
    )
    d_branch_scaled = (d_branch.astype(F32) * output_column_scale).astype(B16)
    d_attended = jnp.stack([dot(d_branch_scaled[w], level(w_out, w), 1, 0) for w in widths]).astype(
        B16
    )
    d_query, d_kv = attend_back(
        d_attended.reshape(3, 2, 64, HD), first, cosine, sine, q_rot, k_rot, v_all
    )
    d_kv = (d_kv[0].astype(F32) + d_kv[1].astype(F32)).astype(B16)
    d_qkv = jnp.concatenate([d_query, d_kv], -1).reshape(3, ROWS, 2 * HD).astype(F32)
    qkv_sums = jnp.sum(d_qkv * qkv_pre, axis=(0, 1)) / scale_qkv
    d_qkv_scaled = (d_qkv * scale_qkv).astype(B16)
    d_input_part = sum(dot(d_qkv_scaled[w], level(w_qkv, w), 1, 1) for w in widths).astype(B16)
    flat = (3 * ROWS, -1)
    parts = (
        dot(normed_input, jnp.sum(d_qkv, axis=0).astype(B16), 0, 0).astype(B16),
        dot(d_branch.reshape(flat), attended.reshape(flat), 0, 0).astype(B16),
        dot(normed_middle.reshape(flat), d_gu_low.reshape(flat), 0, 0).astype(B16),
        dot(d_feed.reshape(flat), hidden.reshape(flat), 0, 0).astype(B16),
    )
    sums = jnp.concatenate(
        [
            branch_sums[1:2],
            branch_sums[0:1],
            feed_sums[0:1],
            branch_sums[2:3] / output_column_scale,
            feed_sums[1:2] / down_column_scale,
        ]
    )
    columns = jnp.pad(jnp.concatenate([qkv_sums, gu_sums]), (0, 8 * EXTRA - 2816))
    g_qkv, g_out, g_gu, g_down, results, input_gradient, sums = finish_layer(
        parts, d_input_part[None], tokens[None], d_middle, gains, final, sums, columns.reshape(8, EXTRA)
    )
    rows = lax.dynamic_slice_in_dim(sums[:, :WIDE], lax.axis_index("dp") * SHARD, SHARD, 1)
    columns = sums[:, WIDE:].reshape(-1)
    return (
        results.reshape(3, 2, 64, 1, WIDE),
        input_gradient.reshape(2, 64, 1, WIDE),
        g_qkv[:, :256],
        g_qkv[:, 256:384],
        g_qkv[:, 384:],
        g_out.T,
        g_gu[:, :half],
        g_gu[:, half:],
        g_down.T,
        columns[:256],
        columns[256:384],
        columns[384:512],
        rows[4],
        columns[512 : 512 + half],
        columns[512 + half : 512 + 2 * half],
        rows[5],
        rows[0],
        rows[1],
        rows[2],
        rows[3],
    )


def solution(mesh):
    matrix, turned = P("dp", "tensor"), P("tensor", "dp")
    columns, whole, shard = P("tensor"), P(), P("dp")
    in_specs = (
        P(None, None, "dp", None),
        P(None, None, None, "dp", None),
        whole,
        *(matrix, matrix, matrix, turned, matrix, matrix, turned),
        *(columns, columns, columns, whole, columns, columns, whole),
        *(whole, whole, whole, whole),
    )
    out_specs = (
        P(None, None, None, "dp", None),
        P(None, None, "dp", None),
        *(matrix, matrix, matrix, turned, matrix, matrix, turned),
        *(columns, columns, columns, shard, columns, columns, shard),
        *(shard, shard, shard, shard),
    )
    return jax.shard_map(body, mesh=mesh, in_specs=in_specs, out_specs=out_specs, check_vma=False)
```

```python
import functools

import jax
import jax.numpy as jnp
from jax import lax
from jax.experimental import pallas as pl
from jax.experimental.pallas import tpu as pltpu
from jax.sharding import PartitionSpec as P

MESH = pl.DeviceIdType.MESH
F32 = jnp.float32
B16 = jnp.bfloat16
EPSILON = 1e-06
SOFTCAP = 50.0
ROPE_BASE = 10000.0
MASKED = -1e30
HD = 256
WIDE = 2304
SHARD = 144
LOW = 64
HIGH = SHARD - LOW
TENSOR = 8
ROWS = 128
SLICE = ROWS // TENSOR
EXTRA = 384
VMEM_BYTES = 63 * 2**20


def here():
    dp = lax.axis_index("dp")
    return lax.div(dp, 4), lax.rem(lax.div(dp, 2), 2), lax.rem(dp, 2), lax.axis_index("tensor")


def rank(y, z_hi, core):
    return (y * 2 + z_hi) * 2 + core


def remote(src, dst, send, recv, dp, tensor):
    return pltpu.make_async_remote_copy(
        src, dst, send, recv, device_id=(dp, tensor), device_id_type=MESH
    )


def greet(devices):
    barrier = pltpu.get_barrier_semaphore()
    for device in devices:
        pl.semaphore_signal(barrier, inc=1, device_id=device, device_id_type=MESH)
    pl.semaphore_wait(barrier, len(devices))


def struct(shape, dtype):
    return jax.ShapeDtypeStruct(shape, dtype)


def any_space(count):
    return [pl.BlockSpec(memory_space=pl.ANY)] * count


def vmem_space(count):
    return [pl.BlockSpec(memory_space=pltpu.VMEM)] * count


def params(collective_id):
    return pltpu.CompilerParams(
        collective_id=collective_id, has_side_effects=True, vmem_limit_bytes=VMEM_BYTES
    )


class Gather:
    def __init__(self, src, out, send, recv, local):
        self.src, self.out, self.send, self.recv, self.local = src, out, send, recv, local
        self.y, self.zh, self.core, self.t = here()
        y, zh, core = self.y, self.zh, self.core
        self.me, self.sib, self.zz = rank(y, zh, core), rank(y, zh, 1 - core), rank(y, 1 - zh, core)
        self.fore = [rank(lax.rem(y + dy, 4), zh, core) for dy in (1, 2, 3)]
        self.behind = [lax.rem(y + 4 - dy, 4) for dy in (1, 2, 3)]
        self.low, self.high = pl.ds(0, LOW), pl.ds(LOW, HIGH)
        self.started = []

    def push(self, slot, src, dst, dp):
        copy = remote(src, dst, self.send.at[slot], self.recv.at[slot], dp, self.t)
        copy.start()
        self.started.append(copy)

    def arrive(self, slot, ref):
        remote(ref, ref, self.send.at[slot], self.recv.at[slot], self.sib, self.t).wait_recv()

    def start(self):
        src, mine = self.src, self.out.at[self.me]
        self.mine = pltpu.make_async_copy(src, mine, self.local)
        self.mine.start()
        low, high = self.low, self.high
        self.push(0, src.at[low], self.out.at[self.me, low], self.zz)
        for i in range(3):
            self.push(4 + i, src.at[high], self.out.at[self.me, high], self.fore[i])
        for i in range(3):
            self.push(1 + i, src.at[low], self.out.at[self.me, low], self.fore[i])
        self.push(7, src.at[high], self.out.at[self.me, high], self.zz)
        self.push(14, src, mine, self.sib)

    def over_y(self):
        block = self.out.at[self.zz, self.low]
        self.arrive(0, block)
        for i in range(3):
            self.push(8 + i, block, block, self.fore[i])
        self.push(15, block, block, self.sib)

    def over_z(self):
        for i in range(3):
            block = self.out.at[rank(self.behind[i], self.zh, self.core), self.high]
            self.arrive(4 + i, block)
            self.push(11 + i, block, block, self.zz)
            self.push(16 + i, block, block, self.sib)

    def near(self):
        for i in range(3):
            block = self.out.at[rank(self.behind[i], self.zh, self.core), self.low]
            self.arrive(1 + i, block)
            self.push(19 + i, block, block, self.sib)
        block = self.out.at[self.zz, self.high]
        self.arrive(7, block)
        self.push(22, block, block, self.sib)

    def far(self):
        for i in range(3):
            dp = rank(self.behind[i], 1 - self.zh, self.core)
            for slot, rows in ((0, self.low), (3, self.high)):
                block = self.out.at[dp, rows]
                self.arrive(8 + slot + i, block)
                self.push(23 + slot + i, block, block, self.sib)

    def end(self):
        out, low, high, other = self.out, self.low, self.high, 1 - self.core
        self.arrive(14, out.at[self.sib])
        far = rank(self.y, 1 - self.zh, other)
        self.arrive(15, out.at[far, low])
        self.arrive(22, out.at[far, high])
        for i in range(3):
            near, far = (rank(self.behind[i], zh, other) for zh in (self.zh, 1 - self.zh))
            self.arrive(16 + i, out.at[near, high])
            self.arrive(19 + i, out.at[near, low])
            self.arrive(23 + i, out.at[far, low])
            self.arrive(26 + i, out.at[far, high])
        self.mine.wait()

    def drain(self):
        for copy in self.started:
            copy.wait_send()


class Rows:
    def __init__(self, part, held_x, held_z, stage, block, out, sems, own=None):
        self.own = own
        self.part, self.held_x, self.held_z, self.stage = part, held_x, held_z, stage
        self.block, self.out = block, out
        self.send, self.recv, self.local = sems
        self.dp, self.t = lax.axis_index("dp"), lax.axis_index("tensor")
        self.zl, self.x = lax.div(self.t, 4), lax.rem(self.t, 4)
        self.ahead = [lax.rem(self.x + k, 4) for k in (1, 2, 3)]
        self.behind = [lax.rem(self.x + 4 - k, 4) for k in (1, 2, 3)]
        self.x_peers = [self.zl * 4 + x for x in self.ahead]
        self.z_peer = (1 - self.zl) * 4 + self.x
        self.started = []

    def peers(self):
        return [(self.dp, t) for t in self.x_peers + [self.z_peer]]

    def push(self, w, slot, src, dst, t):
        copy = remote(src, dst, self.send.at[w, slot], self.recv.at[w, slot], self.dp, t)
        copy.start()
        self.started.append(copy)

    def arrive(self, w, slot, ref):
        remote(
            ref, ref, self.send.at[w, slot], self.recv.at[w, slot], self.dp, self.z_peer
        ).wait_recv()

    def scatter_x(self, w):
        for k in range(3):
            self.push(w, 1 + k, self.part.at[w, :, self.ahead[k]], self.held_x.at[w, k], self.x_peers[k])

    def summed_x(self, w, zl):
        total = (self.part[w, zl, self.x] if self.own is None else self.own[w, zl]).astype(F32)
        for k in range(3):
            total = total + self.held_x[w, k, zl].astype(F32)
        return total

    def scatter_z(self, w):
        for k in range(3):
            self.arrive(w, 1 + k, self.held_x.at[w, k])
        self.stage[w] = self.summed_x(w, 1 - self.zl).astype(B16)
        self.push(w, 0, self.stage.at[w], self.held_z.at[w], self.z_peer)

    def total(self, w):
        self.arrive(w, 0, self.held_z.at[w])
        return self.summed_x(w, self.zl) + self.held_z[w].astype(F32)

    def spread(self, w):
        block, mine = self.block.at[w], self.out.at[w, self.zl, self.x]
        self.push(w, 4, block, mine, self.z_peer)
        for k in range(3):
            self.push(w, 5 + k, block, mine, self.x_peers[k])
        pltpu.make_async_copy(block, mine, self.local.at[w]).start()

    def forward(self, w):
        block = self.out.at[w, 1 - self.zl, self.x]
        self.arrive(w, 4, block)
        for k in range(3):
            self.push(w, 8 + k, block, block, self.x_peers[k])

    def end(self, w):
        for k in range(3):
            self.arrive(w, 5 + k, self.out.at[w, self.zl, self.behind[k]])
            self.arrive(w, 8 + k, self.out.at[w, 1 - self.zl, self.behind[k]])
        pltpu.make_async_copy(
            self.block.at[w], self.out.at[w, self.zl, self.x], self.local.at[w]
        ).wait()

    def drain(self):
        for copy in self.started:
            copy.wait_send()


def rows_scratch(depth):
    return [
        pltpu.VMEM((depth, 3, 2, SLICE, WIDE), B16),
        pltpu.VMEM((depth, SLICE, WIDE), B16),
        pltpu.VMEM((depth, SLICE, WIDE), B16),
        pltpu.VMEM((depth, SLICE, WIDE), B16),
        pltpu.SemaphoreType.DMA((depth, 11)),
        pltpu.SemaphoreType.DMA((depth, 11)),
        pltpu.SemaphoreType.DMA((depth,)),
    ]


class Reduce:
    def __init__(self, columns, away, own, sibs, yrecv, zrecv, ylast, zlast, out, send, recv):
        self.columns, self.away, self.own, self.sibs = columns, away, own, sibs
        self.yrecv, self.zrecv, self.ylast, self.zlast, self.out = yrecv, zrecv, ylast, zlast, out
        self.send, self.recv = send, recv
        self.y, self.zh, self.core, self.t = here()
        y, zh, core = self.y, self.zh, self.core
        self.sib, self.zz = rank(y, zh, 1 - core), rank(y, 1 - zh, core)
        self.ahead = [lax.rem(y + dy, 4) for dy in (1, 2, 3)]
        self.fore = [rank(place, zh, core) for place in self.ahead]
        self.started = []

    def push(self, slot, src, dst, dp):
        copy = remote(src, dst, self.send.at[slot], self.recv.at[slot], dp, self.t)
        copy.start()
        self.started.append(copy)

    def arrive(self, slot, ref):
        remote(ref, ref, self.send.at[slot], self.recv.at[slot], self.sib, self.t).wait_recv()

    def store(self, first, count, cols, block):
        block = block.astype(B16).reshape(count, 2, SHARD, block.shape[-1])
        even = self.core == 0
        chips = pl.ds(first, count)
        self.own[chips, :, cols] = jnp.where(even, block[:, 0], block[:, 1])
        self.away[chips, :, cols] = jnp.where(even, block[:, 1], block[:, 0])

    def to_sibling(self, place):
        pair = pl.ds(place * 2, 2)
        return remote(
            self.away.at[pair, :, pl.ds(0, self.columns)],
            self.sibs.at[pair],
            self.send.at[place],
            self.recv.at[place],
            self.sib,
            self.t,
        )

    def product(self, turned, right, left_columns=0):
        def step(place, _):
            rows = pl.ds(pl.multiple_of(place * 4 * SHARD, 16), 4 * SHARD)
            for i in range(self.columns // 384):
                block = dot(turned[rows], right[:, left_columns + 384 * i : left_columns + 384 * (i + 1)], 1, 0)
                self.store(place * 2, 2, slice(384 * i, 384 * (i + 1)), block)
            self.to_sibling(place).start()
            return 0

        lax.fori_loop(0, 4, step, 0)

    def product_whole(self, left, right):
        for i in range(self.columns // HD):
            cols = slice(HD * i, HD * i + HD)
            self.store(0, 8, cols, dot(left, right[:, cols], 0, 0))
        for place in range(4):
            self.to_sibling(place).start()

    def sent_away(self):
        for place in range(4):
            self.to_sibling(place).wait_send()

    def add(self):
        own, sibs = self.own, self.sibs
        for i, place in enumerate(self.ahead + [self.y]):
            pair = pl.ds(place * 2, 2)
            self.arrive(place, sibs.at[pair])

            def step(step, _, place=place):
                chip = place * 2 + lax.div(step, SHARD // 16)
                rows = pl.ds(pl.multiple_of(lax.rem(step, SHARD // 16) * 16, 16), 16)
                own[chip, rows] = (
                    own[chip, rows].astype(F32) + sibs[chip, rows].astype(F32)
                ).astype(B16)
                return 0

            lax.fori_loop(0, 2 * SHARD // 16, step, 0)
            self.push(
                7 + i, own.at[place * 2 + 1 - self.zh, pl.ds(LOW, HIGH)], self.zrecv.at[place], self.zz
            )
            if i < 3:
                self.push(4 + i, own.at[pair, pl.ds(0, LOW)], self.yrecv.at[i], self.fore[i])

    def merge(self):
        own, zrecv = self.own, self.zrecv
        for i, place in enumerate(self.ahead + [self.y]):
            self.arrive(7 + i, zrecv.at[place])

            def step(step, _, place=place):
                rows = pl.ds(pl.multiple_of(step * 16, 16), 16)
                mine = pl.ds(pl.multiple_of(step * 16 + LOW, 16), 16)
                zrecv[place, rows] = (
                    zrecv[place, rows].astype(F32) + own[place * 2 + self.zh, mine].astype(F32)
                ).astype(B16)
                return 0

            lax.fori_loop(0, HIGH // 16, step, 0)
            if i < 3:
                self.push(11 + i, zrecv.at[place], self.ylast.at[i], self.fore[i])

    def pool(self):
        for i in range(3):
            self.arrive(4 + i, self.yrecv.at[i])

        def step(step, _):
            chip = lax.div(step, LOW // 16)
            rows = pl.ds(pl.multiple_of(lax.rem(step, LOW // 16) * 16, 16), 16)
            total = self.own[self.y * 2 + chip, rows].astype(F32)
            for i in range(3):
                total = total + self.yrecv[i, chip, rows].astype(F32)
            self.own[self.y * 2 + chip, rows] = total.astype(B16)
            return 0

        lax.fori_loop(0, 2 * LOW // 16, step, 0)
        self.push(14, self.own.at[self.y * 2 + 1 - self.zh, pl.ds(0, LOW)], self.zlast, self.zz)

    def end(self):
        self.arrive(14, self.zlast)

        def low(step, _):
            rows = pl.ds(pl.multiple_of(step * 16, 16), 16)
            self.out[rows] = self.own[self.y * 2 + self.zh, rows].astype(F32) + self.zlast[
                rows
            ].astype(F32)
            return 0

        lax.fori_loop(0, LOW // 16, low, 0)
        for i in range(3):
            self.arrive(11 + i, self.ylast.at[i])

        def high(step, _):
            rows = pl.ds(pl.multiple_of(step * 16, 16), 16)
            total = self.zrecv[self.y, rows].astype(F32)
            for i in range(3):
                total = total + self.ylast[i, rows].astype(F32)
            self.out[pl.ds(pl.multiple_of(step * 16 + LOW, 16), 16)] = total
            return 0

        lax.fori_loop(0, HIGH // 16, high, 0)

    def drain(self):
        for copy in self.started:
            copy.wait_send()


def reduce_scratch(columns):
    return [
        pltpu.VMEM((8, SHARD, columns), B16),
        pltpu.VMEM((8, SHARD, columns), B16),
        pltpu.VMEM((3, 2, LOW, columns), B16),
        pltpu.VMEM((4, HIGH, columns), B16),
        pltpu.VMEM((3, HIGH, columns), B16),
        pltpu.VMEM((LOW, columns), B16),
        pltpu.SemaphoreType.DMA((15,)),
        pltpu.SemaphoreType.DMA((15,)),
    ]


def row_block(index):
    return pl.ds(pl.multiple_of(index * SLICE, SLICE), SLICE)


def tensor_peers():
    t = lax.axis_index("tensor")
    return [lax.rem(t + k, TENSOR) for k in range(TENSOR)]


def greet_tensor():
    dp = lax.axis_index("dp")
    greet([(dp, peer) for peer in tensor_peers()[1:]])


def scatter_rows(part, held, send, recv, local):
    dp = lax.axis_index("dp")
    peers = tensor_peers()
    copies = []
    for k in range(1, TENSOR):
        copy = remote(
            part.at[:, row_block(peers[k])], held.at[k], send.at[k], recv.at[k], dp, peers[k]
        )
        copy.start()
        copies.append(copy)
    mine = pltpu.make_async_copy(part.at[:, row_block(peers[0])], held.at[0], local)
    mine.start()
    mine.wait()
    return copies


def summed(held, copies):
    total = held[0].astype(F32)
    for k in range(1, TENSOR):
        copies[k - 1].wait_recv()
        total = total + held[k].astype(F32)
    return total


def spread_rows(block, whole, send, recv, local):
    dp = lax.axis_index("dp")
    peers = tensor_peers()
    here_rows = whole.at[:, row_block(peers[0])]
    copies = []
    for k in range(1, TENSOR):
        copy = remote(block, here_rows, send.at[k], recv.at[k], dp, peers[k])
        copy.start()
        copies.append(copy)
    mine = pltpu.make_async_copy(block, here_rows, local)
    mine.start()

    def finish():
        mine.wait()
        for k in range(1, TENSOR):
            source = whole.at[:, row_block(peers[TENSOR - k])]
            remote(source, source, send.at[k], recv.at[k], dp, peers[k]).wait_recv()
        for copy in copies:
            copy.wait_send()

    return finish


def inverse_rms(signal):
    return lax.rsqrt(jnp.mean(signal * signal, axis=-1, keepdims=True) + EPSILON)


def norm_back(normed, inverse, gain, upstream):
    inner = upstream * (1.0 + gain)
    return inverse * (inner - normed * jnp.mean(inner * normed, axis=-1, keepdims=True))


def over_rows(term):
    return jnp.sum(term, axis=(0, 1))[None]


def load_rows(whole, block, local):
    copy = pltpu.make_async_copy(
        whole.at[:, row_block(lax.axis_index("tensor"))], block, local
    )
    copy.start()
    return copy


def feed_kernel(
    part, cotangent, middle, gains, d_feed, final, sums, held, mine, block, send, recv, local
):
    greet_tensor()
    copies = scatter_rows(part, held, send.at[0], recv.at[0], local.at[0])
    load = load_rows(cotangent, mine, local.at[1])
    load.wait()
    signal = summed(held, copies)
    inverse = inverse_rms(signal)
    normed = signal * inverse
    upstream = mine[...].astype(F32)
    lowered = norm_back(normed, inverse, gains[3:4], upstream).astype(B16)
    block[...] = lowered
    finish = spread_rows(block, d_feed, send.at[1], recv.at[1], local.at[2])
    final[...] = (middle[...] + normed * (1.0 + gains[3:4])).astype(B16)
    sums[0:1] = over_rows(upstream * normed)
    sums[1:2] = over_rows(lowered.astype(F32) * signal)
    for copy in copies:
        copy.wait_send()
    finish()


def tensor_call(
    kernel, name, collective_id, depth, loaded, operands, in_specs, outs, out_specs, blocks
):
    return pl.pallas_call(
        kernel,
        name=name,
        out_shape=outs,
        in_specs=in_specs,
        out_specs=out_specs,
        scratch_shapes=[
            pltpu.VMEM((TENSOR, depth, SLICE, WIDE), B16),
            pltpu.VMEM((loaded, SLICE, WIDE), B16),
        ]
        + blocks
        + [
            pltpu.SemaphoreType.DMA((3, TENSOR)),
            pltpu.SemaphoreType.DMA((3, TENSOR)),
            pltpu.SemaphoreType.DMA((4,)),
        ],
        compiler_params=params(collective_id),
    )(*operands)


def unit_owner(micro, width):
    return rank(width, micro, 0)


def rotate(signal, cosine, sine):
    former, latter = signal[:, : HD // 2], signal[:, HD // 2 :]
    return jnp.concatenate([former * cosine - latter * sine, latter * cosine + former * sine], -1)


def unrotate(signal, cosine, sine):
    former, latter = signal[:, : HD // 2], signal[:, HD // 2 :]
    return jnp.concatenate([former * cosine + latter * sine, latter * cosine - former * sine], -1)


def block_scores(queries, keys, first, b, kb):
    scores = lax.dot_general(queries, keys, (((1,), (1,)), ((), ())), preferred_element_type=F32)
    bent = jnp.tanh(scores * (0.0625 / SOFTCAP))
    lane = lax.broadcasted_iota(jnp.int32, (256, 256), 1)
    row = lax.broadcasted_iota(jnp.int32, (256, 256), 0)
    key_place = (16 * kb + (lane & 15)) * 16 + (lane >> 4)
    query_place = (16 * b + (row & 15)) * 16 + (row >> 4)
    allowed = (key_place >= first) & (key_place <= query_place)
    return bent, jnp.where(allowed, SOFTCAP * bent, MASKED)


def block_probs(queries, keys, first, b):
    pieces = [
        block_scores(queries, keys[kb], first, b, kb) for kb in range(max(0, b - 2), b + 1)
    ]
    peak = functools.reduce(
        jnp.maximum, [jnp.max(capped, axis=-1, keepdims=True) for _, capped in pieces]
    )
    exps = [jnp.exp(capped - peak) for _, capped in pieces]
    total = functools.reduce(jnp.add, [jnp.sum(e, axis=-1, keepdims=True) for e in exps])
    return [bent for bent, _ in pieces], [e / total for e in exps]


def dot(left, right, left_dim, right_dim):
    return lax.dot_general(
        left, right, (((left_dim,), (right_dim,)), ((), ())), preferred_element_type=F32
    )


def front_kernel(*refs):
    shards, refs = refs[:4], refs[4:]
    (tokens, gains, scale_qkv, scale_out, first, cosine, sine), refs = refs[:7], refs[7:]
    (w_qkv, w_out, w_gu, w_down, normed_middle), refs = refs[:5], refs[5:]
    (attended, normed_input, qkv_pre, q_rot, k_rot, v_all, branch, middle), refs = refs[:8], refs[8:]
    (wq, wo, low, rq, rkv, held, att, part), refs = refs[:8], refs[8:]
    (held_x, held_z, stage, block, *row_sems), refs = refs[:7], refs[7:]
    (send_g, recv_g, local_g, send, recv_q, recv_kv, send_back, recv_back, local) = refs
    y, zh, core, t = here()
    me = rank(y, zh, core)
    half = lax.rem(t, 2)
    other = t + 1 - 2 * half
    owner = (y < 3) & (core == 0)
    units = [(m, w) for m in range(2) for w in range(3)]
    gathers = [
        Gather(src, out, send_g.at[k], recv_g.at[k], local_g.at[k])
        for k, (src, out) in enumerate(zip(shards, (wq, wo, w_gu, w_down)))
    ]
    g_qkv, g_out, g_gu, g_down = gathers
    rows = Rows(part, held_x, held_z, stage, block, normed_middle, row_sems)
    barrier = pltpu.get_barrier_semaphore()

    def signal(dp, tensor):
        pl.semaphore_signal(barrier, inc=1, device_id=(dp, tensor), device_id_type=MESH)

    plane = [(g_qkv.sib, t), (g_qkv.zz, t)] + [(dp, t) for dp in g_qkv.fore] + rows.peers()
    for device in plane:
        signal(*device)

    @pl.when(owner)
    def _():
        def each(d, _):
            pl.when(d != me)(lambda: signal(d, t))
            signal(d, other)
            return 0

        lax.fori_loop(0, 16, each, 0)

    for m, w in units:
        pl.when(unit_owner(m, w) != me)(functools.partial(signal, unit_owner(m, w), t))

    @pl.when(owner)
    def _():
        pl.semaphore_wait(barrier, len(plane) + 26)

    @pl.when(jnp.logical_not(owner))
    def _():
        pl.semaphore_wait(barrier, len(plane) + 12)

    g_qkv.start()
    g_out.start()
    inputs = tokens[...].astype(F32)
    normed_input[...] = (inputs * inverse_rms(inputs) * (1.0 + gains[0:1])).astype(B16)
    for gather in (g_qkv, g_out):
        gather.over_y()
        gather.over_z()
    for gather in (g_qkv, g_out):
        gather.near()
        gather.far()
    g_qkv.end()

    for i in range(2):
        cols = slice(HD * i, HD * i + HD)
        codes = wq[:, :, cols].reshape(WIDE, HD)
        for w in range(3):
            product = dot(normed_input[...], level(codes, w), 1, 0) * scale_qkv[:, cols]
            qkv_pre[w, :, cols] = product
            low[w, :, :, cols] = product.astype(B16).reshape(2, 64, HD)

    def to_owner(u, m, w, start):
        o = unit_owner(m, w)
        q_src, kv_src = low.at[w, m, :, pl.ds(0, HD)], low.at[w, m, :, pl.ds(HD, HD)]
        across = remote(kv_src, rkv.at[half, me], send.at[u, 2], recv_kv.at[half, me], o, other)
        away = [
            remote(q_src, rq.at[me], send.at[u, 0], recv_q.at[me], o, t),
            remote(kv_src, rkv.at[half, me], send.at[u, 1], recv_kv.at[half, me], o, t),
        ]
        near = [
            pltpu.make_async_copy(q_src, rq.at[me], local.at[0]),
            pltpu.make_async_copy(kv_src, rkv.at[half, me], local.at[1]),
        ]

        @pl.when(o != me)
        def _():
            for copy in away:
                copy.start() if start else copy.wait_send()

        @pl.when(o == me)
        def _():
            for copy in near:
                copy.start() if start else copy.wait()

        across.start() if start else across.wait_send()

    for u, (m, w) in enumerate(units):
        to_owner(u, m, w, True)

    @pl.when(owner)
    def _():
        for u, (m, w) in enumerate(units):

            @pl.when(unit_owner(m, w) == me)
            def _():
                for i in range(2):
                    ref = (rq.at[me], rkv.at[half, me])[i]
                    pltpu.make_async_copy(ref, ref, local.at[i]).wait()

        def each(d, _):
            @pl.when(d != me)
            def _():
                remote(rq.at[d], rq.at[d], send.at[0, 0], recv_q.at[d], me, other).wait_recv()
                remote(
                    rkv.at[half, d], rkv.at[half, d], send.at[0, 0], recv_kv.at[half, d], me, other
                ).wait_recv()

            remote(
                rkv.at[1 - half, d], rkv.at[1 - half, d], send.at[0, 0], recv_kv.at[1 - half, d], me, other
            ).wait_recv()
            return 0

        lax.fori_loop(0, 16, each, 0)
        for b in range(4):
            rows_b = slice(16 * b, 16 * b + 16)
            c, s = cosine[b], sine[b]
            q = rq[:, rows_b, :].reshape(256, HD).astype(F32)
            q_rot[b] = rotate(q, c, s).astype(B16)
            k = jnp.concatenate(
                [rkv[i, :, rows_b, : HD // 2].reshape(256, HD // 2) for i in range(2)], -1
            )
            k_rot[b] = rotate(k.astype(F32), c, s).astype(B16)
            v_all[b] = jnp.concatenate(
                [rkv[i, :, rows_b, HD // 2 :].reshape(256, HD // 2) for i in range(2)], -1
            )
        for b in range(4):
            keys = {kb: k_rot[kb] for kb in range(max(0, b - 2), b + 1)}
            _, probs = block_probs(q_rot[b], keys, first[b], b)
            out = sum(
                dot(p.astype(B16), v_all[kb], 1, 0) for p, kb in zip(probs, sorted(keys))
            )
            held[:, 16 * b : 16 * b + 16, :] = out.astype(B16).reshape(16, 16, HD)

        def hand_back(d, start):
            @pl.when(d != me)
            def _():
                copy = remote(
                    held.at[d], att.at[y, zh], send_back.at[d], recv_back.at[zh * 3 + y], d, t
                )
                copy.start() if start else copy.wait_send()

            @pl.when(d == me)
            def _():
                copy = pltpu.make_async_copy(held.at[d], att.at[y, zh], local.at[0])
                copy.start() if start else copy.wait()

        lax.fori_loop(0, 16, lambda d, _: (hand_back(d, True), 0)[1], 0)
        lax.fori_loop(0, 16, lambda d, _: (hand_back(d, False), 0)[1], 0)

    g_gu.start()
    g_down.start()
    g_out.end()
    for u, (m, w) in enumerate(units):

        @pl.when(unit_owner(m, w) != me)
        def _():
            ref = att.at[w, m]
            remote(ref, ref, send.at[0, 0], recv_back.at[u], me, other).wait_recv()

    codes = wo[...].reshape(WIDE, HD)
    for w in range(3):
        product = dot(att[w].reshape(ROWS, HD), level(codes, w), 1, 1) * scale_out[...]
        part[w] = product.astype(B16).reshape(2, 4, SLICE, WIDE)
        rows.scatter_x(w)
    attended[...] = att[...]
    keep = [
        pltpu.make_async_copy(src, dst, local.at[i])
        for i, (src, dst) in enumerate(((wq, w_qkv), (wo, w_out)))
    ]
    for copy in keep:
        copy.start()
    g_gu.over_y()
    g_down.over_y()
    g_gu.over_z()
    g_down.over_z()
    for w in range(3):
        rows.scatter_z(w)
    mine = tokens[pl.ds(pl.multiple_of(t * SLICE, SLICE), SLICE)].astype(F32)
    for w in range(3):
        signal_w = rows.total(w)
        branch[w] = signal_w
        total = mine + signal_w * inverse_rms(signal_w) * (1.0 + gains[1:2])
        middle[w] = total
        block[w] = (total * inverse_rms(total) * (1.0 + gains[2:3])).astype(B16)
        rows.spread(w)
    for gather in (g_gu, g_down):
        gather.near()
    for w in range(3):
        rows.forward(w)
    for gather in (g_gu, g_down):
        gather.far()
    for w in range(3):
        rows.end(w)
    for gather in (g_gu, g_down):
        gather.end()
    for copy in keep:
        copy.wait()
    for u, (m, w) in enumerate(units):
        o = unit_owner(m, w)

        @pl.when(o != me)
        def _():
            for slot, src in enumerate((low.at[w, m, :, pl.ds(0, HD)], low.at[w, m, :, pl.ds(HD, HD)])):
                remote(src, src, send.at[u, slot], recv_q.at[0], o, t).wait_send()

        src = low.at[w, m, :, pl.ds(HD, HD)]
        remote(src, src, send.at[u, 2], recv_q.at[0], o, other).wait_send()
    rows.drain()
    for gather in gathers:
        gather.drain()


def front(shards, tokens, gains, scale_qkv, scale_out, first, cosine, sine):
    return pl.pallas_call(
        front_kernel,
        name="front",
        out_shape=[struct((16,) + shard.shape, B16) for shard in shards]
        + [
            struct((3, 2, 4, SLICE, WIDE), B16),
            struct((3, 2, 64, HD), B16),
            struct((ROWS, WIDE), B16),
            struct((3, ROWS, 2 * HD), F32),
        ]
        + [struct((4, 256, HD), B16)] * 3
        + [struct((3, SLICE, WIDE), F32)] * 2,
        in_specs=any_space(4) + vmem_space(7),
        out_specs=any_space(5) + vmem_space(8),
        scratch_shapes=[
            pltpu.VMEM((16, SHARD, 2 * HD), B16),
            pltpu.VMEM((16, SHARD, HD), B16),
            pltpu.VMEM((3, 2, 64, 2 * HD), B16),
            pltpu.VMEM((16, 64, HD), B16),
            pltpu.VMEM((2, 16, 64, HD), B16),
            pltpu.VMEM((16, 64, HD), B16),
            pltpu.VMEM((3, 2, 64, HD), B16),
            pltpu.VMEM((3, 2, 4, SLICE, WIDE), B16),
        ]
        + rows_scratch(3)
        + [
            pltpu.SemaphoreType.DMA((4, 29)),
            pltpu.SemaphoreType.DMA((4, 29)),
            pltpu.SemaphoreType.DMA((4,)),
            pltpu.SemaphoreType.DMA((6, 3)),
            pltpu.SemaphoreType.DMA((16,)),
            pltpu.SemaphoreType.DMA((2, 16)),
            pltpu.SemaphoreType.DMA((16,)),
            pltpu.SemaphoreType.DMA((6,)),
            pltpu.SemaphoreType.DMA((2,)),
        ],
        compiler_params=params(3),
    )(*shards, tokens, gains, scale_qkv[None], scale_out[None], first, cosine, sine)


GRADIENTS = (1152, 1152, 1152, HD, 2 * HD)


def back_kernel(*refs):
    (part, cotangent), refs = refs[:2], refs[2:]
    (turned_middle, turned_feed, d_gu, hidden, middle, branch, final, feed_sums, gu_sums), refs = refs[:9], refs[9:]
    (w_out, w_qkv, scale_out, scale_down, scale_qkv, gains, tokens, attended, normed_input), refs = refs[:9], refs[9:]
    (qkv_pre, first, cosine, sine, q_rot, k_rot, v_all), refs = refs[:7], refs[7:]
    (results, gradient, totals), refs = refs[:3], refs[3:]
    outs, refs = refs[:5], refs[5:]
    aways, refs = refs[:2], refs[2:]
    reduces = []
    for k, columns in enumerate(GRADIENTS):
        held, refs = refs[:8], refs[8:]
        away = aways[k % 2]
        reduces.append(Reduce(columns, away, *held[:6], outs[k], *held[6:]))
    g_gate, g_up, g_down, g_out, g_qkv = reduces
    (own_part, cot, d_branch), refs = refs[:3], refs[3:]
    (held_x, held_z, stage, block, *row_sems), refs = refs[:7], refs[7:]
    (part_in, held_x1, held_z1, stage1, _, *row_sems1), refs = refs[:8], refs[8:]
    (result_sems, block1), refs = (refs[:3], refs[3]), refs[4:]
    (vec_x, vec_z, vec_sib, vec_y, vec_zz, vec, send_v, recv_v), refs = refs[:8], refs[8:]
    (datt, rdo, held_q, held_kv, acc_k, acc_v, d_query, d_kv), refs = refs[:8], refs[8:]
    send, recv, send_q, send_kv, recv_q, recv_kv, local = refs
    y, zh, core, t = here()
    me = rank(y, zh, core)
    half = lax.rem(t, 2)
    other = t + 1 - 2 * half
    owner = (y < 3) & (core == 0)
    units = [(m, w) for m in range(2) for w in range(3)]
    rows = Rows(part, held_x, held_z, stage, block, d_branch, row_sems, own_part)
    rows_in = Rows(part_in, held_x1, held_z1, stage1, block1, gradient, row_sems1)
    rows_out = Rows(None, None, None, None, final, results, result_sems)
    barrier = pltpu.get_barrier_semaphore()

    def signal(dp, tensor):
        pl.semaphore_signal(barrier, inc=1, device_id=(dp, tensor), device_id_type=MESH)

    plane = [(g_gate.sib, t), (g_gate.zz, t)] + [(dp, t) for dp in g_gate.fore] + rows.peers()
    for device in plane:
        signal(*device)

    @pl.when(owner)
    def _():
        def each(d, _):
            pl.when(d != me)(lambda: signal(d, t))
            return 0

        lax.fori_loop(0, 16, each, 0)

    for m, w in units:
        pl.when(unit_owner(m, w) != me)(functools.partial(signal, unit_owner(m, w), t))
        signal(unit_owner(m, w), other)

    @pl.when(owner)
    def _():
        pl.semaphore_wait(barrier, len(plane) + 36)

    @pl.when(jnp.logical_not(owner))
    def _():
        pl.semaphore_wait(barrier, len(plane) + 6)

    for w in range(3):
        rows.scatter_x(w)
    loads = [
        pltpu.make_async_copy(part.at[:, :, rows.x], own_part, local.at[0]),
        pltpu.make_async_copy(cotangent.at[:, rows.zl, rows.x], cot, local.at[1]),
    ]
    for copy in loads:
        copy.start()
    g_gate.product(turned_middle, d_gu)
    for copy in loads:
        copy.wait()
    rows.scatter_z(0)
    g_up.product(turned_middle, d_gu, 1152)
    rows.scatter_z(1)
    g_gate.sent_away()
    g_down.product(turned_feed, hidden)
    rows.scatter_z(2)
    d_middle = jnp.zeros((SLICE, WIDE), F32)
    sums = [jnp.zeros((1, WIDE), F32)] * 3
    for w in range(3):
        upstream = rows.total(w)
        signal_w = middle[w]
        inverse = inverse_rms(signal_w)
        normed = signal_w * inverse
        d_signal = cot[w].astype(F32) + norm_back(normed, inverse, gains[2:3], upstream)
        lower = branch[w]
        inverse_lower = inverse_rms(lower)
        normed_lower = lower * inverse_lower
        lowered = norm_back(normed_lower, inverse_lower, gains[1:2], d_signal).astype(B16)
        block[w] = lowered
        rows.spread(w)
        d_middle = d_middle + d_signal
        terms = (d_signal * normed_lower, upstream * normed, lowered.astype(F32) * lower)
        sums = [old + jnp.sum(new, axis=0, keepdims=True) for old, new in zip(sums, terms)]
        if w == 0:
            g_gate.add()
    g_up.add()
    vec[1:2] = sums[0]
    vec[2:3] = sums[1]
    vec[3:4] = feed_sums[0:1]
    vec[4:5] = sums[2] / scale_out[...]
    vec[5:6] = feed_sums[1:2] / scale_down[...]

    codes = w_out[...].reshape(WIDE, HD)

    def to_owner(u, m, w, start):
        o = unit_owner(m, w)
        src = datt.at[w, m]

        @pl.when(o != me)
        def _():
            copy = remote(src, rdo.at[me], send.at[u], recv.at[me], o, t)
            copy.start() if start else copy.wait_send()

        @pl.when(o == me)
        def _():
            copy = pltpu.make_async_copy(src, rdo.at[me], local.at[0])
            copy.start() if start else copy.wait()

    for w in range(3):
        rows.forward(w)
    for w in range(3):
        rows.end(w)
        scaled = (d_branch[w].reshape(ROWS, WIDE).astype(F32) * scale_out[...]).astype(B16)
        datt[w] = dot(scaled, level(codes, w), 1, 0).astype(B16).reshape(2, 64, HD)
        for m in range(2):
            to_owner(m * 3 + w, m, w, True)
    for u, (m, w) in enumerate(units):
        to_owner(u, m, w, False)

    @pl.when(owner)
    def _():
        def each(d, _):
            @pl.when(d != me)
            def _():
                remote(rdo.at[d], rdo.at[d], send.at[0], recv.at[d], me, other).wait_recv()

            return 0

        lax.fori_loop(0, 16, each, 0)
        acc_k[...] = jnp.zeros_like(acc_k)
        acc_v[...] = jnp.zeros_like(acc_v)
        for b in range(4):
            rows_b = slice(16 * b, 16 * b + 16)
            blocks = list(range(max(0, b - 2), b + 1))
            queries = q_rot[b]
            keys = {kb: k_rot[kb] for kb in blocks}
            upstream = rdo[:, rows_b, :].reshape(256, HD)
            bents, probs = block_probs(queries, keys, first[b], b)
            d_probs = [dot(upstream, v_all[kb], 1, 1) for kb in blocks]
            centre = sum(
                jnp.sum(p * dp, axis=-1, keepdims=True) for p, dp in zip(probs, d_probs)
            )
            d_q = jnp.zeros((256, HD), F32)
            for kb, bent, p, dp in zip(blocks, bents, probs, d_probs):
                d_scores = (p * (dp - centre) * (1.0 - bent * bent)).astype(B16)
                d_q = d_q + dot(d_scores, keys[kb], 1, 0)
                acc_k[kb] += dot(d_scores, queries, 0, 0)
                acc_v[kb] += dot(p.astype(B16), upstream, 0, 0)
            d_q = unrotate(d_q * 0.0625, cosine[b], sine[b])
            held_q[:, rows_b, :] = d_q.astype(B16).reshape(16, 16, HD)
        for b in range(4):
            rows_b = slice(16 * b, 16 * b + 16)
            d_k = unrotate(acc_k[b] * 0.0625, cosine[b], sine[b]).astype(B16)
            d_v = acc_v[b].astype(B16)
            for i in range(2):
                cols = slice(128 * i, 128 * i + 128)
                held_kv[i, :, rows_b, :128] = d_k[:, cols].reshape(16, 16, 128)
                held_kv[i, :, rows_b, 128:] = d_v[:, cols].reshape(16, 16, 128)

    def hand_back(d, start):
        u = zh * 3 + y
        across = remote(
            held_kv.at[1 - half, d], d_kv.at[half, y, zh], send_kv.at[1, d], recv_kv.at[half, u], d, other
        )
        across.start() if start else across.wait_send()

        @pl.when(d != me)
        def _():
            for copy in (
                remote(held_q.at[d], d_query.at[y, zh], send_q.at[d], recv_q.at[u], d, t),
                remote(
                    held_kv.at[half, d], d_kv.at[half, y, zh], send_kv.at[0, d], recv_kv.at[half, u], d, t
                ),
            ):
                copy.start() if start else copy.wait_send()

        @pl.when(d == me)
        def _():
            for copy in (
                pltpu.make_async_copy(held_q.at[d], d_query.at[y, zh], local.at[0]),
                pltpu.make_async_copy(held_kv.at[half, d], d_kv.at[half, y, zh], local.at[1]),
            ):
                copy.start() if start else copy.wait()

    @pl.when(owner)
    def _():
        lax.fori_loop(0, 16, lambda d, _: (hand_back(d, True), 0)[1], 0)
        lax.fori_loop(0, 16, lambda d, _: (hand_back(d, False), 0)[1], 0)

    g_up.sent_away()
    g_out.product_whole(d_branch[...].reshape(3 * ROWS, WIDE), attended[...])
    g_down.add()
    g_gate.merge()
    g_gate.pool()
    for u, (m, w) in enumerate(units):

        @pl.when(unit_owner(m, w) != me)
        def _():
            ref = d_query.at[w, m]
            remote(ref, ref, send.at[0], recv_q.at[u], me, other).wait_recv()
            ref = d_kv.at[half, w, m]
            remote(ref, ref, send.at[0], recv_kv.at[half, u], me, other).wait_recv()

        ref = d_kv.at[1 - half, w, m]
        remote(ref, ref, send.at[0], recv_kv.at[1 - half, u], me, other).wait_recv()

    codes = w_qkv[...].reshape(WIDE, 2 * HD)
    d_input = jnp.zeros((ROWS, WIDE), F32)
    qkv_sums = jnp.zeros((1, 2 * HD), F32)
    d_qkv_all = jnp.zeros((ROWS, 2 * HD), F32)
    for w in range(3):
        both = (d_kv[0, w].astype(F32) + d_kv[1, w].astype(F32)).astype(B16).astype(F32)
        d_qkv = jnp.concatenate([d_query[w].astype(F32), both], -1).reshape(ROWS, 2 * HD)
        qkv_sums = qkv_sums + jnp.sum(d_qkv * qkv_pre[w], axis=0, keepdims=True)
        d_qkv_all = d_qkv_all + d_qkv
        scaled = (d_qkv * scale_qkv[...]).astype(B16)
        d_input = d_input + dot(scaled, level(codes, w), 1, 1)
    part_in[0] = d_input.astype(B16).reshape(2, 4, SLICE, WIDE)
    rows_in.scatter_x(0)
    g_down.sent_away()
    g_qkv.product_whole(normed_input[...], d_qkv_all.astype(B16))
    g_out.add()
    g_up.merge()
    g_up.pool()
    rows_in.scatter_z(0)
    g_qkv.add()

    upstream = rows_in.total(0)
    signal_in = tokens[pl.ds(pl.multiple_of(t * SLICE, SLICE), SLICE)].astype(F32)
    inverse = inverse_rms(signal_in)
    normed = signal_in * inverse
    block1[0] = d_middle + norm_back(normed, inverse, gains[0:1], upstream)
    rows_in.spread(0)

    vec[0:1] = jnp.sum(upstream * normed, axis=0, keepdims=True)
    vec[6:8] = jnp.zeros((2, WIDE), F32)
    x = rows.x
    copies = []

    def exchange(slot, src, dst, dp, tensor):
        copy = remote(src, dst, send_v.at[slot], recv_v.at[slot], dp, tensor)
        copy.start()
        copies.append(copy)

    def exchanged(slot, ref):
        remote(ref, ref, send_v.at[slot], recv_v.at[slot], me, other).wait_recv()

    vec_x[x] = vec[...]
    for k in range(3):
        exchange(k, vec_x.at[x], vec_x.at[x], me, rows.x_peers[k])
    g_down.merge()
    g_down.pool()
    g_gate.end()
    for k in range(3):
        exchanged(k, vec_x.at[rows.behind[k]])
    vec[...] = functools.reduce(jnp.add, [vec_x[i] for i in range(4)])
    exchange(3, vec, vec_z, me, rows.z_peer)
    rows_in.forward(0)
    for w in range(3):
        rows_out.spread(w)
    g_out.merge()
    g_out.pool()
    exchanged(3, vec_z)
    copies[3].wait_send()
    vec[0:6] = vec[0:6] + vec_z[0:6]
    vec[6:7] = gu_sums[...]
    vec[7:8, : 2 * HD] = qkv_sums / scale_qkv[...]
    exchange(4, vec, vec_sib, g_gate.sib, t)
    g_qkv.merge()
    g_qkv.pool()
    for w in range(3):
        rows_out.forward(w)
    exchanged(4, vec_sib)
    vec_y[y] = vec[...] + vec_sib[...]
    for i in range(3):
        exchange(5 + i, vec_y.at[y], vec_y.at[y], g_gate.fore[i], t)
    g_up.end()
    g_down.end()
    for i in range(3):
        exchanged(5 + i, vec_y.at[lax.rem(y + 3 - i, 4)])
    copies[4].wait_send()
    vec[...] = functools.reduce(jnp.add, [vec_y[i] for i in range(4)])
    exchange(8, vec, vec_zz, g_gate.zz, t)
    g_out.end()
    g_qkv.end()
    exchanged(8, vec_zz)
    totals[...] = vec[...] + vec_zz[...]
    rows_in.end(0)
    for w in range(3):
        rows_out.end(w)
    g_out.sent_away()
    g_qkv.sent_away()
    for k in (0, 1, 2, 5, 6, 7, 8):
        copies[k].wait_send()
    for part_of in (rows, rows_in, rows_out, *reduces):
        part_of.drain()


def back(hbm, vmem):
    def vec():
        return pltpu.VMEM((8, WIDE), F32)

    scratch = [pltpu.VMEM((8, SHARD, 1152), B16)] * 2
    for columns in GRADIENTS:
        scratch += reduce_scratch(columns)
    scratch += [
        pltpu.VMEM((3, 2, SLICE, WIDE), B16),
        pltpu.VMEM((3, SLICE, WIDE), B16),
        pltpu.VMEM((3, 2, 4, SLICE, WIDE), B16),
    ]
    scratch += rows_scratch(3)
    scratch += [pltpu.VMEM((1, 2, 4, SLICE, WIDE), B16)] + rows_scratch(1)
    scratch += rows_scratch(3)[4:] + [pltpu.VMEM((1, SLICE, WIDE), F32)]
    scratch += [pltpu.VMEM((4, 8, WIDE), F32), vec(), vec(), pltpu.VMEM((4, 8, WIDE), F32), vec(), vec()]
    scratch += [pltpu.SemaphoreType.DMA((9,))] * 2
    scratch += [
        pltpu.VMEM((3, 2, 64, HD), B16),
        pltpu.VMEM((16, 64, HD), B16),
        pltpu.VMEM((16, 64, HD), B16),
        pltpu.VMEM((2, 16, 64, HD), B16),
        pltpu.VMEM((4, 256, HD), F32),
        pltpu.VMEM((4, 256, HD), F32),
        pltpu.VMEM((3, 2, 64, HD), B16),
        pltpu.VMEM((2, 3, 2, 64, HD), B16),
        pltpu.SemaphoreType.DMA((6,)),
        pltpu.SemaphoreType.DMA((16,)),
        pltpu.SemaphoreType.DMA((16,)),
        pltpu.SemaphoreType.DMA((2, 16)),
        pltpu.SemaphoreType.DMA((6,)),
        pltpu.SemaphoreType.DMA((2, 6)),
        pltpu.SemaphoreType.DMA((2,)),
    ]
    return pl.pallas_call(
        back_kernel,
        name="back",
        out_shape=[
            struct((3, 2, 4, SLICE, WIDE), B16),
            struct((1, 2, 4, SLICE, WIDE), F32),
            struct((8, WIDE), F32),
        ]
        + [struct((SHARD, columns), F32) for columns in GRADIENTS],
        in_specs=any_space(len(hbm)) + vmem_space(len(vmem)),
        out_specs=any_space(2) + vmem_space(6),
        scratch_shapes=scratch,
        compiler_params=params(4),
    )(*hbm, *vmem)


def level(codes, width):
    if width == 0:
        return codes
    stride = (1, 16, 64)[width]
    return jnp.floor(codes * B16(1.0 / stride)) * B16(stride) + B16(stride // 2)


def gelu_parts(value):
    slope = 0.7978845608028654
    inner = jnp.tanh(slope * (value + 0.044715 * value * value * value))
    grown = 0.5 * value * (1.0 + inner)
    rate = 0.5 * (1.0 + inner) + 0.5 * value * (1.0 - inner * inner) * slope * (
        1.0 + 3 * 0.044715 * value * value
    )
    return grown, rate


def body(
    tokens,
    cotangent,
    segments,
    codes_query,
    codes_key,
    codes_value,
    codes_out,
    codes_gate,
    codes_up,
    codes_down,
    query_column_scale,
    key_column_scale,
    value_column_scale,
    output_column_scale,
    gate_column_scale,
    up_column_scale,
    down_column_scale,
    gain_first,
    gain_second,
    gain_third,
    gain_fourth,
):
    widths = range(3)
    z_hi = lax.rem(lax.div(lax.axis_index("dp"), 2), 2)
    tokens = tokens.reshape(ROWS, WIDE)
    cotangent = cotangent.reshape(3, ROWS, WIDE)
    gains = jnp.stack([gain_first, gain_second, gain_third, gain_fourth])
    shards = [
        jnp.concatenate([codes_query, codes_key, codes_value], 1).astype(B16),
        codes_out.astype(B16).T,
        jnp.concatenate([codes_gate, codes_up], 1).astype(B16),
        codes_down.astype(B16).T,
    ]
    scale_qkv = jnp.concatenate([query_column_scale, key_column_scale, value_column_scale])
    scale_gu = jnp.concatenate([gate_column_scale, up_column_scale])

    documents = lax.dynamic_index_in_dim(segments, z_hi, 0, False)
    starts = jnp.sum((documents[None, :] < documents[:, None]).astype(jnp.int32), axis=1)
    place = jnp.arange(1024, dtype=jnp.int32)

    def blocked(rows):
        return rows.reshape(4, 16, 16).transpose(0, 2, 1).reshape(4, 256)

    first = blocked(starts)[:, :, None]
    expo = jnp.arange(HD // 2, dtype=F32) * (2.0 / HD)
    angle = blocked(place - starts).astype(F32)[:, :, None] * jnp.power(ROPE_BASE, -expo)
    cosine, sine = jnp.cos(angle), jnp.sin(angle)

    *weights, normed_middle, attended, normed_input, qkv_pre, q_rot, k_rot, v_all, branch, middle = front(
        shards, tokens, gains, scale_qkv, output_column_scale, first, cosine, sine
    )
    w_qkv, w_out, w_gu, w_down = (gathered.reshape(WIDE, -1) for gathered in weights)
    attended = attended.reshape(3, ROWS, HD)
    normed_middle = normed_middle.reshape(3, ROWS, WIDE)
    gu_pre = jnp.stack([dot(normed_middle[w], level(w_gu, w), 1, 0) * scale_gu for w in widths])
    half = gu_pre.shape[-1] // 2
    gate_pre, up_pre = gu_pre[..., :half], gu_pre[..., half:]
    grown, rate = gelu_parts(gate_pre)
    hidden = (grown * up_pre).astype(B16)
    feed_part = jnp.stack(
        [dot(hidden[w], level(w_down, w), 1, 1) * down_column_scale for w in widths]
    ).astype(B16)
    d_feed, final, feed_sums = tensor_call(
        feed_kernel,
        "feed",
        6,
        3,
        3,
        (feed_part, cotangent, middle, gains),
        any_space(2) + vmem_space(2),
        [struct((3, ROWS, WIDE), B16), struct((3, SLICE, WIDE), B16), struct((8, WIDE), F32)],
        any_space(1) + vmem_space(2),
        [pltpu.VMEM((3, SLICE, WIDE), B16)],
    )

    d_feed_scaled = (d_feed.astype(F32) * down_column_scale).astype(B16)
    d_hidden = jnp.stack([dot(d_feed_scaled[w], level(w_down, w), 1, 0) for w in widths])
    d_gu = jnp.concatenate([d_hidden * up_pre * rate, d_hidden * grown], -1)
    d_gu_low = d_gu.astype(B16)
    gu_sums = jnp.sum(d_gu_low.astype(F32) * gu_pre, axis=(0, 1)) / scale_gu
    d_gu_scaled = (d_gu * scale_gu).astype(B16)
    d_middle_part = jnp.stack([dot(d_gu_scaled[w], level(w_gu, w), 1, 1) for w in widths]).astype(
        B16
    )
    flat = (3 * ROWS, -1)
    grid = (3, 2, 4, SLICE, WIDE)
    results, input_gradient, totals, g_gate, g_up, g_down, g_out, g_qkv = back(
        [d_middle_part.reshape(grid), cotangent.reshape(grid)],
        [
            normed_middle.reshape(flat).T,
            d_feed.reshape(flat).T,
            d_gu_low.reshape(flat),
            hidden.reshape(flat),
            middle,
            branch,
            final,
            feed_sums,
            gu_sums[None],
            weights[1],
            weights[0],
            output_column_scale[None],
            down_column_scale[None],
            scale_qkv[None],
            gains,
            tokens,
            attended.reshape(flat),
            normed_input,
            qkv_pre,
            first,
            cosine,
            sine,
            q_rot,
            k_rot,
            v_all,
        ],
    )
    rows = lax.dynamic_slice_in_dim(totals, lax.axis_index("dp") * SHARD, SHARD, 1)
    return (
        results.reshape(3, 2, 64, 1, WIDE),
        input_gradient.reshape(2, 64, 1, WIDE),
        g_qkv[:, :256],
        g_qkv[:, 256:384],
        g_qkv[:, 384:],
        g_out.T,
        g_gate,
        g_up,
        g_down.T,
        totals[7, :256],
        totals[7, 256:384],
        totals[7, 384:512],
        rows[4],
        totals[6, :half],
        totals[6, half:],
        rows[5],
        rows[0],
        rows[1],
        rows[2],
        rows[3],
    )


def solution(mesh):
    matrix, turned = P("dp", "tensor"), P("tensor", "dp")
    columns, whole, shard = P("tensor"), P(), P("dp")
    in_specs = (
        P(None, None, "dp", None),
        P(None, None, None, "dp", None),
        whole,
        *(matrix, matrix, matrix, turned, matrix, matrix, turned),
        *(columns, columns, columns, whole, columns, columns, whole),
        *(whole, whole, whole, whole),
    )
    out_specs = (
        P(None, None, None, "dp", None),
        P(None, None, "dp", None),
        *(matrix, matrix, matrix, turned, matrix, matrix, turned),
        *(columns, columns, columns, shard, columns, columns, shard),
        *(shard, shard, shard, shard),
    )
    return jax.shard_map(body, mesh=mesh, in_specs=in_specs, out_specs=out_specs, check_vma=False)
```

```python
import functools

import jax
import jax.numpy as jnp
from jax import lax
from jax.experimental import pallas as pl
from jax.experimental.pallas import tpu as pltpu
from jax.sharding import PartitionSpec as P

MESH = pl.DeviceIdType.MESH
F32 = jnp.float32
B16 = jnp.bfloat16
EPSILON = 1e-06
SOFTCAP = 50.0
ROPE_BASE = 10000.0
MASKED = -1e30
HD = 256
WIDE = 2304
FF = 1152
STRIDES = (1, 16, 64)
SHARD = 144
LOW = 64
HIGH = SHARD - LOW
TENSOR = 8
ROWS = 128
SLICE = ROWS // TENSOR
VMEM_BYTES = 63 * 2**20


def here():
    dp = lax.axis_index("dp")
    return lax.div(dp, 4), lax.rem(lax.div(dp, 2), 2), lax.rem(dp, 2), lax.axis_index("tensor")


def rank(y, z_hi, core):
    return (y * 2 + z_hi) * 2 + core


def remote(src, dst, send, recv, dp, tensor):
    return pltpu.make_async_remote_copy(
        src, dst, send, recv, device_id=(dp, tensor), device_id_type=MESH
    )


def greet(devices):
    barrier = pltpu.get_barrier_semaphore()
    for device in devices:
        pl.semaphore_signal(barrier, inc=1, device_id=device, device_id_type=MESH)
    pl.semaphore_wait(barrier, len(devices))


def struct(shape, dtype):
    return jax.ShapeDtypeStruct(shape, dtype)


def any_space(count):
    return [pl.BlockSpec(memory_space=pl.ANY)] * count


def vmem_space(count):
    return [pl.BlockSpec(memory_space=pltpu.VMEM)] * count


def params(collective_id):
    return pltpu.CompilerParams(
        collective_id=collective_id, has_side_effects=True, vmem_limit_bytes=VMEM_BYTES
    )


class Gather:
    def __init__(self, src, out, send, recv, local):
        self.src, self.out, self.send, self.recv, self.local = src, out, send, recv, local
        self.y, self.zh, self.core, self.t = here()
        y, zh, core = self.y, self.zh, self.core
        self.me, self.sib, self.zz = rank(y, zh, core), rank(y, zh, 1 - core), rank(y, 1 - zh, core)
        self.fore = [rank(lax.rem(y + dy, 4), zh, core) for dy in (1, 2, 3)]
        self.behind = [lax.rem(y + 4 - dy, 4) for dy in (1, 2, 3)]
        self.low, self.high = pl.ds(0, LOW), pl.ds(LOW, HIGH)
        self.started = []

    def push(self, slot, src, dst, dp):
        copy = remote(src, dst, self.send.at[slot], self.recv.at[slot], dp, self.t)
        copy.start()
        self.started.append(copy)

    def arrive(self, slot, ref):
        remote(ref, ref, self.send.at[slot], self.recv.at[slot], self.sib, self.t).wait_recv()

    def start(self):
        src, mine = self.src, self.out.at[self.me]
        self.mine = pltpu.make_async_copy(src, mine, self.local)
        self.mine.start()
        low, high = self.low, self.high
        self.push(0, src.at[low], self.out.at[self.me, low], self.zz)
        for i in range(3):
            self.push(4 + i, src.at[high], self.out.at[self.me, high], self.fore[i])
        for i in range(3):
            self.push(1 + i, src.at[low], self.out.at[self.me, low], self.fore[i])
        self.push(7, src.at[high], self.out.at[self.me, high], self.zz)
        self.push(14, src, mine, self.sib)

    def over_y(self):
        block = self.out.at[self.zz, self.low]
        self.arrive(0, block)
        for i in range(3):
            self.push(8 + i, block, block, self.fore[i])
        self.push(15, block, block, self.sib)

    def over_z(self):
        for i in range(3):
            block = self.out.at[rank(self.behind[i], self.zh, self.core), self.high]
            self.arrive(4 + i, block)
            self.push(11 + i, block, block, self.zz)
            self.push(16 + i, block, block, self.sib)

    def near(self):
        for i in range(3):
            block = self.out.at[rank(self.behind[i], self.zh, self.core), self.low]
            self.arrive(1 + i, block)
            self.push(19 + i, block, block, self.sib)
        block = self.out.at[self.zz, self.high]
        self.arrive(7, block)
        self.push(22, block, block, self.sib)

    def far(self):
        for i in range(3):
            dp = rank(self.behind[i], 1 - self.zh, self.core)
            for slot, rows in ((0, self.low), (3, self.high)):
                block = self.out.at[dp, rows]
                self.arrive(8 + slot + i, block)
                self.push(23 + slot + i, block, block, self.sib)

    def end(self):
        out, low, high, other = self.out, self.low, self.high, 1 - self.core
        self.arrive(14, out.at[self.sib])
        far = rank(self.y, 1 - self.zh, other)
        self.arrive(15, out.at[far, low])
        self.arrive(22, out.at[far, high])
        for i in range(3):
            near, far = (rank(self.behind[i], zh, other) for zh in (self.zh, 1 - self.zh))
            self.arrive(16 + i, out.at[near, high])
            self.arrive(19 + i, out.at[near, low])
            self.arrive(23 + i, out.at[far, low])
            self.arrive(26 + i, out.at[far, high])
        self.mine.wait()

    def drain(self):
        for copy in self.started:
            copy.wait_send()


class Rows:
    def __init__(self, part, held_x, held_z, stage, block, out, sems, own=None):
        self.own = own
        self.part, self.held_x, self.held_z, self.stage = part, held_x, held_z, stage
        self.block, self.out = block, out
        self.send, self.recv, self.local = sems
        self.dp, self.t = lax.axis_index("dp"), lax.axis_index("tensor")
        self.zl, self.x = lax.div(self.t, 4), lax.rem(self.t, 4)
        self.ahead = [lax.rem(self.x + k, 4) for k in (1, 2, 3)]
        self.behind = [lax.rem(self.x + 4 - k, 4) for k in (1, 2, 3)]
        self.x_peers = [self.zl * 4 + x for x in self.ahead]
        self.z_peer = (1 - self.zl) * 4 + self.x
        self.started = []

    def peers(self):
        return [(self.dp, t) for t in self.x_peers + [self.z_peer]]

    def push(self, w, slot, src, dst, t):
        copy = remote(src, dst, self.send.at[w, slot], self.recv.at[w, slot], self.dp, t)
        copy.start()
        self.started.append(copy)

    def arrive(self, w, slot, ref):
        remote(
            ref, ref, self.send.at[w, slot], self.recv.at[w, slot], self.dp, self.z_peer
        ).wait_recv()

    def scatter_x(self, w):
        for k in range(3):
            self.push(w, 1 + k, self.part.at[w, :, self.ahead[k]], self.held_x.at[w, k], self.x_peers[k])

    def summed_x(self, w, zl):
        total = (self.part[w, zl, self.x] if self.own is None else self.own[w, zl]).astype(F32)
        for k in range(3):
            total = total + self.held_x[w, k, zl].astype(F32)
        return total

    def scatter_z(self, w):
        for k in range(3):
            self.arrive(w, 1 + k, self.held_x.at[w, k])
        self.stage[w] = self.summed_x(w, 1 - self.zl).astype(B16)
        self.push(w, 0, self.stage.at[w], self.held_z.at[w], self.z_peer)

    def total(self, w):
        self.arrive(w, 0, self.held_z.at[w])
        return self.summed_x(w, self.zl) + self.held_z[w].astype(F32)

    def spread(self, w):
        block, mine = self.block.at[w], self.out.at[w, self.zl, self.x]
        self.push(w, 4, block, mine, self.z_peer)
        for k in range(3):
            self.push(w, 5 + k, block, mine, self.x_peers[k])
        pltpu.make_async_copy(block, mine, self.local.at[w]).start()

    def forward(self, w):
        block = self.out.at[w, 1 - self.zl, self.x]
        self.arrive(w, 4, block)
        for k in range(3):
            self.push(w, 8 + k, block, block, self.x_peers[k])

    def end(self, w):
        for k in range(3):
            self.arrive(w, 5 + k, self.out.at[w, self.zl, self.behind[k]])
            self.arrive(w, 8 + k, self.out.at[w, 1 - self.zl, self.behind[k]])
        pltpu.make_async_copy(
            self.block.at[w], self.out.at[w, self.zl, self.x], self.local.at[w]
        ).wait()

    def drain(self):
        for copy in self.started:
            copy.wait_send()


def rows_scratch(depth):
    return [
        pltpu.VMEM((depth, 3, 2, SLICE, WIDE), B16),
        pltpu.VMEM((depth, SLICE, WIDE), B16),
        pltpu.VMEM((depth, SLICE, WIDE), B16),
        pltpu.VMEM((depth, SLICE, WIDE), B16),
        pltpu.SemaphoreType.DMA((depth, 11)),
        pltpu.SemaphoreType.DMA((depth, 11)),
        pltpu.SemaphoreType.DMA((depth,)),
    ]


class Reduce:
    def __init__(self, columns, away, own, sibs, yrecv, zrecv, ylast, zlast, out, send, recv):
        self.columns, self.away, self.own, self.sibs = columns, away, own, sibs
        self.yrecv, self.zrecv, self.ylast, self.zlast, self.out = yrecv, zrecv, ylast, zlast, out
        self.send, self.recv = send, recv
        self.y, self.zh, self.core, self.t = here()
        y, zh, core = self.y, self.zh, self.core
        self.sib, self.zz = rank(y, zh, 1 - core), rank(y, 1 - zh, core)
        self.ahead = [lax.rem(y + dy, 4) for dy in (1, 2, 3)]
        self.fore = [rank(place, zh, core) for place in self.ahead]
        self.started = []

    def push(self, slot, src, dst, dp):
        copy = remote(src, dst, self.send.at[slot], self.recv.at[slot], dp, self.t)
        copy.start()
        self.started.append(copy)

    def arrive(self, slot, ref):
        remote(ref, ref, self.send.at[slot], self.recv.at[slot], self.sib, self.t).wait_recv()

    def store(self, first, count, cols, block):
        block = block.astype(B16).reshape(count, 2, SHARD, block.shape[-1])
        even = self.core == 0
        chips = pl.ds(first, count)
        self.own[chips, :, cols] = jnp.where(even, block[:, 0], block[:, 1])
        self.away[chips, :, cols] = jnp.where(even, block[:, 1], block[:, 0])

    def to_sibling(self, place):
        pair = pl.ds(place * 2, 2)
        return remote(
            self.away.at[pair, :, pl.ds(0, self.columns)],
            self.sibs.at[pair],
            self.send.at[place],
            self.recv.at[place],
            self.sib,
            self.t,
        )

    def product(self, turned, right, left_columns=0):
        def step(place, _):
            rows = pl.ds(pl.multiple_of(place * 4 * SHARD, 16), 4 * SHARD)
            for i in range(self.columns // 384):
                block = dot(turned[rows], right[:, left_columns + 384 * i : left_columns + 384 * (i + 1)], 1, 0)
                self.store(place * 2, 2, slice(384 * i, 384 * (i + 1)), block)
            self.to_sibling(place).start()
            return 0

        lax.fori_loop(0, 4, step, 0)

    def product_whole(self, left, right):
        for i in range(self.columns // HD):
            cols = slice(HD * i, HD * i + HD)
            self.store(0, 8, cols, dot(left, right[:, cols], 0, 0))
        for place in range(4):
            self.to_sibling(place).start()

    def sent_away(self):
        for place in range(4):
            self.to_sibling(place).wait_send()

    def add(self):
        own, sibs = self.own, self.sibs
        for i, place in enumerate(self.ahead + [self.y]):
            pair = pl.ds(place * 2, 2)
            self.arrive(place, sibs.at[pair])

            def step(step, _, place=place):
                chip = place * 2 + lax.div(step, SHARD // 16)
                rows = pl.ds(pl.multiple_of(lax.rem(step, SHARD // 16) * 16, 16), 16)
                own[chip, rows] = (
                    own[chip, rows].astype(F32) + sibs[chip, rows].astype(F32)
                ).astype(B16)
                return 0

            lax.fori_loop(0, 2 * SHARD // 16, step, 0)
            self.push(
                7 + i, own.at[place * 2 + 1 - self.zh, pl.ds(LOW, HIGH)], self.zrecv.at[place], self.zz
            )
            if i < 3:
                self.push(4 + i, own.at[pair, pl.ds(0, LOW)], self.yrecv.at[i], self.fore[i])

    def merge(self):
        own, zrecv = self.own, self.zrecv
        for i, place in enumerate(self.ahead + [self.y]):
            self.arrive(7 + i, zrecv.at[place])

            def step(step, _, place=place):
                rows = pl.ds(pl.multiple_of(step * 16, 16), 16)
                mine = pl.ds(pl.multiple_of(step * 16 + LOW, 16), 16)
                zrecv[place, rows] = (
                    zrecv[place, rows].astype(F32) + own[place * 2 + self.zh, mine].astype(F32)
                ).astype(B16)
                return 0

            lax.fori_loop(0, HIGH // 16, step, 0)
            if i < 3:
                self.push(11 + i, zrecv.at[place], self.ylast.at[i], self.fore[i])

    def pool(self):
        for i in range(3):
            self.arrive(4 + i, self.yrecv.at[i])

        def step(step, _):
            chip = lax.div(step, LOW // 16)
            rows = pl.ds(pl.multiple_of(lax.rem(step, LOW // 16) * 16, 16), 16)
            total = self.own[self.y * 2 + chip, rows].astype(F32)
            for i in range(3):
                total = total + self.yrecv[i, chip, rows].astype(F32)
            self.own[self.y * 2 + chip, rows] = total.astype(B16)
            return 0

        lax.fori_loop(0, 2 * LOW // 16, step, 0)
        self.push(14, self.own.at[self.y * 2 + 1 - self.zh, pl.ds(0, LOW)], self.zlast, self.zz)

    def end(self):
        self.arrive(14, self.zlast)

        def low(step, _):
            rows = pl.ds(pl.multiple_of(step * 16, 16), 16)
            self.out[rows] = self.own[self.y * 2 + self.zh, rows].astype(F32) + self.zlast[
                rows
            ].astype(F32)
            return 0

        lax.fori_loop(0, LOW // 16, low, 0)
        for i in range(3):
            self.arrive(11 + i, self.ylast.at[i])

        def high(step, _):
            rows = pl.ds(pl.multiple_of(step * 16, 16), 16)
            total = self.zrecv[self.y, rows].astype(F32)
            for i in range(3):
                total = total + self.ylast[i, rows].astype(F32)
            self.out[pl.ds(pl.multiple_of(step * 16 + LOW, 16), 16)] = total
            return 0

        lax.fori_loop(0, HIGH // 16, high, 0)

    def drain(self):
        for copy in self.started:
            copy.wait_send()


def reduce_scratch(columns):
    return [
        pltpu.VMEM((8, SHARD, columns), B16),
        pltpu.VMEM((8, SHARD, columns), B16),
        pltpu.VMEM((3, 2, LOW, columns), B16),
        pltpu.VMEM((4, HIGH, columns), B16),
        pltpu.VMEM((3, HIGH, columns), B16),
        pltpu.VMEM((LOW, columns), B16),
        pltpu.SemaphoreType.DMA((15,)),
        pltpu.SemaphoreType.DMA((15,)),
    ]


def inverse_rms(signal):
    return lax.rsqrt(jnp.mean(signal * signal, axis=-1, keepdims=True) + EPSILON)


def norm_back(normed, inverse, gain, upstream):
    inner = upstream * (1.0 + gain)
    return inverse * (inner - normed * jnp.mean(inner * normed, axis=-1, keepdims=True))


def half_level(codes, width):
    return codes if width == 0 else jnp.floor(codes * B16(1.0 / STRIDES[width]))


def offset(left, width):
    return 0.0 if width == 0 else 0.5 * jnp.sum(left.astype(F32), axis=-1, keepdims=True)


def feed_kernel(
    normed_middle, w_gu, w_down, cotangent, scale_gu, scale_down, middle, gains,
    d_part, turned_middle, turned_feed, d_gu_low, hidden, final, sums, gu_sums,
    nm, wg, wd, gu_pre, part, cot, d_feed, dgs, held_x, held_z, stage, block, *sems,
):
    rows = Rows(part, held_x, held_z, stage, block, d_feed, sems[:3])
    local_g, local_d, local = sems[3:]
    greet(rows.peers())
    loads = [
        pltpu.make_async_copy(normed_middle.at[w], nm.at[w], local.at[w]) for w in range(3)
    ] + [pltpu.make_async_copy(cotangent.at[:, rows.zl, rows.x], cot, local.at[3])]
    for copy in loads:
        copy.start()

    def load_g(j):
        cols = pl.ds(pl.multiple_of(j * 256, 256), 256)
        return pltpu.make_async_copy(w_gu.at[:, cols], wg.at[:, cols], local_g.at[j])

    def load_d(j):
        tile = pl.ds(pl.multiple_of(j * 256, 256), 256)
        return pltpu.make_async_copy(w_down.at[tile], wd.at[tile], local_d.at[j])

    for j in range(9):
        load_g(j).start()
    for j in range(9):
        load_d(j).start()

    def forward(w):
        if w == 0:
            for copy in loads:
                copy.wait()
        stride = STRIDES[w]
        left = nm[w].reshape(ROWS, WIDE)
        extra = offset(left, w)

        def gate_up(j, _):
            cols = pl.ds(pl.multiple_of(j * 256, 256), 256)
            if w == 0:
                load_g(j).wait()
            product = dot(left, half_level(wg[:, cols], w), 1, 0)
            gu_pre[w, :, cols] = (product + extra) * (scale_gu[:, cols] * stride)
            return 0

        lax.fori_loop(0, 9, gate_up, 0)
        gate_pre, up_pre = gu_pre[w, :, :FF], gu_pre[w, :, FF:]
        grown, _ = gelu_parts(gate_pre)
        low = (grown * up_pre).astype(B16)
        hidden[w] = low
        extra_down = offset(low, w)

        def down(j, _):
            tile = pl.ds(pl.multiple_of(j * 256, 256), 256)
            if w == 0:
                load_d(j).wait()
            product = dot(low, half_level(wd[tile], w), 1, 1)
            product = (product + extra_down) * (scale_down[:, tile] * stride)
            part[w, :, :, :, tile] = product.astype(B16).reshape(2, 4, SLICE, 256)
            return 0

        lax.fori_loop(0, 9, down, 0)
        rows.scatter_x(w)

    def norm(w):
        signal = rows.total(w)
        inverse = inverse_rms(signal)
        normed = signal * inverse
        upstream = cot[w].astype(F32)
        lowered = norm_back(normed, inverse, gains[3:4], upstream).astype(B16)
        block[w] = lowered
        rows.spread(w)
        final[w] = (middle[w] + normed * (1.0 + gains[3:4])).astype(B16)
        for i, term in enumerate((upstream * normed, lowered.astype(F32) * signal)):
            term = jnp.sum(term, axis=0, keepdims=True)
            sums[i : i + 1] = term if w == 0 else sums[i : i + 1] + term

    def backward(w):
        stride = STRIDES[w]
        lowered = d_feed[w].reshape(ROWS, WIDE)
        turned_feed[:, w * ROWS : (w + 1) * ROWS] = lowered.T
        scaled = (lowered.astype(F32) * scale_down[...]).astype(B16)
        extra = offset(scaled, w)
        for i in range(3):
            cols = slice(384 * i, 384 * i + 384)
            ups = slice(FF + 384 * i, FF + 384 * i + 384)
            d_hidden = (dot(scaled, half_level(wd[:, cols], w), 1, 0) + extra) * float(stride)
            grown, rate = gelu_parts(gu_pre[w, :, cols])
            for where, value in ((cols, d_hidden * gu_pre[w, :, ups] * rate), (ups, d_hidden * grown)):
                low = value.astype(B16)
                d_gu_low[w, :, where] = low
                dgs[:, where] = (value * scale_gu[:, where]).astype(B16)
                term = jnp.sum(low.astype(F32) * gu_pre[w, :, where], axis=0, keepdims=True)
                term = term / scale_gu[:, where]
                gu_sums[:, where] = term if w == 0 else gu_sums[:, where] + term
        left = dgs[...]
        extra_gu = offset(left, w)

        def gate_up(j, _):
            tile = pl.ds(pl.multiple_of(j * 256, 256), 256)
            product = dot(left, half_level(wg[tile], w), 1, 1)
            product = (product + extra_gu) * float(stride)
            d_part[w, :, :, :, tile] = product.astype(B16).reshape(2, 4, SLICE, 256)
            return 0

        lax.fori_loop(0, 9, gate_up, 0)

    forward(0)
    forward(1)
    rows.scatter_z(0)
    forward(2)
    rows.scatter_z(1)
    norm(0)
    rows.scatter_z(2)
    norm(1)
    rows.forward(0)
    norm(2)
    rows.forward(1)
    for w in range(3):
        turned_middle[:, w * ROWS : (w + 1) * ROWS] = nm[w].reshape(ROWS, WIDE).T
    rows.end(0)
    backward(0)
    rows.forward(2)
    rows.end(1)
    backward(1)
    rows.end(2)
    backward(2)
    rows.drain()


def feed(hbm, vmem):
    return pl.pallas_call(
        feed_kernel,
        name="feed",
        out_shape=[
            struct((3, 2, 4, SLICE, WIDE), B16),
            struct((WIDE, 3 * ROWS), B16),
            struct((WIDE, 3 * ROWS), B16),
            struct((3, ROWS, 2 * FF), B16),
            struct((3, ROWS, FF), B16),
            struct((3, SLICE, WIDE), B16),
            struct((8, WIDE), F32),
            struct((1, 2 * FF), F32),
        ],
        in_specs=any_space(len(hbm)) + vmem_space(len(vmem)),
        out_specs=vmem_space(8),
        scratch_shapes=[
            pltpu.VMEM((3, 2, 4, SLICE, WIDE), B16),
            pltpu.VMEM((WIDE, 2 * FF), B16),
            pltpu.VMEM((WIDE, FF), B16),
            pltpu.VMEM((3, ROWS, 2 * FF), F32),
            pltpu.VMEM((3, 2, 4, SLICE, WIDE), B16),
            pltpu.VMEM((3, SLICE, WIDE), B16),
            pltpu.VMEM((3, 2, 4, SLICE, WIDE), B16),
            pltpu.VMEM((ROWS, 2 * FF), B16),
        ]
        + rows_scratch(3)
        + [
            pltpu.SemaphoreType.DMA((9,)),
            pltpu.SemaphoreType.DMA((9,)),
            pltpu.SemaphoreType.DMA((4,)),
        ],
        compiler_params=params(6),
    )(*hbm, *vmem)


def unit_owner(micro, width):
    return rank(width, micro, 0)


def rotate(signal, cosine, sine):
    former, latter = signal[:, : HD // 2], signal[:, HD // 2 :]
    return jnp.concatenate([former * cosine - latter * sine, latter * cosine + former * sine], -1)


def unrotate(signal, cosine, sine):
    former, latter = signal[:, : HD // 2], signal[:, HD // 2 :]
    return jnp.concatenate([former * cosine + latter * sine, latter * cosine - former * sine], -1)


def block_scores(queries, keys, first, b, kb):
    scores = lax.dot_general(queries, keys, (((1,), (1,)), ((), ())), preferred_element_type=F32)
    bent = jnp.tanh(scores * (0.0625 / SOFTCAP))
    lane = lax.broadcasted_iota(jnp.int32, (256, 256), 1)
    row = lax.broadcasted_iota(jnp.int32, (256, 256), 0)
    key_place = (16 * kb + (lane & 15)) * 16 + (lane >> 4)
    query_place = (16 * b + (row & 15)) * 16 + (row >> 4)
    allowed = (key_place >= first) & (key_place <= query_place)
    return bent, jnp.where(allowed, SOFTCAP * bent, MASKED)


def block_probs(queries, keys, first, b):
    pieces = [
        block_scores(queries, keys[kb], first, b, kb) for kb in range(max(0, b - 2), b + 1)
    ]
    peak = functools.reduce(
        jnp.maximum, [jnp.max(capped, axis=-1, keepdims=True) for _, capped in pieces]
    )
    exps = [jnp.exp(capped - peak) for _, capped in pieces]
    total = functools.reduce(jnp.add, [jnp.sum(e, axis=-1, keepdims=True) for e in exps])
    return [bent for bent, _ in pieces], [e / total for e in exps]


def dot(left, right, left_dim, right_dim):
    return lax.dot_general(
        left, right, (((left_dim,), (right_dim,)), ((), ())), preferred_element_type=F32
    )


def front_kernel(*refs):
    shards, refs = refs[:4], refs[4:]
    (tokens, gains, scale_qkv, scale_out, first, cosine, sine), refs = refs[:7], refs[7:]
    (w_qkv, w_out, w_gu, w_down, normed_middle), refs = refs[:5], refs[5:]
    (attended, normed_input, qkv_pre, q_rot, k_rot, v_all, branch, middle), refs = refs[:8], refs[8:]
    (wq, wo, low, rq, rkv, held, att, part), refs = refs[:8], refs[8:]
    (held_x, held_z, stage, block, *row_sems), refs = refs[:7], refs[7:]
    (send_g, recv_g, local_g, send, recv_q, recv_kv, send_back, recv_back, local) = refs
    y, zh, core, t = here()
    me = rank(y, zh, core)
    half = lax.rem(t, 2)
    other = t + 1 - 2 * half
    owner = (y < 3) & (core == 0)
    units = [(m, w) for m in range(2) for w in range(3)]
    gathers = [
        Gather(src, out, send_g.at[k], recv_g.at[k], local_g.at[k])
        for k, (src, out) in enumerate(zip(shards, (wq, wo, w_gu, w_down)))
    ]
    g_qkv, g_out, g_gu, g_down = gathers
    rows = Rows(part, held_x, held_z, stage, block, normed_middle, row_sems)
    barrier = pltpu.get_barrier_semaphore()

    def signal(dp, tensor):
        pl.semaphore_signal(barrier, inc=1, device_id=(dp, tensor), device_id_type=MESH)

    plane = [(g_qkv.sib, t), (g_qkv.zz, t)] + [(dp, t) for dp in g_qkv.fore] + rows.peers()
    for device in plane:
        signal(*device)

    @pl.when(owner)
    def _():
        def each(d, _):
            pl.when(d != me)(lambda: signal(d, t))
            signal(d, other)
            return 0

        lax.fori_loop(0, 16, each, 0)

    for m, w in units:
        pl.when(unit_owner(m, w) != me)(functools.partial(signal, unit_owner(m, w), t))

    @pl.when(owner)
    def _():
        pl.semaphore_wait(barrier, len(plane) + 26)

    @pl.when(jnp.logical_not(owner))
    def _():
        pl.semaphore_wait(barrier, len(plane) + 12)

    g_qkv.start()
    g_out.start()
    inputs = tokens[...].astype(F32)
    normed_input[...] = (inputs * inverse_rms(inputs) * (1.0 + gains[0:1])).astype(B16)
    for gather in (g_qkv, g_out):
        gather.over_y()
        gather.over_z()
    for gather in (g_qkv, g_out):
        gather.near()
        gather.far()
    g_qkv.end()

    for i in range(2):
        cols = slice(HD * i, HD * i + HD)
        codes = wq[:, :, cols].reshape(WIDE, HD)
        for w in range(3):
            product = dot(normed_input[...], level(codes, w), 1, 0) * scale_qkv[:, cols]
            qkv_pre[w, :, cols] = product
            low[w, :, :, cols] = product.astype(B16).reshape(2, 64, HD)

    def to_owner(u, m, w, start):
        o = unit_owner(m, w)
        q_src, kv_src = low.at[w, m, :, pl.ds(0, HD)], low.at[w, m, :, pl.ds(HD, HD)]
        across = remote(kv_src, rkv.at[half, me], send.at[u, 2], recv_kv.at[half, me], o, other)
        away = [
            remote(q_src, rq.at[me], send.at[u, 0], recv_q.at[me], o, t),
            remote(kv_src, rkv.at[half, me], send.at[u, 1], recv_kv.at[half, me], o, t),
        ]
        near = [
            pltpu.make_async_copy(q_src, rq.at[me], local.at[0]),
            pltpu.make_async_copy(kv_src, rkv.at[half, me], local.at[1]),
        ]

        @pl.when(o != me)
        def _():
            for copy in away:
                copy.start() if start else copy.wait_send()

        @pl.when(o == me)
        def _():
            for copy in near:
                copy.start() if start else copy.wait()

        across.start() if start else across.wait_send()

    for u, (m, w) in enumerate(units):
        to_owner(u, m, w, True)

    @pl.when(owner)
    def _():
        for u, (m, w) in enumerate(units):

            @pl.when(unit_owner(m, w) == me)
            def _():
                for i in range(2):
                    ref = (rq.at[me], rkv.at[half, me])[i]
                    pltpu.make_async_copy(ref, ref, local.at[i]).wait()

        def each(d, _):
            @pl.when(d != me)
            def _():
                remote(rq.at[d], rq.at[d], send.at[0, 0], recv_q.at[d], me, other).wait_recv()
                remote(
                    rkv.at[half, d], rkv.at[half, d], send.at[0, 0], recv_kv.at[half, d], me, other
                ).wait_recv()

            remote(
                rkv.at[1 - half, d], rkv.at[1 - half, d], send.at[0, 0], recv_kv.at[1 - half, d], me, other
            ).wait_recv()
            return 0

        lax.fori_loop(0, 16, each, 0)
        for b in range(4):
            rows_b = slice(16 * b, 16 * b + 16)
            c, s = cosine[b], sine[b]
            q = rq[:, rows_b, :].reshape(256, HD).astype(F32)
            q_rot[b] = rotate(q, c, s).astype(B16)
            k = jnp.concatenate(
                [rkv[i, :, rows_b, : HD // 2].reshape(256, HD // 2) for i in range(2)], -1
            )
            k_rot[b] = rotate(k.astype(F32), c, s).astype(B16)
            v_all[b] = jnp.concatenate(
                [rkv[i, :, rows_b, HD // 2 :].reshape(256, HD // 2) for i in range(2)], -1
            )
        for b in range(4):
            keys = {kb: k_rot[kb] for kb in range(max(0, b - 2), b + 1)}
            _, probs = block_probs(q_rot[b], keys, first[b], b)
            out = sum(
                dot(p.astype(B16), v_all[kb], 1, 0) for p, kb in zip(probs, sorted(keys))
            )
            held[:, 16 * b : 16 * b + 16, :] = out.astype(B16).reshape(16, 16, HD)

        def hand_back(d, start):
            @pl.when(d != me)
            def _():
                copy = remote(
                    held.at[d], att.at[y, zh], send_back.at[d], recv_back.at[zh * 3 + y], d, t
                )
                copy.start() if start else copy.wait_send()

            @pl.when(d == me)
            def _():
                copy = pltpu.make_async_copy(held.at[d], att.at[y, zh], local.at[0])
                copy.start() if start else copy.wait()

        lax.fori_loop(0, 16, lambda d, _: (hand_back(d, True), 0)[1], 0)
        lax.fori_loop(0, 16, lambda d, _: (hand_back(d, False), 0)[1], 0)

    g_gu.start()
    g_down.start()
    g_out.end()
    for u, (m, w) in enumerate(units):

        @pl.when(unit_owner(m, w) != me)
        def _():
            ref = att.at[w, m]
            remote(ref, ref, send.at[0, 0], recv_back.at[u], me, other).wait_recv()

    codes = wo[...].reshape(WIDE, HD)
    for w in range(3):
        product = dot(att[w].reshape(ROWS, HD), level(codes, w), 1, 1) * scale_out[...]
        part[w] = product.astype(B16).reshape(2, 4, SLICE, WIDE)
        rows.scatter_x(w)
    attended[...] = att[...]
    keep = [
        pltpu.make_async_copy(src, dst, local.at[i])
        for i, (src, dst) in enumerate(((wq, w_qkv), (wo, w_out)))
    ]
    for copy in keep:
        copy.start()
    g_gu.over_y()
    g_down.over_y()
    g_gu.over_z()
    g_down.over_z()
    for w in range(3):
        rows.scatter_z(w)
    mine = tokens[pl.ds(pl.multiple_of(t * SLICE, SLICE), SLICE)].astype(F32)
    for w in range(3):
        signal_w = rows.total(w)
        branch[w] = signal_w
        total = mine + signal_w * inverse_rms(signal_w) * (1.0 + gains[1:2])
        middle[w] = total
        block[w] = (total * inverse_rms(total) * (1.0 + gains[2:3])).astype(B16)
        rows.spread(w)
    for gather in (g_gu, g_down):
        gather.near()
    for w in range(3):
        rows.forward(w)
    for gather in (g_gu, g_down):
        gather.far()
    for w in range(3):
        rows.end(w)
    for gather in (g_gu, g_down):
        gather.end()
    for copy in keep:
        copy.wait()
    for u, (m, w) in enumerate(units):
        o = unit_owner(m, w)

        @pl.when(o != me)
        def _():
            for slot, src in enumerate((low.at[w, m, :, pl.ds(0, HD)], low.at[w, m, :, pl.ds(HD, HD)])):
                remote(src, src, send.at[u, slot], recv_q.at[0], o, t).wait_send()

        src = low.at[w, m, :, pl.ds(HD, HD)]
        remote(src, src, send.at[u, 2], recv_q.at[0], o, other).wait_send()
    rows.drain()
    for gather in gathers:
        gather.drain()


def front(shards, tokens, gains, scale_qkv, scale_out, first, cosine, sine):
    return pl.pallas_call(
        front_kernel,
        name="front",
        out_shape=[struct((16,) + shard.shape, B16) for shard in shards]
        + [
            struct((3, 2, 4, SLICE, WIDE), B16),
            struct((3, 2, 64, HD), B16),
            struct((ROWS, WIDE), B16),
            struct((3, ROWS, 2 * HD), F32),
        ]
        + [struct((4, 256, HD), B16)] * 3
        + [struct((3, SLICE, WIDE), F32)] * 2,
        in_specs=any_space(4) + vmem_space(7),
        out_specs=any_space(5) + vmem_space(8),
        scratch_shapes=[
            pltpu.VMEM((16, SHARD, 2 * HD), B16),
            pltpu.VMEM((16, SHARD, HD), B16),
            pltpu.VMEM((3, 2, 64, 2 * HD), B16),
            pltpu.VMEM((16, 64, HD), B16),
            pltpu.VMEM((2, 16, 64, HD), B16),
            pltpu.VMEM((16, 64, HD), B16),
            pltpu.VMEM((3, 2, 64, HD), B16),
            pltpu.VMEM((3, 2, 4, SLICE, WIDE), B16),
        ]
        + rows_scratch(3)
        + [
            pltpu.SemaphoreType.DMA((4, 29)),
            pltpu.SemaphoreType.DMA((4, 29)),
            pltpu.SemaphoreType.DMA((4,)),
            pltpu.SemaphoreType.DMA((6, 3)),
            pltpu.SemaphoreType.DMA((16,)),
            pltpu.SemaphoreType.DMA((2, 16)),
            pltpu.SemaphoreType.DMA((16,)),
            pltpu.SemaphoreType.DMA((6,)),
            pltpu.SemaphoreType.DMA((2,)),
        ],
        compiler_params=params(3),
    )(*shards, tokens, gains, scale_qkv[None], scale_out[None], first, cosine, sine)


GRADIENTS = (1152, 1152, 1152, HD, 2 * HD)


def back_kernel(*refs):
    (part, cotangent), refs = refs[:2], refs[2:]
    (turned_middle, turned_feed, d_gu, hidden, middle, branch, final, feed_sums, gu_sums), refs = refs[:9], refs[9:]
    (w_out, w_qkv, scale_out, scale_down, scale_qkv, gains, tokens, attended, normed_input), refs = refs[:9], refs[9:]
    (qkv_pre, first, cosine, sine, q_rot, k_rot, v_all), refs = refs[:7], refs[7:]
    (results, gradient, totals), refs = refs[:3], refs[3:]
    outs, refs = refs[:5], refs[5:]
    aways, refs = refs[:2], refs[2:]
    reduces = []
    for k, columns in enumerate(GRADIENTS):
        held, refs = refs[:8], refs[8:]
        away = aways[k % 2]
        reduces.append(Reduce(columns, away, *held[:6], outs[k], *held[6:]))
    g_gate, g_up, g_down, g_out, g_qkv = reduces
    (own_part, cot, d_branch), refs = refs[:3], refs[3:]
    (held_x, held_z, stage, block, *row_sems), refs = refs[:7], refs[7:]
    (part_in, held_x1, held_z1, stage1, _, *row_sems1), refs = refs[:8], refs[8:]
    (result_sems, block1), refs = (refs[:3], refs[3]), refs[4:]
    (vec_x, vec_z, vec_sib, vec_y, vec_zz, vec, send_v, recv_v), refs = refs[:8], refs[8:]
    (datt, rdo, held_q, held_kv, acc_k, acc_v, d_query, d_kv), refs = refs[:8], refs[8:]
    send, recv, send_q, send_kv, recv_q, recv_kv, local = refs
    y, zh, core, t = here()
    me = rank(y, zh, core)
    half = lax.rem(t, 2)
    other = t + 1 - 2 * half
    owner = (y < 3) & (core == 0)
    units = [(m, w) for m in range(2) for w in range(3)]
    rows = Rows(part, held_x, held_z, stage, block, d_branch, row_sems, own_part)
    rows_in = Rows(part_in, held_x1, held_z1, stage1, block1, gradient, row_sems1)
    rows_out = Rows(None, None, None, None, final, results, result_sems)
    barrier = pltpu.get_barrier_semaphore()

    def signal(dp, tensor):
        pl.semaphore_signal(barrier, inc=1, device_id=(dp, tensor), device_id_type=MESH)

    plane = [(g_gate.sib, t), (g_gate.zz, t)] + [(dp, t) for dp in g_gate.fore] + rows.peers()
    for device in plane:
        signal(*device)

    @pl.when(owner)
    def _():
        def each(d, _):
            pl.when(d != me)(lambda: signal(d, t))
            return 0

        lax.fori_loop(0, 16, each, 0)

    for m, w in units:
        pl.when(unit_owner(m, w) != me)(functools.partial(signal, unit_owner(m, w), t))
        signal(unit_owner(m, w), other)

    @pl.when(owner)
    def _():
        pl.semaphore_wait(barrier, len(plane) + 36)

    @pl.when(jnp.logical_not(owner))
    def _():
        pl.semaphore_wait(barrier, len(plane) + 6)

    for w in range(3):
        rows.scatter_x(w)
    loads = [
        pltpu.make_async_copy(part.at[:, :, rows.x], own_part, local.at[0]),
        pltpu.make_async_copy(cotangent.at[:, rows.zl, rows.x], cot, local.at[1]),
    ]
    for copy in loads:
        copy.start()
    g_gate.product(turned_middle, d_gu)
    for copy in loads:
        copy.wait()
    rows.scatter_z(0)
    g_up.product(turned_middle, d_gu, 1152)
    rows.scatter_z(1)
    g_gate.sent_away()
    g_down.product(turned_feed, hidden)
    rows.scatter_z(2)
    d_middle = jnp.zeros((SLICE, WIDE), F32)
    sums = [jnp.zeros((1, WIDE), F32)] * 3
    for w in range(3):
        upstream = rows.total(w)
        signal_w = middle[w]
        inverse = inverse_rms(signal_w)
        normed = signal_w * inverse
        d_signal = cot[w].astype(F32) + norm_back(normed, inverse, gains[2:3], upstream)
        lower = branch[w]
        inverse_lower = inverse_rms(lower)
        normed_lower = lower * inverse_lower
        lowered = norm_back(normed_lower, inverse_lower, gains[1:2], d_signal).astype(B16)
        block[w] = lowered
        rows.spread(w)
        d_middle = d_middle + d_signal
        terms = (d_signal * normed_lower, upstream * normed, lowered.astype(F32) * lower)
        sums = [old + jnp.sum(new, axis=0, keepdims=True) for old, new in zip(sums, terms)]
        if w == 0:
            g_gate.add()
    g_up.add()
    vec[1:2] = sums[0]
    vec[2:3] = sums[1]
    vec[3:4] = feed_sums[0:1]
    vec[4:5] = sums[2] / scale_out[...]
    vec[5:6] = feed_sums[1:2] / scale_down[...]

    codes = w_out[...].reshape(WIDE, HD)

    def to_owner(u, m, w, start):
        o = unit_owner(m, w)
        src = datt.at[w, m]

        @pl.when(o != me)
        def _():
            copy = remote(src, rdo.at[me], send.at[u], recv.at[me], o, t)
            copy.start() if start else copy.wait_send()

        @pl.when(o == me)
        def _():
            copy = pltpu.make_async_copy(src, rdo.at[me], local.at[0])
            copy.start() if start else copy.wait()

    for w in range(3):
        rows.forward(w)
    for w in range(3):
        rows.end(w)
        scaled = (d_branch[w].reshape(ROWS, WIDE).astype(F32) * scale_out[...]).astype(B16)
        datt[w] = dot(scaled, level(codes, w), 1, 0).astype(B16).reshape(2, 64, HD)
        for m in range(2):
            to_owner(m * 3 + w, m, w, True)
    for u, (m, w) in enumerate(units):
        to_owner(u, m, w, False)

    @pl.when(owner)
    def _():
        def each(d, _):
            @pl.when(d != me)
            def _():
                remote(rdo.at[d], rdo.at[d], send.at[0], recv.at[d], me, other).wait_recv()

            return 0

        lax.fori_loop(0, 16, each, 0)
        acc_k[...] = jnp.zeros_like(acc_k)
        acc_v[...] = jnp.zeros_like(acc_v)
        for b in range(4):
            rows_b = slice(16 * b, 16 * b + 16)
            blocks = list(range(max(0, b - 2), b + 1))
            queries = q_rot[b]
            keys = {kb: k_rot[kb] for kb in blocks}
            upstream = rdo[:, rows_b, :].reshape(256, HD)
            bents, probs = block_probs(queries, keys, first[b], b)
            d_probs = [dot(upstream, v_all[kb], 1, 1) for kb in blocks]
            centre = sum(
                jnp.sum(p * dp, axis=-1, keepdims=True) for p, dp in zip(probs, d_probs)
            )
            d_q = jnp.zeros((256, HD), F32)
            for kb, bent, p, dp in zip(blocks, bents, probs, d_probs):
                d_scores = (p * (dp - centre) * (1.0 - bent * bent)).astype(B16)
                d_q = d_q + dot(d_scores, keys[kb], 1, 0)
                acc_k[kb] += dot(d_scores, queries, 0, 0)
                acc_v[kb] += dot(p.astype(B16), upstream, 0, 0)
            d_q = unrotate(d_q * 0.0625, cosine[b], sine[b])
            held_q[:, rows_b, :] = d_q.astype(B16).reshape(16, 16, HD)
        for b in range(4):
            rows_b = slice(16 * b, 16 * b + 16)
            d_k = unrotate(acc_k[b] * 0.0625, cosine[b], sine[b]).astype(B16)
            d_v = acc_v[b].astype(B16)
            for i in range(2):
                cols = slice(128 * i, 128 * i + 128)
                held_kv[i, :, rows_b, :128] = d_k[:, cols].reshape(16, 16, 128)
                held_kv[i, :, rows_b, 128:] = d_v[:, cols].reshape(16, 16, 128)

    def hand_back(d, start):
        u = zh * 3 + y
        across = remote(
            held_kv.at[1 - half, d], d_kv.at[half, y, zh], send_kv.at[1, d], recv_kv.at[half, u], d, other
        )
        across.start() if start else across.wait_send()

        @pl.when(d != me)
        def _():
            for copy in (
                remote(held_q.at[d], d_query.at[y, zh], send_q.at[d], recv_q.at[u], d, t),
                remote(
                    held_kv.at[half, d], d_kv.at[half, y, zh], send_kv.at[0, d], recv_kv.at[half, u], d, t
                ),
            ):
                copy.start() if start else copy.wait_send()

        @pl.when(d == me)
        def _():
            for copy in (
                pltpu.make_async_copy(held_q.at[d], d_query.at[y, zh], local.at[0]),
                pltpu.make_async_copy(held_kv.at[half, d], d_kv.at[half, y, zh], local.at[1]),
            ):
                copy.start() if start else copy.wait()

    @pl.when(owner)
    def _():
        lax.fori_loop(0, 16, lambda d, _: (hand_back(d, True), 0)[1], 0)
        lax.fori_loop(0, 16, lambda d, _: (hand_back(d, False), 0)[1], 0)

    g_up.sent_away()
    g_out.product_whole(d_branch[...].reshape(3 * ROWS, WIDE), attended[...])
    g_down.add()
    g_gate.merge()
    g_gate.pool()
    for u, (m, w) in enumerate(units):

        @pl.when(unit_owner(m, w) != me)
        def _():
            ref = d_query.at[w, m]
            remote(ref, ref, send.at[0], recv_q.at[u], me, other).wait_recv()
            ref = d_kv.at[half, w, m]
            remote(ref, ref, send.at[0], recv_kv.at[half, u], me, other).wait_recv()

        ref = d_kv.at[1 - half, w, m]
        remote(ref, ref, send.at[0], recv_kv.at[1 - half, u], me, other).wait_recv()

    codes = w_qkv[...].reshape(WIDE, 2 * HD)
    d_input = jnp.zeros((ROWS, WIDE), F32)
    qkv_sums = jnp.zeros((1, 2 * HD), F32)
    d_qkv_all = jnp.zeros((ROWS, 2 * HD), F32)
    for w in range(3):
        both = (d_kv[0, w].astype(F32) + d_kv[1, w].astype(F32)).astype(B16).astype(F32)
        d_qkv = jnp.concatenate([d_query[w].astype(F32), both], -1).reshape(ROWS, 2 * HD)
        qkv_sums = qkv_sums + jnp.sum(d_qkv * qkv_pre[w], axis=0, keepdims=True)
        d_qkv_all = d_qkv_all + d_qkv
        scaled = (d_qkv * scale_qkv[...]).astype(B16)
        d_input = d_input + dot(scaled, level(codes, w), 1, 1)
    part_in[0] = d_input.astype(B16).reshape(2, 4, SLICE, WIDE)
    rows_in.scatter_x(0)
    g_down.sent_away()
    g_qkv.product_whole(normed_input[...], d_qkv_all.astype(B16))
    g_out.add()
    g_up.merge()
    g_up.pool()
    rows_in.scatter_z(0)
    g_qkv.add()

    upstream = rows_in.total(0)
    signal_in = tokens[pl.ds(pl.multiple_of(t * SLICE, SLICE), SLICE)].astype(F32)
    inverse = inverse_rms(signal_in)
    normed = signal_in * inverse
    block1[0] = d_middle + norm_back(normed, inverse, gains[0:1], upstream)
    rows_in.spread(0)

    vec[0:1] = jnp.sum(upstream * normed, axis=0, keepdims=True)
    vec[6:8] = jnp.zeros((2, WIDE), F32)
    x = rows.x
    copies = []

    def exchange(slot, src, dst, dp, tensor):
        copy = remote(src, dst, send_v.at[slot], recv_v.at[slot], dp, tensor)
        copy.start()
        copies.append(copy)

    def exchanged(slot, ref):
        remote(ref, ref, send_v.at[slot], recv_v.at[slot], me, other).wait_recv()

    vec_x[x] = vec[...]
    for k in range(3):
        exchange(k, vec_x.at[x], vec_x.at[x], me, rows.x_peers[k])
    g_down.merge()
    g_down.pool()
    g_gate.end()
    for k in range(3):
        exchanged(k, vec_x.at[rows.behind[k]])
    vec[...] = functools.reduce(jnp.add, [vec_x[i] for i in range(4)])
    exchange(3, vec, vec_z, me, rows.z_peer)
    rows_in.forward(0)
    for w in range(3):
        rows_out.spread(w)
    g_out.merge()
    g_out.pool()
    exchanged(3, vec_z)
    copies[3].wait_send()
    vec[0:6] = vec[0:6] + vec_z[0:6]
    vec[6:7] = gu_sums[...]
    vec[7:8, : 2 * HD] = qkv_sums / scale_qkv[...]
    exchange(4, vec, vec_sib, g_gate.sib, t)
    g_qkv.merge()
    g_qkv.pool()
    for w in range(3):
        rows_out.forward(w)
    exchanged(4, vec_sib)
    vec_y[y] = vec[...] + vec_sib[...]
    for i in range(3):
        exchange(5 + i, vec_y.at[y], vec_y.at[y], g_gate.fore[i], t)
    g_up.end()
    g_down.end()
    for i in range(3):
        exchanged(5 + i, vec_y.at[lax.rem(y + 3 - i, 4)])
    copies[4].wait_send()
    vec[...] = functools.reduce(jnp.add, [vec_y[i] for i in range(4)])
    exchange(8, vec, vec_zz, g_gate.zz, t)
    g_out.end()
    g_qkv.end()
    exchanged(8, vec_zz)
    totals[...] = vec[...] + vec_zz[...]
    rows_in.end(0)
    for w in range(3):
        rows_out.end(w)
    g_out.sent_away()
    g_qkv.sent_away()
    for k in (0, 1, 2, 5, 6, 7, 8):
        copies[k].wait_send()
    for part_of in (rows, rows_in, rows_out, *reduces):
        part_of.drain()


def back(hbm, vmem):
    def vec():
        return pltpu.VMEM((8, WIDE), F32)

    scratch = [pltpu.VMEM((8, SHARD, 1152), B16)] * 2
    for columns in GRADIENTS:
        scratch += reduce_scratch(columns)
    scratch += [
        pltpu.VMEM((3, 2, SLICE, WIDE), B16),
        pltpu.VMEM((3, SLICE, WIDE), B16),
        pltpu.VMEM((3, 2, 4, SLICE, WIDE), B16),
    ]
    scratch += rows_scratch(3)
    scratch += [pltpu.VMEM((1, 2, 4, SLICE, WIDE), B16)] + rows_scratch(1)
    scratch += rows_scratch(3)[4:] + [pltpu.VMEM((1, SLICE, WIDE), F32)]
    scratch += [pltpu.VMEM((4, 8, WIDE), F32), vec(), vec(), pltpu.VMEM((4, 8, WIDE), F32), vec(), vec()]
    scratch += [pltpu.SemaphoreType.DMA((9,))] * 2
    scratch += [
        pltpu.VMEM((3, 2, 64, HD), B16),
        pltpu.VMEM((16, 64, HD), B16),
        pltpu.VMEM((16, 64, HD), B16),
        pltpu.VMEM((2, 16, 64, HD), B16),
        pltpu.VMEM((4, 256, HD), F32),
        pltpu.VMEM((4, 256, HD), F32),
        pltpu.VMEM((3, 2, 64, HD), B16),
        pltpu.VMEM((2, 3, 2, 64, HD), B16),
        pltpu.SemaphoreType.DMA((6,)),
        pltpu.SemaphoreType.DMA((16,)),
        pltpu.SemaphoreType.DMA((16,)),
        pltpu.SemaphoreType.DMA((2, 16)),
        pltpu.SemaphoreType.DMA((6,)),
        pltpu.SemaphoreType.DMA((2, 6)),
        pltpu.SemaphoreType.DMA((2,)),
    ]
    return pl.pallas_call(
        back_kernel,
        name="back",
        out_shape=[
            struct((3, 2, 4, SLICE, WIDE), B16),
            struct((1, 2, 4, SLICE, WIDE), F32),
            struct((8, WIDE), F32),
        ]
        + [struct((SHARD, columns), F32) for columns in GRADIENTS],
        in_specs=any_space(len(hbm)) + vmem_space(len(vmem)),
        out_specs=any_space(2) + vmem_space(6),
        scratch_shapes=scratch,
        compiler_params=params(4),
    )(*hbm, *vmem)


def level(codes, width):
    if width == 0:
        return codes
    stride = STRIDES[width]
    return jnp.floor(codes * B16(1.0 / stride)) * B16(stride) + B16(stride // 2)


def gelu_parts(value):
    slope = 0.7978845608028654
    inner = jnp.tanh(slope * (value + 0.044715 * value * value * value))
    grown = 0.5 * value * (1.0 + inner)
    rate = 0.5 * (1.0 + inner) + 0.5 * value * (1.0 - inner * inner) * slope * (
        1.0 + 3 * 0.044715 * value * value
    )
    return grown, rate


def body(
    tokens,
    cotangent,
    segments,
    codes_query,
    codes_key,
    codes_value,
    codes_out,
    codes_gate,
    codes_up,
    codes_down,
    query_column_scale,
    key_column_scale,
    value_column_scale,
    output_column_scale,
    gate_column_scale,
    up_column_scale,
    down_column_scale,
    gain_first,
    gain_second,
    gain_third,
    gain_fourth,
):
    z_hi = lax.rem(lax.div(lax.axis_index("dp"), 2), 2)
    tokens = tokens.reshape(ROWS, WIDE)
    cotangent = cotangent.reshape(3, ROWS, WIDE)
    gains = jnp.stack([gain_first, gain_second, gain_third, gain_fourth])
    shards = [
        jnp.concatenate([codes_query, codes_key, codes_value], 1).astype(B16),
        codes_out.astype(B16).T,
        jnp.concatenate([codes_gate, codes_up], 1).astype(B16),
        codes_down.astype(B16).T,
    ]
    scale_qkv = jnp.concatenate([query_column_scale, key_column_scale, value_column_scale])
    scale_gu = jnp.concatenate([gate_column_scale, up_column_scale])

    documents = lax.dynamic_index_in_dim(segments, z_hi, 0, False)
    starts = jnp.sum((documents[None, :] < documents[:, None]).astype(jnp.int32), axis=1)
    place = jnp.arange(1024, dtype=jnp.int32)

    def blocked(rows):
        return rows.reshape(4, 16, 16).transpose(0, 2, 1).reshape(4, 256)

    first = blocked(starts)[:, :, None]
    expo = jnp.arange(HD // 2, dtype=F32) * (2.0 / HD)
    angle = blocked(place - starts).astype(F32)[:, :, None] * jnp.power(ROPE_BASE, -expo)
    cosine, sine = jnp.cos(angle), jnp.sin(angle)

    *weights, normed_middle, attended, normed_input, qkv_pre, q_rot, k_rot, v_all, branch, middle = front(
        shards, tokens, gains, scale_qkv, output_column_scale, first, cosine, sine
    )
    w_gu, w_down = (gathered.reshape(WIDE, -1) for gathered in weights[2:])
    attended = attended.reshape(3, ROWS, HD)
    grid = (3, 2, 4, SLICE, WIDE)
    d_part, turned_middle, turned_feed, d_gu, hidden, final, feed_sums, gu_sums = feed(
        [normed_middle, w_gu, w_down, cotangent.reshape(grid)],
        [scale_gu[None], down_column_scale[None], middle, gains],
    )

    flat = (3 * ROWS, -1)
    results, input_gradient, totals, g_gate, g_up, g_down, g_out, g_qkv = back(
        [d_part, cotangent.reshape(grid)],
        [
            turned_middle,
            turned_feed,
            d_gu.reshape(flat),
            hidden.reshape(flat),
            middle,
            branch,
            final,
            feed_sums,
            gu_sums,
            weights[1],
            weights[0],
            output_column_scale[None],
            down_column_scale[None],
            scale_qkv[None],
            gains,
            tokens,
            attended.reshape(flat),
            normed_input,
            qkv_pre,
            first,
            cosine,
            sine,
            q_rot,
            k_rot,
            v_all,
        ],
    )
    rows = lax.dynamic_slice_in_dim(totals, lax.axis_index("dp") * SHARD, SHARD, 1)
    return (
        results.reshape(3, 2, 64, 1, WIDE),
        input_gradient.reshape(2, 64, 1, WIDE),
        g_qkv[:, :256],
        g_qkv[:, 256:384],
        g_qkv[:, 384:],
        g_out.T,
        g_gate,
        g_up,
        g_down.T,
        totals[7, :256],
        totals[7, 256:384],
        totals[7, 384:512],
        rows[4],
        totals[6, :FF],
        totals[6, FF:],
        rows[5],
        rows[0],
        rows[1],
        rows[2],
        rows[3],
    )


def solution(mesh):
    matrix, turned = P("dp", "tensor"), P("tensor", "dp")
    columns, whole, shard = P("tensor"), P(), P("dp")
    in_specs = (
        P(None, None, "dp", None),
        P(None, None, None, "dp", None),
        whole,
        *(matrix, matrix, matrix, turned, matrix, matrix, turned),
        *(columns, columns, columns, whole, columns, columns, whole),
        *(whole, whole, whole, whole),
    )
    out_specs = (
        P(None, None, None, "dp", None),
        P(None, None, "dp", None),
        *(matrix, matrix, matrix, turned, matrix, matrix, turned),
        *(columns, columns, columns, shard, columns, columns, shard),
        *(shard, shard, shard, shard),
    )
    return jax.shard_map(body, mesh=mesh, in_specs=in_specs, out_specs=out_specs, check_vma=False)
```

```python
import functools

import jax
import jax.numpy as jnp
from jax import lax
from jax.experimental import pallas as pl
from jax.experimental.pallas import tpu as pltpu
from jax.sharding import PartitionSpec as P

MESH = pl.DeviceIdType.MESH
F32 = jnp.float32
B16 = jnp.bfloat16
EPSILON = 1e-06
SOFTCAP = 50.0
ROPE_BASE = 10000.0
MASKED = -1e30
HD = 256
WIDE = 2304
FF = 1152
STRIDES = (1, 16, 64)
SCALE_OUT, SCALE_DOWN, SCALE_GU, SCALE_QKV = (slice(i, i + 1) for i in range(4, 8))
SHARD = 144
LOW = 64
HIGH = SHARD - LOW
TENSOR = 8
ROWS = 128
SLICE = ROWS // TENSOR
VMEM_BYTES = 63 * 2**20


def here():
    dp = lax.axis_index("dp")
    return lax.div(dp, 4), lax.rem(lax.div(dp, 2), 2), lax.rem(dp, 2), lax.axis_index("tensor")


def rank(y, z_hi, core):
    return (y * 2 + z_hi) * 2 + core


def remote(src, dst, send, recv, dp, tensor):
    return pltpu.make_async_remote_copy(
        src, dst, send, recv, device_id=(dp, tensor), device_id_type=MESH
    )


def greet(devices):
    barrier = pltpu.get_barrier_semaphore()
    for device in devices:
        pl.semaphore_signal(barrier, inc=1, device_id=device, device_id_type=MESH)
    pl.semaphore_wait(barrier, len(devices))


def struct(shape, dtype):
    return jax.ShapeDtypeStruct(shape, dtype)


def any_space(count):
    return [pl.BlockSpec(memory_space=pl.ANY)] * count


def vmem_space(count):
    return [pl.BlockSpec(memory_space=pltpu.VMEM)] * count


def params(collective_id):
    return pltpu.CompilerParams(
        collective_id=collective_id, has_side_effects=True, vmem_limit_bytes=VMEM_BYTES
    )


class Gather:
    def __init__(self, src, out, send, recv, local):
        self.src, self.out, self.send, self.recv, self.local = src, out, send, recv, local
        self.y, self.zh, self.core, self.t = here()
        y, zh, core = self.y, self.zh, self.core
        self.me, self.sib, self.zz = rank(y, zh, core), rank(y, zh, 1 - core), rank(y, 1 - zh, core)
        self.fore = [rank(lax.rem(y + dy, 4), zh, core) for dy in (1, 2, 3)]
        self.behind = [lax.rem(y + 4 - dy, 4) for dy in (1, 2, 3)]
        self.low, self.high = pl.ds(0, LOW), pl.ds(LOW, HIGH)
        self.started = []

    def push(self, slot, src, dst, dp):
        copy = remote(src, dst, self.send.at[slot], self.recv.at[slot], dp, self.t)
        copy.start()
        self.started.append(copy)

    def arrive(self, slot, ref):
        remote(ref, ref, self.send.at[slot], self.recv.at[slot], self.sib, self.t).wait_recv()

    def start(self):
        src, mine = self.src, self.out.at[self.me]
        self.mine = pltpu.make_async_copy(src, mine, self.local)
        self.mine.start()
        low, high = self.low, self.high
        self.push(0, src.at[low], self.out.at[self.me, low], self.zz)
        for i in range(3):
            self.push(4 + i, src.at[high], self.out.at[self.me, high], self.fore[i])
        for i in range(3):
            self.push(1 + i, src.at[low], self.out.at[self.me, low], self.fore[i])
        self.push(7, src.at[high], self.out.at[self.me, high], self.zz)
        self.push(14, src, mine, self.sib)

    def over_y(self):
        block = self.out.at[self.zz, self.low]
        self.arrive(0, block)
        for i in range(3):
            self.push(8 + i, block, block, self.fore[i])
        self.push(15, block, block, self.sib)

    def over_z(self):
        for i in range(3):
            block = self.out.at[rank(self.behind[i], self.zh, self.core), self.high]
            self.arrive(4 + i, block)
            self.push(11 + i, block, block, self.zz)
            self.push(16 + i, block, block, self.sib)

    def near(self):
        for i in range(3):
            block = self.out.at[rank(self.behind[i], self.zh, self.core), self.low]
            self.arrive(1 + i, block)
            self.push(19 + i, block, block, self.sib)
        block = self.out.at[self.zz, self.high]
        self.arrive(7, block)
        self.push(22, block, block, self.sib)

    def far(self):
        for i in range(3):
            dp = rank(self.behind[i], 1 - self.zh, self.core)
            for slot, rows in ((0, self.low), (3, self.high)):
                block = self.out.at[dp, rows]
                self.arrive(8 + slot + i, block)
                self.push(23 + slot + i, block, block, self.sib)

    def end(self):
        out, low, high, other = self.out, self.low, self.high, 1 - self.core
        self.arrive(14, out.at[self.sib])
        far = rank(self.y, 1 - self.zh, other)
        self.arrive(15, out.at[far, low])
        self.arrive(22, out.at[far, high])
        for i in range(3):
            near, far = (rank(self.behind[i], zh, other) for zh in (self.zh, 1 - self.zh))
            self.arrive(16 + i, out.at[near, high])
            self.arrive(19 + i, out.at[near, low])
            self.arrive(23 + i, out.at[far, low])
            self.arrive(26 + i, out.at[far, high])
        self.mine.wait()

    def drain(self):
        for copy in self.started:
            copy.wait_send()


class Rows:
    def __init__(self, part, held_x, held_z, stage, block, out, sems, own=None, turned=None):
        self.part, self.own, self.out, self.block = part, own, out, block
        self.held_x, self.held_z, self.stage = held_x, held_z, stage
        self.send, self.recv, self.local = sems
        self.turned = turned
        self.split = WIDE if turned is None else WIDE - turned[0].shape[-1]
        self.low, self.high = pl.ds(0, self.split), pl.ds(self.split, WIDE - self.split)
        self.dp, self.t = lax.axis_index("dp"), lax.axis_index("tensor")
        self.zl, self.x = lax.div(self.t, 4), lax.rem(self.t, 4)
        self.ahead = [lax.rem(self.x + k, 4) for k in (1, 2, 3)]
        self.behind = [lax.rem(self.x + 4 - k, 4) for k in (1, 2, 3)]
        self.x_peers = [self.zl * 4 + x for x in self.ahead]
        self.z_peer = (1 - self.zl) * 4 + self.x
        self.started = []

    def peers(self):
        return [(self.dp, t) for t in self.x_peers + [self.z_peer]]

    def push(self, w, slot, src, dst, t):
        copy = remote(src, dst, self.send.at[w, slot], self.recv.at[w, slot], self.dp, t)
        copy.start()
        self.started.append(copy)

    def arrive(self, w, slot, ref):
        remote(
            ref, ref, self.send.at[w, slot], self.recv.at[w, slot], self.dp, self.z_peer
        ).wait_recv()

    def scatter_x(self, w):
        low, high = self.low, self.high
        for k in range(3):
            self.push(
                w,
                1 + k,
                self.part.at[w, :, self.ahead[k], :, low],
                self.held_x.at[w, k, :, :, low],
                self.x_peers[k],
            )
        if self.turned is not None:
            self.push(
                w, 11, self.part.at[w, 1 - self.zl, :, :, high], self.turned[0].at[w], self.z_peer
            )

    def summed_x(self, w, zl):
        own = self.part[w, zl, self.x] if self.own is None else self.own[w, zl]
        total = own[:, : self.split].astype(F32)
        for k in range(3):
            total = total + self.held_x[w, k, zl, :, : self.split].astype(F32)
        return total

    def summed_z(self, w, x):
        part = self.part[w, self.zl, x, :, self.split :].astype(F32)
        return part + self.turned[0][w, x].astype(F32)

    def scatter_z(self, w):
        for k in range(3):
            self.arrive(w, 1 + k, self.held_x.at[w, k, :, :, self.low])
        self.stage[w, :, : self.split] = self.summed_x(w, 1 - self.zl).astype(B16)
        self.push(w, 0, self.stage.at[w, :, self.low], self.held_z.at[w, :, self.low], self.z_peer)
        if self.turned is not None:
            held, stage, last = self.turned
            self.arrive(w, 11, held.at[w])
            for k in range(3):
                stage[w, k] = self.summed_z(w, self.ahead[k]).astype(B16)
                self.push(w, 12 + k, stage.at[w, k], last.at[w, k], self.x_peers[k])

    def total(self, w):
        self.arrive(w, 0, self.held_z.at[w, :, self.low])
        low = self.summed_x(w, self.zl) + self.held_z[w, :, : self.split].astype(F32)
        if self.turned is None:
            return low
        high = self.summed_z(w, self.x)
        for k in range(3):
            self.arrive(w, 12 + k, self.turned[2].at[w, k])
            high = high + self.turned[2][w, k].astype(F32)
        return jnp.concatenate([low, high], -1)

    def spread(self, w):
        block, mine = self.block.at[w], self.out.at[w, self.zl, self.x]
        self.push(w, 4, block.at[:, self.low], mine.at[:, self.low], self.z_peer)
        for k in range(3):
            self.push(w, 5 + k, block, mine, self.x_peers[k])
        pltpu.make_async_copy(block, mine, self.local.at[w]).start()

    def forward(self, w):
        block = self.out.at[w, 1 - self.zl, self.x, :, self.low]
        self.arrive(w, 4, block)
        for k in range(3):
            self.push(w, 8 + k, block, block, self.x_peers[k])
        if self.turned is not None:
            self.near(w)
            blocks = self.out.at[w, self.zl, :, :, self.high]
            self.push(w, 15, blocks, blocks, self.z_peer)

    def near(self, w):
        for k in range(3):
            self.arrive(w, 5 + k, self.out.at[w, self.zl, self.behind[k]])
        pltpu.make_async_copy(
            self.block.at[w], self.out.at[w, self.zl, self.x], self.local.at[w]
        ).wait()

    def end(self, w):
        for k in range(3):
            self.arrive(w, 8 + k, self.out.at[w, 1 - self.zl, self.behind[k], :, self.low])
        if self.turned is None:
            self.near(w)
        else:
            self.arrive(w, 15, self.out.at[w, 1 - self.zl, :, :, self.high])

    def drain(self):
        for copy in self.started:
            copy.wait_send()


def turned_scratch(columns):
    return [
        pltpu.VMEM((3, 4, SLICE, columns), B16),
        pltpu.VMEM((3, 3, SLICE, columns), B16),
        pltpu.VMEM((3, 3, SLICE, columns), B16),
    ]


def rows_scratch(depth):
    return [
        pltpu.VMEM((depth, 3, 2, SLICE, WIDE), B16),
        pltpu.VMEM((depth, SLICE, WIDE), B16),
        pltpu.VMEM((depth, SLICE, WIDE), B16),
        pltpu.VMEM((depth, SLICE, WIDE), B16),
        pltpu.SemaphoreType.DMA((depth, 16)),
        pltpu.SemaphoreType.DMA((depth, 16)),
        pltpu.SemaphoreType.DMA((depth,)),
    ]


class Reduce:
    def __init__(self, columns, away, own, sibs, yrecv, zrecv, ylast, zlast, out, send, recv):
        self.columns, self.away, self.own, self.sibs = columns, away, own, sibs
        self.yrecv, self.zrecv, self.ylast, self.zlast, self.out = yrecv, zrecv, ylast, zlast, out
        self.send, self.recv = send, recv
        self.y, self.zh, self.core, self.t = here()
        y, zh, core = self.y, self.zh, self.core
        self.sib, self.zz = rank(y, zh, 1 - core), rank(y, 1 - zh, core)
        self.ahead = [lax.rem(y + dy, 4) for dy in (1, 2, 3)]
        self.fore = [rank(place, zh, core) for place in self.ahead]
        self.started = []

    def push(self, slot, src, dst, dp):
        copy = remote(src, dst, self.send.at[slot], self.recv.at[slot], dp, self.t)
        copy.start()
        self.started.append(copy)

    def arrive(self, slot, ref):
        remote(ref, ref, self.send.at[slot], self.recv.at[slot], self.sib, self.t).wait_recv()

    def store(self, first, count, cols, block):
        block = block.astype(B16).reshape(count, 2, SHARD, block.shape[-1])
        even = self.core == 0
        chips = pl.ds(first, count)
        self.own[chips, :, cols] = jnp.where(even, block[:, 0], block[:, 1])
        self.away[chips, :, cols] = jnp.where(even, block[:, 1], block[:, 0])

    def to_sibling(self, place):
        pair = pl.ds(place * 2, 2)
        return remote(
            self.away.at[pair, :, pl.ds(0, self.columns)],
            self.sibs.at[pair],
            self.send.at[place],
            self.recv.at[place],
            self.sib,
            self.t,
        )

    def product(self, turned, right, left_columns=0):
        for place in range(4):
            rows = slice(place * 4 * SHARD, (place + 1) * 4 * SHARD)
            for i in range(self.columns // 384):
                cols = slice(384 * i, 384 * i + 384)
                block = dot(turned[rows], right[:, left_columns + 384 * i : left_columns + 384 * i + 384], 1, 0)
                self.store(place * 2, 2, cols, block)
            self.to_sibling(place).start()

    def product_whole(self, left, right):
        for i in range(self.columns // HD):
            cols = slice(HD * i, HD * i + HD)
            self.store(0, 8, cols, dot(left, right[:, cols], 0, 0))
        for place in range(4):
            self.to_sibling(place).start()

    def sent_away(self):
        for place in range(4):
            self.to_sibling(place).wait_send()

    def add(self):
        own, sibs = self.own, self.sibs
        for i, place in enumerate(self.ahead + [self.y]):
            pair = pl.ds(place * 2, 2)
            self.arrive(place, sibs.at[pair])

            def step(step, _, place=place):
                chip = place * 2 + lax.div(step, SHARD // 48)
                rows = pl.ds(pl.multiple_of(lax.rem(step, SHARD // 48) * 48, 16), 48)
                own[chip, rows] = own[chip, rows] + sibs[chip, rows]
                return 0

            lax.fori_loop(0, 2 * SHARD // 48, step, 0)
            self.push(
                7 + i, own.at[place * 2 + 1 - self.zh, pl.ds(LOW, HIGH)], self.zrecv.at[place], self.zz
            )
            if i < 3:
                self.push(4 + i, own.at[pair, pl.ds(0, LOW)], self.yrecv.at[i], self.fore[i])

    def merge(self):
        own, zrecv = self.own, self.zrecv
        for i, place in enumerate(self.ahead + [self.y]):
            self.arrive(7 + i, zrecv.at[place])

            def step(step, _, place=place):
                rows = pl.ds(pl.multiple_of(step * 16, 16), 16)
                mine = pl.ds(pl.multiple_of(step * 16 + LOW, 16), 16)
                zrecv[place, rows] = zrecv[place, rows] + own[place * 2 + self.zh, mine]
                return 0

            lax.fori_loop(0, HIGH // 16, step, 0)
            if i < 3:
                self.push(11 + i, zrecv.at[place], self.ylast.at[i], self.fore[i])

    def pool(self):
        for i in range(3):
            self.arrive(4 + i, self.yrecv.at[i])

        def step(step, _):
            chip = lax.div(step, LOW // 16)
            rows = pl.ds(pl.multiple_of(lax.rem(step, LOW // 16) * 16, 16), 16)
            total = self.own[self.y * 2 + chip, rows].astype(F32)
            for i in range(3):
                total = total + self.yrecv[i, chip, rows].astype(F32)
            self.own[self.y * 2 + chip, rows] = total.astype(B16)
            return 0

        lax.fori_loop(0, 2 * LOW // 16, step, 0)
        self.push(14, self.own.at[self.y * 2 + 1 - self.zh, pl.ds(0, LOW)], self.zlast, self.zz)

    def write(self, rows, total):
        first = 0
        for out in self.out if isinstance(self.out, tuple) else (self.out,):
            out[rows] = total[:, first : first + out.shape[-1]]
            first += out.shape[-1]

    def end(self):
        self.arrive(14, self.zlast)

        def low(step, _):
            rows = pl.ds(pl.multiple_of(step * 16, 16), 16)
            own = self.own[self.y * 2 + self.zh, rows].astype(F32)
            self.write(rows, own + self.zlast[rows].astype(F32))
            return 0

        lax.fori_loop(0, LOW // 16, low, 0)
        for i in range(3):
            self.arrive(11 + i, self.ylast.at[i])

        def high(step, _):
            rows = pl.ds(pl.multiple_of(step * 16, 16), 16)
            total = self.zrecv[self.y, rows].astype(F32)
            for i in range(3):
                total = total + self.ylast[i, rows].astype(F32)
            self.write(pl.ds(pl.multiple_of(step * 16 + LOW, 16), 16), total)
            return 0

        lax.fori_loop(0, HIGH // 16, high, 0)

    def drain(self):
        for copy in self.started:
            copy.wait_send()


def reduce_scratch(columns):
    return [
        pltpu.VMEM((8, SHARD, columns), B16),
        pltpu.VMEM((8, SHARD, columns), B16),
        pltpu.VMEM((3, 2, LOW, columns), B16),
        pltpu.VMEM((4, HIGH, columns), B16),
        pltpu.VMEM((3, HIGH, columns), B16),
        pltpu.VMEM((LOW, columns), B16),
        pltpu.SemaphoreType.DMA((15,)),
        pltpu.SemaphoreType.DMA((15,)),
    ]


def inverse_rms(signal):
    return lax.rsqrt(jnp.mean(signal * signal, axis=-1, keepdims=True) + EPSILON)


def norm_back(normed, inverse, gain, upstream):
    inner = upstream * (1.0 + gain)
    return inverse * (inner - normed * jnp.mean(inner * normed, axis=-1, keepdims=True))


def half_level(codes, width):
    return codes if width == 0 else jnp.floor(codes * B16(1.0 / STRIDES[width]))


def offset(left, width):
    return 0.0 if width == 0 else 0.5 * jnp.sum(left.astype(F32), axis=-1, keepdims=True)


def unit_owner(micro, width):
    return rank(width, micro, 0)


def rotate(signal, cosine, sine):
    former, latter = signal[:, : HD // 2], signal[:, HD // 2 :]
    return jnp.concatenate([former * cosine - latter * sine, latter * cosine + former * sine], -1)


def unrotate(signal, cosine, sine):
    former, latter = signal[:, : HD // 2], signal[:, HD // 2 :]
    return jnp.concatenate([former * cosine + latter * sine, latter * cosine - former * sine], -1)


def block_scores(queries, keys, first, b, kb):
    scores = lax.dot_general(queries, keys, (((1,), (1,)), ((), ())), preferred_element_type=F32)
    bent = jnp.tanh(scores * (0.0625 / SOFTCAP))
    lane = lax.broadcasted_iota(jnp.int32, (256, 256), 1)
    row = lax.broadcasted_iota(jnp.int32, (256, 256), 0)
    key_place = (16 * kb + (lane & 15)) * 16 + (lane >> 4)
    query_place = (16 * b + (row & 15)) * 16 + (row >> 4)
    allowed = (key_place >= first) & (key_place <= query_place)
    return bent, jnp.where(allowed, SOFTCAP * bent, MASKED)


def block_probs(queries, keys, first, b):
    pieces = [
        block_scores(queries, keys[kb], first, b, kb) for kb in range(max(0, b - 2), b + 1)
    ]
    peak = functools.reduce(
        jnp.maximum, [jnp.max(capped, axis=-1, keepdims=True) for _, capped in pieces]
    )
    exps = [jnp.exp(capped - peak) for _, capped in pieces]
    total = functools.reduce(jnp.add, [jnp.sum(e, axis=-1, keepdims=True) for e in exps])
    return [bent for bent, _ in pieces], [e / total for e in exps]


def dot(left, right, left_dim, right_dim):
    return lax.dot_general(
        left, right, (((left_dim,), (right_dim,)), ((), ())), preferred_element_type=F32
    )


def forward_kernel(*refs):
    shards, refs = refs[:5], refs[5:]
    (tokens, vectors, places, first, rates, cotangent), refs = refs[:6], refs[6:]
    (w_qkv, w_out), refs = refs[:2], refs[2:]
    (attended, normed_input, qkv_pre, q_rot, k_rot, v_all, branch, middle), refs = refs[:8], refs[8:]
    (cosine, sine), refs = refs[:2], refs[2:]
    (d_part, turned_middle, turned_feed, d_gu_low, hidden, final, sums, gu_sums), refs = refs[:8], refs[8:]
    gains, scale_out, scale_qkv = vectors[0:4], vectors[SCALE_OUT], vectors[SCALE_QKV, : 2 * HD]
    scale_down, scale_gu = vectors[SCALE_DOWN], vectors[SCALE_GU]
    (wq, wo, low, rq, rkv, held, att, part), refs = refs[:8], refs[8:]
    (held_x, held_z, stage, block, *row_sems), refs = refs[:7], refs[7:]
    (wg, wu, wd, nm, gu_pre, feed_part, cot, d_feed, dgs), refs = refs[:9], refs[9:]
    (held_x_f, held_z_f, stage_f, feed_block, *feed_sems), refs = refs[:7], refs[7:]
    turned, refs = refs[:3], refs[3:]
    (send_g, recv_g, local_g, send, recv_q, recv_kv, send_back, recv_back, local) = refs
    y, zh, core, t = here()
    me = rank(y, zh, core)
    half = lax.rem(t, 2)
    other = t + 1 - 2 * half
    owner = (y < 3) & (core == 0)
    units = [(m, w) for m in range(2) for w in range(3)]
    gathers = [
        Gather(src, out, send_g.at[k], recv_g.at[k], local_g.at[k])
        for k, (src, out) in enumerate(zip(shards, (wq, wo, wg, wu, wd)))
    ]
    g_qkv, g_out, g_gate, g_up, g_down = gathers
    rows = Rows(part, held_x, held_z, stage, block, nm, row_sems)
    feeds = Rows(feed_part, held_x_f, held_z_f, stage_f, feed_block, d_feed, feed_sems, None, turned)
    barrier = pltpu.get_barrier_semaphore()

    def signal(dp, tensor):
        pl.semaphore_signal(barrier, inc=1, device_id=(dp, tensor), device_id_type=MESH)

    plane = [(g_qkv.sib, t), (g_qkv.zz, t)] + [(dp, t) for dp in g_qkv.fore] + rows.peers()
    for device in plane:
        signal(*device)

    @pl.when(owner)
    def _():
        def each(d, _):
            pl.when(d != me)(lambda: signal(d, t))
            signal(d, other)
            return 0

        lax.fori_loop(0, 16, each, 0)

    for m, w in units:
        pl.when(unit_owner(m, w) != me)(functools.partial(signal, unit_owner(m, w), t))

    @pl.when(owner)
    def _():
        pl.semaphore_wait(barrier, len(plane) + 26)

    @pl.when(jnp.logical_not(owner))
    def _():
        pl.semaphore_wait(barrier, len(plane) + 12)

    g_qkv.start()
    inputs = tokens[...].astype(F32)
    normed_input[...] = (inputs * inverse_rms(inputs) * (1.0 + gains[0:1])).astype(B16)
    for b in range(4):
        angle = places[:, b : b + 1] * rates[...]
        cosine[b], sine[b] = jnp.cos(angle), jnp.sin(angle)
    g_qkv.over_y()
    g_qkv.over_z()
    g_qkv.near()
    g_out.start()
    g_gate.start()
    g_qkv.far()
    g_qkv.end()

    for i in range(2):
        cols = slice(HD * i, HD * i + HD)
        codes = wq[:, :, cols].reshape(WIDE, HD)
        for w in range(3):
            product = dot(normed_input[...], level(codes, w), 1, 0) * scale_qkv[:, cols]
            qkv_pre[w, :, cols] = product
            low[w, :, :, cols] = product.astype(B16).reshape(2, 64, HD)

    def to_owner(u, m, w, start):
        o = unit_owner(m, w)
        q_src, kv_src = low.at[w, m, :, pl.ds(0, HD)], low.at[w, m, :, pl.ds(HD, HD)]
        across = remote(kv_src, rkv.at[half, me], send.at[u, 2], recv_kv.at[half, me], o, other)
        away = [
            remote(q_src, rq.at[me], send.at[u, 0], recv_q.at[me], o, t),
            remote(kv_src, rkv.at[half, me], send.at[u, 1], recv_kv.at[half, me], o, t),
        ]
        near = [
            pltpu.make_async_copy(q_src, rq.at[me], local.at[0]),
            pltpu.make_async_copy(kv_src, rkv.at[half, me], local.at[1]),
        ]

        @pl.when(o != me)
        def _():
            for copy in away:
                copy.start() if start else copy.wait_send()

        @pl.when(o == me)
        def _():
            for copy in near:
                copy.start() if start else copy.wait()

        across.start() if start else across.wait_send()

    for u, (m, w) in enumerate(units):
        to_owner(u, m, w, True)
    for gather in (g_out, g_gate):
        gather.over_y()
        gather.over_z()

    @pl.when(owner)
    def _():
        for u, (m, w) in enumerate(units):

            @pl.when(unit_owner(m, w) == me)
            def _():
                for i in range(2):
                    ref = (rq.at[me], rkv.at[half, me])[i]
                    pltpu.make_async_copy(ref, ref, local.at[i]).wait()

        def each(d, _):
            @pl.when(d != me)
            def _():
                remote(rq.at[d], rq.at[d], send.at[0, 0], recv_q.at[d], me, other).wait_recv()
                remote(
                    rkv.at[half, d], rkv.at[half, d], send.at[0, 0], recv_kv.at[half, d], me, other
                ).wait_recv()

            remote(
                rkv.at[1 - half, d], rkv.at[1 - half, d], send.at[0, 0], recv_kv.at[1 - half, d], me, other
            ).wait_recv()
            return 0

        lax.fori_loop(0, 16, each, 0)
        for b in range(4):
            rows_b = slice(16 * b, 16 * b + 16)
            c, s = cosine[b], sine[b]
            q = rq[:, rows_b, :].reshape(256, HD).astype(F32)
            q_rot[b] = rotate(q, c, s).astype(B16)
            k = jnp.concatenate(
                [rkv[i, :, rows_b, : HD // 2].reshape(256, HD // 2) for i in range(2)], -1
            )
            k_rot[b] = rotate(k.astype(F32), c, s).astype(B16)
            v_all[b] = jnp.concatenate(
                [rkv[i, :, rows_b, HD // 2 :].reshape(256, HD // 2) for i in range(2)], -1
            )
        for b in range(4):
            keys = {kb: k_rot[kb] for kb in range(max(0, b - 2), b + 1)}
            _, probs = block_probs(q_rot[b], keys, first[:, b : b + 1], b)
            out = sum(
                dot(p.astype(B16), v_all[kb], 1, 0) for p, kb in zip(probs, sorted(keys))
            )
            held[:, 16 * b : 16 * b + 16, :] = out.astype(B16).reshape(16, 16, HD)

        def hand_back(d, start):
            @pl.when(d != me)
            def _():
                copy = remote(
                    held.at[d], att.at[y, zh], send_back.at[d], recv_back.at[zh * 3 + y], d, t
                )
                copy.start() if start else copy.wait_send()

            @pl.when(d == me)
            def _():
                copy = pltpu.make_async_copy(held.at[d], att.at[y, zh], local.at[0])
                copy.start() if start else copy.wait()

        lax.fori_loop(0, 16, lambda d, _: (hand_back(d, True), 0)[1], 0)
        lax.fori_loop(0, 16, lambda d, _: (hand_back(d, False), 0)[1], 0)

    g_out.near()
    g_out.far()
    g_up.start()
    g_out.end()
    g_gate.near()
    for u, (m, w) in enumerate(units):

        @pl.when(unit_owner(m, w) != me)
        def _():
            ref = att.at[w, m]
            remote(ref, ref, send.at[0, 0], recv_back.at[u], me, other).wait_recv()

    codes = wo[...].reshape(WIDE, HD)
    for w in range(3):
        product = dot(att[w].reshape(ROWS, HD), level(codes, w), 1, 1) * scale_out
        part[w] = product.astype(B16).reshape(2, 4, SLICE, WIDE)
        rows.scatter_x(w)
    attended[...] = att[...]
    keep = [
        pltpu.make_async_copy(src, dst, local.at[i])
        for i, (src, dst) in enumerate(((wq, w_qkv), (wo, w_out)))
    ]
    for copy in keep:
        copy.start()
    load = pltpu.make_async_copy(cotangent.at[:, rows.zl, rows.x], cot, local.at[2])
    load.start()
    g_gate.far()
    g_up.over_y()
    g_up.over_z()
    g_down.start()
    for w in range(3):
        rows.scatter_z(w)
    mine = tokens[pl.ds(pl.multiple_of(t * SLICE, SLICE), SLICE)].astype(F32)
    for w in range(3):
        signal_w = rows.total(w)
        branch[w] = signal_w
        total = mine + signal_w * inverse_rms(signal_w) * (1.0 + gains[1:2])
        middle[w] = total
        block[w] = (total * inverse_rms(total) * (1.0 + gains[2:3])).astype(B16)
        rows.spread(w)
    g_up.near()
    for w in range(3):
        rows.forward(w)
    g_down.over_y()
    g_down.over_z()
    g_up.far()
    g_gate.end()
    g_up.end()

    def forward(w):
        stride = STRIDES[w]
        left = nm[w].reshape(ROWS, WIDE)
        extra = offset(left, w)
        for k, codes in enumerate((wg, wu)):
            cols = slice(FF * k, FF * k + FF)
            product = dot(left, half_level(codes[...].reshape(WIDE, FF), w), 1, 0)
            gu_pre[w, :, cols] = (product + extra) * (scale_gu[:, cols] * stride)
        gate_pre, up_pre = gu_pre[w, :, :FF], gu_pre[w, :, FF:]
        grown, _ = gelu_parts(gate_pre)
        low = (grown * up_pre).astype(B16)
        hidden[w] = low
        extra_down = offset(low, w)

        if w == 0:
            g_down.far()
            g_down.end()
        product = dot(low, half_level(wd[...].reshape(WIDE, FF), w), 1, 1)
        product = (product + extra_down) * (scale_down * stride)
        feed_part[w] = product.astype(B16).reshape(2, 4, SLICE, WIDE)
        feeds.scatter_x(w)

    def norm(w):
        signal = feeds.total(w)
        inverse = inverse_rms(signal)
        normed = signal * inverse
        upstream = cot[w].astype(F32)
        lowered = norm_back(normed, inverse, gains[3:4], upstream).astype(B16)
        feed_block[w] = lowered
        feeds.spread(w)
        final[w] = (middle[w] + normed * (1.0 + gains[3:4])).astype(B16)
        for i, term in enumerate((upstream * normed, lowered.astype(F32) * signal)):
            term = jnp.sum(term, axis=0, keepdims=True)
            sums[i : i + 1] = term if w == 0 else sums[i : i + 1] + term

    def backward(w):
        stride = STRIDES[w]
        lowered = d_feed[w].reshape(ROWS, WIDE)
        turned_feed[:, w * ROWS : (w + 1) * ROWS] = lowered.T
        scaled = (lowered.astype(F32) * scale_down).astype(B16)
        extra = offset(scaled, w)
        for i in range(3):
            cols = slice(384 * i, 384 * i + 384)
            ups = slice(FF + 384 * i, FF + 384 * i + 384)
            d_hidden = (dot(scaled, half_level(wd[:, :, cols].reshape(WIDE, 384), w), 1, 0) + extra) * float(stride)
            grown, rate = gelu_parts(gu_pre[w, :, cols])
            for where, value in ((cols, d_hidden * gu_pre[w, :, ups] * rate), (ups, d_hidden * grown)):
                low = value.astype(B16)
                d_gu_low[w, :, where] = low
                dgs[:, where] = (value * scale_gu[:, where]).astype(B16)
                term = jnp.sum(low.astype(F32) * gu_pre[w, :, where], axis=0, keepdims=True)
                term = term / scale_gu[:, where]
                gu_sums[:, where] = term if w == 0 else gu_sums[:, where] + term
        left = dgs[...]
        extra_gu = offset(left, w)

        product = sum(
            dot(left[:, FF * k : FF * k + FF], half_level(codes[...].reshape(WIDE, FF), w), 1, 1)
            for k, codes in enumerate((wg, wu))
        )
        product = (product + extra_gu) * float(stride)
        d_part[w] = product.astype(B16).reshape(2, 4, SLICE, WIDE)

    rows.end(0)
    g_down.near()
    forward(0)
    rows.end(1)
    forward(1)
    feeds.scatter_z(0)
    rows.end(2)
    forward(2)
    load.wait()
    feeds.scatter_z(1)
    norm(0)
    feeds.scatter_z(2)
    norm(1)
    feeds.forward(0)
    norm(2)
    feeds.forward(1)
    for w in range(3):
        turned_middle[:, w * ROWS : (w + 1) * ROWS] = nm[w].reshape(ROWS, WIDE).T
    feeds.end(0)
    backward(0)
    feeds.forward(2)
    feeds.end(1)
    backward(1)
    feeds.end(2)
    backward(2)
    for copy in keep:
        copy.wait()
    for u, (m, w) in enumerate(units):
        o = unit_owner(m, w)

        @pl.when(o != me)
        def _():
            for slot, src in enumerate((low.at[w, m, :, pl.ds(0, HD)], low.at[w, m, :, pl.ds(HD, HD)])):
                remote(src, src, send.at[u, slot], recv_q.at[0], o, t).wait_send()

        src = low.at[w, m, :, pl.ds(HD, HD)]
        remote(src, src, send.at[u, 2], recv_q.at[0], o, other).wait_send()
    rows.drain()
    feeds.drain()
    for gather in gathers:
        gather.drain()


def forward_pass(*operands):
    shards = operands[:5]
    return pl.pallas_call(
        forward_kernel,
        name="forward",
        out_shape=[struct((16,) + shard.shape, B16) for shard in shards[:2]]
        + [
            struct((3, 2, 64, HD), B16),
            struct((ROWS, WIDE), B16),
            struct((3, ROWS, 2 * HD), F32),
        ]
        + [struct((4, 256, HD), B16)] * 3
        + [struct((3, SLICE, WIDE), F32)] * 2
        + [struct((4, 256, HD // 2), F32)] * 2
        + [
            struct((3, 2, 4, SLICE, WIDE), B16),
            struct((WIDE, 3 * ROWS), B16),
            struct((WIDE, 3 * ROWS), B16),
            struct((3, ROWS, 2 * FF), B16),
            struct((3, ROWS, FF), B16),
            struct((3, SLICE, WIDE), B16),
            struct((8, WIDE), F32),
            struct((1, 2 * FF), F32),
        ],
        in_specs=vmem_space(len(operands) - 1) + any_space(1),
        out_specs=any_space(2) + vmem_space(18),
        scratch_shapes=[
            pltpu.VMEM((16, SHARD, 2 * HD), B16),
            pltpu.VMEM((16, SHARD, HD), B16),
            pltpu.VMEM((3, 2, 64, 2 * HD), B16),
            pltpu.VMEM((16, 64, HD), B16),
            pltpu.VMEM((2, 16, 64, HD), B16),
            pltpu.VMEM((16, 64, HD), B16),
            pltpu.VMEM((3, 2, 64, HD), B16),
            pltpu.VMEM((3, 2, 4, SLICE, WIDE), B16),
        ]
        + rows_scratch(3)
        + [pltpu.VMEM((16, SHARD, FF), B16)] * 3
        + [
            pltpu.VMEM((3, 2, 4, SLICE, WIDE), B16),
            pltpu.VMEM((3, ROWS, 2 * FF), F32),
            pltpu.VMEM((3, 2, 4, SLICE, WIDE), B16),
            pltpu.VMEM((3, SLICE, WIDE), B16),
            pltpu.VMEM((3, 2, 4, SLICE, WIDE), B16),
            pltpu.VMEM((ROWS, 2 * FF), B16),
        ]
        + rows_scratch(3)
        + turned_scratch(1152)
        + [
            pltpu.SemaphoreType.DMA((5, 29)),
            pltpu.SemaphoreType.DMA((5, 29)),
            pltpu.SemaphoreType.DMA((5,)),
            pltpu.SemaphoreType.DMA((6, 3)),
            pltpu.SemaphoreType.DMA((16,)),
            pltpu.SemaphoreType.DMA((2, 16)),
            pltpu.SemaphoreType.DMA((16,)),
            pltpu.SemaphoreType.DMA((6,)),
            pltpu.SemaphoreType.DMA((3,)),
        ],
        compiler_params=params(3),
    )(*operands)


GRADIENTS = (1152, 1152, 1152, HD, 2 * HD)


def back_kernel(*refs):
    (part, cotangent), refs = refs[:2], refs[2:]
    (turned_middle, turned_feed, d_gu, hidden, middle, branch, final, feed_sums, gu_sums), refs = refs[:9], refs[9:]
    (w_out, w_qkv, vectors, tokens, attended, normed_input), refs = refs[:6], refs[6:]
    (qkv_pre, first, cosine, sine, q_rot, k_rot, v_all), refs = refs[:7], refs[7:]
    (results, gradient, totals), refs = refs[:3], refs[3:]
    (g_query, g_key, g_value), outs, refs = refs[4:7], refs[:4], refs[7:]
    outs = (*outs, (g_query, g_key, g_value))
    gains, scale_out, scale_down = vectors[0:4], vectors[SCALE_OUT], vectors[SCALE_DOWN]
    scale_qkv = vectors[SCALE_QKV, : 2 * HD]
    aways, refs = refs[:2], refs[2:]
    reduces = []
    for k, columns in enumerate(GRADIENTS):
        held, refs = refs[:8], refs[8:]
        away = aways[k % 2]
        reduces.append(Reduce(columns, away, *held[:6], outs[k], *held[6:]))
    g_gate, g_up, g_down, g_out, g_qkv = reduces
    (own_part, cot, d_branch), refs = refs[:3], refs[3:]
    (held_x, held_z, stage, block, *row_sems), refs = refs[:7], refs[7:]
    (part_in, held_x1, held_z1, stage1, _, *row_sems1), refs = refs[:8], refs[8:]
    (result_sems, block1), refs = (refs[:3], refs[3]), refs[4:]
    (vec_x, vec_z, vec_sib, vec_y, vec_zz, vec, send_v, recv_v), refs = refs[:8], refs[8:]
    (datt, rdo, held_q, held_kv, acc_k, acc_v, d_query, d_kv), refs = refs[:8], refs[8:]
    send, recv, send_q, send_kv, recv_q, recv_kv, local = refs
    y, zh, core, t = here()
    me = rank(y, zh, core)
    half = lax.rem(t, 2)
    other = t + 1 - 2 * half
    owner = (y < 3) & (core == 0)
    units = [(m, w) for m in range(2) for w in range(3)]
    rows = Rows(part, held_x, held_z, stage, block, d_branch, row_sems, own_part)
    rows_in = Rows(part_in, held_x1, held_z1, stage1, block1, gradient, row_sems1)
    rows_out = Rows(None, None, None, None, final, results, result_sems)
    barrier = pltpu.get_barrier_semaphore()

    def signal(dp, tensor):
        pl.semaphore_signal(barrier, inc=1, device_id=(dp, tensor), device_id_type=MESH)

    plane = [(g_gate.sib, t), (g_gate.zz, t)] + [(dp, t) for dp in g_gate.fore] + rows.peers()
    for device in plane:
        signal(*device)

    @pl.when(owner)
    def _():
        def each(d, _):
            pl.when(d != me)(lambda: signal(d, t))
            return 0

        lax.fori_loop(0, 16, each, 0)

    for m, w in units:
        pl.when(unit_owner(m, w) != me)(functools.partial(signal, unit_owner(m, w), t))
        signal(unit_owner(m, w), other)

    @pl.when(owner)
    def _():
        pl.semaphore_wait(barrier, len(plane) + 36)

    @pl.when(jnp.logical_not(owner))
    def _():
        pl.semaphore_wait(barrier, len(plane) + 6)

    for w in range(3):
        rows.scatter_x(w)
    loads = [
        pltpu.make_async_copy(part.at[:, :, rows.x], own_part, local.at[0]),
        pltpu.make_async_copy(cotangent.at[:, rows.zl, rows.x], cot, local.at[1]),
    ]
    for copy in loads:
        copy.start()
    g_gate.product(turned_middle, d_gu)
    g_up.product(turned_middle, d_gu, 1152)
    g_gate.add()
    for copy in loads:
        copy.wait()
    rows.scatter_z(0)
    g_gate.sent_away()
    g_down.product(turned_feed, hidden)
    rows.scatter_z(1)
    g_up.add()
    rows.scatter_z(2)
    d_middle = jnp.zeros((SLICE, WIDE), F32)
    sums = [jnp.zeros((1, WIDE), F32)] * 3
    for w in range(3):
        upstream = rows.total(w)
        signal_w = middle[w]
        inverse = inverse_rms(signal_w)
        normed = signal_w * inverse
        d_signal = cot[w].astype(F32) + norm_back(normed, inverse, gains[2:3], upstream)
        lower = branch[w]
        inverse_lower = inverse_rms(lower)
        normed_lower = lower * inverse_lower
        lowered = norm_back(normed_lower, inverse_lower, gains[1:2], d_signal).astype(B16)
        block[w] = lowered
        rows.spread(w)
        d_middle = d_middle + d_signal
        terms = (d_signal * normed_lower, upstream * normed, lowered.astype(F32) * lower)
        sums = [old + jnp.sum(new, axis=0, keepdims=True) for old, new in zip(sums, terms)]
    vec[1:2] = sums[0]
    vec[2:3] = sums[1]
    vec[3:4] = feed_sums[0:1]
    vec[4:5] = sums[2] / scale_out
    vec[5:6] = feed_sums[1:2] / scale_down

    codes = w_out[...].reshape(WIDE, HD)

    def to_owner(u, m, w, start):
        o = unit_owner(m, w)
        src = datt.at[w, m]

        @pl.when(o != me)
        def _():
            copy = remote(src, rdo.at[me], send.at[u], recv.at[me], o, t)
            copy.start() if start else copy.wait_send()

        @pl.when(o == me)
        def _():
            copy = pltpu.make_async_copy(src, rdo.at[me], local.at[0])
            copy.start() if start else copy.wait()

    g_gate.merge()
    g_gate.pool()
    for w in range(3):
        rows.forward(w)
    for w in range(3):
        rows.end(w)
        scaled = (d_branch[w].reshape(ROWS, WIDE).astype(F32) * scale_out).astype(B16)
        datt[w] = dot(scaled, level(codes, w), 1, 0).astype(B16).reshape(2, 64, HD)
        for m in range(2):
            to_owner(m * 3 + w, m, w, True)
    g_down.add()
    for w in range(3):
        rows_out.spread(w)
    for u, (m, w) in enumerate(units):
        to_owner(u, m, w, False)

    @pl.when(owner)
    def _():
        def each(d, _):
            @pl.when(d != me)
            def _():
                remote(rdo.at[d], rdo.at[d], send.at[0], recv.at[d], me, other).wait_recv()

            return 0

        lax.fori_loop(0, 16, each, 0)
        acc_k[...] = jnp.zeros_like(acc_k)
        acc_v[...] = jnp.zeros_like(acc_v)
        for b in range(4):
            rows_b = slice(16 * b, 16 * b + 16)
            blocks = list(range(max(0, b - 2), b + 1))
            queries = q_rot[b]
            keys = {kb: k_rot[kb] for kb in blocks}
            upstream = rdo[:, rows_b, :].reshape(256, HD)
            bents, probs = block_probs(queries, keys, first[:, b : b + 1], b)
            d_probs = [dot(upstream, v_all[kb], 1, 1) for kb in blocks]
            centre = sum(
                jnp.sum(p * dp, axis=-1, keepdims=True) for p, dp in zip(probs, d_probs)
            )
            d_q = jnp.zeros((256, HD), F32)
            for kb, bent, p, dp in zip(blocks, bents, probs, d_probs):
                d_scores = (p * (dp - centre) * (1.0 - bent * bent)).astype(B16)
                d_q = d_q + dot(d_scores, keys[kb], 1, 0)
                acc_k[kb] += dot(d_scores, queries, 0, 0)
                acc_v[kb] += dot(p.astype(B16), upstream, 0, 0)
            d_q = unrotate(d_q * 0.0625, cosine[b], sine[b])
            held_q[:, rows_b, :] = d_q.astype(B16).reshape(16, 16, HD)
        for b in range(4):
            rows_b = slice(16 * b, 16 * b + 16)
            d_k = unrotate(acc_k[b] * 0.0625, cosine[b], sine[b]).astype(B16)
            d_v = acc_v[b].astype(B16)
            for i in range(2):
                cols = slice(128 * i, 128 * i + 128)
                held_kv[i, :, rows_b, :128] = d_k[:, cols].reshape(16, 16, 128)
                held_kv[i, :, rows_b, 128:] = d_v[:, cols].reshape(16, 16, 128)

    def hand_back(d, start):
        u = zh * 3 + y
        across = remote(
            held_kv.at[1 - half, d], d_kv.at[half, y, zh], send_kv.at[1, d], recv_kv.at[half, u], d, other
        )
        across.start() if start else across.wait_send()

        @pl.when(d != me)
        def _():
            for copy in (
                remote(held_q.at[d], d_query.at[y, zh], send_q.at[d], recv_q.at[u], d, t),
                remote(
                    held_kv.at[half, d], d_kv.at[half, y, zh], send_kv.at[0, d], recv_kv.at[half, u], d, t
                ),
            ):
                copy.start() if start else copy.wait_send()

        @pl.when(d == me)
        def _():
            for copy in (
                pltpu.make_async_copy(held_q.at[d], d_query.at[y, zh], local.at[0]),
                pltpu.make_async_copy(held_kv.at[half, d], d_kv.at[half, y, zh], local.at[1]),
            ):
                copy.start() if start else copy.wait()

    @pl.when(owner)
    def _():
        lax.fori_loop(0, 16, lambda d, _: (hand_back(d, True), 0)[1], 0)
        lax.fori_loop(0, 16, lambda d, _: (hand_back(d, False), 0)[1], 0)

    for w in range(3):
        rows_out.forward(w)
    g_up.sent_away()
    g_out.product_whole(d_branch[...].reshape(3 * ROWS, WIDE), attended[...])
    g_up.merge()
    g_up.pool()
    for u, (m, w) in enumerate(units):

        @pl.when(unit_owner(m, w) != me)
        def _():
            ref = d_query.at[w, m]
            remote(ref, ref, send.at[0], recv_q.at[u], me, other).wait_recv()
            ref = d_kv.at[half, w, m]
            remote(ref, ref, send.at[0], recv_kv.at[half, u], me, other).wait_recv()

        ref = d_kv.at[1 - half, w, m]
        remote(ref, ref, send.at[0], recv_kv.at[1 - half, u], me, other).wait_recv()

    codes = w_qkv[...].reshape(WIDE, 2 * HD)
    scaled = []
    qkv_sums = jnp.zeros((1, 2 * HD), F32)
    d_qkv_all = jnp.zeros((ROWS, 2 * HD), F32)
    for w in range(3):
        both = (d_kv[0, w].astype(F32) + d_kv[1, w].astype(F32)).astype(B16).astype(F32)
        d_qkv = jnp.concatenate([d_query[w].astype(F32), both], -1).reshape(ROWS, 2 * HD)
        qkv_sums = qkv_sums + jnp.sum(d_qkv * qkv_pre[w], axis=0, keepdims=True)
        d_qkv_all = d_qkv_all + d_qkv
        scaled.append((d_qkv * scale_qkv).astype(B16))
    whole = tokens[...].astype(F32)
    inverse = inverse_rms(whole)
    for i in range(3):
        tile = slice(768 * i, 768 * i + 768)
        d_input = sum(dot(scaled[w], level(codes[tile], w), 1, 1) for w in range(3))
        part_in[0, :, :, :, tile] = d_input.astype(B16).reshape(2, 4, SLICE, 768)
        normed = tokens[:, tile].astype(F32) * inverse
        vec[0:1, tile] = jnp.sum(d_input * normed, axis=0, keepdims=True)
    rows_in.scatter_x(0)

    vec[6:8] = jnp.zeros((2, WIDE), F32)
    x = rows.x
    copies = []

    def exchange(slot, src, dst, dp, tensor):
        copy = remote(src, dst, send_v.at[slot], recv_v.at[slot], dp, tensor)
        copy.start()
        copies.append(copy)

    def exchanged(slot, ref):
        remote(ref, ref, send_v.at[slot], recv_v.at[slot], me, other).wait_recv()

    vec_x[x] = vec[...]
    for k in range(3):
        exchange(k, vec_x.at[x], vec_x.at[x], me, rows.x_peers[k])
    g_down.sent_away()
    g_qkv.product_whole(normed_input[...], d_qkv_all.astype(B16))
    g_out.add()
    for k in range(3):
        exchanged(k, vec_x.at[rows.behind[k]])
    vec[...] = functools.reduce(jnp.add, [vec_x[i] for i in range(4)])
    exchange(3, vec, vec_z, me, rows.z_peer)
    rows_in.scatter_z(0)
    g_qkv.add()
    exchanged(3, vec_z)
    copies[3].wait_send()
    vec[0:6] = vec[0:6] + vec_z[0:6]
    vec[6:7] = gu_sums[...]
    vec[7:8, : 2 * HD] = qkv_sums / scale_qkv
    exchange(4, vec, vec_sib, g_gate.sib, t)

    upstream = rows_in.total(0)
    signal_in = tokens[pl.ds(pl.multiple_of(t * SLICE, SLICE), SLICE)].astype(F32)
    inverse = inverse_rms(signal_in)
    block1[0] = d_middle + norm_back(signal_in * inverse, inverse, gains[0:1], upstream)
    rows_in.spread(0)
    exchanged(4, vec_sib)
    vec_y[y] = vec[...] + vec_sib[...]
    for i in range(3):
        exchange(5 + i, vec_y.at[y], vec_y.at[y], g_gate.fore[i], t)
    rows_in.forward(0)
    g_out.merge()
    g_out.pool()
    g_qkv.merge()
    g_qkv.pool()
    g_down.merge()
    g_down.pool()
    for i in range(3):
        exchanged(5 + i, vec_y.at[lax.rem(y + 3 - i, 4)])
    copies[4].wait_send()
    vec[...] = functools.reduce(jnp.add, [vec_y[i] for i in range(4)])
    exchange(8, vec, vec_zz, g_gate.zz, t)
    g_gate.end()
    g_up.end()
    g_out.end()
    g_qkv.end()
    g_down.end()
    exchanged(8, vec_zz)
    totals[...] = vec[...] + vec_zz[...]
    rows_in.end(0)
    for w in range(3):
        rows_out.end(w)
    g_out.sent_away()
    g_qkv.sent_away()
    for k in (0, 1, 2, 5, 6, 7, 8):
        copies[k].wait_send()
    for part_of in (rows, rows_in, rows_out, *reduces):
        part_of.drain()


def back(hbm, vmem):
    def vec():
        return pltpu.VMEM((8, WIDE), F32)

    scratch = [pltpu.VMEM((8, SHARD, 1152), B16)] * 2
    for columns in GRADIENTS:
        scratch += reduce_scratch(columns)
    scratch += [
        pltpu.VMEM((3, 2, SLICE, WIDE), B16),
        pltpu.VMEM((3, SLICE, WIDE), B16),
        pltpu.VMEM((3, 2, 4, SLICE, WIDE), B16),
    ]
    scratch += rows_scratch(3)
    scratch += [pltpu.VMEM((1, 2, 4, SLICE, WIDE), B16)] + rows_scratch(1)
    scratch += rows_scratch(3)[4:] + [pltpu.VMEM((1, SLICE, WIDE), F32)]
    scratch += [pltpu.VMEM((4, 8, WIDE), F32), vec(), vec(), pltpu.VMEM((4, 8, WIDE), F32), vec(), vec()]
    scratch += [pltpu.SemaphoreType.DMA((9,))] * 2
    scratch += [
        pltpu.VMEM((3, 2, 64, HD), B16),
        pltpu.VMEM((16, 64, HD), B16),
        pltpu.VMEM((16, 64, HD), B16),
        pltpu.VMEM((2, 16, 64, HD), B16),
        pltpu.VMEM((4, 256, HD), F32),
        pltpu.VMEM((4, 256, HD), F32),
        pltpu.VMEM((3, 2, 64, HD), B16),
        pltpu.VMEM((2, 3, 2, 64, HD), B16),
        pltpu.SemaphoreType.DMA((6,)),
        pltpu.SemaphoreType.DMA((16,)),
        pltpu.SemaphoreType.DMA((16,)),
        pltpu.SemaphoreType.DMA((2, 16)),
        pltpu.SemaphoreType.DMA((6,)),
        pltpu.SemaphoreType.DMA((2, 6)),
        pltpu.SemaphoreType.DMA((2,)),
    ]
    return pl.pallas_call(
        back_kernel,
        name="back",
        out_shape=[
            struct((3, 2, 4, SLICE, WIDE), B16),
            struct((1, 2, 4, SLICE, WIDE), F32),
            struct((8, WIDE), F32),
        ]
        + [struct((SHARD, columns), F32) for columns in (1152, 1152, 1152, HD, HD, 128, 128)],
        in_specs=any_space(len(hbm)) + vmem_space(len(vmem)),
        out_specs=any_space(2) + vmem_space(8),
        scratch_shapes=scratch,
        compiler_params=params(4),
    )(*hbm, *vmem)


def level(codes, width):
    if width == 0:
        return codes
    stride = STRIDES[width]
    return jnp.floor(codes * B16(1.0 / stride)) * B16(stride) + B16(stride // 2)


def gelu_parts(value):
    slope = 0.7978845608028654
    inner = jnp.tanh(slope * (value + 0.044715 * value * value * value))
    grown = 0.5 * value * (1.0 + inner)
    rate = 0.5 * (1.0 + inner) + 0.5 * value * (1.0 - inner * inner) * slope * (
        1.0 + 3 * 0.044715 * value * value
    )
    return grown, rate


def side_by_side(*parts):
    total, first = 0.0, 0
    for part in parts:
        total = total + jnp.pad(part, (first, WIDE - first - part.shape[0]))
        first += part.shape[0]
    return total


def body(
    tokens,
    cotangent,
    segments,
    codes_query,
    codes_key,
    codes_value,
    codes_out,
    codes_gate,
    codes_up,
    codes_down,
    query_column_scale,
    key_column_scale,
    value_column_scale,
    output_column_scale,
    gate_column_scale,
    up_column_scale,
    down_column_scale,
    gain_first,
    gain_second,
    gain_third,
    gain_fourth,
):
    z_hi = lax.rem(lax.div(lax.axis_index("dp"), 2), 2)
    tokens = tokens.reshape(ROWS, WIDE)
    cotangent = cotangent.reshape(3, ROWS, WIDE)
    entries = [gain_first, gain_second, gain_third, gain_fourth, output_column_scale, down_column_scale]
    entries += [side_by_side(gate_column_scale, up_column_scale)]
    entries += [side_by_side(query_column_scale, key_column_scale, value_column_scale)]
    row = lax.broadcasted_iota(jnp.int32, (8, WIDE), 0)
    vectors = functools.reduce(
        lambda rest, i: jnp.where(row == i, entries[i][None], rest), range(7), entries[7][None]
    )
    shards = [
        jnp.concatenate([codes_query, codes_key, codes_value], 1).astype(B16),
        codes_out.astype(B16).T,
        codes_gate.astype(B16),
        codes_up.astype(B16),
        codes_down.astype(B16).T,
    ]

    documents = lax.dynamic_index_in_dim(segments, z_hi, 0, False)
    starts = jnp.sum((documents[None, :] < documents[:, None]).astype(jnp.int32), axis=1)
    place = jnp.arange(1024, dtype=jnp.int32)

    def blocked(rows):
        return rows.reshape(4, 16, 16).transpose(0, 2, 1).reshape(4, 256)

    first = blocked(starts).T
    expo = jnp.arange(HD // 2, dtype=F32) * (2.0 / HD)
    rates = jnp.power(ROPE_BASE, -expo)[None]

    grid = (3, 2, 4, SLICE, WIDE)
    w_qkv, w_out, attended, normed_input, qkv_pre, q_rot, k_rot, v_all, branch, middle, cosine, sine, *rest = (
        forward_pass(
            *shards,
            tokens,
            vectors,
            blocked(place - starts).astype(F32).T,
            first,
            rates,
            cotangent.reshape(grid),
        )
    )
    d_part, turned_middle, turned_feed, d_gu, hidden, final, feed_sums, gu_sums = rest
    flat = (3 * ROWS, -1)
    results, input_gradient, totals, g_gate, g_up, g_down, g_out, g_query, g_key, g_value = back(
        [d_part, cotangent.reshape(grid)],
        [
            turned_middle,
            turned_feed,
            d_gu.reshape(flat),
            hidden.reshape(flat),
            middle,
            branch,
            final,
            feed_sums,
            gu_sums,
            w_out,
            w_qkv,
            vectors,
            tokens,
            attended.reshape(flat),
            normed_input,
            qkv_pre,
            first,
            cosine,
            sine,
            q_rot,
            k_rot,
            v_all,
        ],
    )
    rows = lax.dynamic_slice_in_dim(totals, lax.axis_index("dp") * SHARD, SHARD, 1)
    return (
        results.reshape(3, 2, 64, 1, WIDE),
        input_gradient.reshape(2, 64, 1, WIDE),
        g_query,
        g_key,
        g_value,
        g_out.T,
        g_gate,
        g_up,
        g_down.T,
        totals[7, :256],
        totals[7, 256:384],
        totals[7, 384:512],
        rows[4],
        totals[6, :FF],
        totals[6, FF:],
        rows[5],
        rows[0],
        rows[1],
        rows[2],
        rows[3],
    )


def solution(mesh):
    matrix, turned = P("dp", "tensor"), P("tensor", "dp")
    columns, whole, shard = P("tensor"), P(), P("dp")
    in_specs = (
        P(None, None, "dp", None),
        P(None, None, None, "dp", None),
        whole,
        *(matrix, matrix, matrix, turned, matrix, matrix, turned),
        *(columns, columns, columns, whole, columns, columns, whole),
        *(whole, whole, whole, whole),
    )
    out_specs = (
        P(None, None, None, "dp", None),
        P(None, None, "dp", None),
        *(matrix, matrix, matrix, turned, matrix, matrix, turned),
        *(columns, columns, columns, shard, columns, columns, shard),
        *(shard, shard, shard, shard),
    )
    return jax.shard_map(body, mesh=mesh, in_specs=in_specs, out_specs=out_specs, check_vma=False)
```

```python
import functools

import jax
import jax.numpy as jnp
from jax import lax
from jax.experimental import pallas as pl
from jax.experimental.pallas import tpu as pltpu
from jax.sharding import PartitionSpec as P

MESH = pl.DeviceIdType.MESH
F32 = jnp.float32
B16 = jnp.bfloat16
EPSILON = 1e-06
SOFTCAP = 50.0
ROPE_BASE = 10000.0
MASKED = -1e30
HD = 256
WIDE = 2304
FF = 1152
STRIDES = (1, 16, 64)
SCALE_OUT, SCALE_DOWN, SCALE_GU, SCALE_QKV = (slice(i, i + 1) for i in range(4, 8))
SHARD = 144
LOW = 64
HIGH = SHARD - LOW
TENSOR = 8
ROWS = 128
SLICE = ROWS // TENSOR
VMEM_BYTES = 63 * 2**20


def here():
    dp = lax.axis_index("dp")
    return lax.div(dp, 4), lax.rem(lax.div(dp, 2), 2), lax.rem(dp, 2), lax.axis_index("tensor")


def rank(y, z_hi, core):
    return (y * 2 + z_hi) * 2 + core


def remote(src, dst, send, recv, dp, tensor):
    return pltpu.make_async_remote_copy(
        src, dst, send, recv, device_id=(dp, tensor), device_id_type=MESH
    )


def greet(devices):
    barrier = pltpu.get_barrier_semaphore()
    for device in devices:
        pl.semaphore_signal(barrier, inc=1, device_id=device, device_id_type=MESH)
    pl.semaphore_wait(barrier, len(devices))


def struct(shape, dtype):
    return jax.ShapeDtypeStruct(shape, dtype)


def any_space(count):
    return [pl.BlockSpec(memory_space=pl.ANY)] * count


def vmem_space(count):
    return [pl.BlockSpec(memory_space=pltpu.VMEM)] * count


def params(collective_id):
    return pltpu.CompilerParams(
        collective_id=collective_id, has_side_effects=True, vmem_limit_bytes=VMEM_BYTES
    )


class Gather:
    def __init__(self, src, out, send, recv, local):
        self.src, self.out, self.send, self.recv, self.local = src, out, send, recv, local
        self.y, self.zh, self.core, self.t = here()
        y, zh, core = self.y, self.zh, self.core
        self.me, self.sib, self.zz = rank(y, zh, core), rank(y, zh, 1 - core), rank(y, 1 - zh, core)
        self.fore = [rank(lax.rem(y + dy, 4), zh, core) for dy in (1, 2, 3)]
        self.behind = [lax.rem(y + 4 - dy, 4) for dy in (1, 2, 3)]
        self.low, self.high = pl.ds(0, LOW), pl.ds(LOW, HIGH)
        self.started = []

    def push(self, slot, src, dst, dp):
        copy = remote(src, dst, self.send.at[slot], self.recv.at[slot], dp, self.t)
        copy.start()
        self.started.append(copy)

    def arrive(self, slot, ref):
        remote(ref, ref, self.send.at[slot], self.recv.at[slot], self.sib, self.t).wait_recv()

    def start(self):
        src, mine = self.src, self.out.at[self.me]
        self.mine = pltpu.make_async_copy(src, mine, self.local)
        self.mine.start()
        low, high = self.low, self.high
        self.push(0, src.at[low], self.out.at[self.me, low], self.zz)
        for i in range(3):
            self.push(4 + i, src.at[high], self.out.at[self.me, high], self.fore[i])
        for i in range(3):
            self.push(1 + i, src.at[low], self.out.at[self.me, low], self.fore[i])
        self.push(7, src.at[high], self.out.at[self.me, high], self.zz)
        self.push(14, src, mine, self.sib)

    def over_y(self):
        block = self.out.at[self.zz, self.low]
        self.arrive(0, block)
        for i in range(3):
            self.push(8 + i, block, block, self.fore[i])
        self.push(15, block, block, self.sib)

    def over_z(self):
        for i in range(3):
            block = self.out.at[rank(self.behind[i], self.zh, self.core), self.high]
            self.arrive(4 + i, block)
            self.push(11 + i, block, block, self.zz)
            self.push(16 + i, block, block, self.sib)

    def near(self):
        for i in range(3):
            block = self.out.at[rank(self.behind[i], self.zh, self.core), self.low]
            self.arrive(1 + i, block)
            self.push(19 + i, block, block, self.sib)
        block = self.out.at[self.zz, self.high]
        self.arrive(7, block)
        self.push(22, block, block, self.sib)

    def far(self):
        for i in range(3):
            dp = rank(self.behind[i], 1 - self.zh, self.core)
            for slot, rows in ((0, self.low), (3, self.high)):
                block = self.out.at[dp, rows]
                self.arrive(8 + slot + i, block)
                self.push(23 + slot + i, block, block, self.sib)

    def end(self):
        out, low, high, other = self.out, self.low, self.high, 1 - self.core
        self.arrive(14, out.at[self.sib])
        far = rank(self.y, 1 - self.zh, other)
        self.arrive(15, out.at[far, low])
        self.arrive(22, out.at[far, high])
        for i in range(3):
            near, far = (rank(self.behind[i], zh, other) for zh in (self.zh, 1 - self.zh))
            self.arrive(16 + i, out.at[near, high])
            self.arrive(19 + i, out.at[near, low])
            self.arrive(23 + i, out.at[far, low])
            self.arrive(26 + i, out.at[far, high])
        self.mine.wait()

    def drain(self):
        for copy in self.started:
            copy.wait_send()


class Rows:
    def __init__(self, part, held_x, held_z, stage, block, out, sems, own=None, turned=None):
        self.part, self.own, self.out, self.block = part, own, out, block
        self.held_x, self.held_z, self.stage = held_x, held_z, stage
        self.send, self.recv, self.local = sems
        self.turned = turned
        self.split = WIDE if turned is None else WIDE - turned[0].shape[-1]
        self.low, self.high = pl.ds(0, self.split), pl.ds(self.split, WIDE - self.split)
        self.dp, self.t = lax.axis_index("dp"), lax.axis_index("tensor")
        self.zl, self.x = lax.div(self.t, 4), lax.rem(self.t, 4)
        self.ahead = [lax.rem(self.x + k, 4) for k in (1, 2, 3)]
        self.behind = [lax.rem(self.x + 4 - k, 4) for k in (1, 2, 3)]
        self.x_peers = [self.zl * 4 + x for x in self.ahead]
        self.z_peer = (1 - self.zl) * 4 + self.x
        self.started = []

    def peers(self):
        return [(self.dp, t) for t in self.x_peers + [self.z_peer]]

    def push(self, w, slot, src, dst, t):
        copy = remote(src, dst, self.send.at[w, slot], self.recv.at[w, slot], self.dp, t)
        copy.start()
        self.started.append(copy)

    def arrive(self, w, slot, ref):
        remote(
            ref, ref, self.send.at[w, slot], self.recv.at[w, slot], self.dp, self.z_peer
        ).wait_recv()

    def scatter_x(self, w):
        low, high = self.low, self.high
        for k in range(3):
            self.push(
                w,
                1 + k,
                self.part.at[w, :, self.ahead[k], :, low],
                self.held_x.at[w, k, :, :, low],
                self.x_peers[k],
            )
        if self.turned is not None:
            self.push(
                w, 11, self.part.at[w, 1 - self.zl, :, :, high], self.turned[0].at[w], self.z_peer
            )

    def summed_x(self, w, zl):
        own = self.part[w, zl, self.x] if self.own is None else self.own[w, zl]
        total = own[:, : self.split].astype(F32)
        for k in range(3):
            total = total + self.held_x[w, k, zl, :, : self.split].astype(F32)
        return total

    def summed_z(self, w, x):
        part = self.part[w, self.zl, x, :, self.split :].astype(F32)
        return part + self.turned[0][w, x].astype(F32)

    def scatter_z(self, w):
        for k in range(3):
            self.arrive(w, 1 + k, self.held_x.at[w, k, :, :, self.low])
        self.stage[w, :, : self.split] = self.summed_x(w, 1 - self.zl).astype(B16)
        self.push(w, 0, self.stage.at[w, :, self.low], self.held_z.at[w, :, self.low], self.z_peer)
        if self.turned is not None:
            held, stage, last = self.turned
            self.arrive(w, 11, held.at[w])
            for k in range(3):
                stage[w, k] = self.summed_z(w, self.ahead[k]).astype(B16)
                self.push(w, 12 + k, stage.at[w, k], last.at[w, k], self.x_peers[k])

    def total(self, w):
        self.arrive(w, 0, self.held_z.at[w, :, self.low])
        low = self.summed_x(w, self.zl) + self.held_z[w, :, : self.split].astype(F32)
        if self.turned is None:
            return low
        high = self.summed_z(w, self.x)
        for k in range(3):
            self.arrive(w, 12 + k, self.turned[2].at[w, k])
            high = high + self.turned[2][w, k].astype(F32)
        return jnp.concatenate([low, high], -1)

    def spread(self, w):
        block, mine = self.block.at[w], self.out.at[w, self.zl, self.x]
        self.push(w, 4, block.at[:, self.low], mine.at[:, self.low], self.z_peer)
        for k in range(3):
            self.push(w, 5 + k, block, mine, self.x_peers[k])
        pltpu.make_async_copy(block, mine, self.local.at[w]).start()

    def forward(self, w):
        block = self.out.at[w, 1 - self.zl, self.x, :, self.low]
        self.arrive(w, 4, block)
        for k in range(3):
            self.push(w, 8 + k, block, block, self.x_peers[k])
        if self.turned is not None:
            self.near(w)
            blocks = self.out.at[w, self.zl, :, :, self.high]
            self.push(w, 15, blocks, blocks, self.z_peer)

    def near(self, w):
        for k in range(3):
            self.arrive(w, 5 + k, self.out.at[w, self.zl, self.behind[k]])
        pltpu.make_async_copy(
            self.block.at[w], self.out.at[w, self.zl, self.x], self.local.at[w]
        ).wait()

    def end(self, w):
        for k in range(3):
            self.arrive(w, 8 + k, self.out.at[w, 1 - self.zl, self.behind[k], :, self.low])
        if self.turned is None:
            self.near(w)
        else:
            self.arrive(w, 15, self.out.at[w, 1 - self.zl, :, :, self.high])

    def drain(self):
        for copy in self.started:
            copy.wait_send()


def turned_scratch(columns):
    return [
        pltpu.VMEM((3, 4, SLICE, columns), B16),
        pltpu.VMEM((3, 3, SLICE, columns), B16),
        pltpu.VMEM((3, 3, SLICE, columns), B16),
    ]


def rows_scratch(depth):
    return [
        pltpu.VMEM((depth, 3, 2, SLICE, WIDE), B16),
        pltpu.VMEM((depth, SLICE, WIDE), B16),
        pltpu.VMEM((depth, SLICE, WIDE), B16),
        pltpu.VMEM((depth, SLICE, WIDE), B16),
        pltpu.SemaphoreType.DMA((depth, 16)),
        pltpu.SemaphoreType.DMA((depth, 16)),
        pltpu.SemaphoreType.DMA((depth,)),
    ]


class Reduce:
    def __init__(self, columns, away, own, sibs, yrecv, zrecv, ylast, zlast, out, send, recv):
        self.columns, self.away, self.own, self.sibs = columns, away, own, sibs
        self.yrecv, self.zrecv, self.ylast, self.zlast, self.out = yrecv, zrecv, ylast, zlast, out
        self.send, self.recv = send, recv
        self.y, self.zh, self.core, self.t = here()
        y, zh, core = self.y, self.zh, self.core
        self.sib, self.zz = rank(y, zh, 1 - core), rank(y, 1 - zh, core)
        self.ahead = [lax.rem(y + dy, 4) for dy in (1, 2, 3)]
        self.fore = [rank(place, zh, core) for place in self.ahead]
        self.started = []

    def push(self, slot, src, dst, dp):
        copy = remote(src, dst, self.send.at[slot], self.recv.at[slot], dp, self.t)
        copy.start()
        self.started.append(copy)

    def arrive(self, slot, ref):
        remote(ref, ref, self.send.at[slot], self.recv.at[slot], self.sib, self.t).wait_recv()

    def store(self, first, count, cols, block):
        block = block.astype(B16).reshape(count, 2, SHARD, block.shape[-1])
        even = self.core == 0
        chips = pl.ds(first, count)
        self.own[chips, :, cols] = jnp.where(even, block[:, 0], block[:, 1])
        self.away[chips, :, cols] = jnp.where(even, block[:, 1], block[:, 0])

    def to_sibling(self, place):
        pair = pl.ds(place * 2, 2)
        return remote(
            self.away.at[pair, :, pl.ds(0, self.columns)],
            self.sibs.at[pair],
            self.send.at[place],
            self.recv.at[place],
            self.sib,
            self.t,
        )

    def product(self, turned, right, left_columns=0):
        for place in range(4):
            rows = slice(place * 4 * SHARD, (place + 1) * 4 * SHARD)
            for i in range(self.columns // 384):
                cols = slice(384 * i, 384 * i + 384)
                block = dot(turned[rows], right[:, left_columns + 384 * i : left_columns + 384 * i + 384], 1, 0)
                self.store(place * 2, 2, cols, block)

    def send_away(self):
        for place in range(4):
            self.to_sibling(place).start()

    def product_whole(self, left, right):
        for i in range(self.columns // HD):
            cols = slice(HD * i, HD * i + HD)
            self.store(0, 8, cols, dot(left, right[:, cols], 0, 0))
        self.send_away()

    def sent_away(self):
        for place in range(4):
            self.to_sibling(place).wait_send()

    def add(self):
        own, sibs = self.own, self.sibs
        for i, place in enumerate(self.ahead + [self.y]):
            pair = pl.ds(place * 2, 2)
            self.arrive(place, sibs.at[pair])

            def step(step, _, place=place):
                chip = place * 2 + lax.div(step, SHARD // 48)
                rows = pl.ds(pl.multiple_of(lax.rem(step, SHARD // 48) * 48, 16), 48)
                own[chip, rows] = own[chip, rows] + sibs[chip, rows]
                return 0

            lax.fori_loop(0, 2 * SHARD // 48, step, 0)
            if i < 3:
                self.push(4 + i, own.at[pair, pl.ds(0, LOW)], self.yrecv.at[i], self.fore[i])

    def cross(self):
        for i, place in enumerate(self.ahead + [self.y]):
            block = self.own.at[place * 2 + 1 - self.zh, pl.ds(LOW, HIGH)]
            self.push(7 + i, block, self.zrecv.at[place], self.zz)

    def merge(self):
        own, zrecv = self.own, self.zrecv
        for i, place in enumerate(self.ahead + [self.y]):
            self.arrive(7 + i, zrecv.at[place])

            def step(step, _, place=place):
                rows = pl.ds(pl.multiple_of(step * 16, 16), 16)
                mine = pl.ds(pl.multiple_of(step * 16 + LOW, 16), 16)
                zrecv[place, rows] = zrecv[place, rows] + own[place * 2 + self.zh, mine]
                return 0

            lax.fori_loop(0, HIGH // 16, step, 0)
            if i < 3:
                self.push(11 + i, zrecv.at[place], self.ylast.at[i], self.fore[i])

    def pool(self):
        for i in range(3):
            self.arrive(4 + i, self.yrecv.at[i])

        def step(step, _):
            chip = lax.div(step, LOW // 16)
            rows = pl.ds(pl.multiple_of(lax.rem(step, LOW // 16) * 16, 16), 16)
            total = self.own[self.y * 2 + chip, rows].astype(F32)
            for i in range(3):
                total = total + self.yrecv[i, chip, rows].astype(F32)
            self.own[self.y * 2 + chip, rows] = total.astype(B16)
            return 0

        lax.fori_loop(0, 2 * LOW // 16, step, 0)
        self.push(14, self.own.at[self.y * 2 + 1 - self.zh, pl.ds(0, LOW)], self.zlast, self.zz)

    def write(self, rows, total):
        first = 0
        for out in self.out if isinstance(self.out, tuple) else (self.out,):
            out[rows] = total[:, first : first + out.shape[-1]]
            first += out.shape[-1]

    def end(self):
        self.arrive(14, self.zlast)

        def low(step, _):
            rows = pl.ds(pl.multiple_of(step * 16, 16), 16)
            own = self.own[self.y * 2 + self.zh, rows].astype(F32)
            self.write(rows, own + self.zlast[rows].astype(F32))
            return 0

        lax.fori_loop(0, LOW // 16, low, 0)
        for i in range(3):
            self.arrive(11 + i, self.ylast.at[i])

        def high(step, _):
            rows = pl.ds(pl.multiple_of(step * 16, 16), 16)
            total = self.zrecv[self.y, rows].astype(F32)
            for i in range(3):
                total = total + self.ylast[i, rows].astype(F32)
            self.write(pl.ds(pl.multiple_of(step * 16 + LOW, 16), 16), total)
            return 0

        lax.fori_loop(0, HIGH // 16, high, 0)

    def drain(self):
        for copy in self.started:
            copy.wait_send()


def reduce_scratch(columns):
    return [
        pltpu.VMEM((8, SHARD, columns), B16),
        pltpu.VMEM((8, SHARD, columns), B16),
        pltpu.VMEM((3, 2, LOW, columns), B16),
        pltpu.VMEM((4, HIGH, columns), B16),
        pltpu.VMEM((3, HIGH, columns), B16),
        pltpu.VMEM((LOW, columns), B16),
        pltpu.SemaphoreType.DMA((15,)),
        pltpu.SemaphoreType.DMA((15,)),
    ]


def inverse_rms(signal):
    return lax.rsqrt(jnp.mean(signal * signal, axis=-1, keepdims=True) + EPSILON)


def norm_back(normed, inverse, gain, upstream):
    inner = upstream * (1.0 + gain)
    return inverse * (inner - normed * jnp.mean(inner * normed, axis=-1, keepdims=True))


def half_level(codes, width):
    return codes if width == 0 else jnp.floor(codes * B16(1.0 / STRIDES[width]))


def offset(left, width):
    return 0.0 if width == 0 else 0.5 * jnp.sum(left.astype(F32), axis=-1, keepdims=True)


def unit_owner(micro, width):
    return rank(width, micro, 0)


def rotate(signal, cosine, sine):
    former, latter = signal[:, : HD // 2], signal[:, HD // 2 :]
    return jnp.concatenate([former * cosine - latter * sine, latter * cosine + former * sine], -1)


def unrotate(signal, cosine, sine):
    former, latter = signal[:, : HD // 2], signal[:, HD // 2 :]
    return jnp.concatenate([former * cosine + latter * sine, latter * cosine - former * sine], -1)


def block_scores(queries, keys, first, b, kb):
    scores = lax.dot_general(queries, keys, (((1,), (1,)), ((), ())), preferred_element_type=F32)
    bent = jnp.tanh(scores * (0.0625 / SOFTCAP))
    lane = lax.broadcasted_iota(jnp.int32, (256, 256), 1)
    row = lax.broadcasted_iota(jnp.int32, (256, 256), 0)
    key_place = (16 * kb + (lane & 15)) * 16 + (lane >> 4)
    query_place = (16 * b + (row & 15)) * 16 + (row >> 4)
    allowed = (key_place >= first) & (key_place <= query_place)
    return bent, jnp.where(allowed, SOFTCAP * bent, MASKED)


def block_probs(queries, keys, first, b):
    pieces = [
        block_scores(queries, keys[kb], first, b, kb) for kb in range(max(0, b - 2), b + 1)
    ]
    peak = functools.reduce(
        jnp.maximum, [jnp.max(capped, axis=-1, keepdims=True) for _, capped in pieces]
    )
    exps = [jnp.exp(capped - peak) for _, capped in pieces]
    total = functools.reduce(jnp.add, [jnp.sum(e, axis=-1, keepdims=True) for e in exps])
    return [bent for bent, _ in pieces], [e / total for e in exps]


def dot(left, right, left_dim, right_dim):
    return lax.dot_general(
        left, right, (((left_dim,), (right_dim,)), ((), ())), preferred_element_type=F32
    )


def forward_kernel(*refs):
    (c_query, c_key, c_value, c_out, c_gate, c_up, c_down), refs = refs[:7], refs[7:]
    (tokens, vectors, places, first, rates, cotangent), refs = refs[:6], refs[6:]
    (w_qkv, w_out), refs = refs[:2], refs[2:]
    homes, refs = refs[:13], refs[13:]
    (q_rot, k_rot, v_all, sums, gu_sums), refs = refs[:5], refs[5:]
    kept, refs = refs[:13], refs[13:]
    (att, normed_input, qkv_pre, branch, middle, cosine, sine), (d_part, *late) = kept[:7], kept[7:]
    turned_middle, turned_feed, d_gu_low, hidden, final = late
    (s_qkv, s_gate, s_up, keep_sems), refs = refs[:4], refs[4:]
    shards = (s_qkv, c_out, s_gate, s_up, c_down)
    gains, scale_out, scale_qkv = vectors[0:4], vectors[SCALE_OUT], vectors[SCALE_QKV, : 2 * HD]
    scale_down, scale_gu = vectors[SCALE_DOWN], vectors[SCALE_GU]
    (wq, wo, low, rq, rkv, held, part), refs = refs[:7], refs[7:]
    (held_x, held_z, stage, block, *row_sems), refs = refs[:7], refs[7:]
    (wg, wu, wd, nm, gu_pre, feed_part, cot, d_feed, dgs), refs = refs[:9], refs[9:]
    (held_x_f, held_z_f, stage_f, feed_block, *feed_sems), refs = refs[:7], refs[7:]
    turned, refs = refs[:3], refs[3:]
    (send_g, recv_g, local_g, send, recv_q, recv_kv, send_back, recv_back, local) = refs
    y, zh, core, t = here()
    me = rank(y, zh, core)
    half = lax.rem(t, 2)
    other = t + 1 - 2 * half
    owner = (y < 3) & (core == 0)
    units = [(m, w) for m in range(2) for w in range(3)]
    gathers = [
        Gather(src, out, send_g.at[k], recv_g.at[k], local_g.at[k])
        for k, (src, out) in enumerate(zip(shards, (wq, wo, wg, wu, wd)))
    ]
    g_qkv, g_out, g_gate, g_up, g_down = gathers
    rows = Rows(part, held_x, held_z, stage, block, nm, row_sems)
    feeds = Rows(feed_part, held_x_f, held_z_f, stage_f, feed_block, d_feed, feed_sems, None, turned)
    barrier = pltpu.get_barrier_semaphore()

    def signal(dp, tensor):
        pl.semaphore_signal(barrier, inc=1, device_id=(dp, tensor), device_id_type=MESH)

    plane = [(g_qkv.sib, t), (g_qkv.zz, t)] + [(dp, t) for dp in g_qkv.fore] + rows.peers()
    for device in plane:
        signal(*device)

    @pl.when(owner)
    def _():
        def each(d, _):
            pl.when(d != me)(lambda: signal(d, t))
            signal(d, other)
            return 0

        lax.fori_loop(0, 16, each, 0)

    for m, w in units:
        pl.when(unit_owner(m, w) != me)(functools.partial(signal, unit_owner(m, w), t))

    s_qkv[:, :HD] = c_query[...].astype(B16)
    s_qkv[:, HD : HD + 128] = c_key[...].astype(B16)
    s_qkv[:, HD + 128 :] = c_value[...].astype(B16)
    s_gate[...] = c_gate[...].astype(B16)
    s_up[...] = c_up[...].astype(B16)
    inputs = tokens[...].astype(F32)
    normed_input[...] = (inputs * inverse_rms(inputs) * (1.0 + gains[0:1])).astype(B16)
    keeps = []

    def keep(i, index=None):
        src, dst = (kept[i], homes[i]) if index is None else (kept[i].at[index], homes[i].at[index])
        copy = pltpu.make_async_copy(src, dst, keep_sems.at[len(keeps)])
        copy.start()
        keeps.append(copy)

    @pl.when(owner)
    def _():
        pl.semaphore_wait(barrier, len(plane) + 26)

    @pl.when(jnp.logical_not(owner))
    def _():
        pl.semaphore_wait(barrier, len(plane) + 12)

    g_qkv.start()
    for b in range(4):
        angle = places[:, b : b + 1] * rates[...]
        cosine[b], sine[b] = jnp.cos(angle), jnp.sin(angle)
    g_qkv.over_y()
    g_qkv.over_z()
    g_qkv.near()
    g_out.start()
    g_gate.start()
    g_qkv.far()
    g_qkv.end()

    for i in range(2):
        cols = slice(HD * i, HD * i + HD)
        codes = wq[:, :, cols].reshape(WIDE, HD)
        for w in range(3):
            product = dot(normed_input[...], level(codes, w), 1, 0) * scale_qkv[:, cols]
            qkv_pre[w, :, cols] = product
            low[w, :, :, cols] = product.astype(B16).reshape(2, 64, HD)

    def to_owner(u, m, w, start):
        o = unit_owner(m, w)
        q_src, kv_src = low.at[w, m, :, pl.ds(0, HD)], low.at[w, m, :, pl.ds(HD, HD)]
        across = remote(kv_src, rkv.at[half, me], send.at[u, 2], recv_kv.at[half, me], o, other)
        away = [
            remote(q_src, rq.at[me], send.at[u, 0], recv_q.at[me], o, t),
            remote(kv_src, rkv.at[half, me], send.at[u, 1], recv_kv.at[half, me], o, t),
        ]
        near = [
            pltpu.make_async_copy(q_src, rq.at[me], local.at[0]),
            pltpu.make_async_copy(kv_src, rkv.at[half, me], local.at[1]),
        ]

        @pl.when(o != me)
        def _():
            for copy in away:
                copy.start() if start else copy.wait_send()

        @pl.when(o == me)
        def _():
            for copy in near:
                copy.start() if start else copy.wait()

        across.start() if start else across.wait_send()

    for u, (m, w) in enumerate(units):
        to_owner(u, m, w, True)
    for gather in (g_out, g_gate):
        gather.over_y()
        gather.over_z()

    @pl.when(owner)
    def _():
        for u, (m, w) in enumerate(units):

            @pl.when(unit_owner(m, w) == me)
            def _():
                for i in range(2):
                    ref = (rq.at[me], rkv.at[half, me])[i]
                    pltpu.make_async_copy(ref, ref, local.at[i]).wait()

        def each(d, _):
            @pl.when(d != me)
            def _():
                remote(rq.at[d], rq.at[d], send.at[0, 0], recv_q.at[d], me, other).wait_recv()
                remote(
                    rkv.at[half, d], rkv.at[half, d], send.at[0, 0], recv_kv.at[half, d], me, other
                ).wait_recv()

            remote(
                rkv.at[1 - half, d], rkv.at[1 - half, d], send.at[0, 0], recv_kv.at[1 - half, d], me, other
            ).wait_recv()
            return 0

        lax.fori_loop(0, 16, each, 0)
        for b in range(4):
            rows_b = slice(16 * b, 16 * b + 16)
            c, s = cosine[b], sine[b]
            q = rq[:, rows_b, :].reshape(256, HD).astype(F32)
            q_rot[b] = rotate(q, c, s).astype(B16)
            k = jnp.concatenate(
                [rkv[i, :, rows_b, : HD // 2].reshape(256, HD // 2) for i in range(2)], -1
            )
            k_rot[b] = rotate(k.astype(F32), c, s).astype(B16)
            v_all[b] = jnp.concatenate(
                [rkv[i, :, rows_b, HD // 2 :].reshape(256, HD // 2) for i in range(2)], -1
            )
        for b in range(4):
            keys = {kb: k_rot[kb] for kb in range(max(0, b - 2), b + 1)}
            _, probs = block_probs(q_rot[b], keys, first[:, b : b + 1], b)
            out = sum(
                dot(p.astype(B16), v_all[kb], 1, 0) for p, kb in zip(probs, sorted(keys))
            )
            held[:, 16 * b : 16 * b + 16, :] = out.astype(B16).reshape(16, 16, HD)

        def hand_back(d, start):
            @pl.when(d != me)
            def _():
                copy = remote(
                    held.at[d], att.at[y, zh], send_back.at[d], recv_back.at[zh * 3 + y], d, t
                )
                copy.start() if start else copy.wait_send()

            @pl.when(d == me)
            def _():
                copy = pltpu.make_async_copy(held.at[d], att.at[y, zh], local.at[0])
                copy.start() if start else copy.wait()

        lax.fori_loop(0, 16, lambda d, _: (hand_back(d, True), 0)[1], 0)
        lax.fori_loop(0, 16, lambda d, _: (hand_back(d, False), 0)[1], 0)

    g_out.near()
    g_out.far()
    g_up.start()
    g_out.end()
    g_gate.near()
    for u, (m, w) in enumerate(units):

        @pl.when(unit_owner(m, w) != me)
        def _():
            ref = att.at[w, m]
            remote(ref, ref, send.at[0, 0], recv_back.at[u], me, other).wait_recv()

    codes = wo[...].reshape(WIDE, HD)
    for w in range(3):
        product = dot(att[w].reshape(ROWS, HD), level(codes, w), 1, 1) * scale_out
        part[w] = product.astype(B16).reshape(2, 4, SLICE, WIDE)
        rows.scatter_x(w)
    for i, (src, dst) in enumerate(((wq, w_qkv), (wo, w_out))):
        keeps.append(pltpu.make_async_copy(src, dst, keep_sems.at[i]))
        keeps[i].start()
    for i in (0, 1, 2, 5, 6):
        keep(i)
    load = pltpu.make_async_copy(cotangent.at[:, rows.zl, rows.x], cot, local.at[2])
    load.start()
    g_gate.far()
    g_up.over_y()
    g_up.over_z()
    g_down.start()
    for w in range(3):
        rows.scatter_z(w)
    mine = tokens[pl.ds(pl.multiple_of(t * SLICE, SLICE), SLICE)].astype(F32)
    for w in range(3):
        signal_w = rows.total(w)
        branch[w] = signal_w
        total = mine + signal_w * inverse_rms(signal_w) * (1.0 + gains[1:2])
        middle[w] = total
        block[w] = (total * inverse_rms(total) * (1.0 + gains[2:3])).astype(B16)
        rows.spread(w)
    keep(3)
    keep(4)
    g_up.near()
    for w in range(3):
        rows.forward(w)
    g_down.over_y()
    g_down.over_z()
    g_up.far()
    g_gate.end()
    g_up.end()

    def forward(w):
        stride = STRIDES[w]
        left = nm[w].reshape(ROWS, WIDE)
        extra = offset(left, w)
        for k, codes in enumerate((wg, wu)):
            cols = slice(FF * k, FF * k + FF)
            product = dot(left, half_level(codes[...].reshape(WIDE, FF), w), 1, 0)
            gu_pre[w, :, cols] = (product + extra) * (scale_gu[:, cols] * stride)
        gate_pre, up_pre = gu_pre[w, :, :FF], gu_pre[w, :, FF:]
        grown, _ = gelu_parts(gate_pre)
        low = (grown * up_pre).astype(B16)
        hidden[w] = low
        extra_down = offset(low, w)

        if w == 0:
            g_down.far()
            g_down.end()
        product = dot(low, half_level(wd[...].reshape(WIDE, FF), w), 1, 1)
        product = (product + extra_down) * (scale_down * stride)
        feed_part[w] = product.astype(B16).reshape(2, 4, SLICE, WIDE)
        feeds.scatter_x(w)

    def norm(w):
        signal = feeds.total(w)
        inverse = inverse_rms(signal)
        normed = signal * inverse
        upstream = cot[w].astype(F32)
        lowered = norm_back(normed, inverse, gains[3:4], upstream).astype(B16)
        feed_block[w] = lowered
        feeds.spread(w)
        final[w] = (middle[w] + normed * (1.0 + gains[3:4])).astype(B16)
        for i, term in enumerate((upstream * normed, lowered.astype(F32) * signal)):
            term = jnp.sum(term, axis=0, keepdims=True)
            sums[i : i + 1] = term if w == 0 else sums[i : i + 1] + term

    def backward(w):
        stride = STRIDES[w]
        lowered = d_feed[w].reshape(ROWS, WIDE)
        turned_feed[:, w * ROWS : (w + 1) * ROWS] = lowered.T
        scaled = (lowered.astype(F32) * scale_down).astype(B16)
        extra = offset(scaled, w)
        for i in range(3):
            cols = slice(384 * i, 384 * i + 384)
            ups = slice(FF + 384 * i, FF + 384 * i + 384)
            d_hidden = (dot(scaled, half_level(wd[:, :, cols].reshape(WIDE, 384), w), 1, 0) + extra) * float(stride)
            grown, rate = gelu_parts(gu_pre[w, :, cols])
            for where, value in ((cols, d_hidden * gu_pre[w, :, ups] * rate), (ups, d_hidden * grown)):
                low = value.astype(B16)
                d_gu_low[w, :, where] = low
                dgs[:, where] = (value * scale_gu[:, where]).astype(B16)
                term = jnp.sum(low.astype(F32) * gu_pre[w, :, where], axis=0, keepdims=True)
                term = term / scale_gu[:, where]
                gu_sums[:, where] = term if w == 0 else gu_sums[:, where] + term
        left = dgs[...]
        extra_gu = offset(left, w)

        keep(10, w)
        keep(9, (slice(None), pl.ds(w * ROWS, ROWS)))
        product = sum(
            dot(left[:, FF * k : FF * k + FF], half_level(codes[...].reshape(WIDE, FF), w), 1, 1)
            for k, codes in enumerate((wg, wu))
        )
        product = (product + extra_gu) * float(stride)
        d_part[w] = product.astype(B16).reshape(2, 4, SLICE, WIDE)
        keep(7, w)

    rows.end(0)
    g_down.near()
    forward(0)
    rows.end(1)
    forward(1)
    feeds.scatter_z(0)
    rows.end(2)
    forward(2)
    load.wait()
    feeds.scatter_z(1)
    norm(0)
    feeds.scatter_z(2)
    norm(1)
    feeds.forward(0)
    norm(2)
    feeds.forward(1)
    for w in range(3):
        turned_middle[:, w * ROWS : (w + 1) * ROWS] = nm[w].reshape(ROWS, WIDE).T
    for i in (8, 11, 12):
        keep(i)
    feeds.end(0)
    backward(0)
    feeds.forward(2)
    feeds.end(1)
    backward(1)
    feeds.end(2)
    backward(2)
    for copy in keeps:
        copy.wait()
    for u, (m, w) in enumerate(units):
        o = unit_owner(m, w)

        @pl.when(o != me)
        def _():
            for slot, src in enumerate((low.at[w, m, :, pl.ds(0, HD)], low.at[w, m, :, pl.ds(HD, HD)])):
                remote(src, src, send.at[u, slot], recv_q.at[0], o, t).wait_send()

        src = low.at[w, m, :, pl.ds(HD, HD)]
        remote(src, src, send.at[u, 2], recv_q.at[0], o, other).wait_send()
    rows.drain()
    feeds.drain()
    for gather in gathers:
        gather.drain()


KEPT = (
    ((3, 2, 64, HD), B16),
    ((ROWS, WIDE), B16),
    ((3, ROWS, 2 * HD), F32),
    ((3, SLICE, WIDE), F32),
    ((3, SLICE, WIDE), F32),
    ((4, 256, HD // 2), F32),
    ((4, 256, HD // 2), F32),
    ((3, 2, 4, SLICE, WIDE), B16),
    ((WIDE, 3 * ROWS), B16),
    ((WIDE, 3 * ROWS), B16),
    ((3, ROWS, 2 * FF), B16),
    ((3, ROWS, FF), B16),
    ((3, SLICE, WIDE), B16),
)


def forward_pass(*operands):
    return pl.pallas_call(
        forward_kernel,
        name="forward",
        out_shape=[struct((16, SHARD, 2 * HD), B16), struct((16, SHARD, HD), B16)]
        + [struct(*kept) for kept in KEPT]
        + [struct((4, 256, HD), B16)] * 3
        + [struct((8, WIDE), F32), struct((1, 2 * FF), F32)],
        in_specs=vmem_space(len(operands) - 1) + any_space(1),
        out_specs=any_space(15) + vmem_space(5),
        scratch_shapes=[pltpu.VMEM(*kept) for kept in KEPT]
        + [
            pltpu.VMEM((SHARD, 2 * HD), B16),
            pltpu.VMEM((SHARD, FF), B16),
            pltpu.VMEM((SHARD, FF), B16),
            pltpu.SemaphoreType.DMA((21,)),
        ]
        + [
            pltpu.VMEM((16, SHARD, 2 * HD), B16),
            pltpu.VMEM((16, SHARD, HD), B16),
            pltpu.VMEM((3, 2, 64, 2 * HD), B16),
            pltpu.VMEM((16, 64, HD), B16),
            pltpu.VMEM((2, 16, 64, HD), B16),
            pltpu.VMEM((16, 64, HD), B16),
            pltpu.VMEM((3, 2, 4, SLICE, WIDE), B16),
        ]
        + rows_scratch(3)
        + [pltpu.VMEM((16, SHARD, FF), B16)] * 3
        + [
            pltpu.VMEM((3, 2, 4, SLICE, WIDE), B16),
            pltpu.VMEM((3, ROWS, 2 * FF), F32),
            pltpu.VMEM((3, 2, 4, SLICE, WIDE), B16),
            pltpu.VMEM((3, SLICE, WIDE), B16),
            pltpu.VMEM((3, 2, 4, SLICE, WIDE), B16),
            pltpu.VMEM((ROWS, 2 * FF), B16),
        ]
        + rows_scratch(3)
        + turned_scratch(1152)
        + [
            pltpu.SemaphoreType.DMA((5, 29)),
            pltpu.SemaphoreType.DMA((5, 29)),
            pltpu.SemaphoreType.DMA((5,)),
            pltpu.SemaphoreType.DMA((6, 3)),
            pltpu.SemaphoreType.DMA((16,)),
            pltpu.SemaphoreType.DMA((2, 16)),
            pltpu.SemaphoreType.DMA((16,)),
            pltpu.SemaphoreType.DMA((6,)),
            pltpu.SemaphoreType.DMA((3,)),
        ],
        compiler_params=params(3),
    )(*operands)


GRADIENTS = (1152, 1152, 1152, HD, 2 * HD)


def back_kernel(*refs):
    (part, cotangent), refs = refs[:2], refs[2:]
    sources, refs = refs[:13], refs[13:]
    (turned_middle, d_gu, middle, branch, final, feed_sums, gu_sums, vectors, first), refs = refs[:9], refs[9:]
    (results, gradient, totals), refs = refs[:3], refs[3:]
    (g_query, g_key, g_value), outs, refs = refs[4:7], refs[:4], refs[7:]
    outs = (*outs, (g_query, g_key, g_value))
    gains, scale_out, scale_down = vectors[0:4], vectors[SCALE_OUT], vectors[SCALE_DOWN]
    scale_qkv = vectors[SCALE_QKV, : 2 * HD]
    aways, refs = refs[:2], refs[2:]
    reduces = []
    for k, columns in enumerate(GRADIENTS):
        held, refs = refs[:8], refs[8:]
        away = aways[k % 2]
        reduces.append(Reduce(columns, away, *held[:6], outs[k], *held[6:]))
    g_gate, g_up, g_down, g_out, g_qkv = reduces
    (own_part, cot, d_branch), refs = refs[:3], refs[3:]
    (held_x, held_z, stage, block, *row_sems), refs = refs[:7], refs[7:]
    (part_in, held_x1, held_z1, stage1, block1, *row_sems1), refs = refs[:8], refs[8:]
    result_sems, refs = refs[:3], refs[3:]
    (vec_x, vec_z, vec_sib, vec_y, vec_zz, vec, send_v, recv_v), refs = refs[:8], refs[8:]
    (datt, rdo, held_q, held_kv, acc_k, acc_v, d_query, d_kv), refs = refs[:8], refs[8:]
    (send, recv, send_q, send_kv, recv_q, recv_kv, local), refs = refs[:7], refs[7:]
    places, load_sems = refs[:13], refs[13]
    (turned_feed, hidden, w_out, w_qkv, attended, q_rot, k_rot, v_all, cosine, sine), refs = places[:10], places[10:]
    normed_input, tokens, qkv_pre = refs
    arrivals = [
        pltpu.make_async_copy(src, dst, load_sems.at[i])
        for i, (src, dst) in enumerate(zip(sources, places))
    ]
    for copy in arrivals:
        copy.start()
    y, zh, core, t = here()
    me = rank(y, zh, core)
    half = lax.rem(t, 2)
    other = t + 1 - 2 * half
    owner = (y < 3) & (core == 0)
    units = [(m, w) for m in range(2) for w in range(3)]
    rows = Rows(part, held_x, held_z, stage, block, d_branch, row_sems, own_part)
    rows_in = Rows(part_in, held_x1, held_z1, stage1, block1, gradient, row_sems1)
    rows_out = Rows(None, None, None, None, final, results, result_sems)
    barrier = pltpu.get_barrier_semaphore()

    def signal(dp, tensor):
        pl.semaphore_signal(barrier, inc=1, device_id=(dp, tensor), device_id_type=MESH)

    plane = [(g_gate.sib, t), (g_gate.zz, t)] + [(dp, t) for dp in g_gate.fore] + rows.peers()
    for device in plane:
        signal(*device)

    @pl.when(owner)
    def _():
        def each(d, _):
            pl.when(d != me)(lambda: signal(d, t))
            return 0

        lax.fori_loop(0, 16, each, 0)

    for m, w in units:
        pl.when(unit_owner(m, w) != me)(functools.partial(signal, unit_owner(m, w), t))
        signal(unit_owner(m, w), other)

    g_gate.product(turned_middle, d_gu)

    @pl.when(owner)
    def _():
        pl.semaphore_wait(barrier, len(plane) + 36)

    @pl.when(jnp.logical_not(owner))
    def _():
        pl.semaphore_wait(barrier, len(plane) + 6)

    for w in range(3):
        rows.scatter_x(w)
    loads = [
        pltpu.make_async_copy(part.at[:, :, rows.x], own_part, local.at[0]),
        pltpu.make_async_copy(cotangent.at[:, rows.zl, rows.x], cot, local.at[1]),
    ]
    for copy in loads:
        copy.start()
    g_gate.send_away()
    g_up.product(turned_middle, d_gu, 1152)
    g_up.send_away()
    g_gate.add()
    for copy in loads:
        copy.wait()
    rows.scatter_z(0)
    g_gate.sent_away()
    for copy in arrivals[:2]:
        copy.wait()
    g_down.product(turned_feed, hidden)
    g_down.send_away()
    rows.scatter_z(1)
    g_up.add()
    rows.scatter_z(2)
    d_middle = jnp.zeros((SLICE, WIDE), F32)
    sums = [jnp.zeros((1, WIDE), F32)] * 3
    for w in range(3):
        upstream = rows.total(w)
        signal_w = middle[w]
        inverse = inverse_rms(signal_w)
        normed = signal_w * inverse
        d_signal = cot[w].astype(F32) + norm_back(normed, inverse, gains[2:3], upstream)
        lower = branch[w]
        inverse_lower = inverse_rms(lower)
        normed_lower = lower * inverse_lower
        lowered = norm_back(normed_lower, inverse_lower, gains[1:2], d_signal).astype(B16)
        block[w] = lowered
        rows.spread(w)
        d_middle = d_middle + d_signal
        terms = (d_signal * normed_lower, upstream * normed, lowered.astype(F32) * lower)
        sums = [old + jnp.sum(new, axis=0, keepdims=True) for old, new in zip(sums, terms)]
    vec[1:2] = sums[0]
    vec[2:3] = sums[1]
    vec[3:4] = feed_sums[0:1]
    vec[4:5] = sums[2] / scale_out
    vec[5:6] = feed_sums[1:2] / scale_down

    for copy in arrivals[2:]:
        copy.wait()
    codes = w_out[...].reshape(WIDE, HD)

    def to_owner(u, m, w, start):
        o = unit_owner(m, w)
        src = datt.at[w, m]

        @pl.when(o != me)
        def _():
            copy = remote(src, rdo.at[me], send.at[u], recv.at[me], o, t)
            copy.start() if start else copy.wait_send()

        @pl.when(o == me)
        def _():
            copy = pltpu.make_async_copy(src, rdo.at[me], local.at[0])
            copy.start() if start else copy.wait()

    g_gate.cross()
    g_gate.pool()
    for w in range(3):
        rows.forward(w)
    for w in range(3):
        rows.end(w)
        scaled = (d_branch[w].reshape(ROWS, WIDE).astype(F32) * scale_out).astype(B16)
        datt[w] = dot(scaled, level(codes, w), 1, 0).astype(B16).reshape(2, 64, HD)
        for m in range(2):
            to_owner(m * 3 + w, m, w, True)
    g_up.cross()
    g_down.add()
    for w in range(3):
        rows_out.spread(w)
    for u, (m, w) in enumerate(units):
        to_owner(u, m, w, False)

    @pl.when(owner)
    def _():
        def each(d, _):
            @pl.when(d != me)
            def _():
                remote(rdo.at[d], rdo.at[d], send.at[0], recv.at[d], me, other).wait_recv()

            return 0

        lax.fori_loop(0, 16, each, 0)
        acc_k[...] = jnp.zeros_like(acc_k)
        acc_v[...] = jnp.zeros_like(acc_v)
        for b in range(4):
            rows_b = slice(16 * b, 16 * b + 16)
            blocks = list(range(max(0, b - 2), b + 1))
            queries = q_rot[b]
            keys = {kb: k_rot[kb] for kb in blocks}
            upstream = rdo[:, rows_b, :].reshape(256, HD)
            bents, probs = block_probs(queries, keys, first[:, b : b + 1], b)
            d_probs = [dot(upstream, v_all[kb], 1, 1) for kb in blocks]
            centre = sum(
                jnp.sum(p * dp, axis=-1, keepdims=True) for p, dp in zip(probs, d_probs)
            )
            d_q = jnp.zeros((256, HD), F32)
            for kb, bent, p, dp in zip(blocks, bents, probs, d_probs):
                d_scores = (p * (dp - centre) * (1.0 - bent * bent)).astype(B16)
                d_q = d_q + dot(d_scores, keys[kb], 1, 0)
                acc_k[kb] += dot(d_scores, queries, 0, 0)
                acc_v[kb] += dot(p.astype(B16), upstream, 0, 0)
            d_q = unrotate(d_q * 0.0625, cosine[b], sine[b])
            held_q[:, rows_b, :] = d_q.astype(B16).reshape(16, 16, HD)
        for b in range(4):
            rows_b = slice(16 * b, 16 * b + 16)
            d_k = unrotate(acc_k[b] * 0.0625, cosine[b], sine[b]).astype(B16)
            d_v = acc_v[b].astype(B16)
            for i in range(2):
                cols = slice(128 * i, 128 * i + 128)
                held_kv[i, :, rows_b, :128] = d_k[:, cols].reshape(16, 16, 128)
                held_kv[i, :, rows_b, 128:] = d_v[:, cols].reshape(16, 16, 128)

    def hand_back(d, start):
        u = zh * 3 + y
        across = remote(
            held_kv.at[1 - half, d], d_kv.at[half, y, zh], send_kv.at[1, d], recv_kv.at[half, u], d, other
        )
        across.start() if start else across.wait_send()

        @pl.when(d != me)
        def _():
            for copy in (
                remote(held_q.at[d], d_query.at[y, zh], send_q.at[d], recv_q.at[u], d, t),
                remote(
                    held_kv.at[half, d], d_kv.at[half, y, zh], send_kv.at[0, d], recv_kv.at[half, u], d, t
                ),
            ):
                copy.start() if start else copy.wait_send()

        @pl.when(d == me)
        def _():
            for copy in (
                pltpu.make_async_copy(held_q.at[d], d_query.at[y, zh], local.at[0]),
                pltpu.make_async_copy(held_kv.at[half, d], d_kv.at[half, y, zh], local.at[1]),
            ):
                copy.start() if start else copy.wait()

    @pl.when(owner)
    def _():
        lax.fori_loop(0, 16, lambda d, _: (hand_back(d, True), 0)[1], 0)
        lax.fori_loop(0, 16, lambda d, _: (hand_back(d, False), 0)[1], 0)

    for w in range(3):
        rows_out.forward(w)
    g_down.cross()
    g_up.sent_away()
    g_out.product_whole(d_branch[...].reshape(3 * ROWS, WIDE), attended[...])
    g_gate.merge()
    g_up.pool()
    for u, (m, w) in enumerate(units):

        @pl.when(unit_owner(m, w) != me)
        def _():
            ref = d_query.at[w, m]
            remote(ref, ref, send.at[0], recv_q.at[u], me, other).wait_recv()
            ref = d_kv.at[half, w, m]
            remote(ref, ref, send.at[0], recv_kv.at[half, u], me, other).wait_recv()

        ref = d_kv.at[1 - half, w, m]
        remote(ref, ref, send.at[0], recv_kv.at[1 - half, u], me, other).wait_recv()

    codes = w_qkv[...].reshape(WIDE, 2 * HD)
    scaled = []
    qkv_sums = jnp.zeros((1, 2 * HD), F32)
    d_qkv_all = jnp.zeros((ROWS, 2 * HD), F32)
    for w in range(3):
        both = (d_kv[0, w].astype(F32) + d_kv[1, w].astype(F32)).astype(B16).astype(F32)
        d_qkv = jnp.concatenate([d_query[w].astype(F32), both], -1).reshape(ROWS, 2 * HD)
        qkv_sums = qkv_sums + jnp.sum(d_qkv * qkv_pre[w], axis=0, keepdims=True)
        d_qkv_all = d_qkv_all + d_qkv
        scaled.append((d_qkv * scale_qkv).astype(B16))
    whole = tokens[...].astype(F32)
    inverse = inverse_rms(whole)
    for i in range(3):
        tile = slice(768 * i, 768 * i + 768)
        d_input = sum(dot(scaled[w], level(codes[tile], w), 1, 1) for w in range(3))
        part_in[0, :, :, :, tile] = d_input.astype(B16).reshape(2, 4, SLICE, 768)
        normed = tokens[:, tile].astype(F32) * inverse
        vec[0:1, tile] = jnp.sum(d_input * normed, axis=0, keepdims=True)
    rows_in.scatter_x(0)

    vec[6:8] = jnp.zeros((2, WIDE), F32)
    x = rows.x
    copies = []

    def exchange(slot, src, dst, dp, tensor):
        copy = remote(src, dst, send_v.at[slot], recv_v.at[slot], dp, tensor)
        copy.start()
        copies.append(copy)

    def exchanged(slot, ref):
        remote(ref, ref, send_v.at[slot], recv_v.at[slot], me, other).wait_recv()

    vec_x[x] = vec[...]
    for k in range(3):
        exchange(k, vec_x.at[x], vec_x.at[x], me, rows.x_peers[k])
    g_down.sent_away()
    g_qkv.product_whole(normed_input[...], d_qkv_all.astype(B16))
    g_out.add()
    g_out.cross()
    g_up.merge()
    for k in range(3):
        exchanged(k, vec_x.at[rows.behind[k]])
    vec[...] = functools.reduce(jnp.add, [vec_x[i] for i in range(4)])
    exchange(3, vec, vec_z, me, rows.z_peer)
    rows_in.scatter_z(0)
    g_qkv.add()
    g_qkv.cross()
    exchanged(3, vec_z)
    copies[3].wait_send()
    vec[0:6] = vec[0:6] + vec_z[0:6]
    vec[6:7] = gu_sums[...]
    vec[7:8, : 2 * HD] = qkv_sums / scale_qkv
    exchange(4, vec, vec_sib, g_gate.sib, t)

    upstream = rows_in.total(0)
    signal_in = tokens[pl.ds(pl.multiple_of(t * SLICE, SLICE), SLICE)].astype(F32)
    inverse = inverse_rms(signal_in)
    normed = norm_back(signal_in * inverse, inverse, gains[0:1], upstream)
    block1[0] = (d_middle + normed).astype(B16)
    rows_in.spread(0)
    exchanged(4, vec_sib)
    vec_y[y] = vec[...] + vec_sib[...]
    for i in range(3):
        exchange(5 + i, vec_y.at[y], vec_y.at[y], g_gate.fore[i], t)
    rows_in.forward(0)
    g_out.merge()
    g_out.pool()
    g_qkv.merge()
    g_qkv.pool()
    g_down.merge()
    g_down.pool()
    for i in range(3):
        exchanged(5 + i, vec_y.at[lax.rem(y + 3 - i, 4)])
    copies[4].wait_send()
    vec[...] = functools.reduce(jnp.add, [vec_y[i] for i in range(4)])
    exchange(8, vec, vec_zz, g_gate.zz, t)
    g_gate.end()
    g_up.end()
    g_out.end()
    g_qkv.end()
    g_down.end()
    exchanged(8, vec_zz)
    totals[...] = vec[...] + vec_zz[...]
    rows_in.end(0)
    for w in range(3):
        rows_out.end(w)
    g_out.sent_away()
    g_qkv.sent_away()
    for k in (0, 1, 2, 5, 6, 7, 8):
        copies[k].wait_send()
    for part_of in (rows, rows_in, rows_out, *reduces):
        part_of.drain()


def back(hbm, late, vmem):
    def vec():
        return pltpu.VMEM((8, WIDE), F32)

    scratch = [pltpu.VMEM((8, SHARD, 1152), B16)] * 2
    for columns in GRADIENTS:
        scratch += reduce_scratch(columns)
    scratch += [
        pltpu.VMEM((3, 2, SLICE, WIDE), B16),
        pltpu.VMEM((3, SLICE, WIDE), B16),
        pltpu.VMEM((3, 2, 4, SLICE, WIDE), B16),
    ]
    scratch += rows_scratch(3)
    scratch += [pltpu.VMEM((1, 2, 4, SLICE, WIDE), B16)] + rows_scratch(1)
    scratch += rows_scratch(3)[4:]
    scratch += [pltpu.VMEM((4, 8, WIDE), F32), vec(), vec(), pltpu.VMEM((4, 8, WIDE), F32), vec(), vec()]
    scratch += [pltpu.SemaphoreType.DMA((9,))] * 2
    scratch += [
        pltpu.VMEM((3, 2, 64, HD), B16),
        pltpu.VMEM((16, 64, HD), B16),
        pltpu.VMEM((16, 64, HD), B16),
        pltpu.VMEM((2, 16, 64, HD), B16),
        pltpu.VMEM((4, 256, HD), F32),
        pltpu.VMEM((4, 256, HD), F32),
        pltpu.VMEM((3, 2, 64, HD), B16),
        pltpu.VMEM((2, 3, 2, 64, HD), B16),
        pltpu.SemaphoreType.DMA((6,)),
        pltpu.SemaphoreType.DMA((16,)),
        pltpu.SemaphoreType.DMA((16,)),
        pltpu.SemaphoreType.DMA((2, 16)),
        pltpu.SemaphoreType.DMA((6,)),
        pltpu.SemaphoreType.DMA((2, 6)),
        pltpu.SemaphoreType.DMA((2,)),
    ]
    scratch += [pltpu.VMEM(array.shape, array.dtype) for array in late]
    scratch += [pltpu.SemaphoreType.DMA((len(late),))]
    return pl.pallas_call(
        back_kernel,
        name="back",
        out_shape=[
            struct((3, 2, 4, SLICE, WIDE), B16),
            struct((1, 2, 4, SLICE, WIDE), B16),
            struct((8, WIDE), F32),
        ]
        + [struct((SHARD, columns), F32) for columns in (1152, 1152, 1152, HD, HD, 128, 128)],
        in_specs=any_space(len(hbm) + len(late)) + vmem_space(len(vmem)),
        out_specs=any_space(2) + vmem_space(8),
        scratch_shapes=scratch,
        compiler_params=params(4),
    )(*hbm, *late, *vmem)


def level(codes, width):
    if width == 0:
        return codes
    stride = STRIDES[width]
    return jnp.floor(codes * B16(1.0 / stride)) * B16(stride) + B16(stride // 2)


def gelu_parts(value):
    slope = 0.7978845608028654
    inner = jnp.tanh(slope * (value + 0.044715 * value * value * value))
    grown = 0.5 * value * (1.0 + inner)
    rate = 0.5 * (1.0 + inner) + 0.5 * value * (1.0 - inner * inner) * slope * (
        1.0 + 3 * 0.044715 * value * value
    )
    return grown, rate


def side_by_side(*parts):
    total, first = 0.0, 0
    for part in parts:
        total = total + jnp.pad(part, (first, WIDE - first - part.shape[0]))
        first += part.shape[0]
    return total


def body(
    tokens,
    cotangent,
    segments,
    codes_query,
    codes_key,
    codes_value,
    codes_out,
    codes_gate,
    codes_up,
    codes_down,
    query_column_scale,
    key_column_scale,
    value_column_scale,
    output_column_scale,
    gate_column_scale,
    up_column_scale,
    down_column_scale,
    gain_first,
    gain_second,
    gain_third,
    gain_fourth,
):
    z_hi = lax.rem(lax.div(lax.axis_index("dp"), 2), 2)
    tokens = tokens.reshape(ROWS, WIDE)
    cotangent = cotangent.reshape(3, ROWS, WIDE)
    entries = [gain_first, gain_second, gain_third, gain_fourth, output_column_scale, down_column_scale]
    entries += [side_by_side(gate_column_scale, up_column_scale)]
    entries += [side_by_side(query_column_scale, key_column_scale, value_column_scale)]
    row = lax.broadcasted_iota(jnp.int32, (8, WIDE), 0)
    vectors = functools.reduce(
        lambda rest, i: jnp.where(row == i, entries[i][None], rest), range(7), entries[7][None]
    )
    documents = lax.dynamic_index_in_dim(segments, z_hi, 0, False)
    starts = jnp.sum((documents[None, :] < documents[:, None]).astype(jnp.int32), axis=1)
    place = jnp.arange(1024, dtype=jnp.int32)

    def blocked(rows):
        return rows.reshape(4, 16, 16).transpose(0, 2, 1).reshape(4, 256)

    first = blocked(starts).T
    expo = jnp.arange(HD // 2, dtype=F32) * (2.0 / HD)
    rates = jnp.power(ROPE_BASE, -expo)[None]

    grid = (3, 2, 4, SLICE, WIDE)
    w_qkv, w_out, attended, normed_input, qkv_pre, branch, middle, cosine, sine, *rest = forward_pass(
        codes_query,
        codes_key,
        codes_value,
        codes_out.astype(B16).T,
        codes_gate,
        codes_up,
        codes_down.astype(B16).T,
        tokens,
        vectors,
        blocked(place - starts).astype(F32).T,
        first,
        rates,
        cotangent.reshape(grid),
    )
    d_part, turned_middle, turned_feed, d_gu, hidden, final, *rest = rest
    q_rot, k_rot, v_all, feed_sums, gu_sums = rest
    flat = (3 * ROWS, -1)
    results, input_gradient, totals, g_gate, g_up, g_down, g_out, g_query, g_key, g_value = back(
        [d_part, cotangent.reshape(grid)],
        [
            turned_feed,
            hidden.reshape(flat),
            w_out,
            w_qkv,
            attended.reshape(flat),
            q_rot,
            k_rot,
            v_all,
            cosine,
            sine,
            normed_input,
            tokens,
            qkv_pre,
        ],
        [turned_middle, d_gu.reshape(flat), middle, branch, final, feed_sums, gu_sums, vectors, first],
    )
    rows = lax.dynamic_slice_in_dim(totals, lax.axis_index("dp") * SHARD, SHARD, 1)
    return (
        results.reshape(3, 2, 64, 1, WIDE),
        input_gradient.astype(F32).reshape(2, 64, 1, WIDE),
        g_query,
        g_key,
        g_value,
        g_out.T,
        g_gate,
        g_up,
        g_down.T,
        totals[7, :256],
        totals[7, 256:384],
        totals[7, 384:512],
        rows[4],
        totals[6, :FF],
        totals[6, FF:],
        rows[5],
        rows[0],
        rows[1],
        rows[2],
        rows[3],
    )


def solution(mesh):
    matrix, turned = P("dp", "tensor"), P("tensor", "dp")
    columns, whole, shard = P("tensor"), P(), P("dp")
    in_specs = (
        P(None, None, "dp", None),
        P(None, None, None, "dp", None),
        whole,
        *(matrix, matrix, matrix, turned, matrix, matrix, turned),
        *(columns, columns, columns, whole, columns, columns, whole),
        *(whole, whole, whole, whole),
    )
    out_specs = (
        P(None, None, None, "dp", None),
        P(None, None, "dp", None),
        *(matrix, matrix, matrix, turned, matrix, matrix, turned),
        *(columns, columns, columns, shard, columns, columns, shard),
        *(shard, shard, shard, shard),
    )
    return jax.shard_map(body, mesh=mesh, in_specs=in_specs, out_specs=out_specs, check_vma=False)
```

```python
import functools

import jax
import jax.numpy as jnp
from jax import lax
from jax.experimental import pallas as pl
from jax.experimental.pallas import tpu as pltpu
from jax.sharding import PartitionSpec as P

MESH = pl.DeviceIdType.MESH
F32 = jnp.float32
B16 = jnp.bfloat16
EPSILON = 1e-06
SOFTCAP = 50.0
ROPE_BASE = 10000.0
MASKED = -1e30
HD = 256
WIDE = 2304
FF = 1152
STRIDES = (1, 16, 64)
SCALE_OUT, SCALE_DOWN, SCALE_GU, SCALE_QKV = (slice(i, i + 1) for i in range(4, 8))
SHARD = 144
LOW = 64
HIGH = SHARD - LOW
RLOW = 96
RHIGH = SHARD - RLOW
TENSOR = 8
ROWS = 128
SLICE = ROWS // TENSOR
VMEM_BYTES = 63 * 2**20


def here():
    dp = lax.axis_index("dp")
    return lax.div(dp, 4), lax.rem(lax.div(dp, 2), 2), lax.rem(dp, 2), lax.axis_index("tensor")


def rank(y, z_hi, core):
    return (y * 2 + z_hi) * 2 + core


def remote(src, dst, send, recv, dp, tensor):
    return pltpu.make_async_remote_copy(
        src, dst, send, recv, device_id=(dp, tensor), device_id_type=MESH
    )


def greet(devices):
    barrier = pltpu.get_barrier_semaphore()
    for device in devices:
        pl.semaphore_signal(barrier, inc=1, device_id=device, device_id_type=MESH)
    pl.semaphore_wait(barrier, len(devices))


def struct(shape, dtype):
    return jax.ShapeDtypeStruct(shape, dtype)


def any_space(count):
    return [pl.BlockSpec(memory_space=pl.ANY)] * count


def vmem_space(count):
    return [pl.BlockSpec(memory_space=pltpu.VMEM)] * count


def params(collective_id):
    return pltpu.CompilerParams(
        collective_id=collective_id, has_side_effects=True, vmem_limit_bytes=VMEM_BYTES
    )


class Gather:
    def __init__(self, src, out, send, recv, local):
        self.src, self.out, self.send, self.recv, self.local = src, out, send, recv, local
        self.y, self.zh, self.core, self.t = here()
        y, zh, core = self.y, self.zh, self.core
        self.me, self.sib, self.zz = rank(y, zh, core), rank(y, zh, 1 - core), rank(y, 1 - zh, core)
        self.fore = [rank(lax.rem(y + dy, 4), zh, core) for dy in (1, 2, 3)]
        self.behind = [lax.rem(y + 4 - dy, 4) for dy in (1, 2, 3)]
        self.low, self.high = pl.ds(0, LOW), pl.ds(LOW, HIGH)
        self.started = []

    def push(self, slot, src, dst, dp):
        copy = remote(src, dst, self.send.at[slot], self.recv.at[slot], dp, self.t)
        copy.start()
        self.started.append(copy)

    def arrive(self, slot, ref):
        remote(ref, ref, self.send.at[slot], self.recv.at[slot], self.sib, self.t).wait_recv()

    def start(self):
        src, mine = self.src, self.out.at[self.me]
        self.mine = pltpu.make_async_copy(src, mine, self.local)
        self.mine.start()
        low, high = self.low, self.high
        self.push(0, src.at[low], self.out.at[self.me, low], self.zz)
        for i in range(3):
            self.push(4 + i, src.at[high], self.out.at[self.me, high], self.fore[i])
        for i in range(3):
            self.push(1 + i, src.at[low], self.out.at[self.me, low], self.fore[i])
        self.push(7, src.at[high], self.out.at[self.me, high], self.zz)
        self.push(14, src, mine, self.sib)

    def over_y(self):
        block = self.out.at[self.zz, self.low]
        self.arrive(0, block)
        for i in range(3):
            self.push(8 + i, block, block, self.fore[i])
        self.push(15, block, block, self.sib)

    def over_z(self):
        for i in range(3):
            block = self.out.at[rank(self.behind[i], self.zh, self.core), self.high]
            self.arrive(4 + i, block)
            self.push(11 + i, block, block, self.zz)
            self.push(16 + i, block, block, self.sib)

    def near(self):
        for i in range(3):
            block = self.out.at[rank(self.behind[i], self.zh, self.core), self.low]
            self.arrive(1 + i, block)
            self.push(19 + i, block, block, self.sib)
        block = self.out.at[self.zz, self.high]
        self.arrive(7, block)
        self.push(22, block, block, self.sib)

    def far(self):
        for i in range(3):
            dp = rank(self.behind[i], 1 - self.zh, self.core)
            for slot, rows in ((0, self.low), (3, self.high)):
                block = self.out.at[dp, rows]
                self.arrive(8 + slot + i, block)
                self.push(23 + slot + i, block, block, self.sib)

    def end(self):
        out, low, high, other = self.out, self.low, self.high, 1 - self.core
        self.arrive(14, out.at[self.sib])
        far = rank(self.y, 1 - self.zh, other)
        self.arrive(15, out.at[far, low])
        self.arrive(22, out.at[far, high])
        for i in range(3):
            near, far = (rank(self.behind[i], zh, other) for zh in (self.zh, 1 - self.zh))
            self.arrive(16 + i, out.at[near, high])
            self.arrive(19 + i, out.at[near, low])
            self.arrive(23 + i, out.at[far, low])
            self.arrive(26 + i, out.at[far, high])
        self.mine.wait()

    def drain(self):
        for copy in self.started:
            copy.wait_send()


class Rows:
    def __init__(self, part, held_x, held_z, stage, block, out, sems, own=None, turned=None):
        self.part, self.own, self.out, self.block = part, own, out, block
        self.held_x, self.held_z, self.stage = held_x, held_z, stage
        self.send, self.recv, self.local = sems
        self.turned = turned
        self.split = WIDE if turned is None else WIDE - turned[0].shape[-1]
        self.low, self.high = pl.ds(0, self.split), pl.ds(self.split, WIDE - self.split)
        self.dp, self.t = lax.axis_index("dp"), lax.axis_index("tensor")
        self.zl, self.x = lax.div(self.t, 4), lax.rem(self.t, 4)
        self.ahead = [lax.rem(self.x + k, 4) for k in (1, 2, 3)]
        self.behind = [lax.rem(self.x + 4 - k, 4) for k in (1, 2, 3)]
        self.x_peers = [self.zl * 4 + x for x in self.ahead]
        self.z_peer = (1 - self.zl) * 4 + self.x
        self.started = []

    def peers(self):
        return [(self.dp, t) for t in self.x_peers + [self.z_peer]]

    def push(self, w, slot, src, dst, t):
        copy = remote(src, dst, self.send.at[w, slot], self.recv.at[w, slot], self.dp, t)
        copy.start()
        self.started.append(copy)

    def arrive(self, w, slot, ref):
        remote(
            ref, ref, self.send.at[w, slot], self.recv.at[w, slot], self.dp, self.z_peer
        ).wait_recv()

    def scatter_x(self, w):
        low, high = self.low, self.high
        for k in range(3):
            self.push(
                w,
                1 + k,
                self.part.at[w, :, self.ahead[k], :, low],
                self.held_x.at[w, k, :, :, low],
                self.x_peers[k],
            )
        if self.turned is not None:
            self.push(
                w, 11, self.part.at[w, 1 - self.zl, :, :, high], self.turned[0].at[w], self.z_peer
            )

    def summed_x(self, w, zl):
        own = self.part[w, zl, self.x] if self.own is None else self.own[w, zl]
        total = own[:, : self.split].astype(F32)
        for k in range(3):
            total = total + self.held_x[w, k, zl, :, : self.split].astype(F32)
        return total

    def summed_z(self, w, x):
        part = self.part[w, self.zl, x, :, self.split :].astype(F32)
        return part + self.turned[0][w, x].astype(F32)

    def scatter_z(self, w):
        for k in range(3):
            self.arrive(w, 1 + k, self.held_x.at[w, k, :, :, self.low])
        self.stage[w, :, : self.split] = self.summed_x(w, 1 - self.zl).astype(B16)
        self.push(w, 0, self.stage.at[w, :, self.low], self.held_z.at[w, :, self.low], self.z_peer)
        if self.turned is not None:
            held, stage, last = self.turned
            self.arrive(w, 11, held.at[w])
            for k in range(3):
                stage[w, k] = self.summed_z(w, self.ahead[k]).astype(B16)
                self.push(w, 12 + k, stage.at[w, k], last.at[w, k], self.x_peers[k])

    def total(self, w):
        self.arrive(w, 0, self.held_z.at[w, :, self.low])
        low = self.summed_x(w, self.zl) + self.held_z[w, :, : self.split].astype(F32)
        if self.turned is None:
            return low
        high = self.summed_z(w, self.x)
        for k in range(3):
            self.arrive(w, 12 + k, self.turned[2].at[w, k])
            high = high + self.turned[2][w, k].astype(F32)
        return jnp.concatenate([low, high], -1)

    def spread(self, w):
        block, mine = self.block.at[w], self.out.at[w, self.zl, self.x]
        self.push(w, 4, block.at[:, self.low], mine.at[:, self.low], self.z_peer)
        for k in range(3):
            self.push(w, 5 + k, block, mine, self.x_peers[k])
        pltpu.make_async_copy(block, mine, self.local.at[w]).start()

    def forward(self, w):
        block = self.out.at[w, 1 - self.zl, self.x, :, self.low]
        self.arrive(w, 4, block)
        for k in range(3):
            self.push(w, 8 + k, block, block, self.x_peers[k])
        if self.turned is not None:
            self.near(w)
            blocks = self.out.at[w, self.zl, :, :, self.high]
            self.push(w, 15, blocks, blocks, self.z_peer)

    def near(self, w):
        for k in range(3):
            self.arrive(w, 5 + k, self.out.at[w, self.zl, self.behind[k]])
        pltpu.make_async_copy(
            self.block.at[w], self.out.at[w, self.zl, self.x], self.local.at[w]
        ).wait()

    def end(self, w):
        for k in range(3):
            self.arrive(w, 8 + k, self.out.at[w, 1 - self.zl, self.behind[k], :, self.low])
        if self.turned is None:
            self.near(w)
        else:
            self.arrive(w, 15, self.out.at[w, 1 - self.zl, :, :, self.high])

    def drain(self):
        for copy in self.started:
            copy.wait_send()


def turned_scratch(columns):
    return [
        pltpu.VMEM((3, 4, SLICE, columns), B16),
        pltpu.VMEM((3, 3, SLICE, columns), B16),
        pltpu.VMEM((3, 3, SLICE, columns), B16),
    ]


def rows_scratch(depth):
    return [
        pltpu.VMEM((depth, 3, 2, SLICE, WIDE), B16),
        pltpu.VMEM((depth, SLICE, WIDE), B16),
        pltpu.VMEM((depth, SLICE, WIDE), B16),
        pltpu.VMEM((depth, SLICE, WIDE), B16),
        pltpu.SemaphoreType.DMA((depth, 16)),
        pltpu.SemaphoreType.DMA((depth, 16)),
        pltpu.SemaphoreType.DMA((depth,)),
    ]


class Reduce:
    def __init__(self, columns, away, own, sibs, yrecv, zrecv, ylast, zlast, out, send, recv):
        self.columns, self.away, self.own, self.sibs = columns, away, own, sibs
        self.yrecv, self.zrecv, self.ylast, self.zlast, self.out = yrecv, zrecv, ylast, zlast, out
        self.send, self.recv = send, recv
        self.y, self.zh, self.core, self.t = here()
        y, zh, core = self.y, self.zh, self.core
        self.sib, self.zz = rank(y, zh, 1 - core), rank(y, 1 - zh, core)
        self.ahead = [lax.rem(y + dy, 4) for dy in (1, 2, 3)]
        self.fore = [rank(place, zh, core) for place in self.ahead]
        self.started = []

    def push(self, slot, src, dst, dp):
        copy = remote(src, dst, self.send.at[slot], self.recv.at[slot], dp, self.t)
        copy.start()
        self.started.append(copy)

    def arrive(self, slot, ref):
        remote(ref, ref, self.send.at[slot], self.recv.at[slot], self.sib, self.t).wait_recv()

    def store(self, first, count, cols, block):
        block = block.astype(B16).reshape(count, 2, SHARD, block.shape[-1])
        even = self.core == 0
        chips = pl.ds(first, count)
        self.own[chips, :, cols] = jnp.where(even, block[:, 0], block[:, 1])
        self.away[chips, :, cols] = jnp.where(even, block[:, 1], block[:, 0])

    def to_sibling(self, place):
        pair = pl.ds(place * 2, 2)
        return remote(
            self.away.at[pair, :, pl.ds(0, self.columns)],
            self.sibs.at[pair],
            self.send.at[place],
            self.recv.at[place],
            self.sib,
            self.t,
        )

    def product(self, turned, right, left_columns=0):
        for place in range(4):
            rows = slice(place * 4 * SHARD, (place + 1) * 4 * SHARD)
            for i in range(self.columns // 384):
                cols = slice(384 * i, 384 * i + 384)
                block = dot(turned[rows], right[:, left_columns + 384 * i : left_columns + 384 * i + 384], 1, 0)
                self.store(place * 2, 2, cols, block)

    def send_away(self):
        for place in range(4):
            self.to_sibling(place).start()

    def product_whole(self, left, right):
        for i in range(self.columns // HD):
            cols = slice(HD * i, HD * i + HD)
            self.store(0, 8, cols, dot(left, right[:, cols], 0, 0))
        self.send_away()

    def sent_away(self):
        for place in range(4):
            self.to_sibling(place).wait_send()

    def add(self):
        own, sibs = self.own, self.sibs
        for i, place in enumerate(self.ahead + [self.y]):
            pair = pl.ds(place * 2, 2)
            self.arrive(place, sibs.at[pair])

            def step(step, _, place=place):
                chip = place * 2 + lax.div(step, SHARD // 48)
                rows = pl.ds(pl.multiple_of(lax.rem(step, SHARD // 48) * 48, 16), 48)
                own[chip, rows] = own[chip, rows] + sibs[chip, rows]
                return 0

            lax.fori_loop(0, 2 * SHARD // 48, step, 0)
            if i < 3:
                self.push(4 + i, own.at[pair, pl.ds(0, RLOW)], self.yrecv.at[i], self.fore[i])

    def cross(self):
        for i, place in enumerate(self.ahead + [self.y]):
            block = self.own.at[place * 2 + 1 - self.zh, pl.ds(RLOW, RHIGH)]
            self.push(7 + i, block, self.zrecv.at[place], self.zz)

    def merge(self):
        own, zrecv = self.own, self.zrecv
        for i, place in enumerate(self.ahead + [self.y]):
            self.arrive(7 + i, zrecv.at[place])

            def step(step, _, place=place):
                rows = pl.ds(pl.multiple_of(step * 16, 16), 16)
                mine = pl.ds(pl.multiple_of(step * 16 + RLOW, 16), 16)
                zrecv[place, rows] = zrecv[place, rows] + own[place * 2 + self.zh, mine]
                return 0

            lax.fori_loop(0, RHIGH // 16, step, 0)
            if i < 3:
                self.push(11 + i, zrecv.at[place], self.ylast.at[i], self.fore[i])

    def pool(self):
        for i in range(3):
            self.arrive(4 + i, self.yrecv.at[i])

        def step(step, _):
            chip = lax.div(step, RLOW // 16)
            rows = pl.ds(pl.multiple_of(lax.rem(step, RLOW // 16) * 16, 16), 16)
            total = self.own[self.y * 2 + chip, rows].astype(F32)
            for i in range(3):
                total = total + self.yrecv[i, chip, rows].astype(F32)
            self.own[self.y * 2 + chip, rows] = total.astype(B16)
            return 0

        lax.fori_loop(0, 2 * RLOW // 16, step, 0)
        self.push(14, self.own.at[self.y * 2 + 1 - self.zh, pl.ds(0, RLOW)], self.zlast, self.zz)

    def write(self, rows, total):
        first = 0
        for out in self.out if isinstance(self.out, tuple) else (self.out,):
            out[rows] = total[:, first : first + out.shape[-1]]
            first += out.shape[-1]

    def end(self):
        self.arrive(14, self.zlast)

        def low(step, _):
            rows = pl.ds(pl.multiple_of(step * 16, 16), 16)
            own = self.own[self.y * 2 + self.zh, rows].astype(F32)
            self.write(rows, own + self.zlast[rows].astype(F32))
            return 0

        lax.fori_loop(0, RLOW // 16, low, 0)
        for i in range(3):
            self.arrive(11 + i, self.ylast.at[i])

        def high(step, _):
            rows = pl.ds(pl.multiple_of(step * 16, 16), 16)
            total = self.zrecv[self.y, rows].astype(F32)
            for i in range(3):
                total = total + self.ylast[i, rows].astype(F32)
            self.write(pl.ds(pl.multiple_of(step * 16 + RLOW, 16), 16), total)
            return 0

        lax.fori_loop(0, RHIGH // 16, high, 0)

    def drain(self):
        for copy in self.started:
            copy.wait_send()


def reduce_scratch(columns):
    return [
        pltpu.VMEM((8, SHARD, columns), B16),
        pltpu.VMEM((8, SHARD, columns), B16),
        pltpu.VMEM((3, 2, RLOW, columns), B16),
        pltpu.VMEM((4, RHIGH, columns), B16),
        pltpu.VMEM((3, RHIGH, columns), B16),
        pltpu.VMEM((RLOW, columns), B16),
        pltpu.SemaphoreType.DMA((15,)),
        pltpu.SemaphoreType.DMA((15,)),
    ]


def inverse_rms(signal):
    return lax.rsqrt(jnp.mean(signal * signal, axis=-1, keepdims=True) + EPSILON)


def norm_back(normed, inverse, gain, upstream):
    inner = upstream * (1.0 + gain)
    return inverse * (inner - normed * jnp.mean(inner * normed, axis=-1, keepdims=True))


def half_level(codes, width):
    return codes if width == 0 else jnp.floor(codes * B16(1.0 / STRIDES[width]))


def offset(left, width):
    return 0.0 if width == 0 else 0.5 * jnp.sum(left.astype(F32), axis=-1, keepdims=True)


def unit_owner(micro, width):
    return rank(width, micro, 0)


def rotate(signal, cosine, sine):
    former, latter = signal[:, : HD // 2], signal[:, HD // 2 :]
    return jnp.concatenate([former * cosine - latter * sine, latter * cosine + former * sine], -1)


def unrotate(signal, cosine, sine):
    former, latter = signal[:, : HD // 2], signal[:, HD // 2 :]
    return jnp.concatenate([former * cosine + latter * sine, latter * cosine - former * sine], -1)


def block_scores(queries, keys, first, b, kb):
    scores = lax.dot_general(queries, keys, (((1,), (1,)), ((), ())), preferred_element_type=F32)
    bent = jnp.tanh(scores * (0.0625 / SOFTCAP))
    lane = lax.broadcasted_iota(jnp.int32, (256, 256), 1)
    row = lax.broadcasted_iota(jnp.int32, (256, 256), 0)
    key_place = (16 * kb + (lane & 15)) * 16 + (lane >> 4)
    query_place = (16 * b + (row & 15)) * 16 + (row >> 4)
    allowed = (key_place >= first) & (key_place <= query_place)
    return bent, jnp.where(allowed, SOFTCAP * bent, MASKED)


def block_probs(queries, keys, first, b):
    pieces = [
        block_scores(queries, keys[kb], first, b, kb) for kb in range(max(0, b - 2), b + 1)
    ]
    peak = functools.reduce(
        jnp.maximum, [jnp.max(capped, axis=-1, keepdims=True) for _, capped in pieces]
    )
    exps = [jnp.exp(capped - peak) for _, capped in pieces]
    total = functools.reduce(jnp.add, [jnp.sum(e, axis=-1, keepdims=True) for e in exps])
    return [bent for bent, _ in pieces], [e / total for e in exps]


def dot(left, right, left_dim, right_dim):
    return lax.dot_general(
        left, right, (((left_dim,), (right_dim,)), ((), ())), preferred_element_type=F32
    )


def forward_kernel(*refs):
    (c_query, c_key, c_value, c_out, c_gate, c_up, c_down), refs = refs[:7], refs[7:]
    (tokens, vectors, places, first, rates, cotangent), refs = refs[:6], refs[6:]
    (w_qkv, w_out), refs = refs[:2], refs[2:]
    homes, refs = refs[:13], refs[13:]
    (q_rot, k_rot, v_all, sums, gu_sums), refs = refs[:5], refs[5:]
    kept, refs = refs[:13], refs[13:]
    (att, normed_input, qkv_pre, branch, middle, cosine, sine), (d_part, *late) = kept[:7], kept[7:]
    turned_middle, turned_feed, d_gu_low, hidden, final = late
    (s_qkv, s_gate, s_up, keep_sems), refs = refs[:4], refs[4:]
    shards = (s_qkv, c_out, s_gate, s_up, c_down)
    gains, scale_out, scale_qkv = vectors[0:4], vectors[SCALE_OUT], vectors[SCALE_QKV, : 2 * HD]
    scale_down, scale_gu = vectors[SCALE_DOWN], vectors[SCALE_GU]
    (wq, wo, low, rq, rkv, held, part), refs = refs[:7], refs[7:]
    (held_x, held_z, stage, block, *row_sems), refs = refs[:7], refs[7:]
    (wg, wu, wd, nm, gu_pre, feed_part, cot, d_feed, dgs), refs = refs[:9], refs[9:]
    (held_x_f, held_z_f, stage_f, feed_block, *feed_sems), refs = refs[:7], refs[7:]
    turned, refs = refs[:3], refs[3:]
    (send_g, recv_g, local_g, send, recv_q, recv_kv, send_back, recv_back, local) = refs
    y, zh, core, t = here()
    me = rank(y, zh, core)
    half = lax.rem(t, 2)
    other = t + 1 - 2 * half
    owner = (y < 3) & (core == 0)
    units = [(m, w) for m in range(2) for w in range(3)]
    gathers = [
        Gather(src, out, send_g.at[k], recv_g.at[k], local_g.at[k])
        for k, (src, out) in enumerate(zip(shards, (wq, wo, wg, wu, wd)))
    ]
    g_qkv, g_out, g_gate, g_up, g_down = gathers
    rows = Rows(part, held_x, held_z, stage, block, nm, row_sems)
    feeds = Rows(feed_part, held_x_f, held_z_f, stage_f, feed_block, d_feed, feed_sems, None, turned)
    barrier = pltpu.get_barrier_semaphore()

    def signal(dp, tensor):
        pl.semaphore_signal(barrier, inc=1, device_id=(dp, tensor), device_id_type=MESH)

    plane = [(g_qkv.sib, t), (g_qkv.zz, t)] + [(dp, t) for dp in g_qkv.fore] + rows.peers()
    for device in plane:
        signal(*device)

    @pl.when(owner)
    def _():
        def each(d, _):
            pl.when(d != me)(lambda: signal(d, t))
            signal(d, other)
            return 0

        lax.fori_loop(0, 16, each, 0)

    for m, w in units:
        pl.when(unit_owner(m, w) != me)(functools.partial(signal, unit_owner(m, w), t))

    s_qkv[:, :HD] = c_query[...].astype(B16)
    s_qkv[:, HD : HD + 128] = c_key[...].astype(B16)
    s_qkv[:, HD + 128 :] = c_value[...].astype(B16)
    s_gate[...] = c_gate[...].astype(B16)
    s_up[...] = c_up[...].astype(B16)
    inputs = tokens[...].astype(F32)
    normed_input[...] = (inputs * inverse_rms(inputs) * (1.0 + gains[0:1])).astype(B16)
    keeps = []

    def keep(i, index=None):
        src, dst = (kept[i], homes[i]) if index is None else (kept[i].at[index], homes[i].at[index])
        copy = pltpu.make_async_copy(src, dst, keep_sems.at[len(keeps)])
        copy.start()
        keeps.append(copy)

    @pl.when(owner)
    def _():
        pl.semaphore_wait(barrier, len(plane) + 26)

    @pl.when(jnp.logical_not(owner))
    def _():
        pl.semaphore_wait(barrier, len(plane) + 12)

    g_qkv.start()
    for b in range(4):
        angle = places[:, b : b + 1] * rates[...]
        cosine[b], sine[b] = jnp.cos(angle), jnp.sin(angle)
    g_qkv.over_y()
    g_qkv.over_z()
    g_qkv.near()
    g_out.start()
    g_gate.start()
    g_qkv.far()
    g_qkv.end()

    for i in range(2):
        cols = slice(HD * i, HD * i + HD)
        codes = wq[:, :, cols].reshape(WIDE, HD)
        for w in range(3):
            product = dot(normed_input[...], level(codes, w), 1, 0) * scale_qkv[:, cols]
            qkv_pre[w, :, cols] = product
            low[w, :, :, cols] = product.astype(B16).reshape(2, 64, HD)

    def to_owner(u, m, w, start):
        o = unit_owner(m, w)
        q_src, kv_src = low.at[w, m, :, pl.ds(0, HD)], low.at[w, m, :, pl.ds(HD, HD)]
        across = remote(kv_src, rkv.at[half, me], send.at[u, 2], recv_kv.at[half, me], o, other)
        away = [
            remote(q_src, rq.at[me], send.at[u, 0], recv_q.at[me], o, t),
            remote(kv_src, rkv.at[half, me], send.at[u, 1], recv_kv.at[half, me], o, t),
        ]
        near = [
            pltpu.make_async_copy(q_src, rq.at[me], local.at[0]),
            pltpu.make_async_copy(kv_src, rkv.at[half, me], local.at[1]),
        ]

        @pl.when(o != me)
        def _():
            for copy in away:
                copy.start() if start else copy.wait_send()

        @pl.when(o == me)
        def _():
            for copy in near:
                copy.start() if start else copy.wait()

        across.start() if start else across.wait_send()

    for u, (m, w) in enumerate(units):
        to_owner(u, m, w, True)
    for gather in (g_out, g_gate):
        gather.over_y()
        gather.over_z()

    @pl.when(owner)
    def _():
        for u, (m, w) in enumerate(units):

            @pl.when(unit_owner(m, w) == me)
            def _():
                for i in range(2):
                    ref = (rq.at[me], rkv.at[half, me])[i]
                    pltpu.make_async_copy(ref, ref, local.at[i]).wait()

        def each(d, _):
            @pl.when(d != me)
            def _():
                remote(rq.at[d], rq.at[d], send.at[0, 0], recv_q.at[d], me, other).wait_recv()
                remote(
                    rkv.at[half, d], rkv.at[half, d], send.at[0, 0], recv_kv.at[half, d], me, other
                ).wait_recv()

            remote(
                rkv.at[1 - half, d], rkv.at[1 - half, d], send.at[0, 0], recv_kv.at[1 - half, d], me, other
            ).wait_recv()
            return 0

        lax.fori_loop(0, 16, each, 0)
        for b in range(4):
            rows_b = slice(16 * b, 16 * b + 16)
            c, s = cosine[b], sine[b]
            q = rq[:, rows_b, :].reshape(256, HD).astype(F32)
            q_rot[b] = rotate(q, c, s).astype(B16)
            k = jnp.concatenate(
                [rkv[i, :, rows_b, : HD // 2].reshape(256, HD // 2) for i in range(2)], -1
            )
            k_rot[b] = rotate(k.astype(F32), c, s).astype(B16)
            v_all[b] = jnp.concatenate(
                [rkv[i, :, rows_b, HD // 2 :].reshape(256, HD // 2) for i in range(2)], -1
            )
        for b in range(4):
            keys = {kb: k_rot[kb] for kb in range(max(0, b - 2), b + 1)}
            _, probs = block_probs(q_rot[b], keys, first[:, b : b + 1], b)
            out = sum(
                dot(p.astype(B16), v_all[kb], 1, 0) for p, kb in zip(probs, sorted(keys))
            )
            held[:, 16 * b : 16 * b + 16, :] = out.astype(B16).reshape(16, 16, HD)

        def hand_back(d, start):
            @pl.when(d != me)
            def _():
                copy = remote(
                    held.at[d], att.at[y, zh], send_back.at[d], recv_back.at[zh * 3 + y], d, t
                )
                copy.start() if start else copy.wait_send()

            @pl.when(d == me)
            def _():
                copy = pltpu.make_async_copy(held.at[d], att.at[y, zh], local.at[0])
                copy.start() if start else copy.wait()

        lax.fori_loop(0, 16, lambda d, _: (hand_back(d, True), 0)[1], 0)
        lax.fori_loop(0, 16, lambda d, _: (hand_back(d, False), 0)[1], 0)

    g_out.near()
    g_out.far()
    g_up.start()
    g_out.end()
    g_gate.near()
    for u, (m, w) in enumerate(units):

        @pl.when(unit_owner(m, w) != me)
        def _():
            ref = att.at[w, m]
            remote(ref, ref, send.at[0, 0], recv_back.at[u], me, other).wait_recv()

    codes = wo[...].reshape(WIDE, HD)
    for w in range(3):
        product = dot(att[w].reshape(ROWS, HD), level(codes, w), 1, 1) * scale_out
        part[w] = product.astype(B16).reshape(2, 4, SLICE, WIDE)
        rows.scatter_x(w)
    for i, (src, dst) in enumerate(((wq, w_qkv), (wo, w_out))):
        keeps.append(pltpu.make_async_copy(src, dst, keep_sems.at[i]))
        keeps[i].start()
    for i in (0, 1, 2, 5, 6):
        keep(i)
    load = pltpu.make_async_copy(cotangent.at[:, rows.zl, rows.x], cot, local.at[2])
    load.start()
    g_gate.far()
    g_up.over_y()
    g_up.over_z()
    g_down.start()
    for w in range(3):
        rows.scatter_z(w)
    mine = tokens[pl.ds(pl.multiple_of(t * SLICE, SLICE), SLICE)].astype(F32)
    for w in range(3):
        signal_w = rows.total(w)
        branch[w] = signal_w
        total = mine + signal_w * inverse_rms(signal_w) * (1.0 + gains[1:2])
        middle[w] = total
        block[w] = (total * inverse_rms(total) * (1.0 + gains[2:3])).astype(B16)
        rows.spread(w)
    keep(3)
    keep(4)
    g_up.near()
    for w in range(3):
        rows.forward(w)
    g_down.over_y()
    g_down.over_z()
    g_gate.end()

    def forward(w):
        stride = STRIDES[w]
        left = nm[w].reshape(ROWS, WIDE)
        extra = offset(left, w)
        for k, codes in enumerate((wg, wu)):
            if w == 0 and k == 1:
                g_up.far()
                g_up.end()
            cols = slice(FF * k, FF * k + FF)
            product = dot(left, half_level(codes[...].reshape(WIDE, FF), w), 1, 0)
            gu_pre[w, :, cols] = (product + extra) * (scale_gu[:, cols] * stride)
        gate_pre, up_pre = gu_pre[w, :, :FF], gu_pre[w, :, FF:]
        grown, _ = gelu_parts(gate_pre)
        low = (grown * up_pre).astype(B16)
        hidden[w] = low
        extra_down = offset(low, w)

        if w == 0:
            g_down.near()
            g_down.far()
            g_down.end()
        product = dot(low, half_level(wd[...].reshape(WIDE, FF), w), 1, 1)
        product = (product + extra_down) * (scale_down * stride)
        feed_part[w] = product.astype(B16).reshape(2, 4, SLICE, WIDE)
        feeds.scatter_x(w)

    def norm(w):
        signal = feeds.total(w)
        inverse = inverse_rms(signal)
        normed = signal * inverse
        upstream = cot[w].astype(F32)
        lowered = norm_back(normed, inverse, gains[3:4], upstream).astype(B16)
        feed_block[w] = lowered
        feeds.spread(w)
        final[w] = (middle[w] + normed * (1.0 + gains[3:4])).astype(B16)
        for i, term in enumerate((upstream * normed, lowered.astype(F32) * signal)):
            term = jnp.sum(term, axis=0, keepdims=True)
            sums[i : i + 1] = term if w == 0 else sums[i : i + 1] + term

    def backward(w):
        stride = STRIDES[w]
        lowered = d_feed[w].reshape(ROWS, WIDE)
        turned_feed[:, w * ROWS : (w + 1) * ROWS] = lowered.T
        scaled = (lowered.astype(F32) * scale_down).astype(B16)
        extra = offset(scaled, w)
        for i in range(3):
            cols = slice(384 * i, 384 * i + 384)
            ups = slice(FF + 384 * i, FF + 384 * i + 384)
            d_hidden = (dot(scaled, half_level(wd[:, :, cols].reshape(WIDE, 384), w), 1, 0) + extra) * float(stride)
            grown, rate = gelu_parts(gu_pre[w, :, cols])
            for where, value in ((cols, d_hidden * gu_pre[w, :, ups] * rate), (ups, d_hidden * grown)):
                low = value.astype(B16)
                d_gu_low[w, :, where] = low
                dgs[:, where] = (value * scale_gu[:, where]).astype(B16)
                term = jnp.sum(low.astype(F32) * gu_pre[w, :, where], axis=0, keepdims=True)
                term = term / scale_gu[:, where]
                gu_sums[:, where] = term if w == 0 else gu_sums[:, where] + term
        left = dgs[...]
        extra_gu = offset(left, w)

        keep(10, w)
        keep(9, (slice(None), pl.ds(w * ROWS, ROWS)))
        product = sum(
            dot(left[:, FF * k : FF * k + FF], half_level(codes[...].reshape(WIDE, FF), w), 1, 1)
            for k, codes in enumerate((wg, wu))
        )
        product = (product + extra_gu) * float(stride)
        d_part[w] = product.astype(B16).reshape(2, 4, SLICE, WIDE)
        keep(7, w)

    rows.end(0)
    forward(0)
    rows.end(1)
    forward(1)
    feeds.scatter_z(0)
    rows.end(2)
    forward(2)
    load.wait()
    feeds.scatter_z(1)
    norm(0)
    feeds.scatter_z(2)
    norm(1)
    feeds.forward(0)
    norm(2)
    feeds.forward(1)
    for w in range(3):
        turned_middle[:, w * ROWS : (w + 1) * ROWS] = nm[w].reshape(ROWS, WIDE).T
    for i in (8, 11, 12):
        keep(i)
    feeds.end(0)
    backward(0)
    feeds.forward(2)
    feeds.end(1)
    backward(1)
    feeds.end(2)
    backward(2)
    for copy in keeps:
        copy.wait()
    for u, (m, w) in enumerate(units):
        o = unit_owner(m, w)

        @pl.when(o != me)
        def _():
            for slot, src in enumerate((low.at[w, m, :, pl.ds(0, HD)], low.at[w, m, :, pl.ds(HD, HD)])):
                remote(src, src, send.at[u, slot], recv_q.at[0], o, t).wait_send()

        src = low.at[w, m, :, pl.ds(HD, HD)]
        remote(src, src, send.at[u, 2], recv_q.at[0], o, other).wait_send()
    rows.drain()
    feeds.drain()
    for gather in gathers:
        gather.drain()


KEPT = (
    ((3, 2, 64, HD), B16),
    ((ROWS, WIDE), B16),
    ((3, ROWS, 2 * HD), F32),
    ((3, SLICE, WIDE), F32),
    ((3, SLICE, WIDE), F32),
    ((4, 256, HD // 2), F32),
    ((4, 256, HD // 2), F32),
    ((3, 2, 4, SLICE, WIDE), B16),
    ((WIDE, 3 * ROWS), B16),
    ((WIDE, 3 * ROWS), B16),
    ((3, ROWS, 2 * FF), B16),
    ((3, ROWS, FF), B16),
    ((3, SLICE, WIDE), B16),
)


def forward_pass(*operands):
    return pl.pallas_call(
        forward_kernel,
        name="forward",
        out_shape=[struct((16, SHARD, 2 * HD), B16), struct((16, SHARD, HD), B16)]
        + [struct(*kept) for kept in KEPT]
        + [struct((4, 256, HD), B16)] * 3
        + [struct((8, WIDE), F32), struct((1, 2 * FF), F32)],
        in_specs=vmem_space(len(operands) - 1) + any_space(1),
        out_specs=any_space(15) + vmem_space(5),
        scratch_shapes=[pltpu.VMEM(*kept) for kept in KEPT]
        + [
            pltpu.VMEM((SHARD, 2 * HD), B16),
            pltpu.VMEM((SHARD, FF), B16),
            pltpu.VMEM((SHARD, FF), B16),
            pltpu.SemaphoreType.DMA((21,)),
        ]
        + [
            pltpu.VMEM((16, SHARD, 2 * HD), B16),
            pltpu.VMEM((16, SHARD, HD), B16),
            pltpu.VMEM((3, 2, 64, 2 * HD), B16),
            pltpu.VMEM((16, 64, HD), B16),
            pltpu.VMEM((2, 16, 64, HD), B16),
            pltpu.VMEM((16, 64, HD), B16),
            pltpu.VMEM((3, 2, 4, SLICE, WIDE), B16),
        ]
        + rows_scratch(3)
        + [pltpu.VMEM((16, SHARD, FF), B16)] * 3
        + [
            pltpu.VMEM((3, 2, 4, SLICE, WIDE), B16),
            pltpu.VMEM((3, ROWS, 2 * FF), F32),
            pltpu.VMEM((3, 2, 4, SLICE, WIDE), B16),
            pltpu.VMEM((3, SLICE, WIDE), B16),
            pltpu.VMEM((3, 2, 4, SLICE, WIDE), B16),
            pltpu.VMEM((ROWS, 2 * FF), B16),
        ]
        + rows_scratch(3)
        + turned_scratch(1152)
        + [
            pltpu.SemaphoreType.DMA((5, 29)),
            pltpu.SemaphoreType.DMA((5, 29)),
            pltpu.SemaphoreType.DMA((5,)),
            pltpu.SemaphoreType.DMA((6, 3)),
            pltpu.SemaphoreType.DMA((16,)),
            pltpu.SemaphoreType.DMA((2, 16)),
            pltpu.SemaphoreType.DMA((16,)),
            pltpu.SemaphoreType.DMA((6,)),
            pltpu.SemaphoreType.DMA((3,)),
        ],
        compiler_params=params(3),
    )(*operands)


GRADIENTS = (1152, 1152, 1152, HD, 2 * HD)


def back_kernel(*refs):
    (part, cotangent), refs = refs[:2], refs[2:]
    sources, refs = refs[:13], refs[13:]
    (turned_middle, d_gu, middle, branch, final, feed_sums, gu_sums, vectors, first), refs = refs[:9], refs[9:]
    (results, gradient, totals), refs = refs[:3], refs[3:]
    (g_query, g_key, g_value), outs, refs = refs[4:7], refs[:4], refs[7:]
    outs = (*outs, (g_query, g_key, g_value))
    gains, scale_out, scale_down = vectors[0:4], vectors[SCALE_OUT], vectors[SCALE_DOWN]
    scale_qkv = vectors[SCALE_QKV, : 2 * HD]
    aways, refs = refs[:2], refs[2:]
    reduces = []
    for k, columns in enumerate(GRADIENTS):
        held, refs = refs[:8], refs[8:]
        away = aways[k % 2]
        reduces.append(Reduce(columns, away, *held[:6], outs[k], *held[6:]))
    g_gate, g_up, g_down, g_out, g_qkv = reduces
    (own_part, cot, d_branch), refs = refs[:3], refs[3:]
    (held_x, held_z, stage, block, *row_sems), refs = refs[:7], refs[7:]
    (part_in, held_x1, held_z1, stage1, block1, *row_sems1), refs = refs[:8], refs[8:]
    result_sems, refs = refs[:3], refs[3:]
    (vec_x, vec_z, vec_sib, vec_y, vec_zz, vec, send_v, recv_v), refs = refs[:8], refs[8:]
    (datt, rdo, held_q, held_kv, acc_k, acc_v, d_query, d_kv), refs = refs[:8], refs[8:]
    (send, recv, send_q, send_kv, recv_q, recv_kv, local), refs = refs[:7], refs[7:]
    places, load_sems = refs[:13], refs[13]
    (turned_feed, hidden, w_out, w_qkv, attended, q_rot, k_rot, v_all, cosine, sine), refs = places[:10], places[10:]
    normed_input, tokens, qkv_pre = refs
    arrivals = [
        pltpu.make_async_copy(src, dst, load_sems.at[i])
        for i, (src, dst) in enumerate(zip(sources, places))
    ]
    for copy in arrivals:
        copy.start()
    y, zh, core, t = here()
    me = rank(y, zh, core)
    half = lax.rem(t, 2)
    other = t + 1 - 2 * half
    owner = (y < 3) & (core == 0)
    units = [(m, w) for m in range(2) for w in range(3)]
    rows = Rows(part, held_x, held_z, stage, block, d_branch, row_sems, own_part)
    rows_in = Rows(part_in, held_x1, held_z1, stage1, block1, gradient, row_sems1)
    rows_out = Rows(None, None, None, None, final, results, result_sems)
    barrier = pltpu.get_barrier_semaphore()

    def signal(dp, tensor):
        pl.semaphore_signal(barrier, inc=1, device_id=(dp, tensor), device_id_type=MESH)

    plane = [(g_gate.sib, t), (g_gate.zz, t)] + [(dp, t) for dp in g_gate.fore] + rows.peers()
    for device in plane:
        signal(*device)

    @pl.when(owner)
    def _():
        def each(d, _):
            pl.when(d != me)(lambda: signal(d, t))
            return 0

        lax.fori_loop(0, 16, each, 0)

    for m, w in units:
        pl.when(unit_owner(m, w) != me)(functools.partial(signal, unit_owner(m, w), t))
        signal(unit_owner(m, w), other)

    g_gate.product(turned_middle, d_gu)

    @pl.when(owner)
    def _():
        pl.semaphore_wait(barrier, len(plane) + 36)

    @pl.when(jnp.logical_not(owner))
    def _():
        pl.semaphore_wait(barrier, len(plane) + 6)

    for w in range(3):
        rows.scatter_x(w)
    loads = [
        pltpu.make_async_copy(part.at[:, :, rows.x], own_part, local.at[0]),
        pltpu.make_async_copy(cotangent.at[:, rows.zl, rows.x], cot, local.at[1]),
    ]
    for copy in loads:
        copy.start()
    g_gate.send_away()
    g_up.product(turned_middle, d_gu, 1152)
    g_up.send_away()
    g_gate.add()
    for copy in loads:
        copy.wait()
    rows.scatter_z(0)
    g_gate.sent_away()
    for copy in arrivals[:2]:
        copy.wait()
    g_down.product(turned_feed, hidden)
    g_down.send_away()
    rows.scatter_z(1)
    g_up.add()
    rows.scatter_z(2)
    d_middle = jnp.zeros((SLICE, WIDE), F32)
    sums = [jnp.zeros((1, WIDE), F32)] * 3
    for w in range(3):
        upstream = rows.total(w)
        signal_w = middle[w]
        inverse = inverse_rms(signal_w)
        normed = signal_w * inverse
        d_signal = cot[w].astype(F32) + norm_back(normed, inverse, gains[2:3], upstream)
        lower = branch[w]
        inverse_lower = inverse_rms(lower)
        normed_lower = lower * inverse_lower
        lowered = norm_back(normed_lower, inverse_lower, gains[1:2], d_signal).astype(B16)
        block[w] = lowered
        rows.spread(w)
        d_middle = d_middle + d_signal
        terms = (d_signal * normed_lower, upstream * normed, lowered.astype(F32) * lower)
        sums = [old + jnp.sum(new, axis=0, keepdims=True) for old, new in zip(sums, terms)]
    vec[1:2] = sums[0]
    vec[2:3] = sums[1]
    vec[3:4] = feed_sums[0:1]
    vec[4:5] = sums[2] / scale_out
    vec[5:6] = feed_sums[1:2] / scale_down

    for copy in arrivals[2:]:
        copy.wait()
    codes = w_out[...].reshape(WIDE, HD)

    def to_owner(u, m, w, start):
        o = unit_owner(m, w)
        src = datt.at[w, m]

        @pl.when(o != me)
        def _():
            copy = remote(src, rdo.at[me], send.at[u], recv.at[me], o, t)
            copy.start() if start else copy.wait_send()

        @pl.when(o == me)
        def _():
            copy = pltpu.make_async_copy(src, rdo.at[me], local.at[0])
            copy.start() if start else copy.wait()

    g_gate.cross()
    g_gate.pool()
    for w in range(3):
        rows.forward(w)
    for w in range(3):
        rows.end(w)
        scaled = (d_branch[w].reshape(ROWS, WIDE).astype(F32) * scale_out).astype(B16)
        datt[w] = dot(scaled, level(codes, w), 1, 0).astype(B16).reshape(2, 64, HD)
        for m in range(2):
            to_owner(m * 3 + w, m, w, True)
    g_up.cross()
    g_down.add()
    for w in range(3):
        rows_out.spread(w)
    for u, (m, w) in enumerate(units):
        to_owner(u, m, w, False)

    @pl.when(owner)
    def _():
        def each(d, _):
            @pl.when(d != me)
            def _():
                remote(rdo.at[d], rdo.at[d], send.at[0], recv.at[d], me, other).wait_recv()

            return 0

        lax.fori_loop(0, 16, each, 0)
        acc_k[...] = jnp.zeros_like(acc_k)
        acc_v[...] = jnp.zeros_like(acc_v)
        for b in range(4):
            rows_b = slice(16 * b, 16 * b + 16)
            blocks = list(range(max(0, b - 2), b + 1))
            queries = q_rot[b]
            keys = {kb: k_rot[kb] for kb in blocks}
            upstream = rdo[:, rows_b, :].reshape(256, HD)
            bents, probs = block_probs(queries, keys, first[:, b : b + 1], b)
            d_probs = [dot(upstream, v_all[kb], 1, 1) for kb in blocks]
            centre = sum(
                jnp.sum(p * dp, axis=-1, keepdims=True) for p, dp in zip(probs, d_probs)
            )
            d_q = jnp.zeros((256, HD), F32)
            for kb, bent, p, dp in zip(blocks, bents, probs, d_probs):
                d_scores = (p * (dp - centre) * (1.0 - bent * bent)).astype(B16)
                d_q = d_q + dot(d_scores, keys[kb], 1, 0)
                acc_k[kb] += dot(d_scores, queries, 0, 0)
                acc_v[kb] += dot(p.astype(B16), upstream, 0, 0)
            d_q = unrotate(d_q * 0.0625, cosine[b], sine[b])
            held_q[:, rows_b, :] = d_q.astype(B16).reshape(16, 16, HD)
        for b in range(4):
            rows_b = slice(16 * b, 16 * b + 16)
            d_k = unrotate(acc_k[b] * 0.0625, cosine[b], sine[b]).astype(B16)
            d_v = acc_v[b].astype(B16)
            for i in range(2):
                cols = slice(128 * i, 128 * i + 128)
                held_kv[i, :, rows_b, :128] = d_k[:, cols].reshape(16, 16, 128)
                held_kv[i, :, rows_b, 128:] = d_v[:, cols].reshape(16, 16, 128)

    def hand_back(d, start):
        u = zh * 3 + y
        across = remote(
            held_kv.at[1 - half, d], d_kv.at[half, y, zh], send_kv.at[1, d], recv_kv.at[half, u], d, other
        )
        across.start() if start else across.wait_send()

        @pl.when(d != me)
        def _():
            for copy in (
                remote(held_q.at[d], d_query.at[y, zh], send_q.at[d], recv_q.at[u], d, t),
                remote(
                    held_kv.at[half, d], d_kv.at[half, y, zh], send_kv.at[0, d], recv_kv.at[half, u], d, t
                ),
            ):
                copy.start() if start else copy.wait_send()

        @pl.when(d == me)
        def _():
            for copy in (
                pltpu.make_async_copy(held_q.at[d], d_query.at[y, zh], local.at[0]),
                pltpu.make_async_copy(held_kv.at[half, d], d_kv.at[half, y, zh], local.at[1]),
            ):
                copy.start() if start else copy.wait()

    @pl.when(owner)
    def _():
        lax.fori_loop(0, 16, lambda d, _: (hand_back(d, True), 0)[1], 0)
        lax.fori_loop(0, 16, lambda d, _: (hand_back(d, False), 0)[1], 0)

    for w in range(3):
        rows_out.forward(w)
    g_down.cross()
    g_up.sent_away()
    g_out.product_whole(d_branch[...].reshape(3 * ROWS, WIDE), attended[...])
    g_gate.merge()
    g_up.pool()
    g_out.add()
    g_out.cross()
    g_up.merge()
    for u, (m, w) in enumerate(units):

        @pl.when(unit_owner(m, w) != me)
        def _():
            ref = d_query.at[w, m]
            remote(ref, ref, send.at[0], recv_q.at[u], me, other).wait_recv()
            ref = d_kv.at[half, w, m]
            remote(ref, ref, send.at[0], recv_kv.at[half, u], me, other).wait_recv()

        ref = d_kv.at[1 - half, w, m]
        remote(ref, ref, send.at[0], recv_kv.at[1 - half, u], me, other).wait_recv()

    codes = w_qkv[...].reshape(WIDE, 2 * HD)
    scaled = []
    qkv_sums = jnp.zeros((1, 2 * HD), F32)
    d_qkv_all = jnp.zeros((ROWS, 2 * HD), F32)
    for w in range(3):
        both = (d_kv[0, w].astype(F32) + d_kv[1, w].astype(F32)).astype(B16).astype(F32)
        d_qkv = jnp.concatenate([d_query[w].astype(F32), both], -1).reshape(ROWS, 2 * HD)
        qkv_sums = qkv_sums + jnp.sum(d_qkv * qkv_pre[w], axis=0, keepdims=True)
        d_qkv_all = d_qkv_all + d_qkv
        scaled.append((d_qkv * scale_qkv).astype(B16))
    whole = tokens[...].astype(F32)
    inverse = inverse_rms(whole)
    for i in range(3):
        tile = slice(768 * i, 768 * i + 768)
        d_input = sum(dot(scaled[w], level(codes[tile], w), 1, 1) for w in range(3))
        part_in[0, :, :, :, tile] = d_input.astype(B16).reshape(2, 4, SLICE, 768)
        normed = tokens[:, tile].astype(F32) * inverse
        vec[0:1, tile] = jnp.sum(d_input * normed, axis=0, keepdims=True)
    rows_in.scatter_x(0)

    vec[6:8] = jnp.zeros((2, WIDE), F32)
    x = rows.x
    copies = []

    def exchange(slot, src, dst, dp, tensor):
        copy = remote(src, dst, send_v.at[slot], recv_v.at[slot], dp, tensor)
        copy.start()
        copies.append(copy)

    def exchanged(slot, ref):
        remote(ref, ref, send_v.at[slot], recv_v.at[slot], me, other).wait_recv()

    vec_x[x] = vec[...]
    for k in range(3):
        exchange(k, vec_x.at[x], vec_x.at[x], me, rows.x_peers[k])
    g_down.sent_away()
    g_qkv.product_whole(normed_input[...], d_qkv_all.astype(B16))
    for k in range(3):
        exchanged(k, vec_x.at[rows.behind[k]])
    vec[...] = functools.reduce(jnp.add, [vec_x[i] for i in range(4)])
    exchange(3, vec, vec_z, me, rows.z_peer)
    rows_in.scatter_z(0)
    g_qkv.add()
    g_qkv.cross()
    g_down.pool()
    g_down.merge()
    exchanged(3, vec_z)
    copies[3].wait_send()
    vec[0:6] = vec[0:6] + vec_z[0:6]
    vec[6:7] = gu_sums[...]
    vec[7:8, : 2 * HD] = qkv_sums / scale_qkv
    exchange(4, vec, vec_sib, g_gate.sib, t)

    upstream = rows_in.total(0)
    signal_in = tokens[pl.ds(pl.multiple_of(t * SLICE, SLICE), SLICE)].astype(F32)
    inverse = inverse_rms(signal_in)
    normed = norm_back(signal_in * inverse, inverse, gains[0:1], upstream)
    block1[0] = (d_middle + normed).astype(B16)
    rows_in.spread(0)
    g_qkv.merge()
    g_qkv.pool()
    exchanged(4, vec_sib)
    vec_y[y] = vec[...] + vec_sib[...]
    for i in range(3):
        exchange(5 + i, vec_y.at[y], vec_y.at[y], g_gate.fore[i], t)
    rows_in.forward(0)
    g_out.merge()
    g_out.pool()
    g_gate.end()
    g_up.end()
    for i in range(3):
        exchanged(5 + i, vec_y.at[lax.rem(y + 3 - i, 4)])
    copies[4].wait_send()
    vec[...] = functools.reduce(jnp.add, [vec_y[i] for i in range(4)])
    exchange(8, vec, vec_zz, g_gate.zz, t)
    g_down.end()
    g_out.end()
    g_qkv.end()
    exchanged(8, vec_zz)
    totals[...] = vec[...] + vec_zz[...]
    rows_in.end(0)
    for w in range(3):
        rows_out.end(w)
    g_out.sent_away()
    g_qkv.sent_away()
    for k in (0, 1, 2, 5, 6, 7, 8):
        copies[k].wait_send()
    for part_of in (rows, rows_in, rows_out, *reduces):
        part_of.drain()


def back(hbm, late, vmem):
    def vec():
        return pltpu.VMEM((8, WIDE), F32)

    scratch = [pltpu.VMEM((8, SHARD, 1152), B16)] * 2
    for columns in GRADIENTS:
        scratch += reduce_scratch(columns)
    scratch += [
        pltpu.VMEM((3, 2, SLICE, WIDE), B16),
        pltpu.VMEM((3, SLICE, WIDE), B16),
        pltpu.VMEM((3, 2, 4, SLICE, WIDE), B16),
    ]
    scratch += rows_scratch(3)
    scratch += [pltpu.VMEM((1, 2, 4, SLICE, WIDE), B16)] + rows_scratch(1)
    scratch += rows_scratch(3)[4:]
    scratch += [pltpu.VMEM((4, 8, WIDE), F32), vec(), vec(), pltpu.VMEM((4, 8, WIDE), F32), vec(), vec()]
    scratch += [pltpu.SemaphoreType.DMA((9,))] * 2
    scratch += [
        pltpu.VMEM((3, 2, 64, HD), B16),
        pltpu.VMEM((16, 64, HD), B16),
        pltpu.VMEM((16, 64, HD), B16),
        pltpu.VMEM((2, 16, 64, HD), B16),
        pltpu.VMEM((4, 256, HD), F32),
        pltpu.VMEM((4, 256, HD), F32),
        pltpu.VMEM((3, 2, 64, HD), B16),
        pltpu.VMEM((2, 3, 2, 64, HD), B16),
        pltpu.SemaphoreType.DMA((6,)),
        pltpu.SemaphoreType.DMA((16,)),
        pltpu.SemaphoreType.DMA((16,)),
        pltpu.SemaphoreType.DMA((2, 16)),
        pltpu.SemaphoreType.DMA((6,)),
        pltpu.SemaphoreType.DMA((2, 6)),
        pltpu.SemaphoreType.DMA((2,)),
    ]
    scratch += [pltpu.VMEM(array.shape, array.dtype) for array in late]
    scratch += [pltpu.SemaphoreType.DMA((len(late),))]
    return pl.pallas_call(
        back_kernel,
        name="back",
        out_shape=[
            struct((3, 2, 4, SLICE, WIDE), B16),
            struct((1, 2, 4, SLICE, WIDE), B16),
            struct((8, WIDE), F32),
        ]
        + [struct((SHARD, columns), F32) for columns in (1152, 1152, 1152, HD, HD, 128, 128)],
        in_specs=any_space(len(hbm) + len(late)) + vmem_space(len(vmem)),
        out_specs=any_space(2) + vmem_space(8),
        scratch_shapes=scratch,
        compiler_params=params(4),
    )(*hbm, *late, *vmem)


def level(codes, width):
    if width == 0:
        return codes
    stride = STRIDES[width]
    return jnp.floor(codes * B16(1.0 / stride)) * B16(stride) + B16(stride // 2)


def gelu_parts(value):
    slope = 0.7978845608028654
    inner = jnp.tanh(slope * (value + 0.044715 * value * value * value))
    grown = 0.5 * value * (1.0 + inner)
    rate = 0.5 * (1.0 + inner) + 0.5 * value * (1.0 - inner * inner) * slope * (
        1.0 + 3 * 0.044715 * value * value
    )
    return grown, rate


def side_by_side(*parts):
    total, first = 0.0, 0
    for part in parts:
        total = total + jnp.pad(part, (first, WIDE - first - part.shape[0]))
        first += part.shape[0]
    return total


def body(
    tokens,
    cotangent,
    segments,
    codes_query,
    codes_key,
    codes_value,
    codes_out,
    codes_gate,
    codes_up,
    codes_down,
    query_column_scale,
    key_column_scale,
    value_column_scale,
    output_column_scale,
    gate_column_scale,
    up_column_scale,
    down_column_scale,
    gain_first,
    gain_second,
    gain_third,
    gain_fourth,
):
    z_hi = lax.rem(lax.div(lax.axis_index("dp"), 2), 2)
    tokens = tokens.reshape(ROWS, WIDE)
    cotangent = cotangent.reshape(3, ROWS, WIDE)
    entries = [gain_first, gain_second, gain_third, gain_fourth, output_column_scale, down_column_scale]
    entries += [side_by_side(gate_column_scale, up_column_scale)]
    entries += [side_by_side(query_column_scale, key_column_scale, value_column_scale)]
    row = lax.broadcasted_iota(jnp.int32, (8, WIDE), 0)
    vectors = functools.reduce(
        lambda rest, i: jnp.where(row == i, entries[i][None], rest), range(7), entries[7][None]
    )
    documents = lax.dynamic_index_in_dim(segments, z_hi, 0, False)
    starts = jnp.sum((documents[None, :] < documents[:, None]).astype(jnp.int32), axis=1)
    place = jnp.arange(1024, dtype=jnp.int32)

    def blocked(rows):
        return rows.reshape(4, 16, 16).transpose(0, 2, 1).reshape(4, 256)

    first = blocked(starts).T
    expo = jnp.arange(HD // 2, dtype=F32) * (2.0 / HD)
    rates = jnp.power(ROPE_BASE, -expo)[None]

    grid = (3, 2, 4, SLICE, WIDE)
    w_qkv, w_out, attended, normed_input, qkv_pre, branch, middle, cosine, sine, *rest = forward_pass(
        codes_query,
        codes_key,
        codes_value,
        codes_out.astype(B16).T,
        codes_gate,
        codes_up,
        codes_down.astype(B16).T,
        tokens,
        vectors,
        blocked(place - starts).astype(F32).T,
        first,
        rates,
        cotangent.reshape(grid),
    )
    d_part, turned_middle, turned_feed, d_gu, hidden, final, *rest = rest
    q_rot, k_rot, v_all, feed_sums, gu_sums = rest
    flat = (3 * ROWS, -1)
    results, input_gradient, totals, g_gate, g_up, g_down, g_out, g_query, g_key, g_value = back(
        [d_part, cotangent.reshape(grid)],
        [
            turned_feed,
            hidden.reshape(flat),
            w_out,
            w_qkv,
            attended.reshape(flat),
            q_rot,
            k_rot,
            v_all,
            cosine,
            sine,
            normed_input,
            tokens,
            qkv_pre,
        ],
        [turned_middle, d_gu.reshape(flat), middle, branch, final, feed_sums, gu_sums, vectors, first],
    )
    rows = lax.dynamic_slice_in_dim(totals, lax.axis_index("dp") * SHARD, SHARD, 1)
    return (
        results.reshape(3, 2, 64, 1, WIDE),
        input_gradient.astype(F32).reshape(2, 64, 1, WIDE),
        g_query,
        g_key,
        g_value,
        g_out.T,
        g_gate,
        g_up,
        g_down.T,
        totals[7, :256],
        totals[7, 256:384],
        totals[7, 384:512],
        rows[4],
        totals[6, :FF],
        totals[6, FF:],
        rows[5],
        rows[0],
        rows[1],
        rows[2],
        rows[3],
    )


def solution(mesh):
    matrix, turned = P("dp", "tensor"), P("tensor", "dp")
    columns, whole, shard = P("tensor"), P(), P("dp")
    in_specs = (
        P(None, None, "dp", None),
        P(None, None, None, "dp", None),
        whole,
        *(matrix, matrix, matrix, turned, matrix, matrix, turned),
        *(columns, columns, columns, whole, columns, columns, whole),
        *(whole, whole, whole, whole),
    )
    out_specs = (
        P(None, None, None, "dp", None),
        P(None, None, "dp", None),
        *(matrix, matrix, matrix, turned, matrix, matrix, turned),
        *(columns, columns, columns, shard, columns, columns, shard),
        *(shard, shard, shard, shard),
    )
    return jax.shard_map(body, mesh=mesh, in_specs=in_specs, out_specs=out_specs, check_vma=False)
```

```python
import functools

import jax
import jax.numpy as jnp
from jax import lax
from jax.experimental import pallas as pl
from jax.experimental.pallas import tpu as pltpu
from jax.sharding import PartitionSpec as P

MESH = pl.DeviceIdType.MESH
F32 = jnp.float32
B16 = jnp.bfloat16
EPSILON = 1e-06
SOFTCAP = 50.0
ROPE_BASE = 10000.0
MASKED = -1e30
HD = 256
WIDE = 2304
FF = 1152
STRIDES = (1, 16, 64)
SCALE_OUT, SCALE_DOWN, SCALE_GU, SCALE_QKV = (slice(i, i + 1) for i in range(4, 8))
SHARD = 144
LOW = 64
HIGH = SHARD - LOW
RLOW = 112
RHIGH = SHARD - RLOW
TENSOR = 8
ROWS = 128
SLICE = ROWS // TENSOR
VMEM_BYTES = 63 * 2**20


def here():
    dp = lax.axis_index("dp")
    return lax.div(dp, 4), lax.rem(lax.div(dp, 2), 2), lax.rem(dp, 2), lax.axis_index("tensor")


def rank(y, z_hi, core):
    return (y * 2 + z_hi) * 2 + core


def remote(src, dst, send, recv, dp, tensor):
    return pltpu.make_async_remote_copy(
        src, dst, send, recv, device_id=(dp, tensor), device_id_type=MESH
    )


def greet(devices):
    barrier = pltpu.get_barrier_semaphore()
    for device in devices:
        pl.semaphore_signal(barrier, inc=1, device_id=device, device_id_type=MESH)
    pl.semaphore_wait(barrier, len(devices))


def struct(shape, dtype):
    return jax.ShapeDtypeStruct(shape, dtype)


def any_space(count):
    return [pl.BlockSpec(memory_space=pl.ANY)] * count


def vmem_space(count):
    return [pl.BlockSpec(memory_space=pltpu.VMEM)] * count


def params(collective_id):
    return pltpu.CompilerParams(
        collective_id=collective_id, has_side_effects=True, vmem_limit_bytes=VMEM_BYTES
    )


class Gather:
    def __init__(self, src, out, send, recv, local):
        self.src, self.out, self.send, self.recv, self.local = src, out, send, recv, local
        self.y, self.zh, self.core, self.t = here()
        y, zh, core = self.y, self.zh, self.core
        self.me, self.sib, self.zz = rank(y, zh, core), rank(y, zh, 1 - core), rank(y, 1 - zh, core)
        self.fore = [rank(lax.rem(y + dy, 4), zh, core) for dy in (1, 2, 3)]
        self.behind = [lax.rem(y + 4 - dy, 4) for dy in (1, 2, 3)]
        self.low, self.high = pl.ds(0, LOW), pl.ds(LOW, HIGH)
        self.started = []

    def push(self, slot, src, dst, dp):
        copy = remote(src, dst, self.send.at[slot], self.recv.at[slot], dp, self.t)
        copy.start()
        self.started.append(copy)

    def arrive(self, slot, ref):
        remote(ref, ref, self.send.at[slot], self.recv.at[slot], self.sib, self.t).wait_recv()

    def start(self):
        src, mine = self.src, self.out.at[self.me]
        self.mine = pltpu.make_async_copy(src, mine, self.local)
        self.mine.start()
        low, high = self.low, self.high
        self.push(0, src.at[low], self.out.at[self.me, low], self.zz)
        for i in range(3):
            self.push(4 + i, src.at[high], self.out.at[self.me, high], self.fore[i])
        for i in range(3):
            self.push(1 + i, src.at[low], self.out.at[self.me, low], self.fore[i])
        self.push(7, src.at[high], self.out.at[self.me, high], self.zz)
        self.push(14, src, mine, self.sib)

    def over_y(self):
        block = self.out.at[self.zz, self.low]
        self.arrive(0, block)
        for i in range(3):
            self.push(8 + i, block, block, self.fore[i])
        self.push(15, block, block, self.sib)

    def over_z(self):
        for i in range(3):
            block = self.out.at[rank(self.behind[i], self.zh, self.core), self.high]
            self.arrive(4 + i, block)
            self.push(11 + i, block, block, self.zz)
            self.push(16 + i, block, block, self.sib)

    def near(self):
        for i in range(3):
            block = self.out.at[rank(self.behind[i], self.zh, self.core), self.low]
            self.arrive(1 + i, block)
            self.push(19 + i, block, block, self.sib)
        block = self.out.at[self.zz, self.high]
        self.arrive(7, block)
        self.push(22, block, block, self.sib)

    def far(self):
        for i in range(3):
            dp = rank(self.behind[i], 1 - self.zh, self.core)
            for slot, rows in ((0, self.low), (3, self.high)):
                block = self.out.at[dp, rows]
                self.arrive(8 + slot + i, block)
                self.push(23 + slot + i, block, block, self.sib)

    def end(self):
        out, low, high, other = self.out, self.low, self.high, 1 - self.core
        self.arrive(14, out.at[self.sib])
        far = rank(self.y, 1 - self.zh, other)
        self.arrive(15, out.at[far, low])
        self.arrive(22, out.at[far, high])
        for i in range(3):
            near, far = (rank(self.behind[i], zh, other) for zh in (self.zh, 1 - self.zh))
            self.arrive(16 + i, out.at[near, high])
            self.arrive(19 + i, out.at[near, low])
            self.arrive(23 + i, out.at[far, low])
            self.arrive(26 + i, out.at[far, high])
        self.mine.wait()

    def drain(self):
        for copy in self.started:
            copy.wait_send()


class Rows:
    def __init__(self, part, held_x, held_z, stage, block, out, sems, own=None, turned=None):
        self.part, self.own, self.out, self.block = part, own, out, block
        self.held_x, self.held_z, self.stage = held_x, held_z, stage
        self.send, self.recv, self.local = sems
        self.turned = turned
        self.split = WIDE if turned is None else WIDE - turned[0].shape[-1]
        self.low, self.high = pl.ds(0, self.split), pl.ds(self.split, WIDE - self.split)
        self.dp, self.t = lax.axis_index("dp"), lax.axis_index("tensor")
        self.zl, self.x = lax.div(self.t, 4), lax.rem(self.t, 4)
        self.ahead = [lax.rem(self.x + k, 4) for k in (1, 2, 3)]
        self.behind = [lax.rem(self.x + 4 - k, 4) for k in (1, 2, 3)]
        self.x_peers = [self.zl * 4 + x for x in self.ahead]
        self.z_peer = (1 - self.zl) * 4 + self.x
        self.started = []

    def peers(self):
        return [(self.dp, t) for t in self.x_peers + [self.z_peer]]

    def push(self, w, slot, src, dst, t):
        copy = remote(src, dst, self.send.at[w, slot], self.recv.at[w, slot], self.dp, t)
        copy.start()
        self.started.append(copy)

    def arrive(self, w, slot, ref):
        remote(
            ref, ref, self.send.at[w, slot], self.recv.at[w, slot], self.dp, self.z_peer
        ).wait_recv()

    def scatter_x(self, w):
        low, high = self.low, self.high
        for k in range(3):
            self.push(
                w,
                1 + k,
                self.part.at[w, :, self.ahead[k], :, low],
                self.held_x.at[w, k, :, :, low],
                self.x_peers[k],
            )
        if self.turned is not None:
            self.push(
                w, 11, self.part.at[w, 1 - self.zl, :, :, high], self.turned[0].at[w], self.z_peer
            )

    def summed_x(self, w, zl):
        own = self.part[w, zl, self.x] if self.own is None else self.own[w, zl]
        total = own[:, : self.split].astype(F32)
        for k in range(3):
            total = total + self.held_x[w, k, zl, :, : self.split].astype(F32)
        return total

    def summed_z(self, w, x):
        part = self.part[w, self.zl, x, :, self.split :].astype(F32)
        return part + self.turned[0][w, x].astype(F32)

    def scatter_z(self, w):
        for k in range(3):
            self.arrive(w, 1 + k, self.held_x.at[w, k, :, :, self.low])
        self.stage[w, :, : self.split] = self.summed_x(w, 1 - self.zl).astype(B16)
        self.push(w, 0, self.stage.at[w, :, self.low], self.held_z.at[w, :, self.low], self.z_peer)
        if self.turned is not None:
            held, stage, last = self.turned
            self.arrive(w, 11, held.at[w])
            for k in range(3):
                stage[w, k] = self.summed_z(w, self.ahead[k]).astype(B16)
                self.push(w, 12 + k, stage.at[w, k], last.at[w, k], self.x_peers[k])

    def total(self, w):
        self.arrive(w, 0, self.held_z.at[w, :, self.low])
        low = self.summed_x(w, self.zl) + self.held_z[w, :, : self.split].astype(F32)
        if self.turned is None:
            return low
        high = self.summed_z(w, self.x)
        for k in range(3):
            self.arrive(w, 12 + k, self.turned[2].at[w, k])
            high = high + self.turned[2][w, k].astype(F32)
        return jnp.concatenate([low, high], -1)

    def spread(self, w):
        block, mine = self.block.at[w], self.out.at[w, self.zl, self.x]
        self.push(w, 4, block.at[:, self.low], mine.at[:, self.low], self.z_peer)
        for k in range(3):
            self.push(w, 5 + k, block, mine, self.x_peers[k])
        pltpu.make_async_copy(block, mine, self.local.at[w]).start()

    def forward(self, w):
        block = self.out.at[w, 1 - self.zl, self.x, :, self.low]
        self.arrive(w, 4, block)
        for k in range(3):
            self.push(w, 8 + k, block, block, self.x_peers[k])
        if self.turned is not None:
            self.near(w)
            blocks = self.out.at[w, self.zl, :, :, self.high]
            self.push(w, 15, blocks, blocks, self.z_peer)

    def near(self, w):
        for k in range(3):
            self.arrive(w, 5 + k, self.out.at[w, self.zl, self.behind[k]])
        pltpu.make_async_copy(
            self.block.at[w], self.out.at[w, self.zl, self.x], self.local.at[w]
        ).wait()

    def end(self, w):
        for k in range(3):
            self.arrive(w, 8 + k, self.out.at[w, 1 - self.zl, self.behind[k], :, self.low])
        if self.turned is None:
            self.near(w)
        else:
            self.arrive(w, 15, self.out.at[w, 1 - self.zl, :, :, self.high])

    def drain(self):
        for copy in self.started:
            copy.wait_send()


def turned_scratch(columns):
    return [
        pltpu.VMEM((3, 4, SLICE, columns), B16),
        pltpu.VMEM((3, 3, SLICE, columns), B16),
        pltpu.VMEM((3, 3, SLICE, columns), B16),
    ]


def rows_scratch(depth):
    return [
        pltpu.VMEM((depth, 3, 2, SLICE, WIDE), B16),
        pltpu.VMEM((depth, SLICE, WIDE), B16),
        pltpu.VMEM((depth, SLICE, WIDE), B16),
        pltpu.VMEM((depth, SLICE, WIDE), B16),
        pltpu.SemaphoreType.DMA((depth, 16)),
        pltpu.SemaphoreType.DMA((depth, 16)),
        pltpu.SemaphoreType.DMA((depth,)),
    ]


class Reduce:
    def __init__(self, columns, away, own, sibs, yrecv, zrecv, ylast, zlast, out, send, recv):
        self.columns, self.away, self.own, self.sibs = columns, away, own, sibs
        self.yrecv, self.zrecv, self.ylast, self.zlast, self.out = yrecv, zrecv, ylast, zlast, out
        self.send, self.recv = send, recv
        self.y, self.zh, self.core, self.t = here()
        y, zh, core = self.y, self.zh, self.core
        self.sib, self.zz = rank(y, zh, 1 - core), rank(y, 1 - zh, core)
        self.ahead = [lax.rem(y + dy, 4) for dy in (1, 2, 3)]
        self.fore = [rank(place, zh, core) for place in self.ahead]
        self.started = []

    def push(self, slot, src, dst, dp):
        copy = remote(src, dst, self.send.at[slot], self.recv.at[slot], dp, self.t)
        copy.start()
        self.started.append(copy)

    def arrive(self, slot, ref):
        remote(ref, ref, self.send.at[slot], self.recv.at[slot], self.sib, self.t).wait_recv()

    def store(self, first, count, cols, block):
        block = block.astype(B16).reshape(count, 2, SHARD, block.shape[-1])
        even = self.core == 0
        chips = pl.ds(first, count)
        self.own[chips, :, cols] = jnp.where(even, block[:, 0], block[:, 1])
        self.away[chips, :, cols] = jnp.where(even, block[:, 1], block[:, 0])

    def to_sibling(self, place):
        pair = pl.ds(place * 2, 2)
        return remote(
            self.away.at[pair, :, pl.ds(0, self.columns)],
            self.sibs.at[pair],
            self.send.at[place],
            self.recv.at[place],
            self.sib,
            self.t,
        )

    def product(self, turned, right, left_columns=0):
        for place in range(4):
            rows = slice(place * 4 * SHARD, (place + 1) * 4 * SHARD)
            for i in range(self.columns // 384):
                cols = slice(384 * i, 384 * i + 384)
                block = dot(turned[rows], right[:, left_columns + 384 * i : left_columns + 384 * i + 384], 1, 0)
                self.store(place * 2, 2, cols, block)

    def send_away(self):
        for place in range(4):
            self.to_sibling(place).start()

    def product_whole(self, left, right):
        for i in range(self.columns // HD):
            cols = slice(HD * i, HD * i + HD)
            self.store(0, 8, cols, dot(left, right[:, cols], 0, 0))
        self.send_away()

    def sent_away(self):
        for place in range(4):
            self.to_sibling(place).wait_send()

    def add(self):
        own, sibs = self.own, self.sibs
        for i, place in enumerate(self.ahead + [self.y]):
            pair = pl.ds(place * 2, 2)
            self.arrive(place, sibs.at[pair])

            def step(step, _, place=place):
                chip = place * 2 + lax.div(step, SHARD // 48)
                rows = pl.ds(pl.multiple_of(lax.rem(step, SHARD // 48) * 48, 16), 48)
                own[chip, rows] = own[chip, rows] + sibs[chip, rows]
                return 0

            lax.fori_loop(0, 2 * SHARD // 48, step, 0)
            if i < 3:
                self.push(4 + i, own.at[pair, pl.ds(0, RLOW)], self.yrecv.at[i], self.fore[i])

    def cross(self):
        for i, place in enumerate(self.ahead + [self.y]):
            block = self.own.at[place * 2 + 1 - self.zh, pl.ds(RLOW, RHIGH)]
            self.push(7 + i, block, self.zrecv.at[place], self.zz)

    def merge(self):
        own, zrecv = self.own, self.zrecv
        for i, place in enumerate(self.ahead + [self.y]):
            self.arrive(7 + i, zrecv.at[place])

            def step(step, _, place=place):
                rows = pl.ds(pl.multiple_of(step * 16, 16), 16)
                mine = pl.ds(pl.multiple_of(step * 16 + RLOW, 16), 16)
                zrecv[place, rows] = zrecv[place, rows] + own[place * 2 + self.zh, mine]
                return 0

            lax.fori_loop(0, RHIGH // 16, step, 0)
            if i < 3:
                self.push(11 + i, zrecv.at[place], self.ylast.at[i], self.fore[i])

    def pool(self):
        for i in range(3):
            self.arrive(4 + i, self.yrecv.at[i])

        def step(step, _):
            chip = lax.div(step, RLOW // 16)
            rows = pl.ds(pl.multiple_of(lax.rem(step, RLOW // 16) * 16, 16), 16)
            total = self.own[self.y * 2 + chip, rows].astype(F32)
            for i in range(3):
                total = total + self.yrecv[i, chip, rows].astype(F32)
            self.own[self.y * 2 + chip, rows] = total.astype(B16)
            return 0

        lax.fori_loop(0, 2 * RLOW // 16, step, 0)
        self.push(14, self.own.at[self.y * 2 + 1 - self.zh, pl.ds(0, RLOW)], self.zlast, self.zz)

    def write(self, rows, total):
        first = 0
        for out in self.out if isinstance(self.out, tuple) else (self.out,):
            out[rows] = total[:, first : first + out.shape[-1]]
            first += out.shape[-1]

    def end(self):
        self.arrive(14, self.zlast)

        def low(step, _):
            rows = pl.ds(pl.multiple_of(step * 16, 16), 16)
            own = self.own[self.y * 2 + self.zh, rows].astype(F32)
            self.write(rows, own + self.zlast[rows].astype(F32))
            return 0

        lax.fori_loop(0, RLOW // 16, low, 0)
        for i in range(3):
            self.arrive(11 + i, self.ylast.at[i])

        def high(step, _):
            rows = pl.ds(pl.multiple_of(step * 16, 16), 16)
            total = self.zrecv[self.y, rows].astype(F32)
            for i in range(3):
                total = total + self.ylast[i, rows].astype(F32)
            self.write(pl.ds(pl.multiple_of(step * 16 + RLOW, 16), 16), total)
            return 0

        lax.fori_loop(0, RHIGH // 16, high, 0)

    def drain(self):
        for copy in self.started:
            copy.wait_send()


def reduce_scratch(columns):
    return [
        pltpu.VMEM((8, SHARD, columns), B16),
        pltpu.VMEM((8, SHARD, columns), B16),
        pltpu.VMEM((3, 2, RLOW, columns), B16),
        pltpu.VMEM((4, RHIGH, columns), B16),
        pltpu.VMEM((3, RHIGH, columns), B16),
        pltpu.VMEM((RLOW, columns), B16),
        pltpu.SemaphoreType.DMA((15,)),
        pltpu.SemaphoreType.DMA((15,)),
    ]


def inverse_rms(signal):
    return lax.rsqrt(jnp.mean(signal * signal, axis=-1, keepdims=True) + EPSILON)


def norm_back(normed, inverse, gain, upstream):
    inner = upstream * (1.0 + gain)
    return inverse * (inner - normed * jnp.mean(inner * normed, axis=-1, keepdims=True))


def half_level(codes, width):
    return codes if width == 0 else jnp.floor(codes * B16(1.0 / STRIDES[width]))


def offset(left, width):
    return 0.0 if width == 0 else 0.5 * jnp.sum(left.astype(F32), axis=-1, keepdims=True)


def unit_owner(micro, width):
    return rank(width, micro, 0)


def rotate(signal, cosine, sine):
    former, latter = signal[:, : HD // 2], signal[:, HD // 2 :]
    return jnp.concatenate([former * cosine - latter * sine, latter * cosine + former * sine], -1)


def unrotate(signal, cosine, sine):
    former, latter = signal[:, : HD // 2], signal[:, HD // 2 :]
    return jnp.concatenate([former * cosine + latter * sine, latter * cosine - former * sine], -1)


def block_scores(queries, keys, first, b, kb):
    scores = lax.dot_general(queries, keys, (((1,), (1,)), ((), ())), preferred_element_type=F32)
    bent = jnp.tanh(scores * (0.0625 / SOFTCAP))
    lane = lax.broadcasted_iota(jnp.int32, (256, 256), 1)
    row = lax.broadcasted_iota(jnp.int32, (256, 256), 0)
    key_place = (16 * kb + (lane & 15)) * 16 + (lane >> 4)
    query_place = (16 * b + (row & 15)) * 16 + (row >> 4)
    allowed = (key_place >= first) & (key_place <= query_place)
    return bent, jnp.where(allowed, SOFTCAP * bent, MASKED)


def block_probs(queries, keys, first, b):
    pieces = [
        block_scores(queries, keys[kb], first, b, kb) for kb in range(max(0, b - 2), b + 1)
    ]
    peak = functools.reduce(
        jnp.maximum, [jnp.max(capped, axis=-1, keepdims=True) for _, capped in pieces]
    )
    exps = [jnp.exp(capped - peak) for _, capped in pieces]
    total = functools.reduce(jnp.add, [jnp.sum(e, axis=-1, keepdims=True) for e in exps])
    return [bent for bent, _ in pieces], [e / total for e in exps]


def dot(left, right, left_dim, right_dim):
    return lax.dot_general(
        left, right, (((left_dim,), (right_dim,)), ((), ())), preferred_element_type=F32
    )


def forward_kernel(*refs):
    (c_query, c_key, c_value, c_out, c_gate, c_up, c_down), refs = refs[:7], refs[7:]
    (tokens, vectors, places, first, rates, cotangent), refs = refs[:6], refs[6:]
    (w_qkv, w_out), refs = refs[:2], refs[2:]
    homes, refs = refs[:13], refs[13:]
    (q_rot, k_rot, v_all, sums, gu_sums), refs = refs[:5], refs[5:]
    kept, refs = refs[:13], refs[13:]
    (att, normed_input, qkv_pre, branch, middle, cosine, sine), (d_part, *late) = kept[:7], kept[7:]
    turned_middle, turned_feed, d_gu_low, hidden, final = late
    (s_qkv, s_gate, s_up, keep_sems), refs = refs[:4], refs[4:]
    shards = (s_qkv, c_out, s_gate, s_up, c_down)
    gains, scale_out, scale_qkv = vectors[0:4], vectors[SCALE_OUT], vectors[SCALE_QKV, : 2 * HD]
    scale_down, scale_gu = vectors[SCALE_DOWN], vectors[SCALE_GU]
    (wq, wo, low, rq, rkv, held, part), refs = refs[:7], refs[7:]
    (held_x, held_z, stage, block, *row_sems), refs = refs[:7], refs[7:]
    (wg, wu, wd, nm, gu_pre, feed_part, cot, d_feed, dgs), refs = refs[:9], refs[9:]
    (held_x_f, held_z_f, stage_f, feed_block, *feed_sems), refs = refs[:7], refs[7:]
    turned, refs = refs[:3], refs[3:]
    (send_g, recv_g, local_g, send, recv_q, recv_kv, send_back, recv_back, local) = refs
    y, zh, core, t = here()
    me = rank(y, zh, core)
    half = lax.rem(t, 2)
    other = t + 1 - 2 * half
    owner = (y < 3) & (core == 0)
    units = [(m, w) for m in range(2) for w in range(3)]
    gathers = [
        Gather(src, out, send_g.at[k], recv_g.at[k], local_g.at[k])
        for k, (src, out) in enumerate(zip(shards, (wq, wo, wg, wu, wd)))
    ]
    g_qkv, g_out, g_gate, g_up, g_down = gathers
    rows = Rows(part, held_x, held_z, stage, block, nm, row_sems)
    feeds = Rows(feed_part, held_x_f, held_z_f, stage_f, feed_block, d_feed, feed_sems, None, turned)
    barrier = pltpu.get_barrier_semaphore()

    def signal(dp, tensor):
        pl.semaphore_signal(barrier, inc=1, device_id=(dp, tensor), device_id_type=MESH)

    plane = [(g_qkv.sib, t), (g_qkv.zz, t)] + [(dp, t) for dp in g_qkv.fore] + rows.peers()
    for device in plane:
        signal(*device)

    @pl.when(owner)
    def _():
        def each(d, _):
            pl.when(d != me)(lambda: signal(d, t))
            signal(d, other)
            return 0

        lax.fori_loop(0, 16, each, 0)

    for m, w in units:
        pl.when(unit_owner(m, w) != me)(functools.partial(signal, unit_owner(m, w), t))

    s_qkv[:, :HD] = c_query[...].astype(B16)
    s_qkv[:, HD : HD + 128] = c_key[...].astype(B16)
    s_qkv[:, HD + 128 :] = c_value[...].astype(B16)
    s_gate[...] = c_gate[...].astype(B16)
    s_up[...] = c_up[...].astype(B16)
    inputs = tokens[...].astype(F32)
    normed_input[...] = (inputs * inverse_rms(inputs) * (1.0 + gains[0:1])).astype(B16)
    keeps = []

    def keep(i, index=None):
        src, dst = (kept[i], homes[i]) if index is None else (kept[i].at[index], homes[i].at[index])
        copy = pltpu.make_async_copy(src, dst, keep_sems.at[len(keeps)])
        copy.start()
        keeps.append(copy)

    @pl.when(owner)
    def _():
        pl.semaphore_wait(barrier, len(plane) + 26)

    @pl.when(jnp.logical_not(owner))
    def _():
        pl.semaphore_wait(barrier, len(plane) + 12)

    g_qkv.start()
    for b in range(4):
        angle = places[:, b : b + 1] * rates[...]
        cosine[b], sine[b] = jnp.cos(angle), jnp.sin(angle)
    g_qkv.over_y()
    g_qkv.over_z()
    g_qkv.near()
    g_out.start()
    g_gate.start()
    g_qkv.far()
    g_qkv.end()

    for i in range(2):
        cols = slice(HD * i, HD * i + HD)
        codes = wq[:, :, cols].reshape(WIDE, HD)
        for w in range(3):
            product = dot(normed_input[...], level(codes, w), 1, 0) * scale_qkv[:, cols]
            qkv_pre[w, :, cols] = product
            low[w, :, :, cols] = product.astype(B16).reshape(2, 64, HD)

    def to_owner(u, m, w, start):
        o = unit_owner(m, w)
        q_src, kv_src = low.at[w, m, :, pl.ds(0, HD)], low.at[w, m, :, pl.ds(HD, HD)]
        across = remote(kv_src, rkv.at[half, me], send.at[u, 2], recv_kv.at[half, me], o, other)
        away = [
            remote(q_src, rq.at[me], send.at[u, 0], recv_q.at[me], o, t),
            remote(kv_src, rkv.at[half, me], send.at[u, 1], recv_kv.at[half, me], o, t),
        ]
        near = [
            pltpu.make_async_copy(q_src, rq.at[me], local.at[0]),
            pltpu.make_async_copy(kv_src, rkv.at[half, me], local.at[1]),
        ]

        @pl.when(o != me)
        def _():
            for copy in away:
                copy.start() if start else copy.wait_send()

        @pl.when(o == me)
        def _():
            for copy in near:
                copy.start() if start else copy.wait()

        across.start() if start else across.wait_send()

    for u, (m, w) in enumerate(units):
        to_owner(u, m, w, True)
    for gather in (g_out, g_gate):
        gather.over_y()
        gather.over_z()

    @pl.when(owner)
    def _():
        for u, (m, w) in enumerate(units):

            @pl.when(unit_owner(m, w) == me)
            def _():
                for i in range(2):
                    ref = (rq.at[me], rkv.at[half, me])[i]
                    pltpu.make_async_copy(ref, ref, local.at[i]).wait()

        def each(d, _):
            @pl.when(d != me)
            def _():
                remote(rq.at[d], rq.at[d], send.at[0, 0], recv_q.at[d], me, other).wait_recv()
                remote(
                    rkv.at[half, d], rkv.at[half, d], send.at[0, 0], recv_kv.at[half, d], me, other
                ).wait_recv()

            remote(
                rkv.at[1 - half, d], rkv.at[1 - half, d], send.at[0, 0], recv_kv.at[1 - half, d], me, other
            ).wait_recv()
            return 0

        lax.fori_loop(0, 16, each, 0)
        for b in range(4):
            rows_b = slice(16 * b, 16 * b + 16)
            c, s = cosine[b], sine[b]
            q = rq[:, rows_b, :].reshape(256, HD).astype(F32)
            q_rot[b] = rotate(q, c, s).astype(B16)
            k = jnp.concatenate(
                [rkv[i, :, rows_b, : HD // 2].reshape(256, HD // 2) for i in range(2)], -1
            )
            k_rot[b] = rotate(k.astype(F32), c, s).astype(B16)
            v_all[b] = jnp.concatenate(
                [rkv[i, :, rows_b, HD // 2 :].reshape(256, HD // 2) for i in range(2)], -1
            )
        for b in range(4):
            keys = {kb: k_rot[kb] for kb in range(max(0, b - 2), b + 1)}
            _, probs = block_probs(q_rot[b], keys, first[:, b : b + 1], b)
            out = sum(
                dot(p.astype(B16), v_all[kb], 1, 0) for p, kb in zip(probs, sorted(keys))
            )
            held[:, 16 * b : 16 * b + 16, :] = out.astype(B16).reshape(16, 16, HD)

        def hand_back(d, start):
            @pl.when(d != me)
            def _():
                copy = remote(
                    held.at[d], att.at[y, zh], send_back.at[d], recv_back.at[zh * 3 + y], d, t
                )
                copy.start() if start else copy.wait_send()

            @pl.when(d == me)
            def _():
                copy = pltpu.make_async_copy(held.at[d], att.at[y, zh], local.at[0])
                copy.start() if start else copy.wait()

        lax.fori_loop(0, 16, lambda d, _: (hand_back(d, True), 0)[1], 0)
        lax.fori_loop(0, 16, lambda d, _: (hand_back(d, False), 0)[1], 0)

    g_out.near()
    g_out.far()
    g_up.start()
    g_out.end()
    g_gate.near()
    for u, (m, w) in enumerate(units):

        @pl.when(unit_owner(m, w) != me)
        def _():
            ref = att.at[w, m]
            remote(ref, ref, send.at[0, 0], recv_back.at[u], me, other).wait_recv()

    codes = wo[...].reshape(WIDE, HD)
    for w in range(3):
        product = dot(att[w].reshape(ROWS, HD), level(codes, w), 1, 1) * scale_out
        part[w] = product.astype(B16).reshape(2, 4, SLICE, WIDE)
        rows.scatter_x(w)
    for i, (src, dst) in enumerate(((wq, w_qkv), (wo, w_out))):
        keeps.append(pltpu.make_async_copy(src, dst, keep_sems.at[i]))
        keeps[i].start()
    for i in (0, 1, 2, 5, 6):
        keep(i)
    load = pltpu.make_async_copy(cotangent.at[:, rows.zl, rows.x], cot, local.at[2])
    load.start()
    g_gate.far()
    g_up.over_y()
    g_up.over_z()
    g_down.start()
    for w in range(3):
        rows.scatter_z(w)
    mine = tokens[pl.ds(pl.multiple_of(t * SLICE, SLICE), SLICE)].astype(F32)
    for w in range(3):
        signal_w = rows.total(w)
        branch[w] = signal_w
        total = mine + signal_w * inverse_rms(signal_w) * (1.0 + gains[1:2])
        middle[w] = total
        block[w] = (total * inverse_rms(total) * (1.0 + gains[2:3])).astype(B16)
        rows.spread(w)
    keep(3)
    keep(4)
    g_up.near()
    for w in range(3):
        rows.forward(w)
    g_down.over_y()
    g_down.over_z()
    g_gate.end()

    def forward(w):
        stride = STRIDES[w]
        left = nm[w].reshape(ROWS, WIDE)
        extra = offset(left, w)
        for k, codes in enumerate((wg, wu)):
            if w == 0 and k == 1:
                g_up.far()
                g_up.end()
            cols = slice(FF * k, FF * k + FF)
            product = dot(left, half_level(codes[...].reshape(WIDE, FF), w), 1, 0)
            gu_pre[w, :, cols] = (product + extra) * (scale_gu[:, cols] * stride)
        gate_pre, up_pre = gu_pre[w, :, :FF], gu_pre[w, :, FF:]
        grown, _ = gelu_parts(gate_pre)
        low = (grown * up_pre).astype(B16)
        hidden[w] = low
        extra_down = offset(low, w)

        if w == 0:
            g_down.near()
            g_down.far()
            g_down.end()
        product = dot(low, half_level(wd[...].reshape(WIDE, FF), w), 1, 1)
        product = (product + extra_down) * (scale_down * stride)
        feed_part[w] = product.astype(B16).reshape(2, 4, SLICE, WIDE)
        feeds.scatter_x(w)

    def norm(w):
        signal = feeds.total(w)
        inverse = inverse_rms(signal)
        normed = signal * inverse
        upstream = cot[w].astype(F32)
        lowered = norm_back(normed, inverse, gains[3:4], upstream).astype(B16)
        feed_block[w] = lowered
        feeds.spread(w)
        final[w] = (middle[w] + normed * (1.0 + gains[3:4])).astype(B16)
        for i, term in enumerate((upstream * normed, lowered.astype(F32) * signal)):
            term = jnp.sum(term, axis=0, keepdims=True)
            sums[i : i + 1] = term if w == 0 else sums[i : i + 1] + term

    def backward(w):
        stride = STRIDES[w]
        lowered = d_feed[w].reshape(ROWS, WIDE)
        turned_feed[:, w * ROWS : (w + 1) * ROWS] = lowered.T
        scaled = (lowered.astype(F32) * scale_down).astype(B16)
        extra = offset(scaled, w)
        for i in range(3):
            cols = slice(384 * i, 384 * i + 384)
            ups = slice(FF + 384 * i, FF + 384 * i + 384)
            d_hidden = (dot(scaled, half_level(wd[:, :, cols].reshape(WIDE, 384), w), 1, 0) + extra) * float(stride)
            grown, rate = gelu_parts(gu_pre[w, :, cols])
            for where, value in ((cols, d_hidden * gu_pre[w, :, ups] * rate), (ups, d_hidden * grown)):
                low = value.astype(B16)
                d_gu_low[w, :, where] = low
                dgs[:, where] = (value * scale_gu[:, where]).astype(B16)
                term = jnp.sum(low.astype(F32) * gu_pre[w, :, where], axis=0, keepdims=True)
                term = term / scale_gu[:, where]
                gu_sums[:, where] = term if w == 0 else gu_sums[:, where] + term
        left = dgs[...]
        extra_gu = offset(left, w)

        keep(10, w)
        keep(9, (slice(None), pl.ds(w * ROWS, ROWS)))
        product = sum(
            dot(left[:, FF * k : FF * k + FF], half_level(codes[...].reshape(WIDE, FF), w), 1, 1)
            for k, codes in enumerate((wg, wu))
        )
        product = (product + extra_gu) * float(stride)
        d_part[w] = product.astype(B16).reshape(2, 4, SLICE, WIDE)
        keep(7, w)

    rows.end(0)
    forward(0)
    rows.end(1)
    forward(1)
    feeds.scatter_z(0)
    rows.end(2)
    forward(2)
    load.wait()
    feeds.scatter_z(1)
    norm(0)
    feeds.scatter_z(2)
    norm(1)
    feeds.forward(0)
    norm(2)
    feeds.forward(1)
    for w in range(3):
        turned_middle[:, w * ROWS : (w + 1) * ROWS] = nm[w].reshape(ROWS, WIDE).T
    for i in (8, 11, 12):
        keep(i)
    feeds.end(0)
    backward(0)
    feeds.forward(2)
    feeds.end(1)
    backward(1)
    feeds.end(2)
    backward(2)
    for copy in keeps:
        copy.wait()
    for u, (m, w) in enumerate(units):
        o = unit_owner(m, w)

        @pl.when(o != me)
        def _():
            for slot, src in enumerate((low.at[w, m, :, pl.ds(0, HD)], low.at[w, m, :, pl.ds(HD, HD)])):
                remote(src, src, send.at[u, slot], recv_q.at[0], o, t).wait_send()

        src = low.at[w, m, :, pl.ds(HD, HD)]
        remote(src, src, send.at[u, 2], recv_q.at[0], o, other).wait_send()
    rows.drain()
    feeds.drain()
    for gather in gathers:
        gather.drain()


KEPT = (
    ((3, 2, 64, HD), B16),
    ((ROWS, WIDE), B16),
    ((3, ROWS, 2 * HD), F32),
    ((3, SLICE, WIDE), F32),
    ((3, SLICE, WIDE), F32),
    ((4, 256, HD // 2), F32),
    ((4, 256, HD // 2), F32),
    ((3, 2, 4, SLICE, WIDE), B16),
    ((WIDE, 3 * ROWS), B16),
    ((WIDE, 3 * ROWS), B16),
    ((3, ROWS, 2 * FF), B16),
    ((3, ROWS, FF), B16),
    ((3, SLICE, WIDE), B16),
)


def forward_pass(*operands):
    return pl.pallas_call(
        forward_kernel,
        name="forward",
        out_shape=[struct((16, SHARD, 2 * HD), B16), struct((16, SHARD, HD), B16)]
        + [struct(*kept) for kept in KEPT]
        + [struct((4, 256, HD), B16)] * 3
        + [struct((8, WIDE), F32), struct((1, 2 * FF), F32)],
        in_specs=vmem_space(len(operands) - 1) + any_space(1),
        out_specs=any_space(15) + vmem_space(5),
        scratch_shapes=[pltpu.VMEM(*kept) for kept in KEPT]
        + [
            pltpu.VMEM((SHARD, 2 * HD), B16),
            pltpu.VMEM((SHARD, FF), B16),
            pltpu.VMEM((SHARD, FF), B16),
            pltpu.SemaphoreType.DMA((21,)),
        ]
        + [
            pltpu.VMEM((16, SHARD, 2 * HD), B16),
            pltpu.VMEM((16, SHARD, HD), B16),
            pltpu.VMEM((3, 2, 64, 2 * HD), B16),
            pltpu.VMEM((16, 64, HD), B16),
            pltpu.VMEM((2, 16, 64, HD), B16),
            pltpu.VMEM((16, 64, HD), B16),
            pltpu.VMEM((3, 2, 4, SLICE, WIDE), B16),
        ]
        + rows_scratch(3)
        + [pltpu.VMEM((16, SHARD, FF), B16)] * 3
        + [
            pltpu.VMEM((3, 2, 4, SLICE, WIDE), B16),
            pltpu.VMEM((3, ROWS, 2 * FF), F32),
            pltpu.VMEM((3, 2, 4, SLICE, WIDE), B16),
            pltpu.VMEM((3, SLICE, WIDE), B16),
            pltpu.VMEM((3, 2, 4, SLICE, WIDE), B16),
            pltpu.VMEM((ROWS, 2 * FF), B16),
        ]
        + rows_scratch(3)
        + turned_scratch(1152)
        + [
            pltpu.SemaphoreType.DMA((5, 29)),
            pltpu.SemaphoreType.DMA((5, 29)),
            pltpu.SemaphoreType.DMA((5,)),
            pltpu.SemaphoreType.DMA((6, 3)),
            pltpu.SemaphoreType.DMA((16,)),
            pltpu.SemaphoreType.DMA((2, 16)),
            pltpu.SemaphoreType.DMA((16,)),
            pltpu.SemaphoreType.DMA((6,)),
            pltpu.SemaphoreType.DMA((3,)),
        ],
        compiler_params=params(3),
    )(*operands)


GRADIENTS = (1152, 1152, 1152, HD, 2 * HD)


def back_kernel(*refs):
    (part, cotangent), refs = refs[:2], refs[2:]
    sources, refs = refs[:13], refs[13:]
    (turned_middle, d_gu, middle, branch, final, feed_sums, gu_sums, vectors, first), refs = refs[:9], refs[9:]
    (results, gradient, totals), refs = refs[:3], refs[3:]
    (g_query, g_key, g_value), outs, refs = refs[4:7], refs[:4], refs[7:]
    outs = (*outs, (g_query, g_key, g_value))
    gains, scale_out, scale_down = vectors[0:4], vectors[SCALE_OUT], vectors[SCALE_DOWN]
    scale_qkv = vectors[SCALE_QKV, : 2 * HD]
    aways, refs = refs[:2], refs[2:]
    reduces = []
    for k, columns in enumerate(GRADIENTS):
        held, refs = refs[:8], refs[8:]
        away = aways[k % 2]
        reduces.append(Reduce(columns, away, *held[:6], outs[k], *held[6:]))
    g_gate, g_up, g_down, g_out, g_qkv = reduces
    (own_part, cot, d_branch), refs = refs[:3], refs[3:]
    (held_x, held_z, stage, block, *row_sems), refs = refs[:7], refs[7:]
    (part_in, held_x1, held_z1, stage1, block1, *row_sems1), refs = refs[:8], refs[8:]
    result_sems, refs = refs[:3], refs[3:]
    (vec_x, vec_z, vec_sib, vec_y, vec_zz, vec, send_v, recv_v), refs = refs[:8], refs[8:]
    (datt, rdo, held_q, held_kv, acc_k, acc_v, d_query, d_kv), refs = refs[:8], refs[8:]
    (send, recv, send_q, send_kv, recv_q, recv_kv, local), refs = refs[:7], refs[7:]
    places, load_sems = refs[:13], refs[13]
    (turned_feed, hidden, w_out, w_qkv, attended, q_rot, k_rot, v_all, cosine, sine), refs = places[:10], places[10:]
    normed_input, tokens, qkv_pre = refs
    arrivals = [
        pltpu.make_async_copy(src, dst, load_sems.at[i])
        for i, (src, dst) in enumerate(zip(sources, places))
    ]
    for copy in arrivals:
        copy.start()
    y, zh, core, t = here()
    me = rank(y, zh, core)
    half = lax.rem(t, 2)
    other = t + 1 - 2 * half
    owner = (y < 3) & (core == 0)
    units = [(m, w) for m in range(2) for w in range(3)]
    rows = Rows(part, held_x, held_z, stage, block, d_branch, row_sems, own_part)
    rows_in = Rows(part_in, held_x1, held_z1, stage1, block1, gradient, row_sems1)
    rows_out = Rows(None, None, None, None, final, results, result_sems)
    barrier = pltpu.get_barrier_semaphore()

    def signal(dp, tensor):
        pl.semaphore_signal(barrier, inc=1, device_id=(dp, tensor), device_id_type=MESH)

    plane = [(g_gate.sib, t), (g_gate.zz, t)] + [(dp, t) for dp in g_gate.fore] + rows.peers()
    for device in plane:
        signal(*device)

    @pl.when(owner)
    def _():
        def each(d, _):
            pl.when(d != me)(lambda: signal(d, t))
            return 0

        lax.fori_loop(0, 16, each, 0)

    for m, w in units:
        pl.when(unit_owner(m, w) != me)(functools.partial(signal, unit_owner(m, w), t))
        signal(unit_owner(m, w), other)

    g_gate.product(turned_middle, d_gu)

    @pl.when(owner)
    def _():
        pl.semaphore_wait(barrier, len(plane) + 36)

    @pl.when(jnp.logical_not(owner))
    def _():
        pl.semaphore_wait(barrier, len(plane) + 6)

    for w in range(3):
        rows.scatter_x(w)
    loads = [
        pltpu.make_async_copy(part.at[:, :, rows.x], own_part, local.at[0]),
        pltpu.make_async_copy(cotangent.at[:, rows.zl, rows.x], cot, local.at[1]),
    ]
    for copy in loads:
        copy.start()
    g_gate.send_away()
    g_up.product(turned_middle, d_gu, 1152)
    g_up.send_away()
    g_gate.add()
    for copy in loads:
        copy.wait()
    rows.scatter_z(0)
    g_gate.sent_away()
    for copy in arrivals[:2]:
        copy.wait()
    g_down.product(turned_feed, hidden)
    g_down.send_away()
    rows.scatter_z(1)
    g_up.add()
    rows.scatter_z(2)
    d_middle = jnp.zeros((SLICE, WIDE), F32)
    sums = [jnp.zeros((1, WIDE), F32)] * 3
    for w in range(3):
        upstream = rows.total(w)
        signal_w = middle[w]
        inverse = inverse_rms(signal_w)
        normed = signal_w * inverse
        d_signal = cot[w].astype(F32) + norm_back(normed, inverse, gains[2:3], upstream)
        lower = branch[w]
        inverse_lower = inverse_rms(lower)
        normed_lower = lower * inverse_lower
        lowered = norm_back(normed_lower, inverse_lower, gains[1:2], d_signal).astype(B16)
        block[w] = lowered
        rows.spread(w)
        d_middle = d_middle + d_signal
        terms = (d_signal * normed_lower, upstream * normed, lowered.astype(F32) * lower)
        sums = [old + jnp.sum(new, axis=0, keepdims=True) for old, new in zip(sums, terms)]
    vec[1:2] = sums[0]
    vec[2:3] = sums[1]
    vec[3:4] = feed_sums[0:1]
    vec[4:5] = sums[2] / scale_out
    vec[5:6] = feed_sums[1:2] / scale_down

    for copy in arrivals[2:]:
        copy.wait()
    codes = w_out[...].reshape(WIDE, HD)

    def to_owner(u, m, w, start):
        o = unit_owner(m, w)
        src = datt.at[w, m]

        @pl.when(o != me)
        def _():
            copy = remote(src, rdo.at[me], send.at[u], recv.at[me], o, t)
            copy.start() if start else copy.wait_send()

        @pl.when(o == me)
        def _():
            copy = pltpu.make_async_copy(src, rdo.at[me], local.at[0])
            copy.start() if start else copy.wait()

    g_gate.cross()
    g_gate.pool()
    for w in range(3):
        rows.forward(w)
    for w in range(3):
        rows.end(w)
        scaled = (d_branch[w].reshape(ROWS, WIDE).astype(F32) * scale_out).astype(B16)
        datt[w] = dot(scaled, level(codes, w), 1, 0).astype(B16).reshape(2, 64, HD)
        for m in range(2):
            to_owner(m * 3 + w, m, w, True)
    g_up.cross()
    g_down.add()
    for w in range(3):
        rows_out.spread(w)
    for u, (m, w) in enumerate(units):
        to_owner(u, m, w, False)

    @pl.when(owner)
    def _():
        def each(d, _):
            @pl.when(d != me)
            def _():
                remote(rdo.at[d], rdo.at[d], send.at[0], recv.at[d], me, other).wait_recv()

            return 0

        lax.fori_loop(0, 16, each, 0)
        acc_k[...] = jnp.zeros_like(acc_k)
        acc_v[...] = jnp.zeros_like(acc_v)
        for b in range(4):
            rows_b = slice(16 * b, 16 * b + 16)
            blocks = list(range(max(0, b - 2), b + 1))
            queries = q_rot[b]
            keys = {kb: k_rot[kb] for kb in blocks}
            upstream = rdo[:, rows_b, :].reshape(256, HD)
            bents, probs = block_probs(queries, keys, first[:, b : b + 1], b)
            d_probs = [dot(upstream, v_all[kb], 1, 1) for kb in blocks]
            centre = sum(
                jnp.sum(p * dp, axis=-1, keepdims=True) for p, dp in zip(probs, d_probs)
            )
            d_q = jnp.zeros((256, HD), F32)
            for kb, bent, p, dp in zip(blocks, bents, probs, d_probs):
                d_scores = (p * (dp - centre) * (1.0 - bent * bent)).astype(B16)
                d_q = d_q + dot(d_scores, keys[kb], 1, 0)
                acc_k[kb] += dot(d_scores, queries, 0, 0)
                acc_v[kb] += dot(p.astype(B16), upstream, 0, 0)
            d_q = unrotate(d_q * 0.0625, cosine[b], sine[b])
            held_q[:, rows_b, :] = d_q.astype(B16).reshape(16, 16, HD)
        for b in range(4):
            rows_b = slice(16 * b, 16 * b + 16)
            d_k = unrotate(acc_k[b] * 0.0625, cosine[b], sine[b]).astype(B16)
            d_v = acc_v[b].astype(B16)
            for i in range(2):
                cols = slice(128 * i, 128 * i + 128)
                held_kv[i, :, rows_b, :128] = d_k[:, cols].reshape(16, 16, 128)
                held_kv[i, :, rows_b, 128:] = d_v[:, cols].reshape(16, 16, 128)

    def hand_back(d, start):
        u = zh * 3 + y
        across = remote(
            held_kv.at[1 - half, d], d_kv.at[half, y, zh], send_kv.at[1, d], recv_kv.at[half, u], d, other
        )
        across.start() if start else across.wait_send()

        @pl.when(d != me)
        def _():
            for copy in (
                remote(held_q.at[d], d_query.at[y, zh], send_q.at[d], recv_q.at[u], d, t),
                remote(
                    held_kv.at[half, d], d_kv.at[half, y, zh], send_kv.at[0, d], recv_kv.at[half, u], d, t
                ),
            ):
                copy.start() if start else copy.wait_send()

        @pl.when(d == me)
        def _():
            for copy in (
                pltpu.make_async_copy(held_q.at[d], d_query.at[y, zh], local.at[0]),
                pltpu.make_async_copy(held_kv.at[half, d], d_kv.at[half, y, zh], local.at[1]),
            ):
                copy.start() if start else copy.wait()

    @pl.when(owner)
    def _():
        lax.fori_loop(0, 16, lambda d, _: (hand_back(d, True), 0)[1], 0)
        lax.fori_loop(0, 16, lambda d, _: (hand_back(d, False), 0)[1], 0)

    for w in range(3):
        rows_out.forward(w)
    g_down.cross()
    g_up.sent_away()
    g_out.product_whole(d_branch[...].reshape(3 * ROWS, WIDE), attended[...])
    g_gate.merge()
    g_up.pool()
    g_out.add()
    g_out.cross()
    g_up.merge()
    for u, (m, w) in enumerate(units):

        @pl.when(unit_owner(m, w) != me)
        def _():
            ref = d_query.at[w, m]
            remote(ref, ref, send.at[0], recv_q.at[u], me, other).wait_recv()
            ref = d_kv.at[half, w, m]
            remote(ref, ref, send.at[0], recv_kv.at[half, u], me, other).wait_recv()

        ref = d_kv.at[1 - half, w, m]
        remote(ref, ref, send.at[0], recv_kv.at[1 - half, u], me, other).wait_recv()

    codes = w_qkv[...].reshape(WIDE, 2 * HD)
    scaled = []
    qkv_sums = jnp.zeros((1, 2 * HD), F32)
    d_qkv_all = jnp.zeros((ROWS, 2 * HD), F32)
    for w in range(3):
        both = (d_kv[0, w].astype(F32) + d_kv[1, w].astype(F32)).astype(B16).astype(F32)
        d_qkv = jnp.concatenate([d_query[w].astype(F32), both], -1).reshape(ROWS, 2 * HD)
        qkv_sums = qkv_sums + jnp.sum(d_qkv * qkv_pre[w], axis=0, keepdims=True)
        d_qkv_all = d_qkv_all + d_qkv
        scaled.append((d_qkv * scale_qkv).astype(B16))
    whole = tokens[...].astype(F32)
    inverse = inverse_rms(whole)
    for i in range(3):
        tile = slice(768 * i, 768 * i + 768)
        d_input = sum(dot(scaled[w], level(codes[tile], w), 1, 1) for w in range(3))
        part_in[0, :, :, :, tile] = d_input.astype(B16).reshape(2, 4, SLICE, 768)
        normed = tokens[:, tile].astype(F32) * inverse
        vec[0:1, tile] = jnp.sum(d_input * normed, axis=0, keepdims=True)
    rows_in.scatter_x(0)

    vec[6:8] = jnp.zeros((2, WIDE), F32)
    x = rows.x
    copies = []

    def exchange(slot, src, dst, dp, tensor):
        copy = remote(src, dst, send_v.at[slot], recv_v.at[slot], dp, tensor)
        copy.start()
        copies.append(copy)

    def exchanged(slot, ref):
        remote(ref, ref, send_v.at[slot], recv_v.at[slot], me, other).wait_recv()

    vec_x[x] = vec[...]
    for k in range(3):
        exchange(k, vec_x.at[x], vec_x.at[x], me, rows.x_peers[k])
    g_down.sent_away()
    g_qkv.product_whole(normed_input[...], d_qkv_all.astype(B16))
    for k in range(3):
        exchanged(k, vec_x.at[rows.behind[k]])
    vec[...] = functools.reduce(jnp.add, [vec_x[i] for i in range(4)])
    exchange(3, vec, vec_z, me, rows.z_peer)
    rows_in.scatter_z(0)
    g_qkv.add()
    g_qkv.cross()
    g_down.pool()
    g_down.merge()
    exchanged(3, vec_z)
    copies[3].wait_send()
    vec[0:6] = vec[0:6] + vec_z[0:6]
    vec[6:7] = gu_sums[...]
    vec[7:8, : 2 * HD] = qkv_sums / scale_qkv
    exchange(4, vec, vec_sib, g_gate.sib, t)

    upstream = rows_in.total(0)
    signal_in = tokens[pl.ds(pl.multiple_of(t * SLICE, SLICE), SLICE)].astype(F32)
    inverse = inverse_rms(signal_in)
    normed = norm_back(signal_in * inverse, inverse, gains[0:1], upstream)
    block1[0] = (d_middle + normed).astype(B16)
    rows_in.spread(0)
    g_qkv.merge()
    g_qkv.pool()
    exchanged(4, vec_sib)
    vec_y[y] = vec[...] + vec_sib[...]
    for i in range(3):
        exchange(5 + i, vec_y.at[y], vec_y.at[y], g_gate.fore[i], t)
    rows_in.forward(0)
    g_out.merge()
    g_out.pool()
    g_gate.end()
    g_up.end()
    for i in range(3):
        exchanged(5 + i, vec_y.at[lax.rem(y + 3 - i, 4)])
    copies[4].wait_send()
    vec[...] = functools.reduce(jnp.add, [vec_y[i] for i in range(4)])
    exchange(8, vec, vec_zz, g_gate.zz, t)
    g_down.end()
    g_out.end()
    g_qkv.end()
    exchanged(8, vec_zz)
    totals[...] = vec[...] + vec_zz[...]
    rows_in.end(0)
    for w in range(3):
        rows_out.end(w)
    g_out.sent_away()
    g_qkv.sent_away()
    for k in (0, 1, 2, 5, 6, 7, 8):
        copies[k].wait_send()
    for part_of in (rows, rows_in, rows_out, *reduces):
        part_of.drain()


def back(hbm, late, vmem):
    def vec():
        return pltpu.VMEM((8, WIDE), F32)

    scratch = [pltpu.VMEM((8, SHARD, 1152), B16)] * 2
    for columns in GRADIENTS:
        scratch += reduce_scratch(columns)
    scratch += [
        pltpu.VMEM((3, 2, SLICE, WIDE), B16),
        pltpu.VMEM((3, SLICE, WIDE), B16),
        pltpu.VMEM((3, 2, 4, SLICE, WIDE), B16),
    ]
    scratch += rows_scratch(3)
    scratch += [pltpu.VMEM((1, 2, 4, SLICE, WIDE), B16)] + rows_scratch(1)
    scratch += rows_scratch(3)[4:]
    scratch += [pltpu.VMEM((4, 8, WIDE), F32), vec(), vec(), pltpu.VMEM((4, 8, WIDE), F32), vec(), vec()]
    scratch += [pltpu.SemaphoreType.DMA((9,))] * 2
    scratch += [
        pltpu.VMEM((3, 2, 64, HD), B16),
        pltpu.VMEM((16, 64, HD), B16),
        pltpu.VMEM((16, 64, HD), B16),
        pltpu.VMEM((2, 16, 64, HD), B16),
        pltpu.VMEM((4, 256, HD), F32),
        pltpu.VMEM((4, 256, HD), F32),
        pltpu.VMEM((3, 2, 64, HD), B16),
        pltpu.VMEM((2, 3, 2, 64, HD), B16),
        pltpu.SemaphoreType.DMA((6,)),
        pltpu.SemaphoreType.DMA((16,)),
        pltpu.SemaphoreType.DMA((16,)),
        pltpu.SemaphoreType.DMA((2, 16)),
        pltpu.SemaphoreType.DMA((6,)),
        pltpu.SemaphoreType.DMA((2, 6)),
        pltpu.SemaphoreType.DMA((2,)),
    ]
    scratch += [pltpu.VMEM(array.shape, array.dtype) for array in late]
    scratch += [pltpu.SemaphoreType.DMA((len(late),))]
    return pl.pallas_call(
        back_kernel,
        name="back",
        out_shape=[
            struct((3, 2, 4, SLICE, WIDE), B16),
            struct((1, 2, 4, SLICE, WIDE), B16),
            struct((8, WIDE), F32),
        ]
        + [struct((SHARD, columns), F32) for columns in (1152, 1152, 1152, HD, HD, 128, 128)],
        in_specs=any_space(len(hbm) + len(late)) + vmem_space(len(vmem)),
        out_specs=any_space(2) + vmem_space(8),
        scratch_shapes=scratch,
        compiler_params=params(4),
    )(*hbm, *late, *vmem)


def level(codes, width):
    if width == 0:
        return codes
    stride = STRIDES[width]
    return jnp.floor(codes * B16(1.0 / stride)) * B16(stride) + B16(stride // 2)


def gelu_parts(value):
    slope = 0.7978845608028654
    inner = jnp.tanh(slope * (value + 0.044715 * value * value * value))
    grown = 0.5 * value * (1.0 + inner)
    rate = 0.5 * (1.0 + inner) + 0.5 * value * (1.0 - inner * inner) * slope * (
        1.0 + 3 * 0.044715 * value * value
    )
    return grown, rate


def side_by_side(*parts):
    total, first = 0.0, 0
    for part in parts:
        total = total + jnp.pad(part, (first, WIDE - first - part.shape[0]))
        first += part.shape[0]
    return total


def body(
    tokens,
    cotangent,
    segments,
    codes_query,
    codes_key,
    codes_value,
    codes_out,
    codes_gate,
    codes_up,
    codes_down,
    query_column_scale,
    key_column_scale,
    value_column_scale,
    output_column_scale,
    gate_column_scale,
    up_column_scale,
    down_column_scale,
    gain_first,
    gain_second,
    gain_third,
    gain_fourth,
):
    z_hi = lax.rem(lax.div(lax.axis_index("dp"), 2), 2)
    tokens = tokens.reshape(ROWS, WIDE)
    cotangent = cotangent.reshape(3, ROWS, WIDE)
    entries = [gain_first, gain_second, gain_third, gain_fourth, output_column_scale, down_column_scale]
    entries += [side_by_side(gate_column_scale, up_column_scale)]
    entries += [side_by_side(query_column_scale, key_column_scale, value_column_scale)]
    row = lax.broadcasted_iota(jnp.int32, (8, WIDE), 0)
    vectors = functools.reduce(
        lambda rest, i: jnp.where(row == i, entries[i][None], rest), range(7), entries[7][None]
    )
    documents = lax.dynamic_index_in_dim(segments, z_hi, 0, False)
    starts = jnp.sum((documents[None, :] < documents[:, None]).astype(jnp.int32), axis=1)
    place = jnp.arange(1024, dtype=jnp.int32)

    def blocked(rows):
        return rows.reshape(4, 16, 16).transpose(0, 2, 1).reshape(4, 256)

    first = blocked(starts).T
    expo = jnp.arange(HD // 2, dtype=F32) * (2.0 / HD)
    rates = jnp.power(ROPE_BASE, -expo)[None]

    grid = (3, 2, 4, SLICE, WIDE)
    w_qkv, w_out, attended, normed_input, qkv_pre, branch, middle, cosine, sine, *rest = forward_pass(
        codes_query,
        codes_key,
        codes_value,
        codes_out.astype(B16).T,
        codes_gate,
        codes_up,
        codes_down.astype(B16).T,
        tokens,
        vectors,
        blocked(place - starts).astype(F32).T,
        first,
        rates,
        cotangent.reshape(grid),
    )
    d_part, turned_middle, turned_feed, d_gu, hidden, final, *rest = rest
    q_rot, k_rot, v_all, feed_sums, gu_sums = rest
    flat = (3 * ROWS, -1)
    results, input_gradient, totals, g_gate, g_up, g_down, g_out, g_query, g_key, g_value = back(
        [d_part, cotangent.reshape(grid)],
        [
            turned_feed,
            hidden.reshape(flat),
            w_out,
            w_qkv,
            attended.reshape(flat),
            q_rot,
            k_rot,
            v_all,
            cosine,
            sine,
            normed_input,
            tokens,
            qkv_pre,
        ],
        [turned_middle, d_gu.reshape(flat), middle, branch, final, feed_sums, gu_sums, vectors, first],
    )
    rows = lax.dynamic_slice_in_dim(totals, lax.axis_index("dp") * SHARD, SHARD, 1)
    return (
        results.reshape(3, 2, 64, 1, WIDE),
        input_gradient.astype(F32).reshape(2, 64, 1, WIDE),
        g_query,
        g_key,
        g_value,
        g_out.T,
        g_gate,
        g_up,
        g_down.T,
        totals[7, :256],
        totals[7, 256:384],
        totals[7, 384:512],
        rows[4],
        totals[6, :FF],
        totals[6, FF:],
        rows[5],
        rows[0],
        rows[1],
        rows[2],
        rows[3],
    )


def solution(mesh):
    matrix, turned = P("dp", "tensor"), P("tensor", "dp")
    columns, whole, shard = P("tensor"), P(), P("dp")
    in_specs = (
        P(None, None, "dp", None),
        P(None, None, None, "dp", None),
        whole,
        *(matrix, matrix, matrix, turned, matrix, matrix, turned),
        *(columns, columns, columns, whole, columns, columns, whole),
        *(whole, whole, whole, whole),
    )
    out_specs = (
        P(None, None, None, "dp", None),
        P(None, None, "dp", None),
        *(matrix, matrix, matrix, turned, matrix, matrix, turned),
        *(columns, columns, columns, shard, columns, columns, shard),
        *(shard, shard, shard, shard),
    )
    return jax.shard_map(body, mesh=mesh, in_specs=in_specs, out_specs=out_specs, check_vma=False)
```
